256 devices in a mesh: seq: 32 (over x, z), exp: 8 (over y, core).
Axes of the slice: x: 4, y: 4, z: 8, core: 2. Of those that a mesh axis runs over, the one named last changes fastest.
Arguments:
- x_att: bfloat16 [16384, 2048], P('seq'), may hold values from -200 to 200
- w_qk: bfloat16 [2048, 2048], P(None, 'exp'), may hold values from -1.5 to 1.5
- w_val: bfloat16 [2048, 2048], P(None, 'exp'), may hold values from -0.125 to 0.125
- w_out: bfloat16 [2048, 2048], P('exp'), may hold values from -0.125 to 0.125
- perms: int32 [2, 16384], replicated, may hold values from 0 to 16383, as said below
- tokens_b: bfloat16 [16384, 2048], P('seq'), may hold values from -6 to 6
- expert_ids: int32 [16384, 1], P('seq'), may hold values from 0 to 63; in each aligned block of 512 rows (0 to 511, 512 to 1023, ...) at most 16 rows name the same one
- w_gate: bfloat16 [64, 2048, 2048], P('seq', None, 'exp'), may hold values from -0.125 to 0.125
- w_up: bfloat16 [64, 2048, 2048], P('seq', None, 'exp'), may hold values from -0.125 to 0.125
- w_down: bfloat16 [64, 2048, 2048], P('seq', 'exp'), may hold values from -0.125 to 0.125
Outputs:
- attended: bfloat16 [16384, 2048], P('seq', 'exp')
- mixed: bfloat16 [16384, 2048], P('seq', 'exp')
The draws below stay inside these ranges and needn't reach their ends.
Inputs may be any that keep to these rules, and one draw needn't show every extreme that they name: `perms`: each row is a permutation of the token indices; the 512 sorted positions of every aligned block of 512 hold exactly 16 tokens of every aligned block of 512 token indices. `expert_ids`: in the 512 rows of one index of seq no expert is named by more than 16 rows; in every draw some expert is named by exactly 16 of them.
All inputs are finite; a program needn't handle non-finite values.
Results may differ from the reference program's by a relative error of at most 0.035.
Values may be sent and summed in bfloat16 or wider, within the bound.
No kernel may reach another device: no remote copies, remote signals or barrier semaphores. Data moves between devices by JAX's collectives and lax.ppermute only.
A program may use at most 128 MiB of HBM per device.

```python
import math
import jax
import jax.numpy as jnp
import numpy as np
from jax import lax

D = 2048
HEADS = 16
HEAD_DIM = 128
BLOCK_LEN = 64
ROUNDS = 2
FF = 2048
TOK_DEV = 512
TOKB = 512
SEQ_LEN = 16384
TOKENS_B = 16384
EXPERTS = 64
CAP = 16
N_SEQ = 32


def balanced_orders(key):
    key = jax.random.fold_in(key, 11)
    block_count = SEQ_LEN // TOK_DEV
    per_peer = TOK_DEV // block_count
    orders = []
    for round_no in range(ROUNDS):
        inner = jax.random.fold_in(key, round_no)
        spread_keys = jax.random.split(jax.random.fold_in(inner, 1), block_count)
        spread = jax.vmap(lambda sub_key: jax.random.permutation(sub_key, TOK_DEV))(spread_keys).astype(jnp.int32)
        token_ids = spread + (jnp.arange(block_count, dtype=jnp.int32) * TOK_DEV)[:, None]
        token_ids = token_ids.reshape(block_count, block_count, per_peer)
        arriving = jnp.transpose(token_ids, (1, 0, 2)).reshape(block_count, TOK_DEV)
        mix_keys = jax.random.split(jax.random.fold_in(inner, 2), block_count)
        mixing = jax.vmap(lambda sub_key: jax.random.permutation(sub_key, TOK_DEV))(mix_keys).astype(jnp.int32)
        arranged = jnp.take_along_axis(arriving, mixing, axis=1)
        orders.append(arranged.reshape(SEQ_LEN))
    return jnp.stack(orders).astype(jnp.int32)


def draw_perms(key, part):
    return balanced_orders(key)


def draw_x_att(key, part):
    key = jax.random.fold_in(key, 3)
    values = jnp.clip(jax.random.normal(jax.random.fold_in(key, 1), (SEQ_LEN, D)), -6.0, 6.0)
    return values.astype(jnp.bfloat16)


def block_levels(stream_key, dims, pieces, low, largest):
    gain, own = 1.0, jax.random.fold_in(stream_key, 6)
    for dim, shards_of in pieces:
        heights = jnp.exp(jax.random.uniform(jax.random.fold_in(own, dim), (shards_of,), jnp.float32, low / len(pieces), largest / len(pieces)))
        gain = gain * jnp.repeat(heights, dims[dim] // shards_of).reshape([-1 if axis == dim else 1 for axis in range(len(dims))])
    return gain


def shared_out(stream_key, own, number, rows, amount, top, reach, slope):
    sequence = jax.random.permutation(stream_key, amount)
    packed, usual = load_shares(amount, rows * top, reach, slope, True), load_shares(amount, rows * top, reach, slope, False)
    places = jnp.arange(amount)

    def named(sizes, turn):
        used = int((sizes > 0).sum())
        fixed = max(1, used // 4)
        passed = fixed + (places - fixed + turn * (used - fixed)) % max(1, amount - fixed)
        return jnp.zeros((amount,), jnp.int32).at[sequence[jnp.where(places < fixed, places, passed)]].set(jnp.asarray(sizes, jnp.int32))

    sizes = jnp.where(number % 4 == 0, named(packed, number // 4), named(usual, number - number // 4 - 1))
    mixed = jax.random.permutation(jax.random.fold_in(own, 3), amount)
    donor, taker = mixed[0:amount // 2 * 2:2], mixed[1:amount // 2 * 2:2]
    margin = jnp.minimum(sizes[donor] - 1, reach - sizes[taker]) // 2
    margin = jnp.where((donor == sequence[0]) | (taker == sequence[0]) | (sizes[taker] == 0), 0, jnp.maximum(margin, 0))
    passed = jax.random.randint(jax.random.fold_in(own, 4), (amount // 2,), 0, 1 << 20) % (margin + 1)
    sizes = sizes.at[donor].add(-passed).at[taker].add(passed)
    labels = jnp.searchsorted(jnp.cumsum(sizes), jnp.arange(rows * top), side="right").astype(jnp.int32)
    table = labels.reshape(top, rows).T
    table = table[jax.random.permutation(jax.random.fold_in(own, 1), rows)]
    turn = jax.random.randint(jax.random.fold_in(own, 2), (rows, 1), 0, top)
    return jnp.take_along_axis(table, (jnp.arange(top)[None, :] + turn) % top, axis=1)


def load_shares(count, total, limit, skew, full):
    loads = [(1 << 20) // math.isqrt(rank ** skew) + 1 for rank in range(1, count + 1)]
    largest = limit if full else min(limit, max(-(-total // count), total * loads[0] // sum(loads)))
    least = 1 if total - largest >= count - 1 else 0
    holding, surplus = [largest] + [least] * (count - 1), total - largest - least * (count - 1)
    while surplus > 0:
        candidates = [i for i in range(1, count) if holding[i] < largest] or [i for i in range(1, count) if holding[i] < limit]
        pool, remaining = sum([loads[i] for i in candidates]), surplus
        for i in candidates:
            more = min(limit - holding[i], max(1, remaining * loads[i] // pool), surplus)
            holding[i] = holding[i] + more
            surplus = surplus - more
    return np.array(holding)


def bell_draw(own_key, dims, deviation, bound, cuts=(), kind=jnp.bfloat16):
    drawn = deviation * jax.random.normal(own_key, dims, jnp.float32)
    if cuts:
        drawn = drawn * block_levels(own_key, dims, cuts, -0.22, 0.18)
    return jnp.clip(drawn, -bound, bound).astype(kind)


def setup_inputs(seed: int = 0) -> dict:
    key_of = jax.random.split(jax.random.key(seed), 11)
    x_att = draw_x_att(jax.random.fold_in(key_of[10], 71), 0)
    w_qk = bell_draw(key_of[1], (D, HEADS * HEAD_DIM), (D // HEAD_DIM) ** -0.5, 1.5, ((1, 8),))
    w_val = bell_draw(key_of[2], (D, HEADS * HEAD_DIM), D ** -0.5, 0.125, ((1, 8),))
    w_out = bell_draw(key_of[3], (HEADS * HEAD_DIM, D), (HEADS * HEAD_DIM) ** -0.5, 0.125, ((0, 8),))
    perms = draw_perms(jax.random.fold_in(key_of[10], 71), 0)
    tokens_b = bell_draw(key_of[5], (TOKENS_B, D), 1.0, 6.0, ((0, 32),))
    expert_ids_keys = jax.random.split(jax.random.fold_in(key_of[6], 1), TOKENS_B // TOKB)
    expert_ids_turns = jax.random.permutation(jax.random.fold_in(key_of[6], 3), TOKENS_B // TOKB)
    expert_ids = jax.vmap(lambda own, number: shared_out(jax.random.fold_in(key_of[6], 2), own, number, TOKB, EXPERTS, 1, CAP, 1))(expert_ids_keys, expert_ids_turns).reshape((TOKENS_B, 1))
    w_gate = bell_draw(key_of[7], (EXPERTS, D, FF), D ** -0.5, 0.125, ((0, 32), (2, 8)))
    w_up = bell_draw(key_of[8], (EXPERTS, D, FF), D ** -0.5, 0.125, ((0, 32), (2, 8)))
    w_down = bell_draw(key_of[9], (EXPERTS, FF, D), FF ** -0.5, 0.125, ((0, 32), (1, 8)))
    return dict(x_att=x_att, w_qk=w_qk, w_val=w_val, w_out=w_out, perms=perms, tokens_b=tokens_b, expert_ids=expert_ids, w_gate=w_gate, w_up=w_up, w_down=w_down)


def normalize(queries):
    return queries * lax.rsqrt(lax.optimization_barrier(jnp.sum(queries * queries, axis=-1, keepdims=True)) + 1e-06) / math.sqrt(HEAD_DIM)

def attend(sorted_rows, positions, last_rows, last_positions, head_count):
    span = head_count * HEAD_DIM
    blocks = sorted_rows.shape[0] // BLOCK_LEN
    earlier = jnp.concatenate([last_rows, sorted_rows[:-BLOCK_LEN]], axis=0)
    earlier_pos = jnp.concatenate([last_positions, positions[:-BLOCK_LEN]], axis=0)
    block_shape = (blocks, BLOCK_LEN, head_count, HEAD_DIM)
    queries = sorted_rows[:, :span].astype(jnp.float32).reshape(block_shape)
    all_keys = jnp.concatenate([normalize(earlier[:, :span].astype(jnp.float32).reshape(block_shape)), normalize(queries)], axis=1)
    values = jnp.concatenate([earlier[:, span:].reshape(block_shape), sorted_rows[:, span:].reshape(block_shape)], axis=1).astype(jnp.float32)
    pos_query = positions.reshape(blocks, BLOCK_LEN)
    pos_key = jnp.concatenate([earlier_pos.reshape(blocks, BLOCK_LEN), pos_query], axis=1)
    scores = jnp.einsum('bqhd,bkhd->bhqk', queries, all_keys)
    later = pos_key[:, None, None, :] > pos_query[:, None, :, None]
    itself = pos_key[:, None, None, :] == pos_query[:, None, :, None]
    scores = jnp.where(itself, scores - 10000.0, scores)
    scores = jnp.where(later, -1e+30, scores)
    row_max = lax.optimization_barrier(jnp.max(scores, axis=-1, keepdims=True))
    exponent = jnp.exp(scores - row_max)
    row_total = lax.optimization_barrier(jnp.sum(exponent, axis=-1, keepdims=True))
    weights = lax.optimization_barrier((exponent / row_total).astype(jnp.bfloat16)).astype(jnp.float32)
    outcome = jnp.einsum('bhqk,bkhd->bqhd', weights, values)
    log_total = jnp.transpose((row_max + jnp.log(row_total))[..., 0], (0, 2, 1)).reshape(blocks * BLOCK_LEN, head_count)
    return (outcome.reshape(blocks * BLOCK_LEN, span), log_total)

def combine(round_outs, round_lses):
    round_count, length, head_count = round_lses.shape
    peak = lax.optimization_barrier(jnp.max(round_lses, axis=0, keepdims=True))
    whole = peak + jnp.log(lax.optimization_barrier(jnp.sum(jnp.exp(round_lses - peak), axis=0, keepdims=True)))
    shares = jnp.exp(round_lses - whole)
    weighted = round_outs.reshape(round_count, length, head_count, HEAD_DIM) * shares[..., None]
    return lax.optimization_barrier(jnp.sum(weighted, axis=0)).reshape(length, head_count * HEAD_DIM).astype(jnp.bfloat16)

def reference(x_att, w_qk, w_val, w_out, perms, tokens_b, expert_ids, w_gate, w_up, w_down):
    query_part = jnp.dot(x_att, w_qk, preferred_element_type=jnp.float32).astype(jnp.bfloat16)
    value_part = jnp.dot(x_att, w_val, preferred_element_type=jnp.float32).astype(jnp.bfloat16)
    projected = jnp.concatenate([query_part, value_part], axis=1)
    round_outs = []
    round_lses = []
    for round_no in range(ROUNDS):
        orders = perms[round_no]
        sorted_rows = projected[orders]
        outcome, log_total = attend(sorted_rows, orders, sorted_rows[-BLOCK_LEN:], orders[-BLOCK_LEN:], HEADS)
        round_outs.append(jnp.zeros_like(outcome).at[orders].set(outcome))
        round_lses.append(jnp.zeros_like(log_total).at[orders].set(log_total))
    mixed_heads = combine(jnp.stack(round_outs), jnp.stack(round_lses))
    attended = jnp.dot(mixed_heads, w_out, preferred_element_type=jnp.float32).astype(jnp.bfloat16)
    expert_no = expert_ids[:, 0].astype(jnp.int32)
    expert_hot = (expert_no[:, None] == jnp.arange(EXPERTS, dtype=jnp.int32)[None, :]).astype(jnp.int32)
    expert_rank = lax.optimization_barrier(jnp.sum((jnp.cumsum(expert_hot, axis=0) - expert_hot) * expert_hot, axis=1)).astype(jnp.int32)
    slot_count = N_SEQ * CAP
    slot_table = jnp.full((EXPERTS, slot_count), TOKENS_B, jnp.int32).at[expert_no, expert_rank].set(jnp.arange(TOKENS_B, dtype=jnp.int32))
    padded = jnp.concatenate([tokens_b, jnp.zeros((1, D), tokens_b.dtype)], axis=0)

    def expert_apply(operands):
        indices, gate_w, up_w, down_w = operands
        picked = padded[indices]
        gate = jnp.dot(picked, gate_w, preferred_element_type=jnp.float32)
        up_val = jnp.dot(picked, up_w, preferred_element_type=jnp.float32)
        hidden = (jax.nn.silu(gate) * up_val).astype(jnp.bfloat16)
        return jnp.dot(hidden, down_w, preferred_element_type=jnp.float32).astype(jnp.bfloat16)
    expert_rows = lax.map(expert_apply, (slot_table, w_gate, w_up, w_down))
    mixed = expert_rows[expert_no, expert_rank]
    return (attended, mixed)
```

```python
import functools
import math

import jax
import jax.numpy as jnp
from jax import lax
from jax.experimental import pallas as pl
from jax.experimental.pallas import tpu as pltpu
from jax.sharding import PartitionSpec as P

HEAD_DIM = 128
BLOCK_LEN = 64
EXP_DEV = 2
LANES = 128
F32, BF16, I32 = jnp.float32, jnp.bfloat16, jnp.int32
BIG = pltpu.CompilerParams(vmem_limit_bytes=48 * 1024 * 1024)


def dot(a, b):
    return jnp.dot(a, b, preferred_element_type=F32)


def dot_t(a, b):
    return lax.dot_general(a, b, (((1,), (1,)), ((), ())), preferred_element_type=F32)


def to_col(row):
    return jnp.broadcast_to(row, (LANES, row.shape[1])).T[:, :1]


def to_row(col):
    return jnp.broadcast_to(col, (col.shape[0], LANES)).T[:1, :]


def iota(shape, dim):
    return lax.broadcasted_iota(I32, shape, dim)


def flag(mask, kind=BF16):
    return jnp.where(mask, 1.0, 0.0).astype(kind)


def upper(count):
    return flag(iota((count, count), 0) <= iota((count, count), 1))


def pack_rows_kernel(me_ref, perms_ref, x_ref, qk_ref, val_ref, out_ref, token_ref, scratch):
    length, span = x_ref.shape[0], qk_ref.shape[1]
    rounds, total = perms_ref.shape
    peers = total // length
    per_peer = length // peers
    for peer in range(peers):
        scratch[peer * rounds : (peer + 1) * rounds, :] = perms_ref[
            :, peer * length : (peer + 1) * length
        ]
    perms = scratch[...]
    token = perms & (length - 1)
    mine = (perms >> (length.bit_length() - 1)) == me_ref[0]
    rank = dot(flag(mine), upper(length)).astype(I32) - 1
    slot = jnp.where(mine, rank, -1)
    groups = peers * rounds
    chosen = slot[:, None, :] == iota((groups, per_peer, length), 1)
    token_3d = jnp.where(chosen, token.astype(F32)[:, None, :], 0.0)
    column = jnp.sum(token_3d, axis=-1, keepdims=True).reshape(groups * per_peer, 1)
    token_ref[...] = jnp.broadcast_to(to_row(column), token_ref.shape).astype(I32)
    pick = flag(column.astype(I32) == iota((groups * per_peer, length), 1))
    for part, weight in enumerate((qk_ref, val_ref)):
        rows = dot(x_ref[...], weight[...]).astype(BF16)
        out_ref[:, part * span : (part + 1) * span] = dot(pick, rows).astype(BF16)


def pack_rows(me, perms, x_att, w_qk, w_val):
    length, width = x_att.shape
    rounds, total = perms.shape
    span = w_qk.shape[1]
    groups = rounds * (total // length)
    slots = rounds * length

    def whole(shape):
        return pl.BlockSpec(shape, lambda i, me_ref: (0, 0))

    return pl.pallas_call(
        pack_rows_kernel,
        grid_spec=pltpu.PrefetchScalarGridSpec(
            num_scalar_prefetch=1,
            grid=(1,),
            in_specs=[
                whole((rounds, total)),
                whole((length, width)),
                whole((width, span)),
                whole((width, span)),
            ],
            out_specs=[whole((slots, 2 * span)), whole((8, slots))],
            scratch_shapes=[pltpu.VMEM((groups, length), I32)],
        ),
        out_shape=[
            jax.ShapeDtypeStruct((slots, 2 * span), BF16),
            jax.ShapeDtypeStruct((8, slots), I32),
        ],
        compiler_params=BIG,
        name="pack_rows",
    )(me, perms, x_att, w_qk, w_val)


def pack_tokens_kernel(my_exp_ref, ids_ref, tokens_ref, out_ref, slot_ref):
    length = tokens_ref.shape[0]
    slots = out_ref.shape[0]
    experts = slot_ref.shape[0]
    capacity = slots // experts
    hot = ids_ref[...] == iota((experts, length), 0)
    counts = dot(flag(hot), upper(length))
    rank = jnp.sum(jnp.where(hot, counts, 0.0), axis=0, keepdims=True) - 1.0
    slot = ids_ref[...] * capacity + rank.astype(I32)
    slot_ref[...] = jnp.broadcast_to(slot, slot_ref.shape)
    pick = flag(iota((slots, length), 0) == slot)
    out_ref[...] = dot(pick, tokens_ref[...]).astype(BF16)


def pack_tokens(my_exp, ids, tokens, experts, capacity, part):
    length = tokens.shape[0]
    slots = experts * capacity
    return pl.pallas_call(
        pack_tokens_kernel,
        grid_spec=pltpu.PrefetchScalarGridSpec(
            num_scalar_prefetch=1,
            grid=(1,),
            in_specs=[
                pl.BlockSpec((1, length), lambda i, e: (0, 0)),
                pl.BlockSpec((length, part), lambda i, e: (0, e[0])),
            ],
            out_specs=[
                pl.BlockSpec((slots, part), lambda i, e: (0, 0)),
                pl.BlockSpec((experts, length), lambda i, e: (0, 0)),
            ],
        ),
        out_shape=[
            jax.ShapeDtypeStruct((slots, part), BF16),
            jax.ShapeDtypeStruct((experts, length), I32),
        ],
        compiler_params=BIG,
        name="pack_tokens",
    )(my_exp, ids, tokens)


def experts_kernel(x_ref, gate_ref, up_ref, down_ref, out_ref):
    parts, peers, _, capacity, part = x_ref.shape
    rows = peers * capacity
    gate = jnp.zeros((rows, gate_ref.shape[2]), F32)
    up_val = jnp.zeros((rows, gate_ref.shape[2]), F32)
    for index in range(parts):
        x = x_ref[index, :, 0].reshape(rows, part)
        gate = gate + dot(x, gate_ref[0, index * part : (index + 1) * part, :])
        up_val = up_val + dot(x, up_ref[0, index * part : (index + 1) * part, :])
    hidden = (gate / (1.0 + jnp.exp(-gate)) * up_val).astype(BF16)
    for index in range(parts):
        piece = dot(hidden, down_ref[0, :, index * part : (index + 1) * part])
        out_ref[index, :, 0] = piece.reshape(peers, capacity, part).astype(out_ref.dtype)


def run_experts(x, w_gate, w_up, w_down, kind):
    parts, peers, own, capacity, part = x.shape
    width, hidden = w_gate.shape[1:]
    return pl.pallas_call(
        experts_kernel,
        grid=(own,),
        in_specs=[
            pl.BlockSpec((parts, peers, 1, capacity, part), lambda e: (0, 0, e, 0, 0)),
            pl.BlockSpec((1, width, hidden), lambda e: (e, 0, 0)),
            pl.BlockSpec((1, width, hidden), lambda e: (e, 0, 0)),
            pl.BlockSpec((1, hidden, width), lambda e: (e, 0, 0)),
        ],
        out_specs=pl.BlockSpec((parts, peers, 1, capacity, part), lambda e: (0, 0, e, 0, 0)),
        out_shape=jax.ShapeDtypeStruct((parts, peers, own, capacity, part), kind),
        compiler_params=BIG,
        name="experts",
    )(x, w_gate, w_up, w_down)


def unpack_tokens_kernel(back_ref, slot_ref, out_ref):
    length = out_ref.shape[0]
    column = to_col(slot_ref[:1, :].astype(F32)).astype(I32)
    pick = flag(column == iota((length, back_ref.shape[0]), 1))
    out_ref[...] = dot(pick, back_ref[...]).astype(BF16)


def unpack_tokens(back, slot):
    return pl.pallas_call(
        unpack_tokens_kernel,
        out_shape=jax.ShapeDtypeStruct((slot.shape[1], back.shape[1]), BF16),
        compiler_params=BIG,
        name="unpack_tokens",
    )(back, slot)


def sort_rows_kernel(peers, me_ref, perms_ref, arrived_ref, rows_ref, last_ref, slot_ref):
    rounds, length = perms_ref.shape
    per_peer = length // peers
    for turn in range(rounds):
        source = perms_ref[turn : turn + 1, :] >> (length.bit_length() - 1)
        hot = source == iota((peers, length), 0)
        counts = dot(flag(hot), upper(length))
        rank = jnp.sum(jnp.where(hot, counts, 0.0), axis=0, keepdims=True) - 1.0
        slot = source * per_peer + rank.astype(I32)
        slot_ref[turn] = jnp.broadcast_to(slot, slot_ref.shape[1:])
        pick = flag(to_col(slot.astype(F32)).astype(I32) == iota((length, length), 1))
        have = arrived_ref[:, turn * per_peer : (turn + 1) * per_peer, :]
        rows = dot(pick, have.reshape(length, have.shape[2])).astype(BF16)
        rows_ref[turn] = rows
        last_ref[turn] = rows[length - BLOCK_LEN :]


def sort_rows(me, perms, arrived, length):
    rounds = perms.shape[0]
    peers, _, width = arrived.shape
    return pl.pallas_call(
        functools.partial(sort_rows_kernel, peers),
        grid_spec=pltpu.PrefetchScalarGridSpec(
            num_scalar_prefetch=1,
            grid=(1,),
            in_specs=[
                pl.BlockSpec((rounds, length), lambda i, s: (0, s[0])),
                pl.BlockSpec(arrived.shape, lambda i, s: (0, 0, 0)),
            ],
            out_specs=[
                pl.BlockSpec((rounds, length, width), lambda i, s: (0, 0, 0)),
                pl.BlockSpec((rounds, BLOCK_LEN, width), lambda i, s: (0, 0, 0)),
                pl.BlockSpec((rounds, 8, length), lambda i, s: (0, 0, 0)),
            ],
        ),
        out_shape=[
            jax.ShapeDtypeStruct((rounds, length, width), BF16),
            jax.ShapeDtypeStruct((rounds, BLOCK_LEN, width), BF16),
            jax.ShapeDtypeStruct((rounds, 8, length), I32),
        ],
        compiler_params=BIG,
        name="sort_rows",
    )(me, perms, arrived)


def attend_kernel(
    peers, me_ref, perms_ref, earlier_ref, rows_ref, last_ref, slot_ref, out_ref, lse_ref
):
    rounds, length = perms_ref.shape
    per_peer = length // peers
    span = rows_ref.shape[2] // 2
    tile, window = 2 * BLOCK_LEN, 4 * BLOCK_LEN
    block_q = iota((tile, window), 0) // BLOCK_LEN
    block_k = iota((tile, window), 1) // BLOCK_LEN
    met = (block_k == block_q + 1) | (block_k == block_q + 2)
    for turn in range(rounds):
        position = perms_ref[turn : turn + 1, :].astype(F32)
        position_col = to_col(position)
        positions = jnp.concatenate([earlier_ref[turn : turn + 1, :].astype(F32), position], axis=1)
        back = flag(iota((length, length), 0) == slot_ref[turn, :1, :])
        totals = []
        for head in range(span // HEAD_DIM):
            at = head * HEAD_DIM
            empty = jnp.zeros((BLOCK_LEN, HEAD_DIM), BF16)
            own = rows_ref[turn, :, at : at + HEAD_DIM]
            keys = jnp.concatenate([empty, last_ref[turn, :, at : at + HEAD_DIM], own], axis=0)
            at = span + at
            values = jnp.concatenate(
                [
                    empty,
                    last_ref[turn, :, at : at + HEAD_DIM],
                    rows_ref[turn, :, at : at + HEAD_DIM],
                ],
                axis=0,
            )
            wide = keys.astype(F32)
            squares = jnp.sum(wide * wide, axis=-1, keepdims=True)
            scale = to_row(lax.rsqrt(squares + 1e-06) / math.sqrt(HEAD_DIM))
            outs, lses = [], []
            for first in range(0, length, tile):
                query = own[first : first + tile]
                scores = dot_t(query, keys[first : first + window])
                scores = scores * scale[:, first : first + window]
                pos_q = position_col[first : first + tile]
                pos_k = positions[:, first : first + window]
                scores = jnp.where(pos_k == pos_q, scores - 10000.0, scores)
                scores = jnp.where(met & (pos_k <= pos_q), scores, -1e30)
                peak = jnp.max(scores, axis=-1, keepdims=True)
                exponent = jnp.exp(scores - peak)
                total = jnp.sum(exponent, axis=-1, keepdims=True)
                weights = (exponent / total).astype(BF16)
                outs.append(dot(weights, values[first : first + window]).astype(BF16))
                lses.append(peak + jnp.log(total))
            out = dot(back, jnp.concatenate(outs, axis=0)).astype(BF16)
            at = head * HEAD_DIM
            out_ref[:, turn * per_peer : (turn + 1) * per_peer, at : at + HEAD_DIM] = out.reshape(
                peers, per_peer, HEAD_DIM
            )
            totals.append(jnp.concatenate(lses, axis=0))
        lane = iota((length, LANES), 1)
        logs = jnp.zeros((length, LANES), F32)
        for head, total in enumerate(totals):
            logs = jnp.where(lane == head, total, logs)
        moved = jnp.zeros((length, LANES), F32)
        for _ in range(3):
            piece = logs.astype(BF16)
            moved = moved + dot(back, piece)
            logs = logs - piece.astype(F32)
        lse_ref[:, turn * per_peer : (turn + 1) * per_peer, :] = moved[:, : len(totals)].reshape(
            peers, per_peer, len(totals)
        )


def attend(me, perms, rows, last, slot, peers):
    rounds, length, width = rows.shape
    span = width // 2
    per_peer = length // peers
    lane_blocks = length // LANES
    fixed = lambda shape: pl.BlockSpec(shape, lambda i, s: (0, 0, 0))
    out = (peers, rounds * per_peer, span)
    lse = (peers, rounds * per_peer, span // HEAD_DIM)
    return pl.pallas_call(
        functools.partial(attend_kernel, peers),
        grid_spec=pltpu.PrefetchScalarGridSpec(
            num_scalar_prefetch=1,
            grid=(1,),
            in_specs=[
                pl.BlockSpec((rounds, length), lambda i, s: (0, s[0])),
                pl.BlockSpec(
                    (rounds, LANES),
                    lambda i, s: (
                        0,
                        jnp.where(s[0] == 0, peers * lane_blocks - 1, s[0] * lane_blocks - 1),
                    ),
                ),
                fixed(rows.shape),
                fixed(last.shape),
                fixed(slot.shape),
            ],
            out_specs=[fixed(out), fixed(lse)],
        ),
        out_shape=[jax.ShapeDtypeStruct(out, BF16), jax.ShapeDtypeStruct(lse, F32)],
        compiler_params=BIG,
        name="attend",
    )(me, perms, perms, rows, last, slot)


def combine_kernel(out_ref, lse_ref, token_ref, mixed_ref):
    peers, both, span = out_ref.shape
    length = mixed_ref.shape[0]
    rounds = both * peers // length
    per_peer = both // rounds
    heads = span // HEAD_DIM
    column = iota((length, peers * both), 0)
    pick_all = flag(token_ref[:1, :] == column)
    slot_round = (iota((1, peers * both), 1) // per_peer) % rounds
    outs, lses = [], []
    for turn in range(rounds):
        pick = jnp.where(slot_round == turn, pick_all, jnp.zeros_like(pick_all))
        outs.append(dot(pick, out_ref[...].reshape(peers * both, span)))
        logs = lse_ref[...].reshape(peers * both, heads)
        moved = jnp.zeros((length, heads), F32)
        for _ in range(3):
            piece = logs.astype(BF16)
            moved = moved + dot(pick, piece)
            logs = logs - piece.astype(F32)
        lses.append(moved)
    peak = functools.reduce(jnp.maximum, lses)
    whole = peak + jnp.log(functools.reduce(jnp.add, [jnp.exp(lse - peak) for lse in lses]))
    shares = [jnp.exp(lse - whole) for lse in lses]
    for head in range(heads):
        at = head * HEAD_DIM
        mixed = jnp.zeros((length, HEAD_DIM), F32)
        for out, share in zip(outs, shares):
            mixed = mixed + out[:, at : at + HEAD_DIM] * share[:, head : head + 1]
        mixed_ref[:, at : at + HEAD_DIM] = mixed.astype(BF16)


def combine(out, lse, token, length):
    return pl.pallas_call(
        combine_kernel,
        out_shape=jax.ShapeDtypeStruct((length, out.shape[2]), BF16),
        compiler_params=BIG,
        name="combine",
    )(out, lse, token)


def exchange(x, axis):
    return lax.all_to_all(x, axis, split_axis=0, concat_axis=0, tiled=True)


def body(x_att, w_qk, w_val, w_out, perms, tokens_b, expert_ids, w_gate, w_up, w_down):
    peers, parts = lax.axis_size("seq"), lax.axis_size("exp")
    me = lax.axis_index("seq").astype(I32).reshape(1)
    my_exp = lax.axis_index("exp").astype(I32).reshape(1)
    length, width = x_att.shape
    rounds = perms.shape[0]
    per_peer = length // peers
    experts = EXP_DEV * peers
    tokb = tokens_b.shape[0]
    capacity = 2 * tokb // experts
    part = width // parts
    dispatch, token_slot = pack_tokens(
        my_exp, expert_ids.reshape(1, tokb), tokens_b, experts, capacity, part
    )
    outgoing, slot_token = pack_rows(me, perms, x_att, w_qk, w_val)
    received = exchange(dispatch.reshape(peers, EXP_DEV, capacity, part), "seq")
    arrived = exchange(outgoing.reshape(peers, rounds * per_peer, outgoing.shape[1]), "seq")
    gathered = lax.all_gather(received, "exp", axis=0, tiled=False)
    rows, last, row_slot = sort_rows(me, perms, arrived, length)
    last = lax.ppermute(last, "seq", [(i, (i + 1) % peers) for i in range(peers)])
    outs, lses = attend(me, perms, rows, last, row_slot, peers)
    got_out = exchange(outs, "seq")
    got_lse = exchange(lses, "seq")
    expert_part = run_experts(gathered, w_gate, w_up, w_down, BF16)
    expert_rows = lax.psum_scatter(expert_part, "exp", scatter_dimension=0, tiled=False)
    expert_back = exchange(expert_rows, "seq")
    mixed = unpack_tokens(expert_back.reshape(experts * capacity, part), token_slot)
    mixed_heads = combine(got_out, got_lse, slot_token, length)
    attn_part = dot(mixed_heads, w_out).astype(BF16)
    attended = lax.psum_scatter(attn_part, "exp", scatter_dimension=1, tiled=True)
    return (attended, mixed)


def solution(mesh):
    in_specs = (
        P("seq", None),
        P(None, "exp"),
        P(None, "exp"),
        P("exp", None),
        P(),
        P("seq", None),
        P("seq", None),
        P("seq", None, "exp"),
        P("seq", None, "exp"),
        P("seq", "exp", None),
    )
    out_specs = (P("seq", "exp"), P("seq", "exp"))
    return jax.shard_map(body, mesh=mesh, in_specs=in_specs, out_specs=out_specs, check_vma=False)
```

```python
import functools
import math

import jax
import jax.numpy as jnp
from jax import lax
from jax.experimental import pallas as pl
from jax.experimental.pallas import tpu as pltpu
from jax.sharding import PartitionSpec as P

HEAD_DIM = 128
BLOCK_LEN = 64
EXP_DEV = 2
LANES = 128
F32, BF16, I32 = jnp.float32, jnp.bfloat16, jnp.int32
BIG = pltpu.CompilerParams(vmem_limit_bytes=48 * 1024 * 1024)


def dot(a, b):
    return jnp.dot(a, b, preferred_element_type=F32)


def dot_t(a, b):
    return lax.dot_general(a, b, (((1,), (1,)), ((), ())), preferred_element_type=F32)


def to_col(row):
    return jnp.broadcast_to(row, (LANES, row.shape[1])).T[:, :1]


def to_row(col):
    return jnp.broadcast_to(col, (col.shape[0], LANES)).T[:1, :]


def iota(shape, dim):
    return lax.broadcasted_iota(I32, shape, dim)


def flag(mask, kind=BF16):
    return jnp.where(mask, 1.0, 0.0).astype(kind)


def cost(flops, size):
    return pl.CostEstimate(flops=flops, bytes_accessed=size, transcendentals=0)


def upper(count):
    return flag(iota((count, count), 0) <= iota((count, count), 1))


def pack_rows_kernel(me_ref, perms_ref, x_ref, qk_ref, val_ref, out_ref, token_ref, scratch):
    length, span = x_ref.shape[0], qk_ref.shape[1]
    rounds, total = perms_ref.shape
    peers = total // length
    per_peer = length // peers
    for peer in range(peers):
        scratch[peer * rounds : (peer + 1) * rounds, :] = perms_ref[
            :, peer * length : (peer + 1) * length
        ]
    perms = scratch[...]
    token = perms & (length - 1)
    mine = (perms >> (length.bit_length() - 1)) == me_ref[0]
    rank = dot(flag(mine), upper(length)).astype(I32) - 1
    slot = jnp.where(mine, rank, -1)
    groups = peers * rounds
    chosen = slot[:, None, :] == iota((groups, per_peer, length), 1)
    token_3d = jnp.where(chosen, token.astype(F32)[:, None, :], 0.0)
    column = jnp.sum(token_3d, axis=-1, keepdims=True).reshape(groups * per_peer, 1)
    by_round = column.reshape(peers, rounds, per_peer, 1)
    for turn in range(rounds):
        row = to_row(by_round[:, turn].reshape(peers * per_peer, 1)).astype(I32)
        token_ref[turn] = jnp.broadcast_to(row, token_ref.shape[1:])
    pick = flag(column.astype(I32) == iota((groups * per_peer, length), 1))
    for part, weight in enumerate((qk_ref, val_ref)):
        rows = dot(x_ref[...], weight[...]).astype(BF16)
        out_ref[:, part * span : (part + 1) * span] = dot(pick, rows).astype(BF16)


def pack_rows(me, perms, x_att, w_qk, w_val):
    length, width = x_att.shape
    rounds, total = perms.shape
    span = w_qk.shape[1]
    groups = rounds * (total // length)
    slots = rounds * length

    def whole(shape):
        return pl.BlockSpec(shape, lambda i, me_ref: (0, 0))

    return pl.pallas_call(
        pack_rows_kernel,
        grid_spec=pltpu.PrefetchScalarGridSpec(
            num_scalar_prefetch=1,
            grid=(1,),
            in_specs=[
                whole((rounds, total)),
                whole((length, width)),
                whole((width, span)),
                whole((width, span)),
            ],
            out_specs=[
                whole((slots, 2 * span)),
                pl.BlockSpec((rounds, 8, length), lambda i, me_ref: (0, 0, 0)),
            ],
            scratch_shapes=[pltpu.VMEM((groups, length), I32)],
        ),
        out_shape=[
            jax.ShapeDtypeStruct((slots, 2 * span), BF16),
            jax.ShapeDtypeStruct((rounds, 8, length), I32),
        ],
        cost_estimate=cost(4 * length * width * span + 4 * slots * length * span, 6 << 20),
        compiler_params=BIG,
        name="pack_rows",
    )(me, perms, x_att, w_qk, w_val)


def pack_tokens_kernel(peers, where_ref, ids_ref, tokens_ref, out_ref, slot_ref):
    length = tokens_ref.shape[0]
    slots = out_ref.shape[0]
    capacity = slots // peers
    experts = EXP_DEV * peers
    ids = ids_ref[...]
    hot = ids == iota((experts, length), 0)
    counts = dot(flag(hot), upper(length))
    rank = jnp.sum(jnp.where(hot, counts, 0.0), axis=0, keepdims=True).astype(I32) - 1
    core = where_ref[1]
    turn = (ids % EXP_DEV + core) % EXP_DEV
    peer = ids // EXP_DEV
    slot_ref[...] = jnp.broadcast_to(
        (peer * EXP_DEV + turn) * capacity + rank, slot_ref.shape
    )
    slot = jnp.where(turn == 0, peer * capacity + rank, -1)
    pick = flag(iota((slots, length), 0) == slot)
    out_ref[...] = dot(pick, tokens_ref[...]).astype(BF16)


def pack_tokens(where, ids, tokens, peers, capacity, part):
    length = tokens.shape[0]
    slots = peers * capacity
    return pl.pallas_call(
        functools.partial(pack_tokens_kernel, peers),
        grid_spec=pltpu.PrefetchScalarGridSpec(
            num_scalar_prefetch=1,
            grid=(1,),
            in_specs=[
                pl.BlockSpec((1, length), lambda i, e: (0, 0)),
                pl.BlockSpec((length, part), lambda i, e: (0, e[0])),
            ],
            out_specs=[
                pl.BlockSpec((slots, part), lambda i, e: (0, 0)),
                pl.BlockSpec((8, length), lambda i, e: (0, 0)),
            ],
        ),
        out_shape=[
            jax.ShapeDtypeStruct((slots, part), BF16),
            jax.ShapeDtypeStruct((8, length), I32),
        ],
        cost_estimate=cost(2 * slots * length * part, 2 << 20),
        compiler_params=BIG,
        name="pack_tokens",
    )(where, ids, tokens)


def experts_kernel(where_ref, x_ref, *refs):
    weights, out_ref = refs[:-1], refs[-1]
    parts, peers, capacity, part = x_ref.shape
    rows = peers * capacity
    hiddens = []
    for gate_ref, up_ref in (weights[0:2], weights[3:5]):
        gate = jnp.zeros((rows, gate_ref.shape[2]), F32)
        up_val = jnp.zeros((rows, gate_ref.shape[2]), F32)
        for index in range(parts):
            x = x_ref[index].reshape(rows, part)
            gate = gate + dot(x, gate_ref[0, index * part : (index + 1) * part, :])
            up_val = up_val + dot(x, up_ref[0, index * part : (index + 1) * part, :])
        hiddens.append((gate / (1.0 + jnp.exp(-gate)) * up_val).astype(BF16))
    half = part // EXP_DEV
    for index in range(parts):
        at = index * part
        piece = dot(hiddens[0], weights[2][0, :, at : at + part])
        piece = (piece + dot(hiddens[1], weights[5][0, :, at : at + part])).astype(BF16)
        for side in range(EXP_DEV):
            columns = piece[:, side * half : (side + 1) * half]
            out_ref[index, side] = columns.reshape(peers, capacity, half)


def run_experts(where, x, own, sibling):
    parts, peers, capacity, part = x.shape
    width, hidden = own[0].shape[1:]
    out = (parts, EXP_DEV, peers, capacity, part // EXP_DEV)
    rows = peers * capacity

    def mine(i, e):
        return (e[1], 0, 0)

    def first(i, e):
        return (0, 0, 0)

    up_block, down_block = (1, width, hidden), (1, hidden, width)
    blocks = (up_block, up_block, down_block)
    return pl.pallas_call(
        experts_kernel,
        grid_spec=pltpu.PrefetchScalarGridSpec(
            num_scalar_prefetch=1,
            grid=(1,),
            in_specs=[pl.BlockSpec(x.shape, lambda i, e: (0, 0, 0, 0))]
            + [pl.BlockSpec(block, mine) for block in blocks]
            + [pl.BlockSpec(block, first) for block in blocks],
            out_specs=pl.BlockSpec(out, lambda i, e: (0, 0, 0, 0, 0)),
        ),
        out_shape=jax.ShapeDtypeStruct(out, BF16),
        cost_estimate=cost(12 * rows * width * hidden, 10 << 20),
        compiler_params=BIG,
        name="experts",
    )(where, x, *own, *sibling)


def unpack_tokens_kernel(back_ref, slot_ref, out_ref):
    length = out_ref.shape[0]
    column = to_col(slot_ref[:1, :].astype(F32)).astype(I32)
    pick = flag(column == iota((length, back_ref.shape[0]), 1))
    out_ref[...] = dot(pick, back_ref[...]).astype(BF16)


def unpack_tokens(back, slot):
    length, width = slot.shape[1], back.shape[1]
    return pl.pallas_call(
        unpack_tokens_kernel,
        out_shape=jax.ShapeDtypeStruct((length, width), BF16),
        cost_estimate=cost(2 * length * back.shape[0] * width, 1 << 20),
        compiler_params=BIG,
        name="unpack_tokens",
    )(back, slot)


def sort_rows_kernel(peers, me_ref, perms_ref, arrived_ref, rows_ref, last_ref, slot_ref):
    rounds, length = perms_ref.shape
    per_peer = length // peers
    for turn in range(rounds):
        source = perms_ref[turn : turn + 1, :] >> (length.bit_length() - 1)
        hot = source == iota((peers, length), 0)
        counts = dot(flag(hot), upper(length))
        rank = jnp.sum(jnp.where(hot, counts, 0.0), axis=0, keepdims=True) - 1.0
        slot = source * per_peer + rank.astype(I32)
        slot_ref[turn] = jnp.broadcast_to(slot, slot_ref.shape[1:])
        pick = flag(to_col(slot.astype(F32)).astype(I32) == iota((length, length), 1))
        have = arrived_ref[:, turn * per_peer : (turn + 1) * per_peer, :]
        rows = dot(pick, have.reshape(length, have.shape[2])).astype(BF16)
        rows_ref[turn] = rows
        last_ref[turn] = rows[length - BLOCK_LEN :]


def sort_rows(me, perms, arrived, length):
    rounds = perms.shape[0]
    peers, _, width = arrived.shape
    return pl.pallas_call(
        functools.partial(sort_rows_kernel, peers),
        grid_spec=pltpu.PrefetchScalarGridSpec(
            num_scalar_prefetch=1,
            grid=(1,),
            in_specs=[
                pl.BlockSpec((rounds, length), lambda i, s: (0, s[0])),
                pl.BlockSpec(arrived.shape, lambda i, s: (0, 0, 0)),
            ],
            out_specs=[
                pl.BlockSpec((rounds, length, width), lambda i, s: (0, 0, 0)),
                pl.BlockSpec((rounds, BLOCK_LEN, width), lambda i, s: (0, 0, 0)),
                pl.BlockSpec((rounds, 8, length), lambda i, s: (0, 0, 0)),
            ],
        ),
        out_shape=[
            jax.ShapeDtypeStruct((rounds, length, width), BF16),
            jax.ShapeDtypeStruct((rounds, BLOCK_LEN, width), BF16),
            jax.ShapeDtypeStruct((rounds, 8, length), I32),
        ],
        cost_estimate=cost(2 * rounds * length * length * width, 4 << 20),
        compiler_params=BIG,
        name="sort_rows",
    )(me, perms, arrived)


def window_scale(keys):
    wide = keys.astype(F32)
    squares = jnp.sum(wide * wide, axis=-1, keepdims=True)
    return to_row(lax.rsqrt(squares + 1e-06) / math.sqrt(HEAD_DIM))


def attend_tile(query, keys, values, scale, pos_q, pos_k):
    tile, window = query.shape[0], keys.shape[0]
    block_q = iota((tile, window), 0) // BLOCK_LEN
    block_k = iota((tile, window), 1) // BLOCK_LEN
    met = (block_k == block_q + 1) | (block_k == block_q + 2)
    scores = dot_t(query, keys) * scale
    scores = jnp.where(pos_k == pos_q, scores - 10000.0, scores)
    scores = jnp.where(met & (pos_k <= pos_q), scores, -1e30)
    peak = jnp.max(scores, axis=-1, keepdims=True)
    exponent = jnp.exp(scores - peak)
    total = jnp.sum(exponent, axis=-1, keepdims=True)
    weights = (exponent / total).astype(BF16)
    return dot(weights, values).astype(BF16), peak + jnp.log(total)


TILE, WINDOW, PIECES, GROUP = 2 * BLOCK_LEN, 4 * BLOCK_LEN, 3, 8


def put_logs(totals):
    lane = iota((totals[0].shape[0], LANES), 1) % GROUP
    logs = jnp.zeros(lane.shape, F32)
    for head, total in enumerate(totals):
        rest = total
        for piece in range(PIECES):
            part = rest.astype(BF16).astype(F32)
            logs = jnp.where(lane == head * PIECES + piece, part, logs)
            rest = rest - part
    return logs.astype(BF16)


def attend_later_kernel(me_ref, perms_ref, rows_ref, out_ref):
    rounds, length = perms_ref.shape
    span = rows_ref.shape[2] // 2
    for turn in range(rounds):
        position = perms_ref[turn : turn + 1, :].astype(F32)
        position_col = to_col(position)
        scales = []
        for head in range(span // HEAD_DIM):
            at = head * HEAD_DIM
            scales.append(window_scale(rows_ref[turn, :, at : at + HEAD_DIM]))
        for first in range(TILE, length, TILE):
            totals = []
            window = slice(first + TILE - WINDOW, first + TILE)
            queries = slice(first, first + TILE)
            for head in range(span // HEAD_DIM):
                at = head * HEAD_DIM
                out, total = attend_tile(
                    rows_ref[turn, queries, at : at + HEAD_DIM],
                    rows_ref[turn, window, at : at + HEAD_DIM],
                    rows_ref[turn, window, span + at : span + at + HEAD_DIM],
                    scales[head][:, window],
                    position_col[queries],
                    position[:, window],
                )
                out_ref[turn, first - TILE : first, at : at + HEAD_DIM] = out
                totals.append(total)
            out_ref[turn, first - TILE : first, span:] = put_logs(totals)


def attend_first_kernel(
    peers,
    me_ref,
    perms_ref,
    earlier_ref,
    rows_ref,
    last_ref,
    slot_ref,
    later_ref,
    out_ref,
):
    rounds, length = slot_ref.shape[0], slot_ref.shape[2]
    per_peer = length // peers
    span = rows_ref.shape[2] // 2
    lane_group = iota((peers, per_peer, LANES), 2) // GROUP
    own_group = lane_group == iota((peers, per_peer, LANES), 1)
    empty = jnp.zeros((BLOCK_LEN, HEAD_DIM), BF16)
    for turn in range(rounds):
        position = perms_ref[turn : turn + 1, :].astype(F32)
        positions = jnp.concatenate([earlier_ref[turn : turn + 1, :].astype(F32), position], axis=1)
        position_col = to_col(position)
        totals, outs = [], []
        for head in range(span // HEAD_DIM):
            at = head * HEAD_DIM
            own = rows_ref[turn, :, at : at + HEAD_DIM]
            keys = jnp.concatenate([empty, last_ref[turn, :, at : at + HEAD_DIM], own], axis=0)
            at = span + at
            values = jnp.concatenate(
                [
                    empty,
                    last_ref[turn, :, at : at + HEAD_DIM],
                    rows_ref[turn, :, at : at + HEAD_DIM],
                ],
                axis=0,
            )
            out, total = attend_tile(
                own, keys, values, window_scale(keys), position_col, positions
            )
            outs.append(out)
            totals.append(total)
        top = jnp.concatenate(outs + [put_logs(totals)], axis=1)
        whole = jnp.concatenate([top, later_ref[turn]], axis=0) if length > TILE else top
        back = flag(iota((length, length), 0) == slot_ref[turn, :1, :])
        moved = dot(back, whole)
        at = turn * per_peer
        out_ref[:, at : at + per_peer, :] = (
            moved[:, :span].astype(BF16).reshape(peers, per_peer, span)
        )
        logs = moved[:, span:].reshape(peers, per_peer, LANES)
        logs = jnp.sum(jnp.where(own_group, logs, 0.0), axis=1, keepdims=True)
        at = rounds * per_peer
        out_ref[:, at : at + GROUP, turn * LANES : (turn + 1) * LANES] = jnp.broadcast_to(
            logs, (peers, GROUP, LANES)
        ).astype(BF16)


def attend_later(me, perms, rows):
    rounds, length, width = rows.shape
    span = width // 2
    out = (rounds, length - TILE, span + LANES)
    return pl.pallas_call(
        attend_later_kernel,
        grid_spec=pltpu.PrefetchScalarGridSpec(
            num_scalar_prefetch=1,
            grid=(1,),
            in_specs=[
                pl.BlockSpec((rounds, length), lambda i, s: (0, s[0])),
                pl.BlockSpec(rows.shape, lambda i, s: (0, 0, 0)),
            ],
            out_specs=pl.BlockSpec(out, lambda i, s: (0, 0, 0)),
        ),
        out_shape=jax.ShapeDtypeStruct(out, BF16),
        cost_estimate=cost(2 << 30, 4 << 20),
        compiler_params=BIG,
        name="attend_later",
    )(me, perms, rows)


def attend_first(me, perms, rows, last, slot, later, peers):
    rounds, length, width = rows.shape
    span = width // 2
    per_peer = length // peers
    lane_blocks = length // LANES

    def fixed(shape):
        return pl.BlockSpec(shape, lambda i, s: (0, 0, 0))

    out = (peers, rounds * per_peer + GROUP, span)
    return pl.pallas_call(
        functools.partial(attend_first_kernel, peers),
        grid_spec=pltpu.PrefetchScalarGridSpec(
            num_scalar_prefetch=1,
            grid=(1,),
            in_specs=[
                pl.BlockSpec((rounds, TILE), lambda i, s: (0, s[0] * lane_blocks)),
                pl.BlockSpec(
                    (rounds, LANES),
                    lambda i, s: (
                        0,
                        jnp.where(s[0] == 0, peers * lane_blocks - 1, s[0] * lane_blocks - 1),
                    ),
                ),
                fixed((rounds, TILE, width)),
                fixed(last.shape),
                fixed(slot.shape),
                fixed(later.shape),
            ],
            out_specs=fixed(out),
        ),
        out_shape=jax.ShapeDtypeStruct(out, BF16),
        cost_estimate=cost(2 << 30, 4 << 20),
        compiler_params=BIG,
        name="attend_first",
    )(me, perms, perms, rows, last, slot, later)


def combine_kernel(got_ref, token_ref, mixed_ref):
    peers, _, span = got_ref.shape
    rounds, _, length = token_ref.shape
    per_peer = length // peers
    heads = span // HEAD_DIM
    lane_group = iota((peers, per_peer, LANES), 2) // GROUP
    own_group = lane_group == iota((peers, per_peer, LANES), 1)
    lane = iota((length, LANES), 1) % GROUP // PIECES
    column = iota((length, length), 0)
    outs, lses = [], []
    for turn in range(rounds):
        pick = flag(token_ref[turn, :1, :] == column)
        at = turn * per_peer
        rows = got_ref[:, at : at + per_peer, :].reshape(length, span)
        logs = got_ref[
            :, rounds * per_peer : rounds * per_peer + GROUP, turn * LANES : (turn + 1) * LANES
        ]
        logs = jnp.concatenate([logs] * (per_peer // GROUP), axis=1)
        logs = jnp.where(own_group, logs, jnp.zeros_like(logs)).reshape(length, LANES)
        outs.append(dot(pick, rows))
        moved = dot(pick, logs)
        lses.append(
            [
                jnp.sum(jnp.where(lane == head, moved, 0.0), axis=1, keepdims=True)
                for head in range(heads)
            ]
        )
    for head in range(heads):
        logs = [lse[head] for lse in lses]
        peak = functools.reduce(jnp.maximum, logs)
        whole = peak + jnp.log(functools.reduce(jnp.add, [jnp.exp(lse - peak) for lse in logs]))
        at = head * HEAD_DIM
        mixed = jnp.zeros((length, HEAD_DIM), F32)
        for out, lse in zip(outs, logs):
            mixed = mixed + out[:, at : at + HEAD_DIM] * jnp.exp(lse - whole)
        mixed_ref[:, at : at + HEAD_DIM] = mixed.astype(BF16)


def combine(got, token):
    rounds, _, length = token.shape
    return pl.pallas_call(
        combine_kernel,
        out_shape=jax.ShapeDtypeStruct((length, got.shape[2]), BF16),
        cost_estimate=cost(2 * rounds * length * length * (got.shape[2] + LANES), 1 << 20),
        compiler_params=BIG,
        name="combine",
    )(got, token)


def project_kernel(heads_ref, weight_ref, out_ref):
    span = heads_ref.shape[2]
    total = jnp.zeros(out_ref.shape, F32)
    for index in range(heads_ref.shape[0]):
        total = total + dot(heads_ref[index], weight_ref[index * span : (index + 1) * span, :])
    out_ref[...] = total.astype(BF16)


def project(heads, weight):
    parts, length, span = heads.shape
    return pl.pallas_call(
        project_kernel,
        out_shape=jax.ShapeDtypeStruct((length, weight.shape[1]), BF16),
        cost_estimate=cost(2 * length * parts * span * weight.shape[1], 3 << 20),
        compiler_params=BIG,
        name="project",
    )(heads, weight)


def exchange(x, axis):
    return lax.all_to_all(x, axis, split_axis=0, concat_axis=0, tiled=True)


def after(x, *done):
    return lax.optimization_barrier((x, *done))[0]


def body(x_att, w_qk, w_val, w_out, perms, tokens_b, expert_ids, w_gate, w_up, w_down):
    peers, parts = lax.axis_size("seq"), lax.axis_size("exp")
    chips = parts // EXP_DEV
    me = lax.axis_index("seq").astype(I32).reshape(1)
    my_exp = lax.axis_index("exp").astype(I32)
    core = my_exp % EXP_DEV
    where = jnp.stack([my_exp // EXP_DEV, core])
    length, width = x_att.shape
    rounds = perms.shape[0]
    per_peer = length // peers
    tokb = tokens_b.shape[0]
    capacity = tokb // peers
    part = width // chips
    lines = [[chip * EXP_DEV + side for chip in range(chips)] for side in range(EXP_DEV)]
    siblings = [(i, i ^ 1) for i in range(parts)]

    dispatch, token_slot = pack_tokens(
        where, expert_ids.reshape(1, tokb), tokens_b, peers, capacity, part
    )
    received = exchange(dispatch.reshape(peers, capacity, part), "seq")
    outgoing, slot_token = pack_rows(me, perms, x_att, w_qk, w_val)
    outgoing = after(outgoing, received)
    gathered = lax.all_gather(received, "exp", axis=0, tiled=False, axis_index_groups=lines)
    arrived = exchange(outgoing.reshape(peers, rounds * per_peer, outgoing.shape[1]), "seq")
    own = (w_gate, w_up, w_down)
    sibling = [
        lax.ppermute(
            lax.dynamic_slice_in_dim(after(weight, received), 1 - core, 1, 0), "exp", siblings
        )
        for weight in own
    ]
    w_columns = lax.all_to_all(
        after(w_out, received), "exp", split_axis=1, concat_axis=0, tiled=True
    )
    expert_part = run_experts(where, gathered, own, sibling)
    arrived = after(arrived, expert_part, w_columns)
    expert_rows = lax.psum_scatter(
        expert_part, "exp", scatter_dimension=0, tiled=False, axis_index_groups=lines
    )
    rows, last, row_slot = sort_rows(me, perms, arrived, length)
    last = lax.ppermute(last, "seq", [(i, (i + 1) % peers) for i in range(peers)])
    later = attend_later(me, perms, rows)
    last = after(last, later)
    packed = attend_first(me, perms, rows, last, row_slot, later, peers)
    got = exchange(packed, "seq")
    expert_rows = after(expert_rows, packed)
    kept = lax.dynamic_index_in_dim(expert_rows, core, 0, keepdims=False)
    given = lax.dynamic_index_in_dim(expert_rows, 1 - core, 0, keepdims=False)
    taken = lax.ppermute(given, "exp", siblings)
    expert_rows = jnp.stack([kept, taken], axis=1)
    mixed_heads = combine(got, slot_token)
    expert_rows = after(expert_rows, mixed_heads)
    all_heads = lax.all_gather(mixed_heads, "exp", axis=0, tiled=False)
    expert_back = exchange(expert_rows, "seq")
    mixed = unpack_tokens(
        expert_back.reshape(peers * EXP_DEV * capacity, width // parts), token_slot
    )
    attended = project(after(all_heads, mixed), w_columns)
    return (attended, mixed)


def solution(mesh):
    in_specs = (
        P("seq", None),
        P(None, "exp"),
        P(None, "exp"),
        P("exp", None),
        P(),
        P("seq", None),
        P("seq", None),
        P("seq", None, "exp"),
        P("seq", None, "exp"),
        P("seq", "exp", None),
    )
    out_specs = (P("seq", "exp"), P("seq", "exp"))
    return jax.shard_map(body, mesh=mesh, in_specs=in_specs, out_specs=out_specs, check_vma=False)
```

```python
import functools
import math

import jax
import jax.numpy as jnp
from jax import lax
from jax.experimental import pallas as pl
from jax.experimental.pallas import tpu as pltpu
from jax.sharding import PartitionSpec as P

HEAD_DIM = 128
BLOCK_LEN = 64
EXP_DEV = 2
LANES = 128
F32, BF16, I32 = jnp.float32, jnp.bfloat16, jnp.int32
BIG = pltpu.CompilerParams(vmem_limit_bytes=48 * 1024 * 1024)


def dot(a, b):
    return jnp.dot(a, b, preferred_element_type=F32)


def dot_t(a, b):
    return lax.dot_general(a, b, (((1,), (1,)), ((), ())), preferred_element_type=F32)


def to_col(row):
    return jnp.broadcast_to(row, (LANES, row.shape[1])).T[:, :1]


def to_row(col):
    return jnp.broadcast_to(col, (col.shape[0], LANES)).T[:1, :]


def iota(shape, dim):
    return lax.broadcasted_iota(I32, shape, dim)


def flag(mask, kind=BF16):
    return jnp.where(mask, 1.0, 0.0).astype(kind)


def cost(flops, size):
    return pl.CostEstimate(flops=flops, bytes_accessed=size, transcendentals=0)


def upper(count):
    return flag(iota((count, count), 0) <= iota((count, count), 1))


def pack_rows_kernel(me_ref, perms_ref, x_ref, qk_ref, val_ref, out_ref, token_ref, scratch):
    length, span = x_ref.shape[0], qk_ref.shape[1]
    rounds, total = perms_ref.shape
    peers = total // length
    per_peer = length // peers
    for peer in range(peers):
        scratch[peer * rounds : (peer + 1) * rounds, :] = perms_ref[
            :, peer * length : (peer + 1) * length
        ]
    perms = scratch[...]
    token = perms & (length - 1)
    mine = (perms >> (length.bit_length() - 1)) == me_ref[0]
    rank = dot(flag(mine), upper(length)).astype(I32) - 1
    slot = jnp.where(mine, rank, -1)
    groups = peers * rounds
    chosen = slot[:, None, :] == iota((groups, per_peer, length), 1)
    token_3d = jnp.where(chosen, token.astype(F32)[:, None, :], 0.0)
    column = jnp.sum(token_3d, axis=-1, keepdims=True).reshape(groups * per_peer, 1)
    by_round = column.reshape(peers, rounds, per_peer, 1)
    for turn in range(rounds):
        row = to_row(by_round[:, turn].reshape(peers * per_peer, 1)).astype(I32)
        token_ref[turn] = jnp.broadcast_to(row, token_ref.shape[1:])
    pick = flag(column.astype(I32) == iota((groups * per_peer, length), 1))
    for part, weight in enumerate((qk_ref, val_ref)):
        rows = dot(x_ref[...], weight[...]).astype(BF16)
        out_ref[:, part * span : (part + 1) * span] = dot(pick, rows).astype(BF16)


def pack_rows(me, perms, x_att, w_qk, w_val):
    length, width = x_att.shape
    rounds, total = perms.shape
    span = w_qk.shape[1]
    groups = rounds * (total // length)
    slots = rounds * length

    def whole(shape):
        return pl.BlockSpec(shape, lambda i, me_ref: (0, 0))

    return pl.pallas_call(
        pack_rows_kernel,
        grid_spec=pltpu.PrefetchScalarGridSpec(
            num_scalar_prefetch=1,
            grid=(1,),
            in_specs=[
                whole((rounds, total)),
                whole((length, width)),
                whole((width, span)),
                whole((width, span)),
            ],
            out_specs=[
                whole((slots, 2 * span)),
                pl.BlockSpec((rounds, 8, length), lambda i, me_ref: (0, 0, 0)),
            ],
            scratch_shapes=[pltpu.VMEM((groups, length), I32)],
        ),
        out_shape=[
            jax.ShapeDtypeStruct((slots, 2 * span), BF16),
            jax.ShapeDtypeStruct((rounds, 8, length), I32),
        ],
        cost_estimate=cost(4 * length * width * span + 4 * slots * length * span, 6 << 20),
        compiler_params=BIG,
        name="pack_rows",
    )(me, perms, x_att, w_qk, w_val)


def pack_tokens_kernel(peers, where_ref, ids_ref, tokens_ref, out_ref, slot_ref):
    length = tokens_ref.shape[0]
    slots = out_ref.shape[0]
    capacity = slots // peers
    experts = EXP_DEV * peers
    ids = ids_ref[...]
    hot = ids == iota((experts, length), 0)
    counts = dot(flag(hot), upper(length))
    rank = jnp.sum(jnp.where(hot, counts, 0.0), axis=0, keepdims=True).astype(I32) - 1
    core = where_ref[1]
    turn = (ids % EXP_DEV + core) % EXP_DEV
    peer = ids // EXP_DEV
    slot_ref[...] = jnp.broadcast_to(
        (peer * EXP_DEV + turn) * capacity + rank, slot_ref.shape
    )
    slot = jnp.where(turn == 0, peer * capacity + rank, -1)
    pick = flag(iota((slots, length), 0) == slot)
    out_ref[...] = dot(pick, tokens_ref[...]).astype(BF16)


def pack_tokens(where, ids, tokens, peers, capacity, part):
    length = tokens.shape[0]
    slots = peers * capacity
    return pl.pallas_call(
        functools.partial(pack_tokens_kernel, peers),
        grid_spec=pltpu.PrefetchScalarGridSpec(
            num_scalar_prefetch=1,
            grid=(1,),
            in_specs=[
                pl.BlockSpec((1, length), lambda i, e: (0, 0)),
                pl.BlockSpec((length, part), lambda i, e: (0, e[0])),
            ],
            out_specs=[
                pl.BlockSpec((slots, part), lambda i, e: (0, 0)),
                pl.BlockSpec((8, length), lambda i, e: (0, 0)),
            ],
        ),
        out_shape=[
            jax.ShapeDtypeStruct((slots, part), BF16),
            jax.ShapeDtypeStruct((8, length), I32),
        ],
        cost_estimate=cost(2 * slots * length * part, 2 << 20),
        compiler_params=BIG,
        name="pack_tokens",
    )(where, ids, tokens)


def experts_kernel(where_ref, *refs):
    step = pl.program_id(0)
    shards, far_refs, weights = refs[0:3], refs[3:5], refs[5:11]
    out_ref, total_ref = refs[11:]
    peers, capacity, part = shards[0].shape
    rows = peers * capacity
    ups = (weights[0], weights[1], weights[3], weights[4])

    def add(x, start):
        for index, weight in enumerate(ups):
            product = dot(x, weight[0])
            total_ref[index] = product if start else total_ref[index] + product

    for turn, shard in enumerate(shards):

        @pl.when(step == turn)
        def _(shard=shard, start=turn == 0):
            add(shard[...].reshape(rows, part), start)

    @pl.when(step == len(shards))
    def _():
        add(jnp.concatenate([ref[...].reshape(rows // 2, part) for ref in far_refs], axis=0), False)
        hiddens = []
        for side in range(EXP_DEV):
            gate, up_val = total_ref[2 * side], total_ref[2 * side + 1]
            hiddens.append((gate / (1.0 + jnp.exp(-gate)) * up_val).astype(BF16))
        half = part // EXP_DEV
        for index in range(out_ref.shape[0]):
            at = index * part
            piece = dot(hiddens[0], weights[2][0, :, at : at + part])
            piece = (piece + dot(hiddens[1], weights[5][0, :, at : at + part])).astype(BF16)
            for side in range(EXP_DEV):
                columns = piece[:, side * half : (side + 1) * half]
                out_ref[index, side] = columns.reshape(peers, capacity, half)


def run_experts(where, shards, far, own, sibling):
    peers, capacity, part = shards[0].shape
    width, hidden = own[0].shape[1:]
    chips = width // part
    out = (chips, EXP_DEV, peers, capacity, part // EXP_DEV)
    rows = peers * capacity

    def rows_of(i, e):
        ahead = jnp.where(i == 0, 0, jnp.where(i == 1, chips - 1, jnp.where(i == 2, 1, 2)))
        return (e[0] + ahead) % chips

    up_block, down_block = (1, part, hidden), (1, hidden, width)
    own_up = pl.BlockSpec(up_block, lambda i, e: (e[1], rows_of(i, e), 0))
    sibling_up = pl.BlockSpec(up_block, lambda i, e: (0, rows_of(i, e), 0))
    own_down = pl.BlockSpec(down_block, lambda i, e: (e[1], 0, 0))
    sibling_down = pl.BlockSpec(down_block, lambda i, e: (0, 0, 0))
    return pl.pallas_call(
        experts_kernel,
        grid_spec=pltpu.PrefetchScalarGridSpec(
            num_scalar_prefetch=1,
            grid=(len(shards) + 1,),
            in_specs=[pl.BlockSpec(x.shape, lambda i, e: (0, 0, 0)) for x in (*shards, *far)]
            + [own_up, own_up, own_down, sibling_up, sibling_up, sibling_down],
            out_specs=pl.BlockSpec(out, lambda i, e: (0, 0, 0, 0, 0)),
            scratch_shapes=[pltpu.VMEM((4, rows, hidden), F32)],
        ),
        out_shape=jax.ShapeDtypeStruct(out, BF16),
        cost_estimate=cost(12 * rows * width * hidden, 10 << 20),
        compiler_params=BIG,
        name="experts",
    )(where, *shards, *far, *own, *sibling)


def unpack_tokens_kernel(back_ref, slot_ref, out_ref):
    length = out_ref.shape[0]
    column = to_col(slot_ref[:1, :].astype(F32)).astype(I32)
    pick = flag(column == iota((length, back_ref.shape[0]), 1))
    out_ref[...] = dot(pick, back_ref[...]).astype(BF16)


def unpack_tokens(back, slot):
    length, width = slot.shape[1], back.shape[1]
    return pl.pallas_call(
        unpack_tokens_kernel,
        out_shape=jax.ShapeDtypeStruct((length, width), BF16),
        cost_estimate=cost(2 * length * back.shape[0] * width, 1 << 20),
        compiler_params=BIG,
        name="unpack_tokens",
    )(back, slot)


def sort_rows_kernel(peers, me_ref, perms_ref, arrived_ref, rows_ref, last_ref, slot_ref):
    rounds, length = perms_ref.shape
    per_peer = length // peers
    for turn in range(rounds):
        source = perms_ref[turn : turn + 1, :] >> (length.bit_length() - 1)
        hot = source == iota((peers, length), 0)
        counts = dot(flag(hot), upper(length))
        rank = jnp.sum(jnp.where(hot, counts, 0.0), axis=0, keepdims=True) - 1.0
        slot = source * per_peer + rank.astype(I32)
        slot_ref[turn] = jnp.broadcast_to(slot, slot_ref.shape[1:])
        pick = flag(to_col(slot.astype(F32)).astype(I32) == iota((length, length), 1))
        have = arrived_ref[:, turn * per_peer : (turn + 1) * per_peer, :]
        rows = dot(pick, have.reshape(length, have.shape[2])).astype(BF16)
        rows_ref[turn] = rows
        last_ref[turn] = rows[length - BLOCK_LEN :]


def sort_rows(me, perms, arrived, length):
    rounds = perms.shape[0]
    peers, _, width = arrived.shape
    return pl.pallas_call(
        functools.partial(sort_rows_kernel, peers),
        grid_spec=pltpu.PrefetchScalarGridSpec(
            num_scalar_prefetch=1,
            grid=(1,),
            in_specs=[
                pl.BlockSpec((rounds, length), lambda i, s: (0, s[0])),
                pl.BlockSpec(arrived.shape, lambda i, s: (0, 0, 0)),
            ],
            out_specs=[
                pl.BlockSpec((rounds, length, width), lambda i, s: (0, 0, 0)),
                pl.BlockSpec((rounds, BLOCK_LEN, width), lambda i, s: (0, 0, 0)),
                pl.BlockSpec((rounds, 8, length), lambda i, s: (0, 0, 0)),
            ],
        ),
        out_shape=[
            jax.ShapeDtypeStruct((rounds, length, width), BF16),
            jax.ShapeDtypeStruct((rounds, BLOCK_LEN, width), BF16),
            jax.ShapeDtypeStruct((rounds, 8, length), I32),
        ],
        cost_estimate=cost(2 * rounds * length * length * width, 4 << 20),
        compiler_params=BIG,
        name="sort_rows",
    )(me, perms, arrived)


def window_scale(keys):
    wide = keys.astype(F32)
    squares = jnp.sum(wide * wide, axis=-1, keepdims=True)
    return to_row(lax.rsqrt(squares + 1e-06) / math.sqrt(HEAD_DIM))


def attend_tile(query, keys, values, scale, pos_q, pos_k):
    tile, window = query.shape[0], keys.shape[0]
    block_q = iota((tile, window), 0) // BLOCK_LEN
    block_k = iota((tile, window), 1) // BLOCK_LEN
    met = (block_k == block_q + 1) | (block_k == block_q + 2)
    scores = dot_t(query, keys) * scale
    scores = jnp.where(pos_k == pos_q, scores - 10000.0, scores)
    scores = jnp.where(met & (pos_k <= pos_q), scores, -1e30)
    peak = jnp.max(scores, axis=-1, keepdims=True)
    exponent = jnp.exp(scores - peak)
    total = jnp.sum(exponent, axis=-1, keepdims=True)
    weights = (exponent / total).astype(BF16)
    return dot(weights, values).astype(BF16), peak + jnp.log(total)


TILE, WINDOW, PIECES, GROUP = 2 * BLOCK_LEN, 4 * BLOCK_LEN, 3, 8


def put_logs(totals):
    lane = iota((totals[0].shape[0], LANES), 1) % GROUP
    logs = jnp.zeros(lane.shape, F32)
    for head, total in enumerate(totals):
        rest = total
        for piece in range(PIECES):
            part = rest.astype(BF16).astype(F32)
            logs = jnp.where(lane == head * PIECES + piece, part, logs)
            rest = rest - part
    return logs.astype(BF16)


def attend_later_kernel(me_ref, perms_ref, rows_ref, out_ref):
    rounds, length = perms_ref.shape
    span = rows_ref.shape[2] // 2
    for turn in range(rounds):
        position = perms_ref[turn : turn + 1, :].astype(F32)
        position_col = to_col(position)
        scales = []
        for head in range(span // HEAD_DIM):
            at = head * HEAD_DIM
            scales.append(window_scale(rows_ref[turn, :, at : at + HEAD_DIM]))
        for first in range(TILE, length, TILE):
            totals = []
            window = slice(first + TILE - WINDOW, first + TILE)
            queries = slice(first, first + TILE)
            for head in range(span // HEAD_DIM):
                at = head * HEAD_DIM
                out, total = attend_tile(
                    rows_ref[turn, queries, at : at + HEAD_DIM],
                    rows_ref[turn, window, at : at + HEAD_DIM],
                    rows_ref[turn, window, span + at : span + at + HEAD_DIM],
                    scales[head][:, window],
                    position_col[queries],
                    position[:, window],
                )
                out_ref[turn, first - TILE : first, at : at + HEAD_DIM] = out
                totals.append(total)
            out_ref[turn, first - TILE : first, span:] = put_logs(totals)


def attend_first_kernel(
    peers,
    me_ref,
    perms_ref,
    earlier_ref,
    rows_ref,
    last_ref,
    slot_ref,
    later_ref,
    out_ref,
):
    rounds, length = slot_ref.shape[0], slot_ref.shape[2]
    per_peer = length // peers
    span = rows_ref.shape[2] // 2
    lane_group = iota((peers, per_peer, LANES), 2) // GROUP
    own_group = lane_group == iota((peers, per_peer, LANES), 1)
    empty = jnp.zeros((BLOCK_LEN, HEAD_DIM), BF16)
    for turn in range(rounds):
        position = perms_ref[turn : turn + 1, :].astype(F32)
        positions = jnp.concatenate([earlier_ref[turn : turn + 1, :].astype(F32), position], axis=1)
        position_col = to_col(position)
        totals, outs = [], []
        for head in range(span // HEAD_DIM):
            at = head * HEAD_DIM
            own = rows_ref[turn, :, at : at + HEAD_DIM]
            keys = jnp.concatenate([empty, last_ref[turn, :, at : at + HEAD_DIM], own], axis=0)
            at = span + at
            values = jnp.concatenate(
                [
                    empty,
                    last_ref[turn, :, at : at + HEAD_DIM],
                    rows_ref[turn, :, at : at + HEAD_DIM],
                ],
                axis=0,
            )
            out, total = attend_tile(
                own, keys, values, window_scale(keys), position_col, positions
            )
            outs.append(out)
            totals.append(total)
        top = jnp.concatenate(outs + [put_logs(totals)], axis=1)
        whole = jnp.concatenate([top, later_ref[turn]], axis=0) if length > TILE else top
        back = flag(iota((length, length), 0) == slot_ref[turn, :1, :])
        moved = dot(back, whole)
        at = turn * per_peer
        out_ref[:, at : at + per_peer, :] = (
            moved[:, :span].astype(BF16).reshape(peers, per_peer, span)
        )
        logs = moved[:, span:].reshape(peers, per_peer, LANES)
        logs = jnp.sum(jnp.where(own_group, logs, 0.0), axis=1, keepdims=True)
        at = rounds * per_peer
        out_ref[:, at : at + GROUP, turn * LANES : (turn + 1) * LANES] = jnp.broadcast_to(
            logs, (peers, GROUP, LANES)
        ).astype(BF16)


def attend_later(me, perms, rows):
    rounds, length, width = rows.shape
    span = width // 2
    out = (rounds, length - TILE, span + LANES)
    return pl.pallas_call(
        attend_later_kernel,
        grid_spec=pltpu.PrefetchScalarGridSpec(
            num_scalar_prefetch=1,
            grid=(1,),
            in_specs=[
                pl.BlockSpec((rounds, length), lambda i, s: (0, s[0])),
                pl.BlockSpec(rows.shape, lambda i, s: (0, 0, 0)),
            ],
            out_specs=pl.BlockSpec(out, lambda i, s: (0, 0, 0)),
        ),
        out_shape=jax.ShapeDtypeStruct(out, BF16),
        cost_estimate=cost(2 << 30, 4 << 20),
        compiler_params=BIG,
        name="attend_later",
    )(me, perms, rows)


def attend_first(me, perms, rows, last, slot, later, peers):
    rounds, length, width = rows.shape
    span = width // 2
    per_peer = length // peers
    lane_blocks = length // LANES

    def fixed(shape):
        return pl.BlockSpec(shape, lambda i, s: (0, 0, 0))

    out = (peers, rounds * per_peer + GROUP, span)
    return pl.pallas_call(
        functools.partial(attend_first_kernel, peers),
        grid_spec=pltpu.PrefetchScalarGridSpec(
            num_scalar_prefetch=1,
            grid=(1,),
            in_specs=[
                pl.BlockSpec((rounds, TILE), lambda i, s: (0, s[0] * lane_blocks)),
                pl.BlockSpec(
                    (rounds, LANES),
                    lambda i, s: (
                        0,
                        jnp.where(s[0] == 0, peers * lane_blocks - 1, s[0] * lane_blocks - 1),
                    ),
                ),
                fixed((rounds, TILE, width)),
                fixed(last.shape),
                fixed(slot.shape),
                fixed(later.shape),
            ],
            out_specs=fixed(out),
        ),
        out_shape=jax.ShapeDtypeStruct(out, BF16),
        cost_estimate=cost(2 << 30, 4 << 20),
        compiler_params=BIG,
        name="attend_first",
    )(me, perms, perms, rows, last, slot, later)


def combine_kernel(got_ref, token_ref, mixed_ref):
    peers, _, span = got_ref.shape
    rounds, _, length = token_ref.shape
    per_peer = length // peers
    heads = span // HEAD_DIM
    lane_group = iota((peers, per_peer, LANES), 2) // GROUP
    own_group = lane_group == iota((peers, per_peer, LANES), 1)
    lane = iota((length, LANES), 1) % GROUP // PIECES
    column = iota((length, length), 0)
    outs, lses = [], []
    for turn in range(rounds):
        pick = flag(token_ref[turn, :1, :] == column)
        at = turn * per_peer
        rows = got_ref[:, at : at + per_peer, :].reshape(length, span)
        logs = got_ref[
            :, rounds * per_peer : rounds * per_peer + GROUP, turn * LANES : (turn + 1) * LANES
        ]
        logs = jnp.concatenate([logs] * (per_peer // GROUP), axis=1)
        logs = jnp.where(own_group, logs, jnp.zeros_like(logs)).reshape(length, LANES)
        outs.append(dot(pick, rows))
        moved = dot(pick, logs)
        lses.append(
            [
                jnp.sum(jnp.where(lane == head, moved, 0.0), axis=1, keepdims=True)
                for head in range(heads)
            ]
        )
    for head in range(heads):
        logs = [lse[head] for lse in lses]
        peak = functools.reduce(jnp.maximum, logs)
        whole = peak + jnp.log(functools.reduce(jnp.add, [jnp.exp(lse - peak) for lse in logs]))
        at = head * HEAD_DIM
        mixed = jnp.zeros((length, HEAD_DIM), F32)
        for out, lse in zip(outs, logs):
            mixed = mixed + out[:, at : at + HEAD_DIM] * jnp.exp(lse - whole)
        mixed_ref[:, at : at + HEAD_DIM] = mixed.astype(BF16)


def combine(got, token):
    rounds, _, length = token.shape
    return pl.pallas_call(
        combine_kernel,
        out_shape=jax.ShapeDtypeStruct((length, got.shape[2]), BF16),
        cost_estimate=cost(2 * rounds * length * length * (got.shape[2] + LANES), 1 << 20),
        compiler_params=BIG,
        name="combine",
    )(got, token)


def project_kernel(where_ref, own_ref, prev_ref, next_ref, far_a_ref, far_b_ref, *refs):
    weights, (kept_ref, given_ref) = refs[:-2], refs[-2:]
    far = jnp.concatenate([far_a_ref[...], far_b_ref[...]], axis=0)
    total = dot(own_ref[...], weights[0][...]) + dot(prev_ref[...], weights[1][...])
    total = total + dot(next_ref[...], weights[2][...]) + dot(far, weights[3][...])
    half = kept_ref.shape[1]
    for core in range(EXP_DEV):

        @pl.when(where_ref[1] == core)
        def _(core=core):
            kept_ref[...] = total[:, core * half : (core + 1) * half]
            other = 1 - core
            given_ref[...] = total[:, other * half : (other + 1) * half].astype(BF16)


def project(where, heads, w_out, others):
    length, span = heads[0].shape
    columns = others[0].shape[1]
    half = columns // EXP_DEV
    weights = (w_out, *others)
    shapes = [x.shape for x in heads] + [(span, columns)] + [x.shape for x in others]

    def first(i, e):
        return (0, 0)

    specs = [pl.BlockSpec(shape, first) for shape in shapes]
    specs[len(heads)] = pl.BlockSpec((span, columns), lambda i, e: (0, e[0]))
    return pl.pallas_call(
        project_kernel,
        grid_spec=pltpu.PrefetchScalarGridSpec(
            num_scalar_prefetch=1,
            grid=(1,),
            in_specs=specs,
            out_specs=[pl.BlockSpec((length, half), first)] * 2,
        ),
        out_shape=[
            jax.ShapeDtypeStruct((length, half), F32),
            jax.ShapeDtypeStruct((length, half), BF16),
        ],
        cost_estimate=cost(8 * length * span * columns, 3 << 20),
        compiler_params=BIG,
        name="project",
    )(where, *heads, *weights)


def exchange(x, axis):
    return lax.all_to_all(x, axis, split_axis=0, concat_axis=0, tiled=True)


def hop(x, by, chips):
    pairs = []
    for chip in range(chips):
        for core in range(EXP_DEV):
            there = (chip + by) % chips
            pairs.append((chip * EXP_DEV + core, there * EXP_DEV + core))
    return lax.ppermute(x, "exp", pairs)


def spread(x, chips):
    half = x.shape[0] // 2
    before, behind = hop(x, 1, chips), hop(x, -1, chips)
    far = (hop(before[:half], 1, chips), hop(behind[half:], -1, chips))
    return (x, before, behind), far


def after(x, *done):
    return lax.optimization_barrier((x, *done))[0]


def body(x_att, w_qk, w_val, w_out, perms, tokens_b, expert_ids, w_gate, w_up, w_down):
    peers, parts = lax.axis_size("seq"), lax.axis_size("exp")
    chips = parts // EXP_DEV
    me = lax.axis_index("seq").astype(I32).reshape(1)
    my_exp = lax.axis_index("exp").astype(I32)
    core = my_exp % EXP_DEV
    where = jnp.stack([my_exp // EXP_DEV, core])
    length, width = x_att.shape
    rounds = perms.shape[0]
    per_peer = length // peers
    tokb = tokens_b.shape[0]
    capacity = tokb // peers
    part = width // chips
    lines = [[chip * EXP_DEV + side for chip in range(chips)] for side in range(EXP_DEV)]
    siblings = [(i, i ^ 1) for i in range(parts)]

    dispatch, token_slot = pack_tokens(
        where, expert_ids.reshape(1, tokb), tokens_b, peers, capacity, part
    )
    received = exchange(dispatch.reshape(peers, capacity, part), "seq")
    outgoing, slot_token = pack_rows(me, perms, x_att, w_qk, w_val)
    own = (w_gate, w_up, w_down)
    sibling = [
        lax.ppermute(
            lax.dynamic_slice_in_dim(after(weight, dispatch), 1 - core, 1, 0), "exp", siblings
        )
        for weight in own
    ]
    columns = [
        hop(
            lax.dynamic_slice_in_dim(
                after(w_out, dispatch), (where[0] + by) % chips * part, part, 1
            ),
            by,
            chips,
        )
        for by in (1, chips - 1, 2)
    ]
    received = after(received, outgoing, *sibling, *columns)
    outgoing = after(outgoing, received)
    shards, far = spread(received, chips)
    arrived = exchange(outgoing.reshape(peers, rounds * per_peer, outgoing.shape[1]), "seq")
    expert_part = run_experts(where, shards, far, own, sibling)
    arrived = after(arrived, expert_part)
    expert_rows = lax.psum_scatter(
        expert_part, "exp", scatter_dimension=0, tiled=False, axis_index_groups=lines
    )
    rows, last, row_slot = sort_rows(me, perms, arrived, length)
    last = lax.ppermute(last, "seq", [(i, (i + 1) % peers) for i in range(peers)])
    later = attend_later(me, perms, rows) if length > TILE else rows
    last = after(last, later)
    packed = attend_first(me, perms, rows, last, row_slot, later, peers)
    got = exchange(packed, "seq")
    expert_rows = after(expert_rows, packed)
    kept = lax.dynamic_index_in_dim(expert_rows, core, 0, keepdims=False)
    given = lax.dynamic_index_in_dim(expert_rows, 1 - core, 0, keepdims=False)
    taken = lax.ppermute(given, "exp", siblings)
    expert_rows = jnp.stack([kept, taken], axis=1)
    mixed_heads = combine(after(got, expert_rows), slot_token)
    expert_back = exchange(after(expert_rows, mixed_heads), "seq")
    heads, far_heads = spread(mixed_heads, chips)
    attn_kept, attn_given = project(where, (*heads, *far_heads), w_out, columns)
    attended = attn_kept + lax.ppermute(attn_given, "exp", siblings).astype(F32)
    attended = attended.astype(BF16)
    expert_back = after(expert_back, attended)
    mixed = unpack_tokens(
        expert_back.reshape(peers * EXP_DEV * capacity, width // parts), token_slot
    )
    return (attended, mixed)


def solution(mesh):
    in_specs = (
        P("seq", None),
        P(None, "exp"),
        P(None, "exp"),
        P("exp", None),
        P(),
        P("seq", None),
        P("seq", None),
        P("seq", None, "exp"),
        P("seq", None, "exp"),
        P("seq", "exp", None),
    )
    out_specs = (P("seq", "exp"), P("seq", "exp"))
    return jax.shard_map(body, mesh=mesh, in_specs=in_specs, out_specs=out_specs, check_vma=False)
```

```python
import functools
import math

import jax
import jax.numpy as jnp
from jax import lax
from jax.experimental import pallas as pl
from jax.experimental.pallas import tpu as pltpu
from jax.sharding import PartitionSpec as P

HEAD_DIM = 128
BLOCK_LEN = 64
EXP_DEV = 2
LANES = 128
F32, BF16, I32 = jnp.float32, jnp.bfloat16, jnp.int32
BIG = pltpu.CompilerParams(vmem_limit_bytes=48 * 1024 * 1024)


def dot(a, b):
    return jnp.dot(a, b, preferred_element_type=F32)


def dot_t(a, b):
    return lax.dot_general(a, b, (((1,), (1,)), ((), ())), preferred_element_type=F32)


def to_col(row):
    return jnp.broadcast_to(row, (LANES, row.shape[1])).T[:, :1]


def to_row(col):
    return jnp.broadcast_to(col, (col.shape[0], LANES)).T[:1, :]


def iota(shape, dim):
    return lax.broadcasted_iota(I32, shape, dim)


def flag(mask, kind=BF16):
    return jnp.where(mask, 1.0, 0.0).astype(kind)


def cost(flops, size):
    return pl.CostEstimate(flops=flops, bytes_accessed=size, transcendentals=0)


def upper(count):
    return flag(iota((count, count), 0) <= iota((count, count), 1))


def pack_rows_kernel(me_ref, perms_ref, x_ref, qk_ref, val_ref, out_ref, token_ref, scratch):
    length, span = x_ref.shape[0], qk_ref.shape[1]
    rounds, total = perms_ref.shape
    peers = total // length
    per_peer = length // peers
    for peer in range(peers):
        scratch[peer * rounds : (peer + 1) * rounds, :] = perms_ref[
            :, peer * length : (peer + 1) * length
        ]
    perms = scratch[...]
    token = perms & (length - 1)
    mine = (perms >> (length.bit_length() - 1)) == me_ref[0]
    rank = dot(flag(mine), upper(length)).astype(I32) - 1
    slot = jnp.where(mine, rank, -1)
    groups = peers * rounds
    chosen = slot[:, None, :] == iota((groups, per_peer, length), 1)
    token_3d = jnp.where(chosen, token.astype(F32)[:, None, :], 0.0)
    column = jnp.sum(token_3d, axis=-1, keepdims=True).reshape(groups * per_peer, 1)
    by_round = column.reshape(peers, rounds, per_peer, 1)
    for turn in range(rounds):
        row = to_row(by_round[:, turn].reshape(peers * per_peer, 1)).astype(I32)
        token_ref[turn] = jnp.broadcast_to(row, token_ref.shape[1:])
    pick = flag(column.astype(I32) == iota((groups * per_peer, length), 1))
    for part, weight in enumerate((qk_ref, val_ref)):
        rows = dot(x_ref[...], weight[...]).astype(BF16)
        out_ref[:, part * span : (part + 1) * span] = dot(pick, rows).astype(BF16)


def pack_rows(me, perms, x_att, w_qk, w_val):
    length, width = x_att.shape
    rounds, total = perms.shape
    span = w_qk.shape[1]
    groups = rounds * (total // length)
    slots = rounds * length

    def whole(shape):
        return pl.BlockSpec(shape, lambda i, me_ref: (0, 0))

    return pl.pallas_call(
        pack_rows_kernel,
        grid_spec=pltpu.PrefetchScalarGridSpec(
            num_scalar_prefetch=1,
            grid=(1,),
            in_specs=[
                whole((rounds, total)),
                whole((length, width)),
                whole((width, span)),
                whole((width, span)),
            ],
            out_specs=[
                whole((slots, 2 * span)),
                pl.BlockSpec((rounds, 8, length), lambda i, me_ref: (0, 0, 0)),
            ],
            scratch_shapes=[pltpu.VMEM((groups, length), I32)],
        ),
        out_shape=[
            jax.ShapeDtypeStruct((slots, 2 * span), BF16),
            jax.ShapeDtypeStruct((rounds, 8, length), I32),
        ],
        cost_estimate=cost(4 * length * width * span + 4 * slots * length * span, 6 << 20),
        compiler_params=BIG,
        name="pack_rows",
    )(me, perms, x_att, w_qk, w_val)


def pack_tokens_kernel(peers, where_ref, ids_ref, tokens_ref, out_ref, slot_ref):
    length = tokens_ref.shape[0]
    slots = out_ref.shape[0]
    capacity = slots // peers
    experts = EXP_DEV * peers
    ids = ids_ref[...]
    hot = ids == iota((experts, length), 0)
    counts = dot(flag(hot), upper(length))
    rank = jnp.sum(jnp.where(hot, counts, 0.0), axis=0, keepdims=True).astype(I32) - 1
    core = where_ref[1]
    turn = (ids % EXP_DEV + core) % EXP_DEV
    peer = ids // EXP_DEV
    slot_ref[...] = jnp.broadcast_to(
        (peer * EXP_DEV + turn) * capacity + rank, slot_ref.shape
    )
    slot = jnp.where(turn == 0, peer * capacity + rank, -1)
    pick = flag(iota((slots, length), 0) == slot)
    out_ref[...] = dot(pick, tokens_ref[...]).astype(BF16)


def pack_tokens(where, ids, tokens, peers, capacity, part):
    length = tokens.shape[0]
    slots = peers * capacity
    return pl.pallas_call(
        functools.partial(pack_tokens_kernel, peers),
        grid_spec=pltpu.PrefetchScalarGridSpec(
            num_scalar_prefetch=1,
            grid=(1,),
            in_specs=[
                pl.BlockSpec((1, length), lambda i, e: (0, 0)),
                pl.BlockSpec((length, part), lambda i, e: (0, e[0])),
            ],
            out_specs=[
                pl.BlockSpec((slots, part), lambda i, e: (0, 0)),
                pl.BlockSpec((8, length), lambda i, e: (0, 0)),
            ],
        ),
        out_shape=[
            jax.ShapeDtypeStruct((slots, part), BF16),
            jax.ShapeDtypeStruct((8, length), I32),
        ],
        cost_estimate=cost(2 * slots * length * part, 2 << 20),
        compiler_params=BIG,
        name="pack_tokens",
    )(where, ids, tokens)


def experts_kernel(where_ref, *refs):
    step = pl.program_id(0)
    shards, far_refs, weights = refs[0:3], refs[3:5], refs[5:11]
    out_ref, total_ref = refs[11:]
    peers, capacity, part = shards[0].shape
    rows = peers * capacity
    ups = (weights[0], weights[1], weights[3], weights[4])

    def add(x, start):
        for index, weight in enumerate(ups):
            product = dot(x, weight[0])
            total_ref[index] = product if start else total_ref[index] + product

    for turn, shard in enumerate(shards):

        @pl.when(step == turn)
        def _(shard=shard, start=turn == 0):
            add(shard[...].reshape(rows, part), start)

    @pl.when(step == len(shards))
    def _():
        add(jnp.concatenate([ref[...].reshape(rows // 2, part) for ref in far_refs], axis=0), False)
        hiddens = []
        for side in range(EXP_DEV):
            gate, up_val = total_ref[2 * side], total_ref[2 * side + 1]
            hiddens.append((gate / (1.0 + jnp.exp(-gate)) * up_val).astype(BF16))
        half = part // EXP_DEV
        for index in range(out_ref.shape[0]):
            at = index * part
            piece = dot(hiddens[0], weights[2][0, :, at : at + part])
            piece = (piece + dot(hiddens[1], weights[5][0, :, at : at + part])).astype(BF16)
            for side in range(EXP_DEV):
                columns = piece[:, side * half : (side + 1) * half]
                out_ref[index, side] = columns.reshape(peers, capacity, half)


def run_experts(where, shards, far, own, sibling):
    peers, capacity, part = shards[0].shape
    width, hidden = own[0].shape[1:]
    chips = width // part
    out = (chips, EXP_DEV, peers, capacity, part // EXP_DEV)
    rows = peers * capacity

    def rows_of(i, e):
        ahead = jnp.where(i == 0, 0, jnp.where(i == 1, chips - 1, jnp.where(i == 2, 1, 2)))
        return (e[0] + ahead) % chips

    up_block, down_block = (1, part, hidden), (1, hidden, width)
    own_up = pl.BlockSpec(up_block, lambda i, e: (e[1], rows_of(i, e), 0))
    sibling_up = pl.BlockSpec(up_block, lambda i, e: (0, rows_of(i, e), 0))
    own_down = pl.BlockSpec(down_block, lambda i, e: (e[1], 0, 0))
    sibling_down = pl.BlockSpec(down_block, lambda i, e: (0, 0, 0))
    return pl.pallas_call(
        experts_kernel,
        grid_spec=pltpu.PrefetchScalarGridSpec(
            num_scalar_prefetch=1,
            grid=(len(shards) + 1,),
            in_specs=[pl.BlockSpec(x.shape, lambda i, e: (0, 0, 0)) for x in (*shards, *far)]
            + [own_up, own_up, own_down, sibling_up, sibling_up, sibling_down],
            out_specs=pl.BlockSpec(out, lambda i, e: (0, 0, 0, 0, 0)),
            scratch_shapes=[pltpu.VMEM((4, rows, hidden), F32)],
        ),
        out_shape=jax.ShapeDtypeStruct(out, BF16),
        cost_estimate=cost(12 * rows * width * hidden, 10 << 20),
        compiler_params=BIG,
        name="experts",
    )(where, *shards, *far, *own, *sibling)


def unpack_tokens_kernel(back_ref, slot_ref, out_ref):
    length = out_ref.shape[0]
    column = to_col(slot_ref[:1, :].astype(F32)).astype(I32)
    pick = flag(column == iota((length, back_ref.shape[0]), 1))
    out_ref[...] = dot(pick, back_ref[...]).astype(BF16)


def unpack_tokens(back, slot):
    length, width = slot.shape[1], back.shape[1]
    return pl.pallas_call(
        unpack_tokens_kernel,
        out_shape=jax.ShapeDtypeStruct((length, width), BF16),
        cost_estimate=cost(2 * length * back.shape[0] * width, 1 << 20),
        compiler_params=BIG,
        name="unpack_tokens",
    )(back, slot)


def sort_rows_kernel(peers, me_ref, perms_ref, arrived_ref, rows_ref, last_ref, slot_ref):
    rounds, length = perms_ref.shape
    per_peer = length // peers
    for turn in range(rounds):
        source = perms_ref[turn : turn + 1, :] >> (length.bit_length() - 1)
        hot = source == iota((peers, length), 0)
        counts = dot(flag(hot), upper(length))
        rank = jnp.sum(jnp.where(hot, counts, 0.0), axis=0, keepdims=True) - 1.0
        slot = source * per_peer + rank.astype(I32)
        slot_ref[turn] = jnp.broadcast_to(slot, slot_ref.shape[1:])
        pick = flag(to_col(slot.astype(F32)).astype(I32) == iota((length, length), 1))
        have = arrived_ref[:, turn * per_peer : (turn + 1) * per_peer, :]
        rows = dot(pick, have.reshape(length, have.shape[2])).astype(BF16)
        rows_ref[turn] = rows
        last_ref[turn] = rows[length - BLOCK_LEN :]


def sort_rows(me, perms, arrived, length):
    rounds = perms.shape[0]
    peers, _, width = arrived.shape
    return pl.pallas_call(
        functools.partial(sort_rows_kernel, peers),
        grid_spec=pltpu.PrefetchScalarGridSpec(
            num_scalar_prefetch=1,
            grid=(1,),
            in_specs=[
                pl.BlockSpec((rounds, length), lambda i, s: (0, s[0])),
                pl.BlockSpec(arrived.shape, lambda i, s: (0, 0, 0)),
            ],
            out_specs=[
                pl.BlockSpec((rounds, length, width), lambda i, s: (0, 0, 0)),
                pl.BlockSpec((rounds, BLOCK_LEN, width), lambda i, s: (0, 0, 0)),
                pl.BlockSpec((rounds, 8, length), lambda i, s: (0, 0, 0)),
            ],
        ),
        out_shape=[
            jax.ShapeDtypeStruct((rounds, length, width), BF16),
            jax.ShapeDtypeStruct((rounds, BLOCK_LEN, width), BF16),
            jax.ShapeDtypeStruct((rounds, 8, length), I32),
        ],
        cost_estimate=cost(2 * rounds * length * length * width, 4 << 20),
        compiler_params=BIG,
        name="sort_rows",
    )(me, perms, arrived)


def window_scale(keys):
    wide = keys.astype(F32)
    squares = jnp.sum(wide * wide, axis=-1, keepdims=True)
    return to_row(lax.rsqrt(squares + 1e-06) / math.sqrt(HEAD_DIM))


def attend_tile(query, keys, values, scale, pos_q, pos_k):
    tile, window = query.shape[0], keys.shape[0]
    block_q = iota((tile, window), 0) // BLOCK_LEN
    block_k = iota((tile, window), 1) // BLOCK_LEN
    met = (block_k == block_q + 1) | (block_k == block_q + 2)
    scores = dot_t(query, keys) * scale
    scores = jnp.where(pos_k == pos_q, scores - 10000.0, scores)
    scores = jnp.where(met & (pos_k <= pos_q), scores, -1e30)
    peak = jnp.max(scores, axis=-1, keepdims=True)
    exponent = jnp.exp(scores - peak)
    total = jnp.sum(exponent, axis=-1, keepdims=True)
    weights = (exponent / total).astype(BF16)
    return dot(weights, values).astype(BF16), peak + jnp.log(total)


TILE, WINDOW, PIECES, GROUP = 2 * BLOCK_LEN, 4 * BLOCK_LEN, 3, 8


def put_logs(totals):
    lane = iota((totals[0].shape[0], LANES), 1) % GROUP
    logs = jnp.zeros(lane.shape, F32)
    for head, total in enumerate(totals):
        rest = total
        for piece in range(PIECES):
            part = rest.astype(BF16).astype(F32)
            logs = jnp.where(lane == head * PIECES + piece, part, logs)
            rest = rest - part
    return logs.astype(BF16)


def attend_later_kernel(me_ref, perms_ref, rows_ref, out_ref):
    rounds, length = perms_ref.shape
    span = rows_ref.shape[2] // 2
    for turn in range(rounds):
        position = perms_ref[turn : turn + 1, :].astype(F32)
        position_col = to_col(position)
        scales = []
        for head in range(span // HEAD_DIM):
            at = head * HEAD_DIM
            scales.append(window_scale(rows_ref[turn, :, at : at + HEAD_DIM]))
        for first in range(TILE, length, TILE):
            totals = []
            window = slice(first + TILE - WINDOW, first + TILE)
            queries = slice(first, first + TILE)
            for head in range(span // HEAD_DIM):
                at = head * HEAD_DIM
                out, total = attend_tile(
                    rows_ref[turn, queries, at : at + HEAD_DIM],
                    rows_ref[turn, window, at : at + HEAD_DIM],
                    rows_ref[turn, window, span + at : span + at + HEAD_DIM],
                    scales[head][:, window],
                    position_col[queries],
                    position[:, window],
                )
                out_ref[turn, first - TILE : first, at : at + HEAD_DIM] = out
                totals.append(total)
            out_ref[turn, first - TILE : first, span:] = put_logs(totals)


def attend_first_kernel(
    peers,
    me_ref,
    perms_ref,
    earlier_ref,
    rows_ref,
    last_ref,
    slot_ref,
    later_ref,
    out_ref,
):
    rounds, length = slot_ref.shape[0], slot_ref.shape[2]
    per_peer = length // peers
    span = rows_ref.shape[2] // 2
    lane_group = iota((peers, per_peer, LANES), 2) // GROUP
    own_group = lane_group == iota((peers, per_peer, LANES), 1)
    empty = jnp.zeros((BLOCK_LEN, HEAD_DIM), BF16)
    for turn in range(rounds):
        position = perms_ref[turn : turn + 1, :].astype(F32)
        positions = jnp.concatenate([earlier_ref[turn : turn + 1, :].astype(F32), position], axis=1)
        position_col = to_col(position)
        totals, outs = [], []
        for head in range(span // HEAD_DIM):
            at = head * HEAD_DIM
            own = rows_ref[turn, :, at : at + HEAD_DIM]
            keys = jnp.concatenate([empty, last_ref[turn, :, at : at + HEAD_DIM], own], axis=0)
            at = span + at
            values = jnp.concatenate(
                [
                    empty,
                    last_ref[turn, :, at : at + HEAD_DIM],
                    rows_ref[turn, :, at : at + HEAD_DIM],
                ],
                axis=0,
            )
            out, total = attend_tile(
                own, keys, values, window_scale(keys), position_col, positions
            )
            outs.append(out)
            totals.append(total)
        top = jnp.concatenate(outs + [put_logs(totals)], axis=1)
        whole = jnp.concatenate([top, later_ref[turn]], axis=0) if length > TILE else top
        back = flag(iota((length, length), 0) == slot_ref[turn, :1, :])
        moved = dot(back, whole)
        at = turn * per_peer
        out_ref[:, at : at + per_peer, :] = (
            moved[:, :span].astype(BF16).reshape(peers, per_peer, span)
        )
        logs = moved[:, span:].reshape(peers, per_peer, LANES)
        logs = jnp.sum(jnp.where(own_group, logs, 0.0), axis=1, keepdims=True)
        at = rounds * per_peer
        out_ref[:, at : at + GROUP, turn * LANES : (turn + 1) * LANES] = jnp.broadcast_to(
            logs, (peers, GROUP, LANES)
        ).astype(BF16)


def attend_later(me, perms, rows):
    rounds, length, width = rows.shape
    span = width // 2
    out = (rounds, length - TILE, span + LANES)
    return pl.pallas_call(
        attend_later_kernel,
        grid_spec=pltpu.PrefetchScalarGridSpec(
            num_scalar_prefetch=1,
            grid=(1,),
            in_specs=[
                pl.BlockSpec((rounds, length), lambda i, s: (0, s[0])),
                pl.BlockSpec(rows.shape, lambda i, s: (0, 0, 0)),
            ],
            out_specs=pl.BlockSpec(out, lambda i, s: (0, 0, 0)),
        ),
        out_shape=jax.ShapeDtypeStruct(out, BF16),
        cost_estimate=cost(2 << 30, 4 << 20),
        compiler_params=BIG,
        name="attend_later",
    )(me, perms, rows)


def attend_first(me, perms, rows, last, slot, later, peers):
    rounds, length, width = rows.shape
    span = width // 2
    per_peer = length // peers
    lane_blocks = length // LANES

    def fixed(shape):
        return pl.BlockSpec(shape, lambda i, s: (0, 0, 0))

    out = (peers, rounds * per_peer + GROUP, span)
    return pl.pallas_call(
        functools.partial(attend_first_kernel, peers),
        grid_spec=pltpu.PrefetchScalarGridSpec(
            num_scalar_prefetch=1,
            grid=(1,),
            in_specs=[
                pl.BlockSpec((rounds, TILE), lambda i, s: (0, s[0] * lane_blocks)),
                pl.BlockSpec(
                    (rounds, LANES),
                    lambda i, s: (
                        0,
                        jnp.where(s[0] == 0, peers * lane_blocks - 1, s[0] * lane_blocks - 1),
                    ),
                ),
                fixed((rounds, TILE, width)),
                fixed(last.shape),
                fixed(slot.shape),
                fixed(later.shape),
            ],
            out_specs=fixed(out),
        ),
        out_shape=jax.ShapeDtypeStruct(out, BF16),
        cost_estimate=cost(2 << 30, 4 << 20),
        compiler_params=BIG,
        name="attend_first",
    )(me, perms, perms, rows, last, slot, later)


def combine_kernel(got_ref, token_ref, mixed_ref):
    peers, _, span = got_ref.shape
    rounds, _, length = token_ref.shape
    per_peer = length // peers
    heads = span // HEAD_DIM
    lane_group = iota((peers, per_peer, LANES), 2) // GROUP
    own_group = lane_group == iota((peers, per_peer, LANES), 1)
    lane = iota((length, LANES), 1) % GROUP // PIECES
    column = iota((length, length), 0)
    outs, lses = [], []
    for turn in range(rounds):
        pick = flag(token_ref[turn, :1, :] == column)
        at = turn * per_peer
        rows = got_ref[:, at : at + per_peer, :].reshape(length, span)
        logs = got_ref[
            :, rounds * per_peer : rounds * per_peer + GROUP, turn * LANES : (turn + 1) * LANES
        ]
        logs = jnp.concatenate([logs] * (per_peer // GROUP), axis=1)
        logs = jnp.where(own_group, logs, jnp.zeros_like(logs)).reshape(length, LANES)
        outs.append(dot(pick, rows))
        moved = dot(pick, logs)
        lses.append(
            [
                jnp.sum(jnp.where(lane == head, moved, 0.0), axis=1, keepdims=True)
                for head in range(heads)
            ]
        )
    for head in range(heads):
        logs = [lse[head] for lse in lses]
        peak = functools.reduce(jnp.maximum, logs)
        whole = peak + jnp.log(functools.reduce(jnp.add, [jnp.exp(lse - peak) for lse in logs]))
        at = head * HEAD_DIM
        mixed = jnp.zeros((length, HEAD_DIM), F32)
        for out, lse in zip(outs, logs):
            mixed = mixed + out[:, at : at + HEAD_DIM] * jnp.exp(lse - whole)
        mixed_ref[:, at : at + HEAD_DIM] = mixed.astype(BF16)


def combine(got, token):
    rounds, _, length = token.shape
    return pl.pallas_call(
        combine_kernel,
        out_shape=jax.ShapeDtypeStruct((length, got.shape[2]), BF16),
        cost_estimate=cost(2 * rounds * length * length * (got.shape[2] + LANES), 1 << 20),
        compiler_params=BIG,
        name="combine",
    )(got, token)


def project_kernel(where_ref, own_ref, prev_ref, next_ref, far_a_ref, far_b_ref, *refs):
    weights, (kept_ref, given_ref) = refs[:-2], refs[-2:]
    far = jnp.concatenate([far_a_ref[...], far_b_ref[...]], axis=0)
    total = dot(own_ref[...], weights[0][...]) + dot(prev_ref[...], weights[1][...])
    total = total + dot(next_ref[...], weights[2][...]) + dot(far, weights[3][...])
    half = kept_ref.shape[1]
    for core in range(EXP_DEV):

        @pl.when(where_ref[1] == core)
        def _(core=core):
            kept_ref[...] = total[:, core * half : (core + 1) * half]
            other = 1 - core
            given_ref[...] = total[:, other * half : (other + 1) * half].astype(BF16)


def project(where, heads, w_out, others):
    length, span = heads[0].shape
    columns = others[0].shape[1]
    half = columns // EXP_DEV
    weights = (w_out, *others)
    shapes = [x.shape for x in heads] + [(span, columns)] + [x.shape for x in others]

    def first(i, e):
        return (0, 0)

    specs = [pl.BlockSpec(shape, first) for shape in shapes]
    specs[len(heads)] = pl.BlockSpec((span, columns), lambda i, e: (0, e[0]))
    return pl.pallas_call(
        project_kernel,
        grid_spec=pltpu.PrefetchScalarGridSpec(
            num_scalar_prefetch=1,
            grid=(1,),
            in_specs=specs,
            out_specs=[pl.BlockSpec((length, half), first)] * 2,
        ),
        out_shape=[
            jax.ShapeDtypeStruct((length, half), F32),
            jax.ShapeDtypeStruct((length, half), BF16),
        ],
        cost_estimate=cost(8 * length * span * columns, 3 << 20),
        compiler_params=BIG,
        name="project",
    )(where, *heads, *weights)


def exchange(x, axis):
    return lax.all_to_all(x, axis, split_axis=0, concat_axis=0, tiled=True)


def hop(x, by, chips):
    pairs = []
    for chip in range(chips):
        for core in range(EXP_DEV):
            there = (chip + by) % chips
            pairs.append((chip * EXP_DEV + core, there * EXP_DEV + core))
    return lax.ppermute(x, "exp", pairs)


def spread(x, chips, ready=()):
    half = x.shape[0] // 2
    before, behind = hop(x, 1, chips), hop(x, -1, chips)
    before, behind = (after(side, *ready) if ready else side for side in (before, behind))
    far = (hop(before[:half], 1, chips), hop(behind[half:], -1, chips))
    return (x, before, behind), far


def after(x, *done):
    return lax.optimization_barrier((x, *done))[0]


def body(x_att, w_qk, w_val, w_out, perms, tokens_b, expert_ids, w_gate, w_up, w_down):
    peers, parts = lax.axis_size("seq"), lax.axis_size("exp")
    chips = parts // EXP_DEV
    me = lax.axis_index("seq").astype(I32).reshape(1)
    my_exp = lax.axis_index("exp").astype(I32)
    core = my_exp % EXP_DEV
    where = jnp.stack([my_exp // EXP_DEV, core])
    length, width = x_att.shape
    rounds = perms.shape[0]
    per_peer = length // peers
    tokb = tokens_b.shape[0]
    capacity = tokb // peers
    part = width // chips
    lines = [[chip * EXP_DEV + side for chip in range(chips)] for side in range(EXP_DEV)]
    siblings = [(i, i ^ 1) for i in range(parts)]

    dispatch, token_slot = pack_tokens(
        where, expert_ids.reshape(1, tokb), tokens_b, peers, capacity, part
    )
    received = exchange(dispatch.reshape(peers, capacity, part), "seq")
    outgoing, slot_token = pack_rows(me, perms, x_att, w_qk, w_val)
    columns = [
        hop(
            lax.dynamic_slice_in_dim(
                after(w_out, dispatch), (where[0] + by) % chips * part, part, 1
            ),
            by,
            chips,
        )
        for by in (1, chips - 1, 2)
    ]
    received = after(received, outgoing, *columns)
    outgoing = after(outgoing, received)
    own = (w_gate, w_up, w_down)
    sibling = [
        lax.ppermute(
            lax.dynamic_slice_in_dim(after(weight, received), 1 - core, 1, 0), "exp", siblings
        )
        for weight in own
    ]
    shards, far = spread(received, chips)
    arrived = exchange(outgoing.reshape(peers, rounds * per_peer, outgoing.shape[1]), "seq")
    expert_part = run_experts(where, shards, far, own, sibling)
    arrived = after(arrived, expert_part)
    rows, last, row_slot = sort_rows(me, perms, arrived, length)
    expert_rows = lax.psum_scatter(
        after(expert_part, last),
        "exp",
        scatter_dimension=0,
        tiled=False,
        axis_index_groups=lines,
    )
    last = lax.ppermute(last, "seq", [(i, (i + 1) % peers) for i in range(peers)])
    later = attend_later(me, perms, rows) if length > TILE else rows
    last = after(last, later)
    packed = attend_first(me, perms, rows, last, row_slot, later, peers)
    got = exchange(packed, "seq")
    expert_rows = after(expert_rows, packed)
    kept = lax.dynamic_index_in_dim(expert_rows, core, 0, keepdims=False)
    given = lax.dynamic_index_in_dim(expert_rows, 1 - core, 0, keepdims=False)
    taken = lax.ppermute(given, "exp", siblings)
    expert_rows = jnp.stack([kept, taken], axis=1)
    mixed_heads = combine(got, slot_token)
    expert_back = exchange(after(expert_rows, mixed_heads), "seq")
    heads, far_heads = spread(mixed_heads, chips, (expert_rows,))
    attn_kept, attn_given = project(where, (*heads, *far_heads), w_out, columns)
    attended = attn_kept + lax.ppermute(attn_given, "exp", siblings).astype(F32)
    attended = attended.astype(BF16)
    expert_back = after(expert_back, attended)
    mixed = unpack_tokens(
        expert_back.reshape(peers * EXP_DEV * capacity, width // parts), token_slot
    )
    return (attended, mixed)


def solution(mesh):
    in_specs = (
        P("seq", None),
        P(None, "exp"),
        P(None, "exp"),
        P("exp", None),
        P(),
        P("seq", None),
        P("seq", None),
        P("seq", None, "exp"),
        P("seq", None, "exp"),
        P("seq", "exp", None),
    )
    out_specs = (P("seq", "exp"), P("seq", "exp"))
    return jax.shard_map(body, mesh=mesh, in_specs=in_specs, out_specs=out_specs, check_vma=False)
```

```python
import functools
import math

import jax
import jax.numpy as jnp
from jax import lax
from jax.experimental import pallas as pl
from jax.experimental.pallas import tpu as pltpu
from jax.sharding import PartitionSpec as P

HEAD_DIM = 128
BLOCK_LEN = 64
EXP_DEV = 2
LANES = 128
F32, BF16, I32 = jnp.float32, jnp.bfloat16, jnp.int32
BIG = pltpu.CompilerParams(vmem_limit_bytes=48 * 1024 * 1024)


def dot(a, b):
    return jnp.dot(a, b, preferred_element_type=F32)


def dot_t(a, b):
    return lax.dot_general(a, b, (((1,), (1,)), ((), ())), preferred_element_type=F32)


def to_col(row):
    return jnp.broadcast_to(row, (LANES, row.shape[1])).T[:, :1]


def to_row(col):
    return jnp.broadcast_to(col, (col.shape[0], LANES)).T[:1, :]


def iota(shape, dim):
    return lax.broadcasted_iota(I32, shape, dim)


def flag(mask, kind=BF16):
    return jnp.where(mask, 1.0, 0.0).astype(kind)


def cost(flops, size):
    return pl.CostEstimate(flops=flops, bytes_accessed=size, transcendentals=0)


def upper(count):
    return flag(iota((count, count), 0) <= iota((count, count), 1))


def pack_rows_kernel(me_ref, perms_ref, x_ref, qk_ref, val_ref, out_ref, token_ref, scratch):
    length, span = x_ref.shape[0], qk_ref.shape[1]
    rounds, total = perms_ref.shape
    peers = total // length
    per_peer = length // peers
    for peer in range(peers):
        scratch[peer * rounds : (peer + 1) * rounds, :] = perms_ref[
            :, peer * length : (peer + 1) * length
        ]
    perms = scratch[...]
    token = perms & (length - 1)
    mine = (perms >> (length.bit_length() - 1)) == me_ref[0]
    rank = dot(flag(mine), upper(length)).astype(I32) - 1
    slot = jnp.where(mine, rank, -1)
    groups = peers * rounds
    chosen = slot[:, None, :] == iota((groups, per_peer, length), 1)
    token_3d = jnp.where(chosen, token.astype(F32)[:, None, :], 0.0)
    column = jnp.sum(token_3d, axis=-1, keepdims=True).reshape(groups * per_peer, 1)
    by_round = column.reshape(peers, rounds, per_peer, 1)
    for turn in range(rounds):
        row = to_row(by_round[:, turn].reshape(peers * per_peer, 1)).astype(I32)
        token_ref[turn] = jnp.broadcast_to(row, token_ref.shape[1:])
    pick = flag(column.astype(I32) == iota((groups * per_peer, length), 1))
    for part, weight in enumerate((qk_ref, val_ref)):
        rows = dot(x_ref[...], weight[...]).astype(BF16)
        out_ref[:, part * span : (part + 1) * span] = dot(pick, rows).astype(BF16)


def pack_rows(me, perms, x_att, w_qk, w_val):
    length, width = x_att.shape
    rounds, total = perms.shape
    span = w_qk.shape[1]
    groups = rounds * (total // length)
    slots = rounds * length

    def whole(shape):
        return pl.BlockSpec(shape, lambda i, me_ref: (0, 0))

    return pl.pallas_call(
        pack_rows_kernel,
        grid_spec=pltpu.PrefetchScalarGridSpec(
            num_scalar_prefetch=1,
            grid=(1,),
            in_specs=[
                whole((rounds, total)),
                whole((length, width)),
                whole((width, span)),
                whole((width, span)),
            ],
            out_specs=[
                whole((slots, 2 * span)),
                pl.BlockSpec((rounds, 8, length), lambda i, me_ref: (0, 0, 0)),
            ],
            scratch_shapes=[pltpu.VMEM((groups, length), I32)],
        ),
        out_shape=[
            jax.ShapeDtypeStruct((slots, 2 * span), BF16),
            jax.ShapeDtypeStruct((rounds, 8, length), I32),
        ],
        cost_estimate=cost(4 * length * width * span + 4 * slots * length * span, 6 << 20),
        compiler_params=BIG,
        name="pack_rows",
    )(me, perms, x_att, w_qk, w_val)


def pack_tokens_kernel(peers, where_ref, ids_ref, tokens_ref, out_ref, slot_ref):
    length = tokens_ref.shape[0]
    slots = out_ref.shape[0]
    capacity = slots // peers
    experts = EXP_DEV * peers
    ids = ids_ref[...]
    hot = ids == iota((experts, length), 0)
    counts = dot(flag(hot), upper(length))
    rank = jnp.sum(jnp.where(hot, counts, 0.0), axis=0, keepdims=True).astype(I32) - 1
    core = where_ref[1]
    turn = (ids % EXP_DEV + core) % EXP_DEV
    peer = ids // EXP_DEV
    slot_ref[...] = jnp.broadcast_to(
        (peer * EXP_DEV + turn) * capacity + rank, slot_ref.shape
    )
    slot = jnp.where(turn == 0, peer * capacity + rank, -1)
    pick = flag(iota((slots, length), 0) == slot)
    out_ref[...] = dot(pick, tokens_ref[...]).astype(BF16)


def pack_tokens(where, ids, tokens, peers, capacity, part):
    length = tokens.shape[0]
    slots = peers * capacity
    return pl.pallas_call(
        functools.partial(pack_tokens_kernel, peers),
        grid_spec=pltpu.PrefetchScalarGridSpec(
            num_scalar_prefetch=1,
            grid=(1,),
            in_specs=[
                pl.BlockSpec((1, length), lambda i, e: (0, 0)),
                pl.BlockSpec((length, part), lambda i, e: (0, e[0])),
            ],
            out_specs=[
                pl.BlockSpec((slots, part), lambda i, e: (0, 0)),
                pl.BlockSpec((8, length), lambda i, e: (0, 0)),
            ],
        ),
        out_shape=[
            jax.ShapeDtypeStruct((slots, part), BF16),
            jax.ShapeDtypeStruct((8, length), I32),
        ],
        cost_estimate=cost(2 * slots * length * part, 2 << 20),
        compiler_params=BIG,
        name="pack_tokens",
    )(where, ids, tokens)


def experts_kernel(where_ref, x_ref, *refs):
    step = pl.program_id(0)
    weights, (out_ref, total_ref, hidden_ref) = refs[:-3], refs[-3:]
    parts = pl.num_programs(0) // 2
    _, peers, capacity, part = x_ref.shape
    rows = peers * capacity
    ups = (weights[0], weights[1], weights[3], weights[4])

    @pl.when(step == 0)
    def _():
        for index, weight in enumerate(ups):
            total_ref[index] = dot(x_ref[0].reshape(rows, part), weight[0])

    @pl.when((step > 0) & (step < parts))
    def _():
        for index, weight in enumerate(ups):
            total_ref[index] += dot(x_ref[0].reshape(rows, part), weight[0])

    @pl.when(step == parts - 1)
    def _():
        for side in range(EXP_DEV):
            gate, up_val = total_ref[2 * side], total_ref[2 * side + 1]
            hidden_ref[side] = (gate / (1.0 + jnp.exp(-gate)) * up_val).astype(BF16)

    @pl.when(step >= parts)
    def _():
        piece = dot(hidden_ref[0], weights[2][0]) + dot(hidden_ref[1], weights[5][0])
        piece = piece.astype(BF16)
        half = part // EXP_DEV
        for side in range(EXP_DEV):
            columns = piece[:, side * half : (side + 1) * half]
            out_ref[0, side] = columns.reshape(peers, capacity, half)


def run_experts(where, x, own, sibling):
    parts, peers, capacity, part = x.shape
    width, hidden = own[0].shape[1:]
    out = (parts, EXP_DEV, peers, capacity, part // EXP_DEV)
    rows = peers * capacity

    def early(i):
        return jnp.minimum(i, parts - 1)

    def late(i):
        return jnp.maximum(i - parts, 0)

    up_block, down_block = (1, part, hidden), (1, hidden, part)
    own_up = pl.BlockSpec(up_block, lambda i, e: (e[1], early(i), 0))
    sibling_up = pl.BlockSpec(up_block, lambda i, e: (0, early(i), 0))
    own_down = pl.BlockSpec(down_block, lambda i, e: (e[1], 0, late(i)))
    sibling_down = pl.BlockSpec(down_block, lambda i, e: (0, 0, late(i)))
    return pl.pallas_call(
        experts_kernel,
        grid_spec=pltpu.PrefetchScalarGridSpec(
            num_scalar_prefetch=1,
            grid=(2 * parts,),
            in_specs=[pl.BlockSpec((1, *x.shape[1:]), lambda i, e: (early(i), 0, 0, 0))]
            + [own_up, own_up, own_down, sibling_up, sibling_up, sibling_down],
            out_specs=pl.BlockSpec((1, *out[1:]), lambda i, e: (late(i), 0, 0, 0, 0)),
            scratch_shapes=[
                pltpu.VMEM((2 * EXP_DEV, rows, hidden), F32),
                pltpu.VMEM((EXP_DEV, rows, hidden), BF16),
            ],
        ),
        out_shape=jax.ShapeDtypeStruct(out, BF16),
        cost_estimate=cost(12 * rows * width * hidden, 10 << 20),
        compiler_params=BIG,
        name="experts",
    )(where, x, *own, *sibling)


def unpack_tokens_kernel(back_ref, slot_ref, out_ref):
    length = out_ref.shape[0]
    column = to_col(slot_ref[:1, :].astype(F32)).astype(I32)
    pick = flag(column == iota((length, back_ref.shape[0]), 1))
    out_ref[...] = dot(pick, back_ref[...]).astype(BF16)


def unpack_tokens(back, slot):
    length, width = slot.shape[1], back.shape[1]
    return pl.pallas_call(
        unpack_tokens_kernel,
        out_shape=jax.ShapeDtypeStruct((length, width), BF16),
        cost_estimate=cost(2 * length * back.shape[0] * width, 1 << 20),
        compiler_params=BIG,
        name="unpack_tokens",
    )(back, slot)


def sort_rows_kernel(peers, me_ref, perms_ref, arrived_ref, rows_ref, last_ref, slot_ref):
    rounds, length = perms_ref.shape
    per_peer = length // peers
    for turn in range(rounds):
        source = perms_ref[turn : turn + 1, :] >> (length.bit_length() - 1)
        hot = source == iota((peers, length), 0)
        counts = dot(flag(hot), upper(length))
        rank = jnp.sum(jnp.where(hot, counts, 0.0), axis=0, keepdims=True) - 1.0
        slot = source * per_peer + rank.astype(I32)
        slot_ref[turn] = jnp.broadcast_to(slot, slot_ref.shape[1:])
        pick = flag(to_col(slot.astype(F32)).astype(I32) == iota((length, length), 1))
        have = arrived_ref[:, turn * per_peer : (turn + 1) * per_peer, :]
        rows = dot(pick, have.reshape(length, have.shape[2])).astype(BF16)
        rows_ref[turn] = rows
        last_ref[turn] = rows[length - BLOCK_LEN :]


def sort_rows(me, perms, arrived, length):
    rounds = perms.shape[0]
    peers, _, width = arrived.shape
    return pl.pallas_call(
        functools.partial(sort_rows_kernel, peers),
        grid_spec=pltpu.PrefetchScalarGridSpec(
            num_scalar_prefetch=1,
            grid=(1,),
            in_specs=[
                pl.BlockSpec((rounds, length), lambda i, s: (0, s[0])),
                pl.BlockSpec(arrived.shape, lambda i, s: (0, 0, 0)),
            ],
            out_specs=[
                pl.BlockSpec((rounds, length, width), lambda i, s: (0, 0, 0)),
                pl.BlockSpec((rounds, BLOCK_LEN, width), lambda i, s: (0, 0, 0)),
                pl.BlockSpec((rounds, 8, length), lambda i, s: (0, 0, 0)),
            ],
        ),
        out_shape=[
            jax.ShapeDtypeStruct((rounds, length, width), BF16),
            jax.ShapeDtypeStruct((rounds, BLOCK_LEN, width), BF16),
            jax.ShapeDtypeStruct((rounds, 8, length), I32),
        ],
        cost_estimate=cost(2 * rounds * length * length * width, 4 << 20),
        compiler_params=BIG,
        name="sort_rows",
    )(me, perms, arrived)


def window_scale(keys):
    wide = keys.astype(F32)
    squares = jnp.sum(wide * wide, axis=-1, keepdims=True)
    return to_row(lax.rsqrt(squares + 1e-06) / math.sqrt(HEAD_DIM))


def attend_tile(query, keys, values, scale, pos_q, pos_k):
    tile, window = query.shape[0], keys.shape[0]
    block_q = iota((tile, window), 0) // BLOCK_LEN
    block_k = iota((tile, window), 1) // BLOCK_LEN
    met = (block_k == block_q + 1) | (block_k == block_q + 2)
    scores = dot_t(query, keys) * scale
    scores = jnp.where(pos_k == pos_q, scores - 10000.0, scores)
    scores = jnp.where(met & (pos_k <= pos_q), scores, -1e30)
    peak = jnp.max(scores, axis=-1, keepdims=True)
    exponent = jnp.exp(scores - peak)
    total = jnp.sum(exponent, axis=-1, keepdims=True)
    weights = (exponent / total).astype(BF16)
    return dot(weights, values).astype(BF16), peak + jnp.log(total)


TILE, WINDOW, PIECES, GROUP = 2 * BLOCK_LEN, 4 * BLOCK_LEN, 3, 8


def put_logs(totals):
    lane = iota((totals[0].shape[0], LANES), 1) % GROUP
    logs = jnp.zeros(lane.shape, F32)
    for head, total in enumerate(totals):
        rest = total
        for piece in range(PIECES):
            part = rest.astype(BF16).astype(F32)
            logs = jnp.where(lane == head * PIECES + piece, part, logs)
            rest = rest - part
    return logs.astype(BF16)


def attend_later_kernel(me_ref, perms_ref, rows_ref, out_ref):
    rounds, length = perms_ref.shape
    span = rows_ref.shape[2] // 2
    for turn in range(rounds):
        position = perms_ref[turn : turn + 1, :].astype(F32)
        position_col = to_col(position)
        scales = []
        for head in range(span // HEAD_DIM):
            at = head * HEAD_DIM
            scales.append(window_scale(rows_ref[turn, :, at : at + HEAD_DIM]))
        for first in range(TILE, length, TILE):
            totals = []
            window = slice(first + TILE - WINDOW, first + TILE)
            queries = slice(first, first + TILE)
            for head in range(span // HEAD_DIM):
                at = head * HEAD_DIM
                out, total = attend_tile(
                    rows_ref[turn, queries, at : at + HEAD_DIM],
                    rows_ref[turn, window, at : at + HEAD_DIM],
                    rows_ref[turn, window, span + at : span + at + HEAD_DIM],
                    scales[head][:, window],
                    position_col[queries],
                    position[:, window],
                )
                out_ref[turn, first - TILE : first, at : at + HEAD_DIM] = out
                totals.append(total)
            out_ref[turn, first - TILE : first, span:] = put_logs(totals)


def attend_first_kernel(
    peers,
    me_ref,
    perms_ref,
    earlier_ref,
    rows_ref,
    last_ref,
    slot_ref,
    later_ref,
    out_ref,
):
    rounds, length = slot_ref.shape[0], slot_ref.shape[2]
    per_peer = length // peers
    span = rows_ref.shape[2] // 2
    lane_group = iota((peers, per_peer, LANES), 2) // GROUP
    own_group = lane_group == iota((peers, per_peer, LANES), 1)
    empty = jnp.zeros((BLOCK_LEN, HEAD_DIM), BF16)
    for turn in range(rounds):
        position = perms_ref[turn : turn + 1, :].astype(F32)
        positions = jnp.concatenate([earlier_ref[turn : turn + 1, :].astype(F32), position], axis=1)
        position_col = to_col(position)
        totals, outs = [], []
        for head in range(span // HEAD_DIM):
            at = head * HEAD_DIM
            own = rows_ref[turn, :, at : at + HEAD_DIM]
            keys = jnp.concatenate([empty, last_ref[turn, :, at : at + HEAD_DIM], own], axis=0)
            at = span + at
            values = jnp.concatenate(
                [
                    empty,
                    last_ref[turn, :, at : at + HEAD_DIM],
                    rows_ref[turn, :, at : at + HEAD_DIM],
                ],
                axis=0,
            )
            out, total = attend_tile(
                own, keys, values, window_scale(keys), position_col, positions
            )
            outs.append(out)
            totals.append(total)
        top = jnp.concatenate(outs + [put_logs(totals)], axis=1)
        whole = jnp.concatenate([top, later_ref[turn]], axis=0) if length > TILE else top
        back = flag(iota((length, length), 0) == slot_ref[turn, :1, :])
        moved = dot(back, whole)
        at = turn * per_peer
        out_ref[:, at : at + per_peer, :] = (
            moved[:, :span].astype(BF16).reshape(peers, per_peer, span)
        )
        logs = moved[:, span:].reshape(peers, per_peer, LANES)
        logs = jnp.sum(jnp.where(own_group, logs, 0.0), axis=1, keepdims=True)
        at = rounds * per_peer
        out_ref[:, at : at + GROUP, turn * LANES : (turn + 1) * LANES] = jnp.broadcast_to(
            logs, (peers, GROUP, LANES)
        ).astype(BF16)


def attend_later(me, perms, rows):
    rounds, length, width = rows.shape
    span = width // 2
    out = (rounds, length - TILE, span + LANES)
    return pl.pallas_call(
        attend_later_kernel,
        grid_spec=pltpu.PrefetchScalarGridSpec(
            num_scalar_prefetch=1,
            grid=(1,),
            in_specs=[
                pl.BlockSpec((rounds, length), lambda i, s: (0, s[0])),
                pl.BlockSpec(rows.shape, lambda i, s: (0, 0, 0)),
            ],
            out_specs=pl.BlockSpec(out, lambda i, s: (0, 0, 0)),
        ),
        out_shape=jax.ShapeDtypeStruct(out, BF16),
        cost_estimate=cost(2 << 30, 4 << 20),
        compiler_params=BIG,
        name="attend_later",
    )(me, perms, rows)


def attend_first(me, perms, rows, last, slot, later, peers):
    rounds, length, width = rows.shape
    span = width // 2
    per_peer = length // peers
    lane_blocks = length // LANES

    def fixed(shape):
        return pl.BlockSpec(shape, lambda i, s: (0, 0, 0))

    out = (peers, rounds * per_peer + GROUP, span)
    return pl.pallas_call(
        functools.partial(attend_first_kernel, peers),
        grid_spec=pltpu.PrefetchScalarGridSpec(
            num_scalar_prefetch=1,
            grid=(1,),
            in_specs=[
                pl.BlockSpec((rounds, TILE), lambda i, s: (0, s[0] * lane_blocks)),
                pl.BlockSpec(
                    (rounds, LANES),
                    lambda i, s: (
                        0,
                        jnp.where(s[0] == 0, peers * lane_blocks - 1, s[0] * lane_blocks - 1),
                    ),
                ),
                fixed((rounds, TILE, width)),
                fixed(last.shape),
                fixed(slot.shape),
                fixed(later.shape),
            ],
            out_specs=fixed(out),
        ),
        out_shape=jax.ShapeDtypeStruct(out, BF16),
        cost_estimate=cost(2 << 30, 4 << 20),
        compiler_params=BIG,
        name="attend_first",
    )(me, perms, perms, rows, last, slot, later)


def combine_kernel(got_ref, token_ref, mixed_ref):
    peers, _, span = got_ref.shape
    rounds, _, length = token_ref.shape
    per_peer = length // peers
    heads = span // HEAD_DIM
    lane_group = iota((peers, per_peer, LANES), 2) // GROUP
    own_group = lane_group == iota((peers, per_peer, LANES), 1)
    lane = iota((length, LANES), 1) % GROUP // PIECES
    column = iota((length, length), 0)
    outs, lses = [], []
    for turn in range(rounds):
        pick = flag(token_ref[turn, :1, :] == column)
        at = turn * per_peer
        rows = got_ref[:, at : at + per_peer, :].reshape(length, span)
        logs = got_ref[
            :, rounds * per_peer : rounds * per_peer + GROUP, turn * LANES : (turn + 1) * LANES
        ]
        logs = jnp.concatenate([logs] * (per_peer // GROUP), axis=1)
        logs = jnp.where(own_group, logs, jnp.zeros_like(logs)).reshape(length, LANES)
        outs.append(dot(pick, rows))
        moved = dot(pick, logs)
        lses.append(
            [
                jnp.sum(jnp.where(lane == head, moved, 0.0), axis=1, keepdims=True)
                for head in range(heads)
            ]
        )
    for head in range(heads):
        logs = [lse[head] for lse in lses]
        peak = functools.reduce(jnp.maximum, logs)
        whole = peak + jnp.log(functools.reduce(jnp.add, [jnp.exp(lse - peak) for lse in logs]))
        at = head * HEAD_DIM
        mixed = jnp.zeros((length, HEAD_DIM), F32)
        for out, lse in zip(outs, logs):
            mixed = mixed + out[:, at : at + HEAD_DIM] * jnp.exp(lse - whole)
        mixed_ref[:, at : at + HEAD_DIM] = mixed.astype(BF16)


def combine(got, token):
    rounds, _, length = token.shape
    return pl.pallas_call(
        combine_kernel,
        out_shape=jax.ShapeDtypeStruct((length, got.shape[2]), BF16),
        cost_estimate=cost(2 * rounds * length * length * (got.shape[2] + LANES), 1 << 20),
        compiler_params=BIG,
        name="combine",
    )(got, token)


def project_kernel(where_ref, own_ref, prev_ref, next_ref, far_a_ref, far_b_ref, *refs):
    weights, (kept_ref, given_ref) = refs[:-2], refs[-2:]
    far = jnp.concatenate([far_a_ref[...], far_b_ref[...]], axis=0)
    total = dot(own_ref[...], weights[0][...]) + dot(prev_ref[...], weights[1][...])
    total = total + dot(next_ref[...], weights[2][...]) + dot(far, weights[3][...])
    half = kept_ref.shape[1]
    for core in range(EXP_DEV):

        @pl.when(where_ref[1] == core)
        def _(core=core):
            kept_ref[...] = total[:, core * half : (core + 1) * half]
            other = 1 - core
            given_ref[...] = total[:, other * half : (other + 1) * half].astype(BF16)


def project(where, heads, w_out, others):
    length, span = heads[0].shape
    columns = others[0].shape[1]
    half = columns // EXP_DEV
    weights = (w_out, *others)
    shapes = [x.shape for x in heads] + [(span, columns)] + [x.shape for x in others]

    def first(i, e):
        return (0, 0)

    specs = [pl.BlockSpec(shape, first) for shape in shapes]
    specs[len(heads)] = pl.BlockSpec((span, columns), lambda i, e: (0, e[0]))
    return pl.pallas_call(
        project_kernel,
        grid_spec=pltpu.PrefetchScalarGridSpec(
            num_scalar_prefetch=1,
            grid=(1,),
            in_specs=specs,
            out_specs=[pl.BlockSpec((length, half), first)] * 2,
        ),
        out_shape=[
            jax.ShapeDtypeStruct((length, half), F32),
            jax.ShapeDtypeStruct((length, half), BF16),
        ],
        cost_estimate=cost(8 * length * span * columns, 3 << 20),
        compiler_params=BIG,
        name="project",
    )(where, *heads, *weights)


def exchange(x, axis):
    return lax.all_to_all(x, axis, split_axis=0, concat_axis=0, tiled=True)


def hop(x, by, chips):
    pairs = []
    for chip in range(chips):
        for core in range(EXP_DEV):
            there = (chip + by) % chips
            pairs.append((chip * EXP_DEV + core, there * EXP_DEV + core))
    return lax.ppermute(x, "exp", pairs)


def after(x, *done):
    return lax.optimization_barrier((x, *done))[0]


def body(x_att, w_qk, w_val, w_out, perms, tokens_b, expert_ids, w_gate, w_up, w_down):
    peers, parts = lax.axis_size("seq"), lax.axis_size("exp")
    chips = parts // EXP_DEV
    me = lax.axis_index("seq").astype(I32).reshape(1)
    my_exp = lax.axis_index("exp").astype(I32)
    core = my_exp % EXP_DEV
    where = jnp.stack([my_exp // EXP_DEV, core])
    length, width = x_att.shape
    rounds = perms.shape[0]
    per_peer = length // peers
    tokb = tokens_b.shape[0]
    capacity = tokb // peers
    part = width // chips
    lines = [[chip * EXP_DEV + side for chip in range(chips)] for side in range(EXP_DEV)]
    siblings = [(i, i ^ 1) for i in range(parts)]

    dispatch, token_slot = pack_tokens(
        where, expert_ids.reshape(1, tokb), tokens_b, peers, capacity, part
    )
    received = exchange(dispatch.reshape(peers, capacity, part), "seq")
    outgoing, slot_token = pack_rows(me, perms, x_att, w_qk, w_val)
    columns = [
        hop(
            lax.dynamic_slice_in_dim(
                after(w_out, dispatch), (where[0] + by) % chips * part, part, 1
            ),
            by,
            chips,
        )
        for by in (1, chips - 1, 2)
    ]
    received = after(received, outgoing, *columns)
    outgoing = after(outgoing, received)
    own = (w_gate, w_up, w_down)
    sibling = [
        lax.ppermute(
            lax.dynamic_slice_in_dim(after(weight, received), 1 - core, 1, 0), "exp", siblings
        )
        for weight in own
    ]
    gathered = lax.all_gather(received, "exp", axis=0, tiled=False, axis_index_groups=lines)
    arrived = exchange(outgoing.reshape(peers, rounds * per_peer, outgoing.shape[1]), "seq")
    expert_part = run_experts(where, gathered, own, sibling)
    arrived = after(arrived, expert_part)
    rows, last, row_slot = sort_rows(me, perms, arrived, length)
    expert_rows = lax.psum_scatter(
        after(expert_part, last),
        "exp",
        scatter_dimension=0,
        tiled=False,
        axis_index_groups=lines,
    )
    last = lax.ppermute(last, "seq", [(i, (i + 1) % peers) for i in range(peers)])
    later = attend_later(me, perms, rows) if length > TILE else rows
    last = after(last, later)
    packed = attend_first(me, perms, rows, last, row_slot, later, peers)
    got = exchange(packed, "seq")
    expert_rows = after(expert_rows, packed)
    kept = lax.dynamic_index_in_dim(expert_rows, core, 0, keepdims=False)
    given = lax.dynamic_index_in_dim(expert_rows, 1 - core, 0, keepdims=False)
    taken = lax.ppermute(given, "exp", siblings)
    expert_rows = jnp.stack([kept, taken], axis=1)
    mixed_heads = combine(got, slot_token)
    before, behind = hop(mixed_heads, 1, chips), hop(mixed_heads, -1, chips)
    expert_back = exchange(after(expert_rows, before, behind), "seq")
    middle = length // 2
    heads = (
        mixed_heads,
        before,
        behind,
        hop(before[:middle], 1, chips),
        hop(behind[middle:], -1, chips),
    )
    attn_kept, attn_given = project(where, heads, w_out, columns)
    attended = attn_kept + lax.ppermute(attn_given, "exp", siblings).astype(F32)
    attended = attended.astype(BF16)
    expert_back = after(expert_back, attended)
    mixed = unpack_tokens(
        expert_back.reshape(peers * EXP_DEV * capacity, width // parts), token_slot
    )
    return (attended, mixed)


def solution(mesh):
    in_specs = (
        P("seq", None),
        P(None, "exp"),
        P(None, "exp"),
        P("exp", None),
        P(),
        P("seq", None),
        P("seq", None),
        P("seq", None, "exp"),
        P("seq", None, "exp"),
        P("seq", "exp", None),
    )
    out_specs = (P("seq", "exp"), P("seq", "exp"))
    return jax.shard_map(body, mesh=mesh, in_specs=in_specs, out_specs=out_specs, check_vma=False)
```

```python
import functools
import math

import jax
import jax.numpy as jnp
from jax import lax
from jax.experimental import pallas as pl
from jax.experimental.pallas import tpu as pltpu
from jax.sharding import PartitionSpec as P

HEAD_DIM = 128
BLOCK_LEN = 64
EXP_DEV = 2
LANES = 128
F32, BF16, I32 = jnp.float32, jnp.bfloat16, jnp.int32
LONG = 1 << 35
BIG = pltpu.CompilerParams(vmem_limit_bytes=48 * 1024 * 1024)


def dot(a, b):
    return jnp.dot(a, b, preferred_element_type=F32)


def dot_t(a, b):
    return lax.dot_general(a, b, (((1,), (1,)), ((), ())), preferred_element_type=F32)


def to_col(row):
    return jnp.broadcast_to(row, (LANES, row.shape[1])).T[:, :1]


def to_row(col):
    return jnp.broadcast_to(col, (col.shape[0], LANES)).T[:1, :]


def iota(shape, dim):
    return lax.broadcasted_iota(I32, shape, dim)


def flag(mask, kind=BF16):
    return jnp.where(mask, 1.0, 0.0).astype(kind)


def cost(flops, size):
    return pl.CostEstimate(flops=flops, bytes_accessed=size, transcendentals=0)


def upper(count):
    return flag(iota((count, count), 0) <= iota((count, count), 1))


def project_rows_kernel(me_ref, perms_ref, x_ref, qk_ref, val_ref, rows_ref, pick_ref, token_ref, scratch):
    length, span = x_ref.shape[0], qk_ref.shape[1]
    rounds, total = perms_ref.shape
    peers = total // length
    per_peer = length // peers
    for peer in range(peers):
        scratch[peer * rounds : (peer + 1) * rounds, :] = perms_ref[
            :, peer * length : (peer + 1) * length
        ]
    perms = scratch[...]
    token = perms & (length - 1)
    mine = (perms >> (length.bit_length() - 1)) == me_ref[0]
    rank = dot(flag(mine), upper(length)).astype(I32) - 1
    slot = jnp.where(mine, rank, -1)
    groups = peers * rounds
    chosen = slot[:, None, :] == iota((groups, per_peer, length), 1)
    token_3d = jnp.where(chosen, token.astype(F32)[:, None, :], 0.0)
    column = jnp.sum(token_3d, axis=-1, keepdims=True).reshape(groups * per_peer, 1)
    by_round = column.reshape(peers, rounds, per_peer, 1)
    for turn in range(rounds):
        row = to_row(by_round[:, turn].reshape(peers * per_peer, 1)).astype(I32)
        token_ref[turn] = jnp.broadcast_to(row, token_ref.shape[1:])
    pick_ref[...] = flag(column.astype(I32) == iota((groups * per_peer, length), 1))
    for part, weight in enumerate((qk_ref, val_ref)):
        rows = dot(x_ref[...], weight[...]).astype(BF16)
        rows_ref[:, part * span : (part + 1) * span] = rows


def project_rows(me, perms, x_att, w_qk, w_val):
    length, width = x_att.shape
    rounds, total = perms.shape
    span = w_qk.shape[1]
    groups = rounds * (total // length)
    slots = rounds * length

    def whole(shape):
        return pl.BlockSpec(shape, lambda i, me_ref: (0, 0))

    return pl.pallas_call(
        project_rows_kernel,
        grid_spec=pltpu.PrefetchScalarGridSpec(
            num_scalar_prefetch=1,
            grid=(1,),
            in_specs=[
                whole((rounds, total)),
                whole((length, width)),
                whole((width, span)),
                whole((width, span)),
            ],
            out_specs=[
                whole((length, 2 * span)),
                whole((slots, length)),
                pl.BlockSpec((rounds, 8, length), lambda i, me_ref: (0, 0, 0)),
            ],
            scratch_shapes=[pltpu.VMEM((groups, length), I32)],
        ),
        out_shape=[
            jax.ShapeDtypeStruct((length, 2 * span), BF16),
            jax.ShapeDtypeStruct((slots, length), BF16),
            jax.ShapeDtypeStruct((rounds, 8, length), I32),
        ],
        cost_estimate=cost(4 * length * width * span + 4 * slots * length * span, 6 << 20),
        compiler_params=BIG,
        name="project_rows",
    )(me, perms, x_att, w_qk, w_val)


def pack_rows_kernel(pick_ref, rows_ref, out_ref):
    out_ref[...] = dot(pick_ref[...], rows_ref[...]).astype(BF16)


def pack_rows(pick, rows):
    return pl.pallas_call(
        pack_rows_kernel,
        out_shape=jax.ShapeDtypeStruct((pick.shape[0], rows.shape[1]), BF16),
        cost_estimate=cost(LONG, 2 << 20),
        compiler_params=BIG,
        name="pack_rows",
    )(pick, rows)


def pack_tokens_kernel(peers, where_ref, ids_ref, tokens_ref, out_ref, slot_ref):
    length = tokens_ref.shape[0]
    slots = out_ref.shape[0]
    capacity = slots // peers
    experts = EXP_DEV * peers
    ids = ids_ref[...]
    hot = ids == iota((experts, length), 0)
    counts = dot(flag(hot), upper(length))
    rank = jnp.sum(jnp.where(hot, counts, 0.0), axis=0, keepdims=True).astype(I32) - 1
    core = where_ref[1]
    turn = (ids % EXP_DEV + core) % EXP_DEV
    peer = ids // EXP_DEV
    slot_ref[...] = jnp.broadcast_to(
        (peer * EXP_DEV + turn) * capacity + rank, slot_ref.shape
    )
    slot = jnp.where(turn == 0, peer * capacity + rank, -1)
    pick = flag(iota((slots, length), 0) == slot)
    out_ref[...] = dot(pick, tokens_ref[...]).astype(BF16)


def pack_tokens(where, ids, tokens, peers, capacity, part):
    length = tokens.shape[0]
    slots = peers * capacity
    return pl.pallas_call(
        functools.partial(pack_tokens_kernel, peers),
        grid_spec=pltpu.PrefetchScalarGridSpec(
            num_scalar_prefetch=1,
            grid=(1,),
            in_specs=[
                pl.BlockSpec((1, length), lambda i, e: (0, 0)),
                pl.BlockSpec((length, part), lambda i, e: (0, e[0])),
            ],
            out_specs=[
                pl.BlockSpec((slots, part), lambda i, e: (0, 0)),
                pl.BlockSpec((8, length), lambda i, e: (0, 0)),
            ],
        ),
        out_shape=[
            jax.ShapeDtypeStruct((slots, part), BF16),
            jax.ShapeDtypeStruct((8, length), I32),
        ],
        cost_estimate=cost(2 * slots * length * part, 2 << 20),
        compiler_params=BIG,
        name="pack_tokens",
    )(where, ids, tokens)


def experts_kernel(where_ref, *refs):
    step = pl.program_id(0)
    shards, far_refs, weights = refs[0:3], refs[3:5], refs[5:11]
    out_ref, total_ref = refs[11:]
    peers, capacity, part = shards[0].shape
    rows = peers * capacity
    ups = (weights[0], weights[1], weights[3], weights[4])

    def add(x, start):
        for index, weight in enumerate(ups):
            product = dot(x, weight[0])
            total_ref[index] = product if start else total_ref[index] + product

    for turn, shard in enumerate(shards):

        @pl.when(step == turn)
        def _(shard=shard, start=turn == 0):
            add(shard[...].reshape(rows, part), start)

    @pl.when(step == len(shards))
    def _():
        add(jnp.concatenate([ref[...].reshape(rows // 2, part) for ref in far_refs], axis=0), False)
        hiddens = []
        for side in range(EXP_DEV):
            gate, up_val = total_ref[2 * side], total_ref[2 * side + 1]
            hiddens.append((gate / (1.0 + jnp.exp(-gate)) * up_val).astype(BF16))
        half = part // EXP_DEV
        for index in range(out_ref.shape[0]):
            at = index * part
            piece = dot(hiddens[0], weights[2][0, :, at : at + part])
            piece = (piece + dot(hiddens[1], weights[5][0, :, at : at + part])).astype(BF16)
            for side in range(EXP_DEV):
                columns = piece[:, side * half : (side + 1) * half]
                out_ref[index, side] = columns.reshape(peers, capacity, half)


def run_experts(where, shards, far, own, sibling):
    peers, capacity, part = shards[0].shape
    width, hidden = own[0].shape[1:]
    chips = width // part
    out = (chips, EXP_DEV, peers, capacity, part // EXP_DEV)
    rows = peers * capacity

    def rows_of(i, e):
        ahead = jnp.where(i == 0, 0, jnp.where(i == 1, chips - 1, jnp.where(i == 2, 1, 2)))
        return (e[0] + ahead) % chips

    up_block, down_block = (1, part, hidden), (1, hidden, width)
    own_up = pl.BlockSpec(up_block, lambda i, e: (e[1], rows_of(i, e), 0))
    sibling_up = pl.BlockSpec(up_block, lambda i, e: (0, rows_of(i, e), 0))
    own_down = pl.BlockSpec(down_block, lambda i, e: (e[1], 0, 0))
    sibling_down = pl.BlockSpec(down_block, lambda i, e: (0, 0, 0))
    return pl.pallas_call(
        experts_kernel,
        grid_spec=pltpu.PrefetchScalarGridSpec(
            num_scalar_prefetch=1,
            grid=(len(shards) + 1,),
            in_specs=[pl.BlockSpec(x.shape, lambda i, e: (0, 0, 0)) for x in (*shards, *far)]
            + [own_up, own_up, own_down, sibling_up, sibling_up, sibling_down],
            out_specs=pl.BlockSpec(out, lambda i, e: (0, 0, 0, 0, 0)),
            scratch_shapes=[pltpu.VMEM((4, rows, hidden), F32)],
        ),
        out_shape=jax.ShapeDtypeStruct(out, BF16),
        cost_estimate=cost(12 * rows * width * hidden, 10 << 20),
        compiler_params=BIG,
        name="experts",
    )(where, *shards, *far, *own, *sibling)


def place_rows_kernel(where_ref, rows_ref, taken_ref, out_ref):
    out_ref[:, 0] = rows_ref[0]
    out_ref[:, 1] = taken_ref[...]


def place_rows(where, rows, taken):
    peers, capacity, half = taken.shape
    out = (peers, EXP_DEV, capacity, half)
    return pl.pallas_call(
        place_rows_kernel,
        grid_spec=pltpu.PrefetchScalarGridSpec(
            num_scalar_prefetch=1,
            grid=(1,),
            in_specs=[
                pl.BlockSpec((1, *taken.shape), lambda i, e: (e[1], 0, 0, 0)),
                pl.BlockSpec(taken.shape, lambda i, e: (0, 0, 0)),
            ],
            out_specs=pl.BlockSpec(out, lambda i, e: (0, 0, 0, 0)),
        ),
        out_shape=jax.ShapeDtypeStruct(out, BF16),
        cost_estimate=cost(LONG, 1 << 20),
        compiler_params=BIG,
        name="place_rows",
    )(where, rows, taken)


def unpack_tokens_kernel(back_ref, slot_ref, out_ref):
    length = out_ref.shape[0]
    column = to_col(slot_ref[:1, :].astype(F32)).astype(I32)
    pick = flag(column == iota((length, back_ref.shape[0]), 1))
    out_ref[...] = dot(pick, back_ref[...]).astype(BF16)


def unpack_tokens(back, slot):
    length, width = slot.shape[1], back.shape[1]
    return pl.pallas_call(
        unpack_tokens_kernel,
        out_shape=jax.ShapeDtypeStruct((length, width), BF16),
        cost_estimate=cost(2 * length * back.shape[0] * width, 1 << 20),
        compiler_params=BIG,
        name="unpack_tokens",
    )(back, slot)


def sort_rows_kernel(peers, me_ref, perms_ref, arrived_ref, rows_ref, last_ref, slot_ref):
    rounds, length = perms_ref.shape
    per_peer = length // peers
    for turn in range(rounds):
        source = perms_ref[turn : turn + 1, :] >> (length.bit_length() - 1)
        hot = source == iota((peers, length), 0)
        counts = dot(flag(hot), upper(length))
        rank = jnp.sum(jnp.where(hot, counts, 0.0), axis=0, keepdims=True) - 1.0
        slot = source * per_peer + rank.astype(I32)
        slot_ref[turn] = jnp.broadcast_to(slot, slot_ref.shape[1:])
        pick = flag(to_col(slot.astype(F32)).astype(I32) == iota((length, length), 1))
        have = arrived_ref[:, turn * per_peer : (turn + 1) * per_peer, :]
        rows = dot(pick, have.reshape(length, have.shape[2])).astype(BF16)
        rows_ref[turn] = rows
        last_ref[turn] = rows[length - BLOCK_LEN :]


def sort_rows(me, perms, arrived, length):
    rounds = perms.shape[0]
    peers, _, width = arrived.shape
    return pl.pallas_call(
        functools.partial(sort_rows_kernel, peers),
        grid_spec=pltpu.PrefetchScalarGridSpec(
            num_scalar_prefetch=1,
            grid=(1,),
            in_specs=[
                pl.BlockSpec((rounds, length), lambda i, s: (0, s[0])),
                pl.BlockSpec(arrived.shape, lambda i, s: (0, 0, 0)),
            ],
            out_specs=[
                pl.BlockSpec((rounds, length, width), lambda i, s: (0, 0, 0)),
                pl.BlockSpec((rounds, BLOCK_LEN, width), lambda i, s: (0, 0, 0)),
                pl.BlockSpec((rounds, 8, length), lambda i, s: (0, 0, 0)),
            ],
        ),
        out_shape=[
            jax.ShapeDtypeStruct((rounds, length, width), BF16),
            jax.ShapeDtypeStruct((rounds, BLOCK_LEN, width), BF16),
            jax.ShapeDtypeStruct((rounds, 8, length), I32),
        ],
        cost_estimate=cost(LONG, 4 << 20),
        compiler_params=BIG,
        name="sort_rows",
    )(me, perms, arrived)


def window_scale(keys):
    wide = keys.astype(F32)
    squares = jnp.sum(wide * wide, axis=-1, keepdims=True)
    return to_row(lax.rsqrt(squares + 1e-06) / math.sqrt(HEAD_DIM))


def attend_tile(query, keys, values, scale, pos_q, pos_k):
    tile, window = query.shape[0], keys.shape[0]
    block_q = iota((tile, window), 0) // BLOCK_LEN
    block_k = iota((tile, window), 1) // BLOCK_LEN
    met = (block_k == block_q + 1) | (block_k == block_q + 2)
    scores = dot_t(query, keys) * scale
    scores = jnp.where(pos_k == pos_q, scores - 10000.0, scores)
    scores = jnp.where(met & (pos_k <= pos_q), scores, -1e30)
    peak = jnp.max(scores, axis=-1, keepdims=True)
    exponent = jnp.exp(scores - peak)
    total = jnp.sum(exponent, axis=-1, keepdims=True)
    weights = (exponent / total).astype(BF16)
    return dot(weights, values).astype(BF16), peak + jnp.log(total)


TILE, WINDOW, PIECES, GROUP = 2 * BLOCK_LEN, 4 * BLOCK_LEN, 3, 8


def put_logs(totals):
    lane = iota((totals[0].shape[0], LANES), 1) % GROUP
    logs = jnp.zeros(lane.shape, F32)
    for head, total in enumerate(totals):
        rest = total
        for piece in range(PIECES):
            part = rest.astype(BF16).astype(F32)
            logs = jnp.where(lane == head * PIECES + piece, part, logs)
            rest = rest - part
    return logs.astype(BF16)


def attend_later_kernel(me_ref, perms_ref, rows_ref, out_ref):
    rounds, length = perms_ref.shape
    span = rows_ref.shape[2] // 2
    for turn in range(rounds):
        position = perms_ref[turn : turn + 1, :].astype(F32)
        position_col = to_col(position)
        scales = []
        for head in range(span // HEAD_DIM):
            at = head * HEAD_DIM
            scales.append(window_scale(rows_ref[turn, :, at : at + HEAD_DIM]))
        for first in range(TILE, length, TILE):
            totals = []
            window = slice(first + TILE - WINDOW, first + TILE)
            queries = slice(first, first + TILE)
            for head in range(span // HEAD_DIM):
                at = head * HEAD_DIM
                out, total = attend_tile(
                    rows_ref[turn, queries, at : at + HEAD_DIM],
                    rows_ref[turn, window, at : at + HEAD_DIM],
                    rows_ref[turn, window, span + at : span + at + HEAD_DIM],
                    scales[head][:, window],
                    position_col[queries],
                    position[:, window],
                )
                out_ref[turn, first - TILE : first, at : at + HEAD_DIM] = out
                totals.append(total)
            out_ref[turn, first - TILE : first, span:] = put_logs(totals)


def attend_first_kernel(
    peers,
    me_ref,
    perms_ref,
    earlier_ref,
    rows_ref,
    last_ref,
    slot_ref,
    later_ref,
    out_ref,
):
    rounds, length = slot_ref.shape[0], slot_ref.shape[2]
    per_peer = length // peers
    span = rows_ref.shape[2] // 2
    lane_group = iota((peers, per_peer, LANES), 2) // GROUP
    own_group = lane_group == iota((peers, per_peer, LANES), 1)
    empty = jnp.zeros((BLOCK_LEN, HEAD_DIM), BF16)
    for turn in range(rounds):
        position = perms_ref[turn : turn + 1, :].astype(F32)
        positions = jnp.concatenate([earlier_ref[turn : turn + 1, :].astype(F32), position], axis=1)
        position_col = to_col(position)
        totals, outs = [], []
        for head in range(span // HEAD_DIM):
            at = head * HEAD_DIM
            own = rows_ref[turn, :, at : at + HEAD_DIM]
            keys = jnp.concatenate([empty, last_ref[turn, :, at : at + HEAD_DIM], own], axis=0)
            at = span + at
            values = jnp.concatenate(
                [
                    empty,
                    last_ref[turn, :, at : at + HEAD_DIM],
                    rows_ref[turn, :, at : at + HEAD_DIM],
                ],
                axis=0,
            )
            out, total = attend_tile(
                own, keys, values, window_scale(keys), position_col, positions
            )
            outs.append(out)
            totals.append(total)
        top = jnp.concatenate(outs + [put_logs(totals)], axis=1)
        whole = jnp.concatenate([top, later_ref[turn]], axis=0) if length > TILE else top
        back = flag(iota((length, length), 0) == slot_ref[turn, :1, :])
        moved = dot(back, whole)
        at = turn * per_peer
        out_ref[:, at : at + per_peer, :] = (
            moved[:, :span].astype(BF16).reshape(peers, per_peer, span)
        )
        logs = moved[:, span:].reshape(peers, per_peer, LANES)
        logs = jnp.sum(jnp.where(own_group, logs, 0.0), axis=1, keepdims=True)
        at = rounds * per_peer
        out_ref[:, at : at + GROUP, turn * LANES : (turn + 1) * LANES] = jnp.broadcast_to(
            logs, (peers, GROUP, LANES)
        ).astype(BF16)


def attend_later(me, perms, rows):
    rounds, length, width = rows.shape
    span = width // 2
    out = (rounds, length - TILE, span + LANES)
    return pl.pallas_call(
        attend_later_kernel,
        grid_spec=pltpu.PrefetchScalarGridSpec(
            num_scalar_prefetch=1,
            grid=(1,),
            in_specs=[
                pl.BlockSpec((rounds, length), lambda i, s: (0, s[0])),
                pl.BlockSpec(rows.shape, lambda i, s: (0, 0, 0)),
            ],
            out_specs=pl.BlockSpec(out, lambda i, s: (0, 0, 0)),
        ),
        out_shape=jax.ShapeDtypeStruct(out, BF16),
        cost_estimate=cost(LONG, 4 << 20),
        compiler_params=BIG,
        name="attend_later",
    )(me, perms, rows)


def attend_first(me, perms, rows, last, slot, later, peers):
    rounds, length, width = rows.shape
    span = width // 2
    per_peer = length // peers
    lane_blocks = length // LANES

    def fixed(shape):
        return pl.BlockSpec(shape, lambda i, s: (0, 0, 0))

    out = (peers, rounds * per_peer + GROUP, span)
    return pl.pallas_call(
        functools.partial(attend_first_kernel, peers),
        grid_spec=pltpu.PrefetchScalarGridSpec(
            num_scalar_prefetch=1,
            grid=(1,),
            in_specs=[
                pl.BlockSpec((rounds, TILE), lambda i, s: (0, s[0] * lane_blocks)),
                pl.BlockSpec(
                    (rounds, LANES),
                    lambda i, s: (
                        0,
                        jnp.where(s[0] == 0, peers * lane_blocks - 1, s[0] * lane_blocks - 1),
                    ),
                ),
                fixed((rounds, TILE, width)),
                fixed(last.shape),
                fixed(slot.shape),
                fixed(later.shape),
            ],
            out_specs=fixed(out),
        ),
        out_shape=jax.ShapeDtypeStruct(out, BF16),
        cost_estimate=cost(LONG, 4 << 20),
        compiler_params=BIG,
        name="attend_first",
    )(me, perms, perms, rows, last, slot, later)


def combine_kernel(got_ref, token_ref, mixed_ref):
    peers, _, span = got_ref.shape
    rounds, _, length = token_ref.shape
    per_peer = length // peers
    heads = span // HEAD_DIM
    lane_group = iota((peers, per_peer, LANES), 2) // GROUP
    own_group = lane_group == iota((peers, per_peer, LANES), 1)
    lane = iota((length, LANES), 1) % GROUP // PIECES
    column = iota((length, length), 0)
    outs, lses = [], []
    for turn in range(rounds):
        pick = flag(token_ref[turn, :1, :] == column)
        at = turn * per_peer
        rows = got_ref[:, at : at + per_peer, :].reshape(length, span)
        logs = got_ref[
            :, rounds * per_peer : rounds * per_peer + GROUP, turn * LANES : (turn + 1) * LANES
        ]
        logs = jnp.concatenate([logs] * (per_peer // GROUP), axis=1)
        logs = jnp.where(own_group, logs, jnp.zeros_like(logs)).reshape(length, LANES)
        outs.append(dot(pick, rows))
        moved = dot(pick, logs)
        lses.append(
            [
                jnp.sum(jnp.where(lane == head, moved, 0.0), axis=1, keepdims=True)
                for head in range(heads)
            ]
        )
    for head in range(heads):
        logs = [lse[head] for lse in lses]
        peak = functools.reduce(jnp.maximum, logs)
        whole = peak + jnp.log(functools.reduce(jnp.add, [jnp.exp(lse - peak) for lse in logs]))
        at = head * HEAD_DIM
        mixed = jnp.zeros((length, HEAD_DIM), F32)
        for out, lse in zip(outs, logs):
            mixed = mixed + out[:, at : at + HEAD_DIM] * jnp.exp(lse - whole)
        mixed_ref[:, at : at + HEAD_DIM] = mixed.astype(BF16)


def combine(got, token):
    rounds, _, length = token.shape
    return pl.pallas_call(
        combine_kernel,
        out_shape=jax.ShapeDtypeStruct((length, got.shape[2]), BF16),
        cost_estimate=cost(2 * rounds * length * length * (got.shape[2] + LANES), 1 << 20),
        compiler_params=BIG,
        name="combine",
    )(got, token)


def project_kernel(where_ref, own_ref, prev_ref, next_ref, far_a_ref, far_b_ref, *refs):
    weights, (kept_ref, given_ref) = refs[:-2], refs[-2:]
    far = jnp.concatenate([far_a_ref[...], far_b_ref[...]], axis=0)
    total = dot(own_ref[...], weights[0][...]) + dot(prev_ref[...], weights[1][...])
    total = total + dot(next_ref[...], weights[2][...]) + dot(far, weights[3][...])
    half = kept_ref.shape[1]
    for core in range(EXP_DEV):

        @pl.when(where_ref[1] == core)
        def _(core=core):
            kept_ref[...] = total[:, core * half : (core + 1) * half]
            other = 1 - core
            given_ref[...] = total[:, other * half : (other + 1) * half].astype(BF16)


def project(where, heads, w_out, others):
    length, span = heads[0].shape
    columns = others[0].shape[1]
    half = columns // EXP_DEV
    weights = (w_out, *others)
    shapes = [x.shape for x in heads] + [(span, columns)] + [x.shape for x in others]

    def first(i, e):
        return (0, 0)

    specs = [pl.BlockSpec(shape, first) for shape in shapes]
    specs[len(heads)] = pl.BlockSpec((span, columns), lambda i, e: (0, e[0]))
    return pl.pallas_call(
        project_kernel,
        grid_spec=pltpu.PrefetchScalarGridSpec(
            num_scalar_prefetch=1,
            grid=(1,),
            in_specs=specs,
            out_specs=[pl.BlockSpec((length, half), first)] * 2,
        ),
        out_shape=[
            jax.ShapeDtypeStruct((length, half), F32),
            jax.ShapeDtypeStruct((length, half), BF16),
        ],
        cost_estimate=cost(8 * length * span * columns, 3 << 20),
        compiler_params=BIG,
        name="project",
    )(where, *heads, *weights)


def exchange(x, axis):
    return lax.all_to_all(x, axis, split_axis=0, concat_axis=0, tiled=True)


def hop(x, by, chips):
    pairs = []
    for chip in range(chips):
        for core in range(EXP_DEV):
            there = (chip + by) % chips
            pairs.append((chip * EXP_DEV + core, there * EXP_DEV + core))
    return lax.ppermute(x, "exp", pairs)


def spread(x, chips, ready=()):
    half = x.shape[0] // 2
    before, behind = hop(x, 1, chips), hop(x, -1, chips)
    before, behind = (after(side, *ready) if ready else side for side in (before, behind))
    far = (hop(before[:half], 1, chips), hop(behind[half:], -1, chips))
    return (x, before, behind), far


def after(x, *done):
    return lax.optimization_barrier((x, *done))[0]


def body(x_att, w_qk, w_val, w_out, perms, tokens_b, expert_ids, w_gate, w_up, w_down):
    peers, parts = lax.axis_size("seq"), lax.axis_size("exp")
    chips = parts // EXP_DEV
    me = lax.axis_index("seq").astype(I32).reshape(1)
    my_exp = lax.axis_index("exp").astype(I32)
    core = my_exp % EXP_DEV
    where = jnp.stack([my_exp // EXP_DEV, core])
    length, width = x_att.shape
    rounds = perms.shape[0]
    per_peer = length // peers
    tokb = tokens_b.shape[0]
    capacity = tokb // peers
    part = width // chips
    lines = [[chip * EXP_DEV + side for chip in range(chips)] for side in range(EXP_DEV)]
    siblings = [(i, i ^ 1) for i in range(parts)]

    dispatch, token_slot = pack_tokens(
        where, expert_ids.reshape(1, tokb), tokens_b, peers, capacity, part
    )
    received = exchange(dispatch.reshape(peers, capacity, part), "seq")
    projected, pick, slot_token = project_rows(me, perms, x_att, w_qk, w_val)
    columns = [
        hop(
            lax.dynamic_slice_in_dim(
                after(w_out, dispatch), (where[0] + by) % chips * part, part, 1
            ),
            by,
            chips,
        )
        for by in (1, chips - 1, 2)
    ]
    received = after(received, projected, *columns)
    outgoing = pack_rows(pick, after(projected, received))
    own = (w_gate, w_up, w_down)
    sibling = [
        lax.ppermute(
            lax.dynamic_slice_in_dim(after(weight, received), 1 - core, 1, 0), "exp", siblings
        )
        for weight in own
    ]
    shards, far = spread(received, chips)
    arrived = exchange(outgoing.reshape(peers, rounds * per_peer, outgoing.shape[1]), "seq")
    expert_part = run_experts(where, shards, far, own, sibling)
    arrived = after(arrived, expert_part)
    rows, last, row_slot = sort_rows(me, perms, arrived, length)
    expert_rows = lax.psum_scatter(
        expert_part,
        "exp",
        scatter_dimension=0,
        tiled=False,
        axis_index_groups=lines,
    )
    last = lax.ppermute(last, "seq", [(i, (i + 1) % peers) for i in range(peers)])
    later = attend_later(me, perms, rows) if length > TILE else rows
    last = after(last, later)
    packed = attend_first(me, perms, rows, last, row_slot, later, peers)
    got = exchange(packed, "seq")
    expert_rows = after(expert_rows, packed)
    given = lax.dynamic_index_in_dim(expert_rows, 1 - core, 0, keepdims=False)
    taken = lax.ppermute(given, "exp", siblings)
    mixed_heads = combine(got, slot_token)
    expert_rows = place_rows(where, expert_rows, after(taken, mixed_heads))
    expert_back = exchange(expert_rows, "seq")
    heads, far_heads = spread(mixed_heads, chips, (expert_rows,))
    attn_kept, attn_given = project(where, (*heads, *far_heads), w_out, columns)
    attended = attn_kept + lax.ppermute(attn_given, "exp", siblings).astype(F32)
    attended = attended.astype(BF16)
    expert_back = after(expert_back, attended)
    mixed = unpack_tokens(
        expert_back.reshape(peers * EXP_DEV * capacity, width // parts), token_slot
    )
    return (attended, mixed)


def solution(mesh):
    in_specs = (
        P("seq", None),
        P(None, "exp"),
        P(None, "exp"),
        P("exp", None),
        P(),
        P("seq", None),
        P("seq", None),
        P("seq", None, "exp"),
        P("seq", None, "exp"),
        P("seq", "exp", None),
    )
    out_specs = (P("seq", "exp"), P("seq", "exp"))
    return jax.shard_map(body, mesh=mesh, in_specs=in_specs, out_specs=out_specs, check_vma=False)
```

```python
import functools
import math

import jax
import jax.numpy as jnp
from jax import lax
from jax.experimental import pallas as pl
from jax.experimental.pallas import tpu as pltpu
from jax.sharding import PartitionSpec as P

HEAD_DIM = 128
BLOCK_LEN = 64
EXP_DEV = 2
LANES = 128
F32, BF16, I32 = jnp.float32, jnp.bfloat16, jnp.int32
LONG = 1 << 35
BIG = pltpu.CompilerParams(vmem_limit_bytes=48 * 1024 * 1024)


def dot(a, b):
    return jnp.dot(a, b, preferred_element_type=F32)


def dot_t(a, b):
    return lax.dot_general(a, b, (((1,), (1,)), ((), ())), preferred_element_type=F32)


def to_col(row):
    return jnp.broadcast_to(row, (LANES, row.shape[1])).T[:, :1]


def to_row(col):
    return jnp.broadcast_to(col, (col.shape[0], LANES)).T[:1, :]


def iota(shape, dim):
    return lax.broadcasted_iota(I32, shape, dim)


def flag(mask, kind=BF16):
    return jnp.where(mask, 1.0, 0.0).astype(kind)


def cost(flops, size):
    return pl.CostEstimate(flops=flops, bytes_accessed=size, transcendentals=0)


def upper(count):
    return flag(iota((count, count), 0) <= iota((count, count), 1))


def pack_rows_kernel(me_ref, perms_ref, x_ref, qk_ref, val_ref, out_ref, token_ref, scratch):
    length, span = x_ref.shape[0], qk_ref.shape[1]
    rounds, total = perms_ref.shape
    peers = total // length
    per_peer = length // peers
    for peer in range(peers):
        scratch[peer * rounds : (peer + 1) * rounds, :] = perms_ref[
            :, peer * length : (peer + 1) * length
        ]
    perms = scratch[...]
    token = perms & (length - 1)
    mine = (perms >> (length.bit_length() - 1)) == me_ref[0]
    rank = dot(flag(mine), upper(length)).astype(I32) - 1
    slot = jnp.where(mine, rank, -1)
    groups = peers * rounds
    chosen = slot[:, None, :] == iota((groups, per_peer, length), 1)
    token_3d = jnp.where(chosen, token.astype(F32)[:, None, :], 0.0)
    column = jnp.sum(token_3d, axis=-1, keepdims=True).reshape(groups * per_peer, 1)
    by_round = column.reshape(peers, rounds, per_peer, 1)
    for turn in range(rounds):
        row = to_row(by_round[:, turn].reshape(peers * per_peer, 1)).astype(I32)
        token_ref[turn] = jnp.broadcast_to(row, token_ref.shape[1:])
    pick = flag(column.astype(I32) == iota((groups * per_peer, length), 1))
    for part, weight in enumerate((qk_ref, val_ref)):
        rows = dot(x_ref[...], weight[...]).astype(BF16)
        out_ref[:, part * span : (part + 1) * span] = dot(pick, rows).astype(BF16)


def pack_rows(me, perms, x_att, w_qk, w_val):
    length, width = x_att.shape
    rounds, total = perms.shape
    span = w_qk.shape[1]
    groups = rounds * (total // length)
    slots = rounds * length

    def whole(shape):
        return pl.BlockSpec(shape, lambda i, me_ref: (0, 0))

    return pl.pallas_call(
        pack_rows_kernel,
        grid_spec=pltpu.PrefetchScalarGridSpec(
            num_scalar_prefetch=1,
            grid=(1,),
            in_specs=[
                whole((rounds, total)),
                whole((length, width)),
                whole((width, span)),
                whole((width, span)),
            ],
            out_specs=[
                whole((slots, 2 * span)),
                pl.BlockSpec((rounds, 8, length), lambda i, me_ref: (0, 0, 0)),
            ],
            scratch_shapes=[pltpu.VMEM((groups, length), I32)],
        ),
        out_shape=[
            jax.ShapeDtypeStruct((slots, 2 * span), BF16),
            jax.ShapeDtypeStruct((rounds, 8, length), I32),
        ],
        cost_estimate=cost(4 * length * width * span + 4 * slots * length * span, 6 << 20),
        compiler_params=BIG,
        name="pack_rows",
    )(me, perms, x_att, w_qk, w_val)


def pack_tokens_kernel(peers, where_ref, ids_ref, tokens_ref, out_ref, slot_ref):
    length = tokens_ref.shape[0]
    slots = out_ref.shape[0]
    capacity = slots // peers
    experts = EXP_DEV * peers
    ids = ids_ref[...]
    hot = ids == iota((experts, length), 0)
    counts = dot(flag(hot), upper(length))
    rank = jnp.sum(jnp.where(hot, counts, 0.0), axis=0, keepdims=True).astype(I32) - 1
    core = where_ref[1]
    turn = (ids % EXP_DEV + core) % EXP_DEV
    peer = ids // EXP_DEV
    slot_ref[...] = jnp.broadcast_to(
        (peer * EXP_DEV + turn) * capacity + rank, slot_ref.shape
    )
    slot = jnp.where(turn == 0, peer * capacity + rank, -1)
    pick = flag(iota((slots, length), 0) == slot)
    out_ref[...] = dot(pick, tokens_ref[...]).astype(BF16)


def pack_tokens(where, ids, tokens, peers, capacity, part):
    length = tokens.shape[0]
    slots = peers * capacity
    return pl.pallas_call(
        functools.partial(pack_tokens_kernel, peers),
        grid_spec=pltpu.PrefetchScalarGridSpec(
            num_scalar_prefetch=1,
            grid=(1,),
            in_specs=[
                pl.BlockSpec((1, length), lambda i, e: (0, 0)),
                pl.BlockSpec((length, part), lambda i, e: (0, e[0])),
            ],
            out_specs=[
                pl.BlockSpec((slots, part), lambda i, e: (0, 0)),
                pl.BlockSpec((8, length), lambda i, e: (0, 0)),
            ],
        ),
        out_shape=[
            jax.ShapeDtypeStruct((slots, part), BF16),
            jax.ShapeDtypeStruct((8, length), I32),
        ],
        cost_estimate=cost(2 * slots * length * part, 2 << 20),
        compiler_params=BIG,
        name="pack_tokens",
    )(where, ids, tokens)


def chip_at(place, core, chips):
    return jnp.where(core == 0, place, chips - 1 - place)


def experts_kernel(where_ref, x_ref, *refs):
    step, chips = pl.program_id(0), pl.num_programs(0)
    weights, (out_ref, total_ref) = refs[:-2], refs[-2:]
    _, peers, capacity, part = x_ref.shape
    rows = peers * capacity
    ups = (weights[0], weights[1], weights[3], weights[4])

    @pl.when(step == 0)
    def _():
        for index, weight in enumerate(ups):
            total_ref[index] = dot(x_ref[0].reshape(rows, part), weight[0])

    @pl.when(step > 0)
    def _():
        for index, weight in enumerate(ups):
            total_ref[index] += dot(x_ref[0].reshape(rows, part), weight[0])

    @pl.when(step == chips - 1)
    def _():
        hiddens = []
        for side in range(EXP_DEV):
            gate, up_val = total_ref[2 * side], total_ref[2 * side + 1]
            hiddens.append((gate / (1.0 + jnp.exp(-gate)) * up_val).astype(BF16))
        half = part // EXP_DEV
        for index in range(out_ref.shape[0]):
            chip = chip_at(index, where_ref[1], out_ref.shape[0])
            columns = pl.ds(pl.multiple_of(chip * part, part), part)
            piece = dot(hiddens[0], weights[2][0, :, columns])
            piece = (piece + dot(hiddens[1], weights[5][0, :, columns])).astype(BF16)
            for side in range(EXP_DEV):
                columns = piece[:, side * half : (side + 1) * half]
                out_ref[index, side] = columns.reshape(peers, capacity, half)


def run_experts(where, x, own, sibling):
    chips, peers, capacity, part = x.shape
    width, hidden = own[0].shape[1:]
    out = (chips, EXP_DEV, peers, capacity, part // EXP_DEV)
    rows = peers * capacity
    up_block, down_block = (1, part, hidden), (1, hidden, width)
    own_up = pl.BlockSpec(up_block, lambda i, e: (e[1], chip_at(i, e[1], chips), 0))
    sibling_up = pl.BlockSpec(up_block, lambda i, e: (0, chip_at(i, e[1], chips), 0))
    own_down = pl.BlockSpec(down_block, lambda i, e: (e[1], 0, 0))
    sibling_down = pl.BlockSpec(down_block, lambda i, e: (0, 0, 0))
    return pl.pallas_call(
        experts_kernel,
        grid_spec=pltpu.PrefetchScalarGridSpec(
            num_scalar_prefetch=1,
            grid=(chips,),
            in_specs=[pl.BlockSpec((1, *x.shape[1:]), lambda i, e: (i, 0, 0, 0))]
            + [own_up, own_up, own_down, sibling_up, sibling_up, sibling_down],
            out_specs=pl.BlockSpec(out, lambda i, e: (0, 0, 0, 0, 0)),
            scratch_shapes=[pltpu.VMEM((2 * EXP_DEV, rows, hidden), F32)],
        ),
        out_shape=jax.ShapeDtypeStruct(out, BF16),
        cost_estimate=cost(12 * rows * width * hidden, 10 << 20),
        compiler_params=BIG,
        name="experts",
    )(where, x, *own, *sibling)


def place_rows_kernel(where_ref, rows_ref, taken_ref, out_ref):
    out_ref[:, 0] = rows_ref[0]
    out_ref[:, 1] = taken_ref[...]


def place_rows(where, rows, taken):
    peers, capacity, half = taken.shape
    out = (peers, EXP_DEV, capacity, half)
    return pl.pallas_call(
        place_rows_kernel,
        grid_spec=pltpu.PrefetchScalarGridSpec(
            num_scalar_prefetch=1,
            grid=(1,),
            in_specs=[
                pl.BlockSpec((1, *taken.shape), lambda i, e: (e[1], 0, 0, 0)),
                pl.BlockSpec(taken.shape, lambda i, e: (0, 0, 0)),
            ],
            out_specs=pl.BlockSpec(out, lambda i, e: (0, 0, 0, 0)),
        ),
        out_shape=jax.ShapeDtypeStruct(out, BF16),
        cost_estimate=cost(LONG, 1 << 20),
        compiler_params=BIG,
        name="place_rows",
    )(where, rows, taken)


def unpack_tokens_kernel(back_ref, slot_ref, out_ref):
    length = out_ref.shape[0]
    column = to_col(slot_ref[:1, :].astype(F32)).astype(I32)
    pick = flag(column == iota((length, back_ref.shape[0]), 1))
    out_ref[...] = dot(pick, back_ref[...]).astype(BF16)


def unpack_tokens(back, slot):
    length, width = slot.shape[1], back.shape[1]
    return pl.pallas_call(
        unpack_tokens_kernel,
        out_shape=jax.ShapeDtypeStruct((length, width), BF16),
        cost_estimate=cost(2 * length * back.shape[0] * width, 1 << 20),
        compiler_params=BIG,
        name="unpack_tokens",
    )(back, slot)


def sort_rows_kernel(peers, me_ref, perms_ref, arrived_ref, rows_ref, last_ref, slot_ref):
    rounds, length = perms_ref.shape
    per_peer = length // peers
    for turn in range(rounds):
        source = perms_ref[turn : turn + 1, :] >> (length.bit_length() - 1)
        hot = source == iota((peers, length), 0)
        counts = dot(flag(hot), upper(length))
        rank = jnp.sum(jnp.where(hot, counts, 0.0), axis=0, keepdims=True) - 1.0
        slot = source * per_peer + rank.astype(I32)
        slot_ref[turn] = jnp.broadcast_to(slot, slot_ref.shape[1:])
        pick = flag(to_col(slot.astype(F32)).astype(I32) == iota((length, length), 1))
        have = arrived_ref[:, turn * per_peer : (turn + 1) * per_peer, :]
        rows = dot(pick, have.reshape(length, have.shape[2])).astype(BF16)
        rows_ref[turn] = rows
        last_ref[turn] = rows[length - BLOCK_LEN :]


def sort_rows(me, perms, arrived, length):
    rounds = perms.shape[0]
    peers, _, width = arrived.shape
    return pl.pallas_call(
        functools.partial(sort_rows_kernel, peers),
        grid_spec=pltpu.PrefetchScalarGridSpec(
            num_scalar_prefetch=1,
            grid=(1,),
            in_specs=[
                pl.BlockSpec((rounds, length), lambda i, s: (0, s[0])),
                pl.BlockSpec(arrived.shape, lambda i, s: (0, 0, 0)),
            ],
            out_specs=[
                pl.BlockSpec((rounds, length, width), lambda i, s: (0, 0, 0)),
                pl.BlockSpec((rounds, BLOCK_LEN, width), lambda i, s: (0, 0, 0)),
                pl.BlockSpec((rounds, 8, length), lambda i, s: (0, 0, 0)),
            ],
        ),
        out_shape=[
            jax.ShapeDtypeStruct((rounds, length, width), BF16),
            jax.ShapeDtypeStruct((rounds, BLOCK_LEN, width), BF16),
            jax.ShapeDtypeStruct((rounds, 8, length), I32),
        ],
        cost_estimate=cost(LONG, 4 << 20),
        compiler_params=BIG,
        name="sort_rows",
    )(me, perms, arrived)


def window_scale(keys):
    wide = keys.astype(F32)
    squares = jnp.sum(wide * wide, axis=-1, keepdims=True)
    return to_row(lax.rsqrt(squares + 1e-06) / math.sqrt(HEAD_DIM))


def attend_tile(query, keys, values, scale, pos_q, pos_k):
    tile, window = query.shape[0], keys.shape[0]
    block_q = iota((tile, window), 0) // BLOCK_LEN
    block_k = iota((tile, window), 1) // BLOCK_LEN
    met = (block_k == block_q + 1) | (block_k == block_q + 2)
    scores = dot_t(query, keys) * scale
    scores = jnp.where(pos_k == pos_q, scores - 10000.0, scores)
    scores = jnp.where(met & (pos_k <= pos_q), scores, -1e30)
    peak = jnp.max(scores, axis=-1, keepdims=True)
    exponent = jnp.exp(scores - peak)
    total = jnp.sum(exponent, axis=-1, keepdims=True)
    weights = (exponent / total).astype(BF16)
    return dot(weights, values).astype(BF16), peak + jnp.log(total)


TILE, WINDOW, PIECES, GROUP = 2 * BLOCK_LEN, 4 * BLOCK_LEN, 3, 8


def put_logs(totals):
    lane = iota((totals[0].shape[0], LANES), 1) % GROUP
    logs = jnp.zeros(lane.shape, F32)
    for head, total in enumerate(totals):
        rest = total
        for piece in range(PIECES):
            part = rest.astype(BF16).astype(F32)
            logs = jnp.where(lane == head * PIECES + piece, part, logs)
            rest = rest - part
    return logs.astype(BF16)


def attend_later_kernel(me_ref, perms_ref, rows_ref, out_ref):
    rounds, length = perms_ref.shape
    span = rows_ref.shape[2] // 2
    for turn in range(rounds):
        position = perms_ref[turn : turn + 1, :].astype(F32)
        position_col = to_col(position)
        scales = []
        for head in range(span // HEAD_DIM):
            at = head * HEAD_DIM
            scales.append(window_scale(rows_ref[turn, :, at : at + HEAD_DIM]))
        for first in range(TILE, length, TILE):
            totals = []
            window = slice(first + TILE - WINDOW, first + TILE)
            queries = slice(first, first + TILE)
            for head in range(span // HEAD_DIM):
                at = head * HEAD_DIM
                out, total = attend_tile(
                    rows_ref[turn, queries, at : at + HEAD_DIM],
                    rows_ref[turn, window, at : at + HEAD_DIM],
                    rows_ref[turn, window, span + at : span + at + HEAD_DIM],
                    scales[head][:, window],
                    position_col[queries],
                    position[:, window],
                )
                out_ref[turn, first - TILE : first, at : at + HEAD_DIM] = out
                totals.append(total)
            out_ref[turn, first - TILE : first, span:] = put_logs(totals)


def attend_first_kernel(
    peers,
    me_ref,
    perms_ref,
    earlier_ref,
    rows_ref,
    last_ref,
    slot_ref,
    later_ref,
    out_ref,
):
    rounds, length = slot_ref.shape[0], slot_ref.shape[2]
    per_peer = length // peers
    span = rows_ref.shape[2] // 2
    lane_group = iota((peers, per_peer, LANES), 2) // GROUP
    own_group = lane_group == iota((peers, per_peer, LANES), 1)
    empty = jnp.zeros((BLOCK_LEN, HEAD_DIM), BF16)
    for turn in range(rounds):
        position = perms_ref[turn : turn + 1, :].astype(F32)
        positions = jnp.concatenate([earlier_ref[turn : turn + 1, :].astype(F32), position], axis=1)
        position_col = to_col(position)
        totals, outs = [], []
        for head in range(span // HEAD_DIM):
            at = head * HEAD_DIM
            own = rows_ref[turn, :, at : at + HEAD_DIM]
            keys = jnp.concatenate([empty, last_ref[turn, :, at : at + HEAD_DIM], own], axis=0)
            at = span + at
            values = jnp.concatenate(
                [
                    empty,
                    last_ref[turn, :, at : at + HEAD_DIM],
                    rows_ref[turn, :, at : at + HEAD_DIM],
                ],
                axis=0,
            )
            out, total = attend_tile(
                own, keys, values, window_scale(keys), position_col, positions
            )
            outs.append(out)
            totals.append(total)
        top = jnp.concatenate(outs + [put_logs(totals)], axis=1)
        whole = jnp.concatenate([top, later_ref[turn]], axis=0) if length > TILE else top
        back = flag(iota((length, length), 0) == slot_ref[turn, :1, :])
        moved = dot(back, whole)
        at = turn * per_peer
        out_ref[:, at : at + per_peer, :] = (
            moved[:, :span].astype(BF16).reshape(peers, per_peer, span)
        )
        logs = moved[:, span:].reshape(peers, per_peer, LANES)
        logs = jnp.sum(jnp.where(own_group, logs, 0.0), axis=1, keepdims=True)
        at = rounds * per_peer
        out_ref[:, at : at + GROUP, turn * LANES : (turn + 1) * LANES] = jnp.broadcast_to(
            logs, (peers, GROUP, LANES)
        ).astype(BF16)


def attend_later(me, perms, rows):
    rounds, length, width = rows.shape
    span = width // 2
    out = (rounds, length - TILE, span + LANES)
    return pl.pallas_call(
        attend_later_kernel,
        grid_spec=pltpu.PrefetchScalarGridSpec(
            num_scalar_prefetch=1,
            grid=(1,),
            in_specs=[
                pl.BlockSpec((rounds, length), lambda i, s: (0, s[0])),
                pl.BlockSpec(rows.shape, lambda i, s: (0, 0, 0)),
            ],
            out_specs=pl.BlockSpec(out, lambda i, s: (0, 0, 0)),
        ),
        out_shape=jax.ShapeDtypeStruct(out, BF16),
        cost_estimate=cost(LONG, 4 << 20),
        compiler_params=BIG,
        name="attend_later",
    )(me, perms, rows)


def attend_first(me, perms, rows, last, slot, later, peers):
    rounds, length, width = rows.shape
    span = width // 2
    per_peer = length // peers
    lane_blocks = length // LANES

    def fixed(shape):
        return pl.BlockSpec(shape, lambda i, s: (0, 0, 0))

    out = (peers, rounds * per_peer + GROUP, span)
    return pl.pallas_call(
        functools.partial(attend_first_kernel, peers),
        grid_spec=pltpu.PrefetchScalarGridSpec(
            num_scalar_prefetch=1,
            grid=(1,),
            in_specs=[
                pl.BlockSpec((rounds, TILE), lambda i, s: (0, s[0] * lane_blocks)),
                pl.BlockSpec(
                    (rounds, LANES),
                    lambda i, s: (
                        0,
                        jnp.where(s[0] == 0, peers * lane_blocks - 1, s[0] * lane_blocks - 1),
                    ),
                ),
                fixed((rounds, TILE, width)),
                fixed(last.shape),
                fixed(slot.shape),
                fixed(later.shape),
            ],
            out_specs=fixed(out),
        ),
        out_shape=jax.ShapeDtypeStruct(out, BF16),
        cost_estimate=cost(LONG, 4 << 20),
        compiler_params=BIG,
        name="attend_first",
    )(me, perms, perms, rows, last, slot, later)


def combine_kernel(got_ref, token_ref, mixed_ref):
    peers, _, span = got_ref.shape
    rounds, _, length = token_ref.shape
    per_peer = length // peers
    heads = span // HEAD_DIM
    lane_group = iota((peers, per_peer, LANES), 2) // GROUP
    own_group = lane_group == iota((peers, per_peer, LANES), 1)
    lane = iota((length, LANES), 1) % GROUP // PIECES
    column = iota((length, length), 0)
    outs, lses = [], []
    for turn in range(rounds):
        pick = flag(token_ref[turn, :1, :] == column)
        at = turn * per_peer
        rows = got_ref[:, at : at + per_peer, :].reshape(length, span)
        logs = got_ref[
            :, rounds * per_peer : rounds * per_peer + GROUP, turn * LANES : (turn + 1) * LANES
        ]
        logs = jnp.concatenate([logs] * (per_peer // GROUP), axis=1)
        logs = jnp.where(own_group, logs, jnp.zeros_like(logs)).reshape(length, LANES)
        outs.append(dot(pick, rows))
        moved = dot(pick, logs)
        lses.append(
            [
                jnp.sum(jnp.where(lane == head, moved, 0.0), axis=1, keepdims=True)
                for head in range(heads)
            ]
        )
    for head in range(heads):
        logs = [lse[head] for lse in lses]
        peak = functools.reduce(jnp.maximum, logs)
        whole = peak + jnp.log(functools.reduce(jnp.add, [jnp.exp(lse - peak) for lse in logs]))
        at = head * HEAD_DIM
        mixed = jnp.zeros((length, HEAD_DIM), F32)
        for out, lse in zip(outs, logs):
            mixed = mixed + out[:, at : at + HEAD_DIM] * jnp.exp(lse - whole)
        mixed_ref[:, at : at + HEAD_DIM] = mixed.astype(BF16)


def combine(got, token):
    rounds, _, length = token.shape
    return pl.pallas_call(
        combine_kernel,
        out_shape=jax.ShapeDtypeStruct((length, got.shape[2]), BF16),
        cost_estimate=cost(2 * rounds * length * length * (got.shape[2] + LANES), 1 << 20),
        compiler_params=BIG,
        name="combine",
    )(got, token)


def project_kernel(where_ref, heads_ref, *refs):
    weights, (kept_ref, given_ref) = refs[:-2], refs[-2:]
    chips = heads_ref.shape[0]
    total = jnp.zeros((kept_ref.shape[0], 2 * kept_ref.shape[1]), F32)
    for ahead, weight in zip((0, chips - 1, 1, 2), weights):
        place = chip_at((where_ref[0] + ahead) % chips, where_ref[1], chips)
        total = total + dot(heads_ref[place], weight[...])
    half = kept_ref.shape[1]
    for core in range(EXP_DEV):

        @pl.when(where_ref[1] == core)
        def _(core=core):
            kept_ref[...] = total[:, core * half : (core + 1) * half]
            other = 1 - core
            given_ref[...] = total[:, other * half : (other + 1) * half].astype(BF16)


def project(where, heads, w_out, others):
    _, length, span = heads.shape
    columns = others[0].shape[1]
    half = columns // EXP_DEV

    def first(i, e):
        return (0, 0)

    return pl.pallas_call(
        project_kernel,
        grid_spec=pltpu.PrefetchScalarGridSpec(
            num_scalar_prefetch=1,
            grid=(1,),
            in_specs=[
                pl.BlockSpec(heads.shape, lambda i, e: (0, 0, 0)),
                pl.BlockSpec((span, columns), lambda i, e: (0, e[0])),
            ]
            + [pl.BlockSpec(x.shape, first) for x in others],
            out_specs=[pl.BlockSpec((length, half), first)] * 2,
        ),
        out_shape=[
            jax.ShapeDtypeStruct((length, half), F32),
            jax.ShapeDtypeStruct((length, half), BF16),
        ],
        cost_estimate=cost(8 * length * span * columns, 3 << 20),
        compiler_params=BIG,
        name="project",
    )(where, heads, w_out, *others)


def exchange(x, axis):
    return lax.all_to_all(x, axis, split_axis=0, concat_axis=0, tiled=True)


def hop(x, by, chips):
    pairs = []
    for chip in range(chips):
        for core in range(EXP_DEV):
            there = (chip + by) % chips
            pairs.append((chip * EXP_DEV + core, there * EXP_DEV + core))
    return lax.ppermute(x, "exp", pairs)


def after(x, *done):
    return lax.optimization_barrier((x, *done))[0]


def body(x_att, w_qk, w_val, w_out, perms, tokens_b, expert_ids, w_gate, w_up, w_down):
    peers, parts = lax.axis_size("seq"), lax.axis_size("exp")
    chips = parts // EXP_DEV
    me = lax.axis_index("seq").astype(I32).reshape(1)
    my_exp = lax.axis_index("exp").astype(I32)
    core = my_exp % EXP_DEV
    where = jnp.stack([my_exp // EXP_DEV, core])
    length, width = x_att.shape
    rounds = perms.shape[0]
    per_peer = length // peers
    tokb = tokens_b.shape[0]
    capacity = tokb // peers
    part = width // chips
    lines = [[chip * EXP_DEV + side for chip in range(chips)] for side in range(EXP_DEV)]
    lines[1].reverse()
    siblings = [(i, i ^ 1) for i in range(parts)]

    dispatch, token_slot = pack_tokens(
        where, expert_ids.reshape(1, tokb), tokens_b, peers, capacity, part
    )
    received = exchange(dispatch.reshape(peers, capacity, part), "seq")
    outgoing, slot_token = pack_rows(me, perms, x_att, w_qk, w_val)
    columns = [
        hop(
            lax.dynamic_slice_in_dim(
                after(w_out, dispatch), (where[0] + by) % chips * part, part, 1
            ),
            by,
            chips,
        )
        for by in (1, chips - 1, 2)
    ]
    received = after(received, outgoing, *columns)
    outgoing = after(outgoing, received)
    own = (w_gate, w_up, w_down)
    sibling = [
        lax.ppermute(
            lax.dynamic_slice_in_dim(after(weight, received), 1 - core, 1, 0), "exp", siblings
        )
        for weight in own
    ]
    gathered = lax.all_gather(received, "exp", axis=0, tiled=False, axis_index_groups=lines)
    arrived = exchange(outgoing.reshape(peers, rounds * per_peer, outgoing.shape[1]), "seq")
    expert_part = run_experts(where, gathered, own, sibling)
    arrived = after(arrived, expert_part)
    rows, last, row_slot = sort_rows(me, perms, arrived, length)
    expert_rows = lax.psum_scatter(
        expert_part,
        "exp",
        scatter_dimension=0,
        tiled=False,
        axis_index_groups=lines,
    )
    last = lax.ppermute(last, "seq", [(i, (i + 1) % peers) for i in range(peers)])
    later = attend_later(me, perms, rows) if length > TILE else rows
    last = after(last, later)
    packed = attend_first(me, perms, rows, last, row_slot, later, peers)
    got = exchange(packed, "seq")
    expert_rows = after(expert_rows, packed)
    given = lax.dynamic_index_in_dim(expert_rows, 1 - core, 0, keepdims=False)
    taken = lax.ppermute(given, "exp", siblings)
    mixed_heads = combine(after(got, expert_rows), slot_token)
    expert_rows = place_rows(where, expert_rows, after(taken, mixed_heads))
    expert_back = exchange(expert_rows, "seq")
    heads = lax.all_gather(mixed_heads, "exp", axis=0, tiled=False, axis_index_groups=lines)
    attn_kept, attn_given = project(where, heads, w_out, columns)
    attended = attn_kept + lax.ppermute(attn_given, "exp", siblings).astype(F32)
    attended = attended.astype(BF16)
    expert_back = after(expert_back, attended)
    mixed = unpack_tokens(
        expert_back.reshape(peers * EXP_DEV * capacity, width // parts), token_slot
    )
    return (attended, mixed)


def solution(mesh):
    in_specs = (
        P("seq", None),
        P(None, "exp"),
        P(None, "exp"),
        P("exp", None),
        P(),
        P("seq", None),
        P("seq", None),
        P("seq", None, "exp"),
        P("seq", None, "exp"),
        P("seq", "exp", None),
    )
    out_specs = (P("seq", "exp"), P("seq", "exp"))
    return jax.shard_map(body, mesh=mesh, in_specs=in_specs, out_specs=out_specs, check_vma=False)
```

```python
import functools
import math

import jax
import jax.numpy as jnp
from jax import lax
from jax.experimental import pallas as pl
from jax.experimental.pallas import tpu as pltpu
from jax.sharding import PartitionSpec as P

HEAD_DIM = 128
BLOCK_LEN = 64
EXP_DEV = 2
LANES = 128
F32, BF16, I32 = jnp.float32, jnp.bfloat16, jnp.int32
LONG = 1 << 35
BIG = pltpu.CompilerParams(vmem_limit_bytes=48 * 1024 * 1024)


def dot(a, b):
    return jnp.dot(a, b, preferred_element_type=F32)


def dot_t(a, b):
    return lax.dot_general(a, b, (((1,), (1,)), ((), ())), preferred_element_type=F32)


def to_col(row):
    return jnp.broadcast_to(row, (LANES, row.shape[1])).T[:, :1]


def to_row(col):
    return jnp.broadcast_to(col, (col.shape[0], LANES)).T[:1, :]


def iota(shape, dim):
    return lax.broadcasted_iota(I32, shape, dim)


def flag(mask, kind=BF16):
    return jnp.where(mask, 1.0, 0.0).astype(kind)


def cost(flops, size):
    return pl.CostEstimate(flops=flops, bytes_accessed=size, transcendentals=0)


def upper(count):
    return flag(iota((count, count), 0) <= iota((count, count), 1))


def pack_rows_kernel(me_ref, perms_ref, x_ref, qk_ref, val_ref, out_ref, token_ref, scratch):
    length, span = x_ref.shape[0], qk_ref.shape[1]
    rounds, total = perms_ref.shape
    peers = total // length
    per_peer = length // peers
    for peer in range(peers):
        scratch[peer * rounds : (peer + 1) * rounds, :] = perms_ref[
            :, peer * length : (peer + 1) * length
        ]
    perms = scratch[...]
    token = perms & (length - 1)
    mine = (perms >> (length.bit_length() - 1)) == me_ref[0]
    rank = dot(flag(mine), upper(length)).astype(I32) - 1
    slot = jnp.where(mine, rank, -1)
    groups = peers * rounds
    chosen = slot[:, None, :] == iota((groups, per_peer, length), 1)
    token_3d = jnp.where(chosen, token.astype(F32)[:, None, :], 0.0)
    column = jnp.sum(token_3d, axis=-1, keepdims=True).reshape(groups * per_peer, 1)
    by_round = column.reshape(peers, rounds, per_peer, 1)
    for turn in range(rounds):
        row = to_row(by_round[:, turn].reshape(peers * per_peer, 1)).astype(I32)
        token_ref[turn] = jnp.broadcast_to(row, token_ref.shape[1:])
    pick = flag(column.astype(I32) == iota((groups * per_peer, length), 1))
    for part, weight in enumerate((qk_ref, val_ref)):
        rows = dot(x_ref[...], weight[...]).astype(BF16)
        out_ref[:, part * span : (part + 1) * span] = dot(pick, rows).astype(BF16)


def pack_rows(me, perms, x_att, w_qk, w_val):
    length, width = x_att.shape
    rounds, total = perms.shape
    span = w_qk.shape[1]
    groups = rounds * (total // length)
    slots = rounds * length

    def whole(shape):
        return pl.BlockSpec(shape, lambda i, me_ref: (0, 0))

    return pl.pallas_call(
        pack_rows_kernel,
        grid_spec=pltpu.PrefetchScalarGridSpec(
            num_scalar_prefetch=1,
            grid=(1,),
            in_specs=[
                whole((rounds, total)),
                whole((length, width)),
                whole((width, span)),
                whole((width, span)),
            ],
            out_specs=[
                whole((slots, 2 * span)),
                pl.BlockSpec((rounds, 8, length), lambda i, me_ref: (0, 0, 0)),
            ],
            scratch_shapes=[pltpu.VMEM((groups, length), I32)],
        ),
        out_shape=[
            jax.ShapeDtypeStruct((slots, 2 * span), BF16),
            jax.ShapeDtypeStruct((rounds, 8, length), I32),
        ],
        cost_estimate=cost(4 * length * width * span + 4 * slots * length * span, 6 << 20),
        compiler_params=BIG,
        name="pack_rows",
    )(me, perms, x_att, w_qk, w_val)


def pack_tokens_kernel(peers, where_ref, ids_ref, tokens_ref, out_ref, slot_ref):
    length = tokens_ref.shape[0]
    slots = out_ref.shape[0]
    capacity = slots // peers
    experts = EXP_DEV * peers
    ids = ids_ref[...]
    hot = ids == iota((experts, length), 0)
    counts = dot(flag(hot), upper(length))
    rank = jnp.sum(jnp.where(hot, counts, 0.0), axis=0, keepdims=True).astype(I32) - 1
    core = where_ref[1]
    turn = (ids % EXP_DEV + core) % EXP_DEV
    peer = ids // EXP_DEV
    slot_ref[...] = jnp.broadcast_to(
        (peer * EXP_DEV + turn) * capacity + rank, slot_ref.shape
    )
    slot = jnp.where(turn == 0, peer * capacity + rank, -1)
    pick = flag(iota((slots, length), 0) == slot)
    out_ref[...] = dot(pick, tokens_ref[...]).astype(BF16)


def pack_tokens(where, ids, tokens, peers, capacity, part):
    length = tokens.shape[0]
    slots = peers * capacity
    return pl.pallas_call(
        functools.partial(pack_tokens_kernel, peers),
        grid_spec=pltpu.PrefetchScalarGridSpec(
            num_scalar_prefetch=1,
            grid=(1,),
            in_specs=[
                pl.BlockSpec((1, length), lambda i, e: (0, 0)),
                pl.BlockSpec((length, part), lambda i, e: (0, e[0])),
            ],
            out_specs=[
                pl.BlockSpec((slots, part), lambda i, e: (0, 0)),
                pl.BlockSpec((8, length), lambda i, e: (0, 0)),
            ],
        ),
        out_shape=[
            jax.ShapeDtypeStruct((slots, part), BF16),
            jax.ShapeDtypeStruct((8, length), I32),
        ],
        cost_estimate=cost(2 * slots * length * part, 2 << 20),
        compiler_params=BIG,
        name="pack_tokens",
    )(where, ids, tokens)


def experts_kernel(where_ref, *refs):
    step = pl.program_id(0)
    shards, far_refs, weights = refs[0:3], refs[3:5], refs[5:11]
    out_ref, total_ref = refs[11:]
    peers, capacity, part = shards[0].shape
    rows = peers * capacity
    ups = (weights[0], weights[1], weights[3], weights[4])

    def add(x, start):
        for index, weight in enumerate(ups):
            product = dot(x, weight[0])
            total_ref[index] = product if start else total_ref[index] + product

    for turn, shard in enumerate(shards):

        @pl.when(step == turn)
        def _(shard=shard, start=turn == 0):
            add(shard[...].reshape(rows, part), start)

    @pl.when(step == len(shards))
    def _():
        add(jnp.concatenate([ref[...].reshape(rows // 2, part) for ref in far_refs], axis=0), False)
        hiddens = []
        for side in range(EXP_DEV):
            gate, up_val = total_ref[2 * side], total_ref[2 * side + 1]
            hiddens.append((gate / (1.0 + jnp.exp(-gate)) * up_val).astype(BF16))
        half = part // EXP_DEV
        for index in range(out_ref.shape[0]):
            at = index * part
            piece = dot(hiddens[0], weights[2][0, :, at : at + part])
            piece = (piece + dot(hiddens[1], weights[5][0, :, at : at + part])).astype(BF16)
            for side in range(EXP_DEV):
                columns = piece[:, side * half : (side + 1) * half]
                out_ref[index, side] = columns.reshape(peers, capacity, half)


def run_experts(where, shards, far, own, sibling):
    peers, capacity, part = shards[0].shape
    width, hidden = own[0].shape[1:]
    chips = width // part
    out = (chips, EXP_DEV, peers, capacity, part // EXP_DEV)
    rows = peers * capacity

    def rows_of(i, e):
        ahead = jnp.where(i == 0, 0, jnp.where(i == 1, chips - 1, jnp.where(i == 2, 1, 2)))
        return (e[0] + ahead) % chips

    up_block, down_block = (1, part, hidden), (1, hidden, width)
    own_up = pl.BlockSpec(up_block, lambda i, e: (e[1], rows_of(i, e), 0))
    sibling_up = pl.BlockSpec(up_block, lambda i, e: (0, rows_of(i, e), 0))
    own_down = pl.BlockSpec(down_block, lambda i, e: (e[1], 0, 0))
    sibling_down = pl.BlockSpec(down_block, lambda i, e: (0, 0, 0))
    return pl.pallas_call(
        experts_kernel,
        grid_spec=pltpu.PrefetchScalarGridSpec(
            num_scalar_prefetch=1,
            grid=(len(shards) + 1,),
            in_specs=[pl.BlockSpec(x.shape, lambda i, e: (0, 0, 0)) for x in (*shards, *far)]
            + [own_up, own_up, own_down, sibling_up, sibling_up, sibling_down],
            out_specs=pl.BlockSpec(out, lambda i, e: (0, 0, 0, 0, 0)),
            scratch_shapes=[pltpu.VMEM((4, rows, hidden), F32)],
        ),
        out_shape=jax.ShapeDtypeStruct(out, BF16),
        cost_estimate=cost(15 * 10**9, 10 << 20),
        compiler_params=BIG,
        name="experts",
    )(where, *shards, *far, *own, *sibling)


def place_rows_kernel(where_ref, rows_ref, taken_ref, out_ref):
    out_ref[:, 0] = rows_ref[0]
    out_ref[:, 1] = taken_ref[...]


def place_rows(where, rows, taken):
    peers, capacity, half = taken.shape
    out = (peers, EXP_DEV, capacity, half)
    return pl.pallas_call(
        place_rows_kernel,
        grid_spec=pltpu.PrefetchScalarGridSpec(
            num_scalar_prefetch=1,
            grid=(1,),
            in_specs=[
                pl.BlockSpec((1, *taken.shape), lambda i, e: (e[1], 0, 0, 0)),
                pl.BlockSpec(taken.shape, lambda i, e: (0, 0, 0)),
            ],
            out_specs=pl.BlockSpec(out, lambda i, e: (0, 0, 0, 0)),
        ),
        out_shape=jax.ShapeDtypeStruct(out, BF16),
        cost_estimate=cost(LONG, 1 << 20),
        compiler_params=BIG,
        name="place_rows",
    )(where, rows, taken)


def unpack_tokens_kernel(back_ref, slot_ref, out_ref):
    length = out_ref.shape[0]
    column = to_col(slot_ref[:1, :].astype(F32)).astype(I32)
    pick = flag(column == iota((length, back_ref.shape[0]), 1))
    out_ref[...] = dot(pick, back_ref[...]).astype(BF16)


def unpack_tokens(back, slot):
    length, width = slot.shape[1], back.shape[1]
    return pl.pallas_call(
        unpack_tokens_kernel,
        out_shape=jax.ShapeDtypeStruct((length, width), BF16),
        cost_estimate=cost(2 * length * back.shape[0] * width, 1 << 20),
        compiler_params=BIG,
        name="unpack_tokens",
    )(back, slot)


def sort_rows_kernel(peers, me_ref, perms_ref, arrived_ref, rows_ref, last_ref, slot_ref):
    rounds, length = perms_ref.shape
    per_peer = length // peers
    for turn in range(rounds):
        source = perms_ref[turn : turn + 1, :] >> (length.bit_length() - 1)
        hot = source == iota((peers, length), 0)
        counts = dot(flag(hot), upper(length))
        rank = jnp.sum(jnp.where(hot, counts, 0.0), axis=0, keepdims=True) - 1.0
        slot = source * per_peer + rank.astype(I32)
        slot_ref[turn] = jnp.broadcast_to(slot, slot_ref.shape[1:])
        pick = flag(to_col(slot.astype(F32)).astype(I32) == iota((length, length), 1))
        have = arrived_ref[:, turn * per_peer : (turn + 1) * per_peer, :]
        rows = dot(pick, have.reshape(length, have.shape[2])).astype(BF16)
        rows_ref[turn] = rows
        last_ref[turn] = rows[length - BLOCK_LEN :]


def sort_rows(me, perms, arrived, length):
    rounds = perms.shape[0]
    peers, _, width = arrived.shape
    return pl.pallas_call(
        functools.partial(sort_rows_kernel, peers),
        grid_spec=pltpu.PrefetchScalarGridSpec(
            num_scalar_prefetch=1,
            grid=(1,),
            in_specs=[
                pl.BlockSpec((rounds, length), lambda i, s: (0, s[0])),
                pl.BlockSpec(arrived.shape, lambda i, s: (0, 0, 0)),
            ],
            out_specs=[
                pl.BlockSpec((rounds, length, width), lambda i, s: (0, 0, 0)),
                pl.BlockSpec((rounds, BLOCK_LEN, width), lambda i, s: (0, 0, 0)),
                pl.BlockSpec((rounds, 8, length), lambda i, s: (0, 0, 0)),
            ],
        ),
        out_shape=[
            jax.ShapeDtypeStruct((rounds, length, width), BF16),
            jax.ShapeDtypeStruct((rounds, BLOCK_LEN, width), BF16),
            jax.ShapeDtypeStruct((rounds, 8, length), I32),
        ],
        cost_estimate=cost(LONG, 4 << 20),
        compiler_params=BIG,
        name="sort_rows",
    )(me, perms, arrived)


def window_scale(keys):
    wide = keys.astype(F32)
    squares = jnp.sum(wide * wide, axis=-1, keepdims=True)
    return to_row(lax.rsqrt(squares + 1e-06) / math.sqrt(HEAD_DIM))


def attend_tile(query, keys, values, scale, pos_q, pos_k):
    tile, window = query.shape[0], keys.shape[0]
    block_q = iota((tile, window), 0) // BLOCK_LEN
    block_k = iota((tile, window), 1) // BLOCK_LEN
    met = (block_k == block_q + 1) | (block_k == block_q + 2)
    scores = dot_t(query, keys) * scale
    scores = jnp.where(pos_k == pos_q, scores - 10000.0, scores)
    scores = jnp.where(met & (pos_k <= pos_q), scores, -1e30)
    peak = jnp.max(scores, axis=-1, keepdims=True)
    exponent = jnp.exp(scores - peak)
    total = jnp.sum(exponent, axis=-1, keepdims=True)
    weights = (exponent / total).astype(BF16)
    return dot(weights, values).astype(BF16), peak + jnp.log(total)


TILE, WINDOW, PIECES, GROUP = 2 * BLOCK_LEN, 4 * BLOCK_LEN, 3, 8


def put_logs(totals):
    lane = iota((totals[0].shape[0], LANES), 1) % GROUP
    logs = jnp.zeros(lane.shape, F32)
    for head, total in enumerate(totals):
        rest = total
        for piece in range(PIECES):
            part = rest.astype(BF16).astype(F32)
            logs = jnp.where(lane == head * PIECES + piece, part, logs)
            rest = rest - part
    return logs.astype(BF16)


def attend_later_kernel(me_ref, perms_ref, rows_ref, out_ref):
    rounds, length = perms_ref.shape
    span = rows_ref.shape[2] // 2
    for turn in range(rounds):
        position = perms_ref[turn : turn + 1, :].astype(F32)
        position_col = to_col(position)
        scales = []
        for head in range(span // HEAD_DIM):
            at = head * HEAD_DIM
            scales.append(window_scale(rows_ref[turn, :, at : at + HEAD_DIM]))
        for first in range(TILE, length, TILE):
            totals = []
            window = slice(first + TILE - WINDOW, first + TILE)
            queries = slice(first, first + TILE)
            for head in range(span // HEAD_DIM):
                at = head * HEAD_DIM
                out, total = attend_tile(
                    rows_ref[turn, queries, at : at + HEAD_DIM],
                    rows_ref[turn, window, at : at + HEAD_DIM],
                    rows_ref[turn, window, span + at : span + at + HEAD_DIM],
                    scales[head][:, window],
                    position_col[queries],
                    position[:, window],
                )
                out_ref[turn, first - TILE : first, at : at + HEAD_DIM] = out
                totals.append(total)
            out_ref[turn, first - TILE : first, span:] = put_logs(totals)


def attend_first_kernel(
    peers,
    me_ref,
    perms_ref,
    earlier_ref,
    rows_ref,
    last_ref,
    slot_ref,
    later_ref,
    out_ref,
):
    rounds, length = slot_ref.shape[0], slot_ref.shape[2]
    per_peer = length // peers
    span = rows_ref.shape[2] // 2
    lane_group = iota((peers, per_peer, LANES), 2) // GROUP
    own_group = lane_group == iota((peers, per_peer, LANES), 1)
    empty = jnp.zeros((BLOCK_LEN, HEAD_DIM), BF16)
    for turn in range(rounds):
        position = perms_ref[turn : turn + 1, :].astype(F32)
        positions = jnp.concatenate([earlier_ref[turn : turn + 1, :].astype(F32), position], axis=1)
        position_col = to_col(position)
        totals, outs = [], []
        for head in range(span // HEAD_DIM):
            at = head * HEAD_DIM
            own = rows_ref[turn, :, at : at + HEAD_DIM]
            keys = jnp.concatenate([empty, last_ref[turn, :, at : at + HEAD_DIM], own], axis=0)
            at = span + at
            values = jnp.concatenate(
                [
                    empty,
                    last_ref[turn, :, at : at + HEAD_DIM],
                    rows_ref[turn, :, at : at + HEAD_DIM],
                ],
                axis=0,
            )
            out, total = attend_tile(
                own, keys, values, window_scale(keys), position_col, positions
            )
            outs.append(out)
            totals.append(total)
        top = jnp.concatenate(outs + [put_logs(totals)], axis=1)
        whole = jnp.concatenate([top, later_ref[turn]], axis=0) if length > TILE else top
        back = flag(iota((length, length), 0) == slot_ref[turn, :1, :])
        moved = dot(back, whole)
        at = turn * per_peer
        out_ref[:, at : at + per_peer, :] = (
            moved[:, :span].astype(BF16).reshape(peers, per_peer, span)
        )
        logs = moved[:, span:].reshape(peers, per_peer, LANES)
        logs = jnp.sum(jnp.where(own_group, logs, 0.0), axis=1, keepdims=True)
        at = rounds * per_peer
        out_ref[:, at : at + GROUP, turn * LANES : (turn + 1) * LANES] = jnp.broadcast_to(
            logs, (peers, GROUP, LANES)
        ).astype(BF16)


def attend_later(me, perms, rows):
    rounds, length, width = rows.shape
    span = width // 2
    out = (rounds, length - TILE, span + LANES)
    return pl.pallas_call(
        attend_later_kernel,
        grid_spec=pltpu.PrefetchScalarGridSpec(
            num_scalar_prefetch=1,
            grid=(1,),
            in_specs=[
                pl.BlockSpec((rounds, length), lambda i, s: (0, s[0])),
                pl.BlockSpec(rows.shape, lambda i, s: (0, 0, 0)),
            ],
            out_specs=pl.BlockSpec(out, lambda i, s: (0, 0, 0)),
        ),
        out_shape=jax.ShapeDtypeStruct(out, BF16),
        cost_estimate=cost(LONG, 4 << 20),
        compiler_params=BIG,
        name="attend_later",
    )(me, perms, rows)


def attend_first(me, perms, rows, last, slot, later, peers):
    rounds, length, width = rows.shape
    span = width // 2
    per_peer = length // peers
    lane_blocks = length // LANES

    def fixed(shape):
        return pl.BlockSpec(shape, lambda i, s: (0, 0, 0))

    out = (peers, rounds * per_peer + GROUP, span)
    return pl.pallas_call(
        functools.partial(attend_first_kernel, peers),
        grid_spec=pltpu.PrefetchScalarGridSpec(
            num_scalar_prefetch=1,
            grid=(1,),
            in_specs=[
                pl.BlockSpec((rounds, TILE), lambda i, s: (0, s[0] * lane_blocks)),
                pl.BlockSpec(
                    (rounds, LANES),
                    lambda i, s: (
                        0,
                        jnp.where(s[0] == 0, peers * lane_blocks - 1, s[0] * lane_blocks - 1),
                    ),
                ),
                fixed((rounds, TILE, width)),
                fixed(last.shape),
                fixed(slot.shape),
                fixed(later.shape),
            ],
            out_specs=fixed(out),
        ),
        out_shape=jax.ShapeDtypeStruct(out, BF16),
        cost_estimate=cost(LONG, 4 << 20),
        compiler_params=BIG,
        name="attend_first",
    )(me, perms, perms, rows, last, slot, later)


def combine_kernel(got_ref, token_ref, mixed_ref):
    peers, _, span = got_ref.shape
    rounds, _, length = token_ref.shape
    per_peer = length // peers
    heads = span // HEAD_DIM
    lane_group = iota((peers, per_peer, LANES), 2) // GROUP
    own_group = lane_group == iota((peers, per_peer, LANES), 1)
    lane = iota((length, LANES), 1) % GROUP // PIECES
    column = iota((length, length), 0)
    outs, lses = [], []
    for turn in range(rounds):
        pick = flag(token_ref[turn, :1, :] == column)
        at = turn * per_peer
        rows = got_ref[:, at : at + per_peer, :].reshape(length, span)
        logs = got_ref[
            :, rounds * per_peer : rounds * per_peer + GROUP, turn * LANES : (turn + 1) * LANES
        ]
        logs = jnp.concatenate([logs] * (per_peer // GROUP), axis=1)
        logs = jnp.where(own_group, logs, jnp.zeros_like(logs)).reshape(length, LANES)
        outs.append(dot(pick, rows))
        moved = dot(pick, logs)
        lses.append(
            [
                jnp.sum(jnp.where(lane == head, moved, 0.0), axis=1, keepdims=True)
                for head in range(heads)
            ]
        )
    for head in range(heads):
        logs = [lse[head] for lse in lses]
        peak = functools.reduce(jnp.maximum, logs)
        whole = peak + jnp.log(functools.reduce(jnp.add, [jnp.exp(lse - peak) for lse in logs]))
        at = head * HEAD_DIM
        mixed = jnp.zeros((length, HEAD_DIM), F32)
        for out, lse in zip(outs, logs):
            mixed = mixed + out[:, at : at + HEAD_DIM] * jnp.exp(lse - whole)
        mixed_ref[:, at : at + HEAD_DIM] = mixed.astype(BF16)


def combine(got, token):
    rounds, _, length = token.shape
    return pl.pallas_call(
        combine_kernel,
        out_shape=jax.ShapeDtypeStruct((length, got.shape[2]), BF16),
        cost_estimate=cost(2 * rounds * length * length * (got.shape[2] + LANES), 1 << 20),
        compiler_params=BIG,
        name="combine",
    )(got, token)


def project_kernel(where_ref, own_ref, prev_ref, next_ref, far_a_ref, far_b_ref, *refs):
    weights, (kept_ref, given_ref) = refs[:-2], refs[-2:]
    far = jnp.concatenate([far_a_ref[...], far_b_ref[...]], axis=0)
    total = dot(own_ref[...], weights[0][...]) + dot(prev_ref[...], weights[1][...])
    total = total + dot(next_ref[...], weights[2][...]) + dot(far, weights[3][...])
    half = kept_ref.shape[1]
    for core in range(EXP_DEV):

        @pl.when(where_ref[1] == core)
        def _(core=core):
            kept_ref[...] = total[:, core * half : (core + 1) * half]
            other = 1 - core
            given_ref[...] = total[:, other * half : (other + 1) * half].astype(BF16)


def project(where, heads, w_out, others):
    length, span = heads[0].shape
    columns = others[0].shape[1]
    half = columns // EXP_DEV
    weights = (w_out, *others)
    shapes = [x.shape for x in heads] + [(span, columns)] + [x.shape for x in others]

    def first(i, e):
        return (0, 0)

    specs = [pl.BlockSpec(shape, first) for shape in shapes]
    specs[len(heads)] = pl.BlockSpec((span, columns), lambda i, e: (0, e[0]))
    return pl.pallas_call(
        project_kernel,
        grid_spec=pltpu.PrefetchScalarGridSpec(
            num_scalar_prefetch=1,
            grid=(1,),
            in_specs=specs,
            out_specs=[pl.BlockSpec((length, half), first)] * 2,
        ),
        out_shape=[
            jax.ShapeDtypeStruct((length, half), F32),
            jax.ShapeDtypeStruct((length, half), BF16),
        ],
        cost_estimate=cost(35 * 10**8, 3 << 20),
        compiler_params=BIG,
        name="project",
    )(where, *heads, *weights)


def exchange(x, axis):
    return lax.all_to_all(x, axis, split_axis=0, concat_axis=0, tiled=True)


def hop(x, by, chips):
    pairs = []
    for chip in range(chips):
        for core in range(EXP_DEV):
            there = (chip + by) % chips
            pairs.append((chip * EXP_DEV + core, there * EXP_DEV + core))
    return lax.ppermute(x, "exp", pairs)


def spread(x, chips, ready=()):
    half = x.shape[0] // 2
    before, behind = hop(x, 1, chips), hop(x, -1, chips)
    before, behind = (after(side, *ready) if ready else side for side in (before, behind))
    far = (hop(before[:half], 1, chips), hop(behind[half:], -1, chips))
    return (x, before, behind), far


def after(x, *done):
    return lax.optimization_barrier((x, *done))[0]


def body(x_att, w_qk, w_val, w_out, perms, tokens_b, expert_ids, w_gate, w_up, w_down):
    peers, parts = lax.axis_size("seq"), lax.axis_size("exp")
    chips = parts // EXP_DEV
    me = lax.axis_index("seq").astype(I32).reshape(1)
    my_exp = lax.axis_index("exp").astype(I32)
    core = my_exp % EXP_DEV
    where = jnp.stack([my_exp // EXP_DEV, core])
    length, width = x_att.shape
    rounds = perms.shape[0]
    per_peer = length // peers
    tokb = tokens_b.shape[0]
    capacity = tokb // peers
    part = width // chips
    lines = [[chip * EXP_DEV + side for chip in range(chips)] for side in range(EXP_DEV)]
    siblings = [(i, i ^ 1) for i in range(parts)]

    dispatch, token_slot = pack_tokens(
        where, expert_ids.reshape(1, tokb), tokens_b, peers, capacity, part
    )
    received = exchange(dispatch.reshape(peers, capacity, part), "seq")
    outgoing, slot_token = pack_rows(me, perms, x_att, w_qk, w_val)
    columns = [
        hop(
            lax.dynamic_slice_in_dim(
                after(w_out, dispatch), (where[0] + by) % chips * part, part, 1
            ),
            by,
            chips,
        )
        for by in (1, chips - 1, 2)
    ]
    received = after(received, outgoing, *columns)
    outgoing = after(outgoing, received)
    own = (w_gate, w_up, w_down)
    sibling = [
        lax.ppermute(
            lax.dynamic_slice_in_dim(after(weight, received), 1 - core, 1, 0), "exp", siblings
        )
        for weight in own
    ]
    shards, far = spread(received, chips)
    arrived = exchange(outgoing.reshape(peers, rounds * per_peer, outgoing.shape[1]), "seq")
    expert_part = run_experts(where, shards, far, own, sibling)
    arrived = after(arrived, expert_part)
    rows, last, row_slot = sort_rows(me, perms, arrived, length)
    expert_rows = lax.psum_scatter(
        expert_part,
        "exp",
        scatter_dimension=0,
        tiled=False,
        axis_index_groups=lines,
    )
    last = lax.ppermute(last, "seq", [(i, (i + 1) % peers) for i in range(peers)])
    later = attend_later(me, perms, rows) if length > TILE else rows
    last = after(last, later)
    packed = attend_first(me, perms, rows, last, row_slot, later, peers)
    got = exchange(packed, "seq")
    expert_rows = after(expert_rows, packed)
    given = lax.dynamic_index_in_dim(expert_rows, 1 - core, 0, keepdims=False)
    taken = lax.ppermute(given, "exp", siblings)
    mixed_heads = combine(got, slot_token)
    expert_rows = place_rows(where, expert_rows, after(taken, mixed_heads))
    expert_back = exchange(expert_rows, "seq")
    heads, far_heads = spread(mixed_heads, chips, (expert_rows,))
    attn_kept, attn_given = project(where, (*heads, *far_heads), w_out, columns)
    attended = attn_kept + lax.ppermute(attn_given, "exp", siblings).astype(F32)
    attended = attended.astype(BF16)
    expert_back = after(expert_back, attended)
    mixed = unpack_tokens(
        expert_back.reshape(peers * EXP_DEV * capacity, width // parts), token_slot
    )
    return (attended, mixed)


def solution(mesh):
    in_specs = (
        P("seq", None),
        P(None, "exp"),
        P(None, "exp"),
        P("exp", None),
        P(),
        P("seq", None),
        P("seq", None),
        P("seq", None, "exp"),
        P("seq", None, "exp"),
        P("seq", "exp", None),
    )
    out_specs = (P("seq", "exp"), P("seq", "exp"))
    return jax.shard_map(body, mesh=mesh, in_specs=in_specs, out_specs=out_specs, check_vma=False)
```

```python
import functools
import math

import jax
import jax.numpy as jnp
from jax import lax
from jax.experimental import pallas as pl
from jax.experimental.pallas import tpu as pltpu
from jax.sharding import PartitionSpec as P

HEAD_DIM = 128
BLOCK_LEN = 64
EXP_DEV = 2
LANES = 128
F32, BF16, I32 = jnp.float32, jnp.bfloat16, jnp.int32
LONG = 1 << 35
BIG = pltpu.CompilerParams(vmem_limit_bytes=48 * 1024 * 1024)


def dot(a, b):
    return jnp.dot(a, b, preferred_element_type=F32)


def dot_t(a, b):
    return lax.dot_general(a, b, (((1,), (1,)), ((), ())), preferred_element_type=F32)


def to_col(row):
    return jnp.broadcast_to(row, (LANES, row.shape[1])).T[:, :1]


def to_row(col):
    return jnp.broadcast_to(col, (col.shape[0], LANES)).T[:1, :]


def iota(shape, dim):
    return lax.broadcasted_iota(I32, shape, dim)


def flag(mask, kind=BF16):
    return jnp.where(mask, 1.0, 0.0).astype(kind)


def cost(flops, size):
    return pl.CostEstimate(flops=flops, bytes_accessed=size, transcendentals=0)


def upper(count):
    return flag(iota((count, count), 0) <= iota((count, count), 1))


def pack_rows_kernel(me_ref, perms_ref, x_ref, qk_ref, val_ref, out_ref, token_ref, scratch):
    length, span = x_ref.shape[0], qk_ref.shape[1]
    rounds, total = perms_ref.shape
    peers = total // length
    per_peer = length // peers
    for peer in range(peers):
        scratch[peer * rounds : (peer + 1) * rounds, :] = perms_ref[
            :, peer * length : (peer + 1) * length
        ]
    perms = scratch[...]
    token = perms & (length - 1)
    mine = (perms >> (length.bit_length() - 1)) == me_ref[0]
    rank = dot(flag(mine), upper(length)).astype(I32) - 1
    slot = jnp.where(mine, rank, -1)
    groups = peers * rounds
    chosen = slot[:, None, :] == iota((groups, per_peer, length), 1)
    token_3d = jnp.where(chosen, token.astype(F32)[:, None, :], 0.0)
    column = jnp.sum(token_3d, axis=-1, keepdims=True).reshape(groups * per_peer, 1)
    by_round = column.reshape(peers, rounds, per_peer, 1)
    for turn in range(rounds):
        row = to_row(by_round[:, turn].reshape(peers * per_peer, 1)).astype(I32)
        token_ref[turn] = jnp.broadcast_to(row, token_ref.shape[1:])
    pick = flag(column.astype(I32) == iota((groups * per_peer, length), 1))
    for part, weight in enumerate((qk_ref, val_ref)):
        rows = dot(x_ref[...], weight[...]).astype(BF16)
        out_ref[:, part * span : (part + 1) * span] = dot(pick, rows).astype(BF16)


def pack_rows(me, perms, x_att, w_qk, w_val):
    length, width = x_att.shape
    rounds, total = perms.shape
    span = w_qk.shape[1]
    groups = rounds * (total // length)
    slots = rounds * length

    def whole(shape):
        return pl.BlockSpec(shape, lambda i, me_ref: (0, 0))

    return pl.pallas_call(
        pack_rows_kernel,
        grid_spec=pltpu.PrefetchScalarGridSpec(
            num_scalar_prefetch=1,
            grid=(1,),
            in_specs=[
                whole((rounds, total)),
                whole((length, width)),
                whole((width, span)),
                whole((width, span)),
            ],
            out_specs=[
                whole((slots, 2 * span)),
                pl.BlockSpec((rounds, 8, length), lambda i, me_ref: (0, 0, 0)),
            ],
            scratch_shapes=[pltpu.VMEM((groups, length), I32)],
        ),
        out_shape=[
            jax.ShapeDtypeStruct((slots, 2 * span), BF16),
            jax.ShapeDtypeStruct((rounds, 8, length), I32),
        ],
        cost_estimate=cost(4 * length * width * span + 4 * slots * length * span, 6 << 20),
        compiler_params=BIG,
        name="pack_rows",
    )(me, perms, x_att, w_qk, w_val)


def pack_tokens_kernel(
    peers, where_ref, ids_ref, tokens_ref, out_ref, slot_ref, mine_ref, copied
):
    length = tokens_ref.shape[0]
    slots, part = out_ref.shape
    columns = pl.ds(pl.multiple_of(where_ref[0] * part, part), part)
    copy = pltpu.make_async_copy(tokens_ref.at[:, columns], mine_ref, copied)
    copy.start()
    capacity = slots // peers
    experts = EXP_DEV * peers
    ids = ids_ref[...]
    hot = ids == iota((experts, length), 0)
    counts = dot(flag(hot), upper(length))
    rank = jnp.sum(jnp.where(hot, counts, 0.0), axis=0, keepdims=True).astype(I32) - 1
    core = where_ref[1]
    turn = (ids % EXP_DEV + core) % EXP_DEV
    peer = ids // EXP_DEV
    slot_ref[...] = jnp.broadcast_to(
        (peer * EXP_DEV + turn) * capacity + rank, slot_ref.shape
    )
    slot = jnp.where(turn == 0, peer * capacity + rank, -1)
    pick = flag(iota((slots, length), 0) == slot)
    copy.wait()
    out_ref[...] = dot(pick, mine_ref[...]).astype(BF16)


def pack_tokens(where, ids, tokens, peers, capacity, part):
    length = tokens.shape[0]
    slots = peers * capacity
    return pl.pallas_call(
        functools.partial(pack_tokens_kernel, peers),
        grid_spec=pltpu.PrefetchScalarGridSpec(
            num_scalar_prefetch=1,
            grid=(1,),
            in_specs=[
                pl.BlockSpec((1, length), lambda i, e: (0, 0)),
                pl.BlockSpec(memory_space=pl.ANY),
            ],
            out_specs=[
                pl.BlockSpec((slots, part), lambda i, e: (0, 0)),
                pl.BlockSpec((8, length), lambda i, e: (0, 0)),
            ],
            scratch_shapes=[pltpu.VMEM((length, part), BF16), pltpu.SemaphoreType.DMA],
        ),
        out_shape=[
            jax.ShapeDtypeStruct((slots, part), BF16),
            jax.ShapeDtypeStruct((8, length), I32),
        ],
        cost_estimate=cost(2 * slots * length * part, 2 << 20),
        compiler_params=BIG,
        name="pack_tokens",
    )(where, ids, tokens)


def experts_kernel(where_ref, *refs):
    step = pl.program_id(0)
    shards, far_refs, weights = refs[0:3], refs[3:5], refs[5:11]
    out_ref, total_ref = refs[11:]
    peers, capacity, part = shards[0].shape
    rows = peers * capacity
    ups = (weights[0], weights[1], weights[3], weights[4])

    def add(x, start):
        for index, weight in enumerate(ups):
            product = dot(x, weight[0])
            total_ref[index] = product if start else total_ref[index] + product

    for turn, shard in enumerate(shards):

        @pl.when(step == turn)
        def _(shard=shard, start=turn == 0):
            add(shard[...].reshape(rows, part), start)

    @pl.when(step == len(shards))
    def _():
        add(jnp.concatenate([ref[...].reshape(rows // 2, part) for ref in far_refs], axis=0), False)
        hiddens = []
        for side in range(EXP_DEV):
            gate, up_val = total_ref[2 * side], total_ref[2 * side + 1]
            hiddens.append((gate / (1.0 + jnp.exp(-gate)) * up_val).astype(BF16))
        half = part // EXP_DEV
        for index in range(out_ref.shape[0]):
            at = index * part
            piece = dot(hiddens[0], weights[2][0, :, at : at + part])
            piece = (piece + dot(hiddens[1], weights[5][0, :, at : at + part])).astype(BF16)
            for side in range(EXP_DEV):
                columns = piece[:, side * half : (side + 1) * half]
                out_ref[index, side] = columns.reshape(peers, capacity, half)


def run_experts(where, shards, far, own, sibling):
    peers, capacity, part = shards[0].shape
    width, hidden = own[0].shape[1:]
    chips = width // part
    out = (chips, EXP_DEV, peers, capacity, part // EXP_DEV)
    rows = peers * capacity

    def rows_of(i, e):
        ahead = jnp.where(i == 0, 0, jnp.where(i == 1, chips - 1, jnp.where(i == 2, 1, 2)))
        return (e[0] + ahead) % chips

    up_block, down_block = (1, part, hidden), (1, hidden, width)
    own_up = pl.BlockSpec(up_block, lambda i, e: (e[1], rows_of(i, e), 0))
    own_down = pl.BlockSpec(down_block, lambda i, e: (e[1], 0, 0))
    return pl.pallas_call(
        experts_kernel,
        grid_spec=pltpu.PrefetchScalarGridSpec(
            num_scalar_prefetch=1,
            grid=(len(shards) + 1,),
            in_specs=[pl.BlockSpec(x.shape, lambda i, e: (0, 0, 0)) for x in (*shards, *far)]
            + [own_up, own_up, own_down] * 2,
            out_specs=pl.BlockSpec(out, lambda i, e: (0, 0, 0, 0, 0)),
            scratch_shapes=[pltpu.VMEM((4, rows, hidden), F32)],
        ),
        out_shape=jax.ShapeDtypeStruct(out, BF16),
        cost_estimate=cost(15 * 10**9, 10 << 20),
        compiler_params=BIG,
        name="experts",
    )(where, *shards, *far, *own, *sibling)


def place_rows_kernel(where_ref, rows_ref, taken_ref, out_ref):
    out_ref[:, 0] = rows_ref[0]
    out_ref[:, 1] = taken_ref[...]


def place_rows(where, rows, taken):
    peers, capacity, half = taken.shape
    out = (peers, EXP_DEV, capacity, half)
    return pl.pallas_call(
        place_rows_kernel,
        grid_spec=pltpu.PrefetchScalarGridSpec(
            num_scalar_prefetch=1,
            grid=(1,),
            in_specs=[
                pl.BlockSpec((1, *taken.shape), lambda i, e: (e[1], 0, 0, 0)),
                pl.BlockSpec(taken.shape, lambda i, e: (0, 0, 0)),
            ],
            out_specs=pl.BlockSpec(out, lambda i, e: (0, 0, 0, 0)),
        ),
        out_shape=jax.ShapeDtypeStruct(out, BF16),
        cost_estimate=cost(1 << 20, 1 << 20),
        compiler_params=BIG,
        name="place_rows",
    )(where, rows, taken)


def finish_kernel(back_ref, slot_ref, kept_ref, taken_ref, attended_ref, mixed_ref):
    length = mixed_ref.shape[0]
    column = to_col(slot_ref[:1, :].astype(F32)).astype(I32)
    pick = flag(column == iota((length, back_ref.shape[0]), 1))
    mixed_ref[...] = dot(pick, back_ref[...]).astype(BF16)
    attended_ref[...] = (kept_ref[...] + taken_ref[...].astype(F32)).astype(BF16)


def finish(back, slot, kept, taken):
    length, width = slot.shape[1], back.shape[1]
    return pl.pallas_call(
        finish_kernel,
        out_shape=[
            jax.ShapeDtypeStruct(kept.shape, BF16),
            jax.ShapeDtypeStruct((length, width), BF16),
        ],
        cost_estimate=cost(2 * length * back.shape[0] * width, 1 << 20),
        compiler_params=BIG,
        name="finish",
    )(back, slot, kept, taken)


def sort_rows_kernel(peers, me_ref, perms_ref, arrived_ref, rows_ref, last_ref, slot_ref):
    rounds, length = perms_ref.shape
    per_peer = length // peers
    for turn in range(rounds):
        source = perms_ref[turn : turn + 1, :] >> (length.bit_length() - 1)
        hot = source == iota((peers, length), 0)
        counts = dot(flag(hot), upper(length))
        rank = jnp.sum(jnp.where(hot, counts, 0.0), axis=0, keepdims=True) - 1.0
        slot = source * per_peer + rank.astype(I32)
        slot_ref[turn] = jnp.broadcast_to(slot, slot_ref.shape[1:])
        pick = flag(to_col(slot.astype(F32)).astype(I32) == iota((length, length), 1))
        have = arrived_ref[:, turn * per_peer : (turn + 1) * per_peer, :]
        rows = dot(pick, have.reshape(length, have.shape[2])).astype(BF16)
        rows_ref[turn] = rows
        last_ref[turn] = rows[length - BLOCK_LEN :]


def sort_rows(me, perms, arrived, length):
    rounds = perms.shape[0]
    peers, _, width = arrived.shape
    return pl.pallas_call(
        functools.partial(sort_rows_kernel, peers),
        grid_spec=pltpu.PrefetchScalarGridSpec(
            num_scalar_prefetch=1,
            grid=(1,),
            in_specs=[
                pl.BlockSpec((rounds, length), lambda i, s: (0, s[0])),
                pl.BlockSpec(arrived.shape, lambda i, s: (0, 0, 0)),
            ],
            out_specs=[
                pl.BlockSpec((rounds, length, width), lambda i, s: (0, 0, 0)),
                pl.BlockSpec((rounds, BLOCK_LEN, width), lambda i, s: (0, 0, 0)),
                pl.BlockSpec((rounds, 8, length), lambda i, s: (0, 0, 0)),
            ],
        ),
        out_shape=[
            jax.ShapeDtypeStruct((rounds, length, width), BF16),
            jax.ShapeDtypeStruct((rounds, BLOCK_LEN, width), BF16),
            jax.ShapeDtypeStruct((rounds, 8, length), I32),
        ],
        cost_estimate=cost(LONG, 4 << 20),
        compiler_params=BIG,
        name="sort_rows",
    )(me, perms, arrived)


def window_scale(keys):
    wide = keys.astype(F32)
    squares = jnp.sum(wide * wide, axis=-1, keepdims=True)
    return to_row(lax.rsqrt(squares + 1e-06) / math.sqrt(HEAD_DIM))


def attend_tile(query, keys, values, scale, pos_q, pos_k):
    tile, window = query.shape[0], keys.shape[0]
    block_q = iota((tile, window), 0) // BLOCK_LEN
    block_k = iota((tile, window), 1) // BLOCK_LEN
    met = (block_k == block_q + 1) | (block_k == block_q + 2)
    scores = dot_t(query, keys) * scale
    scores = jnp.where(pos_k == pos_q, scores - 10000.0, scores)
    scores = jnp.where(met & (pos_k <= pos_q), scores, -1e30)
    peak = jnp.max(scores, axis=-1, keepdims=True)
    exponent = jnp.exp(scores - peak)
    total = jnp.sum(exponent, axis=-1, keepdims=True)
    weights = (exponent / total).astype(BF16)
    return dot(weights, values).astype(BF16), peak + jnp.log(total)


TILE, WINDOW, PIECES, GROUP = 2 * BLOCK_LEN, 4 * BLOCK_LEN, 3, 8


def put_logs(totals):
    lane = iota((totals[0].shape[0], LANES), 1) % GROUP
    logs = jnp.zeros(lane.shape, F32)
    for head, total in enumerate(totals):
        rest = total
        for piece in range(PIECES):
            part = rest.astype(BF16).astype(F32)
            logs = jnp.where(lane == head * PIECES + piece, part, logs)
            rest = rest - part
    return logs.astype(BF16)


def attend_later_kernel(me_ref, perms_ref, rows_ref, out_ref):
    rounds, length = perms_ref.shape
    span = rows_ref.shape[2] // 2
    for turn in range(rounds):
        position = perms_ref[turn : turn + 1, :].astype(F32)
        position_col = to_col(position)
        scales = []
        for head in range(span // HEAD_DIM):
            at = head * HEAD_DIM
            scales.append(window_scale(rows_ref[turn, :, at : at + HEAD_DIM]))
        for first in range(TILE, length, TILE):
            totals = []
            window = slice(first + TILE - WINDOW, first + TILE)
            queries = slice(first, first + TILE)
            for head in range(span // HEAD_DIM):
                at = head * HEAD_DIM
                out, total = attend_tile(
                    rows_ref[turn, queries, at : at + HEAD_DIM],
                    rows_ref[turn, window, at : at + HEAD_DIM],
                    rows_ref[turn, window, span + at : span + at + HEAD_DIM],
                    scales[head][:, window],
                    position_col[queries],
                    position[:, window],
                )
                out_ref[turn, first - TILE : first, at : at + HEAD_DIM] = out
                totals.append(total)
            out_ref[turn, first - TILE : first, span:] = put_logs(totals)


def attend_first_kernel(
    peers,
    me_ref,
    perms_ref,
    earlier_ref,
    rows_ref,
    last_ref,
    slot_ref,
    later_ref,
    out_ref,
):
    rounds, length = slot_ref.shape[0], slot_ref.shape[2]
    per_peer = length // peers
    span = rows_ref.shape[2] // 2
    lane_group = iota((peers, per_peer, LANES), 2) // GROUP
    own_group = lane_group == iota((peers, per_peer, LANES), 1)
    empty = jnp.zeros((BLOCK_LEN, HEAD_DIM), BF16)
    log_row = iota((peers, GROUP, LANES), 1)
    all_logs = jnp.zeros((peers, GROUP, LANES), F32)
    for turn in range(rounds):
        position = perms_ref[turn : turn + 1, :].astype(F32)
        positions = jnp.concatenate([earlier_ref[turn : turn + 1, :].astype(F32), position], axis=1)
        position_col = to_col(position)
        totals, outs = [], []
        for head in range(span // HEAD_DIM):
            at = head * HEAD_DIM
            own = rows_ref[turn, :, at : at + HEAD_DIM]
            keys = jnp.concatenate([empty, last_ref[turn, :, at : at + HEAD_DIM], own], axis=0)
            at = span + at
            values = jnp.concatenate(
                [
                    empty,
                    last_ref[turn, :, at : at + HEAD_DIM],
                    rows_ref[turn, :, at : at + HEAD_DIM],
                ],
                axis=0,
            )
            out, total = attend_tile(
                own, keys, values, window_scale(keys), position_col, positions
            )
            outs.append(out)
            totals.append(total)
        top = jnp.concatenate(outs + [put_logs(totals)], axis=1)
        whole = jnp.concatenate([top, later_ref[turn]], axis=0) if length > TILE else top
        back = flag(iota((length, length), 0) == slot_ref[turn, :1, :])
        moved = dot(back, whole)
        for head in range(span // HEAD_DIM):
            at = (head * rounds + turn) * per_peer
            lanes = moved[:, head * HEAD_DIM : (head + 1) * HEAD_DIM]
            out_ref[:, at : at + per_peer, :] = lanes.astype(BF16).reshape(
                peers, per_peer, HEAD_DIM
            )
        logs = moved[:, span:].reshape(peers, per_peer, LANES)
        logs = jnp.sum(jnp.where(own_group, logs, 0.0), axis=1, keepdims=True)
        all_logs = jnp.where(log_row == turn, logs, all_logs)
    out_ref[:, out_ref.shape[1] - GROUP :, :] = all_logs.astype(BF16)


def attend_later(me, perms, rows):
    rounds, length, width = rows.shape
    span = width // 2
    out = (rounds, length - TILE, span + LANES)
    return pl.pallas_call(
        attend_later_kernel,
        grid_spec=pltpu.PrefetchScalarGridSpec(
            num_scalar_prefetch=1,
            grid=(1,),
            in_specs=[
                pl.BlockSpec((rounds, length), lambda i, s: (0, s[0])),
                pl.BlockSpec(rows.shape, lambda i, s: (0, 0, 0)),
            ],
            out_specs=pl.BlockSpec(out, lambda i, s: (0, 0, 0)),
        ),
        out_shape=jax.ShapeDtypeStruct(out, BF16),
        cost_estimate=cost(LONG, 4 << 20),
        compiler_params=BIG,
        name="attend_later",
    )(me, perms, rows)


def attend_first(me, perms, rows, last, slot, later, peers):
    rounds, length, width = rows.shape
    span = width // 2
    per_peer = length // peers
    lane_blocks = length // LANES

    def fixed(shape):
        return pl.BlockSpec(shape, lambda i, s: (0, 0, 0))

    out = (peers, span // HEAD_DIM * rounds * per_peer + GROUP, HEAD_DIM)
    return pl.pallas_call(
        functools.partial(attend_first_kernel, peers),
        grid_spec=pltpu.PrefetchScalarGridSpec(
            num_scalar_prefetch=1,
            grid=(1,),
            in_specs=[
                pl.BlockSpec((rounds, TILE), lambda i, s: (0, s[0] * lane_blocks)),
                pl.BlockSpec(
                    (rounds, LANES),
                    lambda i, s: (
                        0,
                        jnp.where(s[0] == 0, peers * lane_blocks - 1, s[0] * lane_blocks - 1),
                    ),
                ),
                fixed((rounds, TILE, width)),
                fixed(last.shape),
                fixed(slot.shape),
                fixed(later.shape),
            ],
            out_specs=fixed(out),
        ),
        out_shape=jax.ShapeDtypeStruct(out, BF16),
        cost_estimate=cost(LONG, 4 << 20),
        compiler_params=BIG,
        name="attend_first",
    )(me, perms, perms, rows, last, slot, later)


def combine_kernel(got_ref, token_ref, mixed_ref):
    peers = got_ref.shape[0]
    rounds, _, length = token_ref.shape
    per_peer = length // peers
    heads = mixed_ref.shape[1] // HEAD_DIM
    lane_group = iota((peers, per_peer, LANES), 2) // GROUP
    own_group = lane_group == iota((peers, per_peer, LANES), 1)
    lane = iota((length, LANES), 1) % GROUP // PIECES
    column = iota((length, length), 0)
    log_row = iota((peers, GROUP, LANES), 1)
    all_logs = got_ref[:, got_ref.shape[1] - GROUP :, :].astype(F32)
    outs, lses = [], []
    for turn in range(rounds):
        pick = flag(token_ref[turn, :1, :] == column)
        logs = jnp.sum(jnp.where(log_row == turn, all_logs, 0.0), axis=1, keepdims=True)
        logs = jnp.where(own_group, logs, 0.0).astype(BF16)
        sides = []
        for head in range(heads):
            at = (head * rounds + turn) * per_peer
            sides.append(got_ref[:, at : at + per_peer, :].reshape(length, HEAD_DIM))
        outs.append(dot(pick, jnp.concatenate(sides, axis=1)))
        moved = dot(pick, logs.reshape(length, LANES))
        lses.append(
            [
                jnp.sum(jnp.where(lane == head, moved, 0.0), axis=1, keepdims=True)
                for head in range(heads)
            ]
        )
    for head in range(heads):
        logs = [lse[head] for lse in lses]
        peak = functools.reduce(jnp.maximum, logs)
        whole = peak + jnp.log(functools.reduce(jnp.add, [jnp.exp(lse - peak) for lse in logs]))
        at = head * HEAD_DIM
        mixed = jnp.zeros((length, HEAD_DIM), F32)
        for out, lse in zip(outs, logs):
            mixed = mixed + out[:, at : at + HEAD_DIM] * jnp.exp(lse - whole)
        mixed_ref[:, at : at + HEAD_DIM] = mixed.astype(BF16)


def combine(got, token, span):
    rounds, _, length = token.shape
    return pl.pallas_call(
        combine_kernel,
        out_shape=jax.ShapeDtypeStruct((length, span), BF16),
        cost_estimate=cost(2 * rounds * length * length * (span + LANES), 1 << 20),
        compiler_params=BIG,
        name="combine",
    )(got, token)


def project_kernel(where_ref, own_ref, prev_ref, next_ref, far_a_ref, far_b_ref, *refs):
    weights, (kept_ref, given_ref) = refs[:-2], refs[-2:]
    far = jnp.concatenate([far_a_ref[...], far_b_ref[...]], axis=0)
    total = dot(own_ref[...], weights[0][...]) + dot(prev_ref[...], weights[1][...])
    total = total + dot(next_ref[...], weights[2][...]) + dot(far, weights[3][...])
    half = kept_ref.shape[1]
    for core in range(EXP_DEV):

        @pl.when(where_ref[1] == core)
        def _(core=core):
            kept_ref[...] = total[:, core * half : (core + 1) * half]
            other = 1 - core
            given_ref[...] = total[:, other * half : (other + 1) * half].astype(BF16)


def project(where, heads, w_out, others):
    length, span = heads[0].shape
    columns = others[0].shape[1]
    half = columns // EXP_DEV
    weights = (w_out, *others)
    shapes = [x.shape for x in heads] + [(span, columns)] + [x.shape for x in others]

    def first(i, e):
        return (0, 0)

    specs = [pl.BlockSpec(shape, first) for shape in shapes]
    specs[len(heads)] = pl.BlockSpec((span, columns), lambda i, e: (0, e[0]))
    return pl.pallas_call(
        project_kernel,
        grid_spec=pltpu.PrefetchScalarGridSpec(
            num_scalar_prefetch=1,
            grid=(1,),
            in_specs=specs,
            out_specs=[pl.BlockSpec((length, half), first)] * 2,
        ),
        out_shape=[
            jax.ShapeDtypeStruct((length, half), F32),
            jax.ShapeDtypeStruct((length, half), BF16),
        ],
        cost_estimate=cost(35 * 10**8, 3 << 20),
        compiler_params=BIG,
        name="project",
    )(where, *heads, *weights)


def exchange(x, axis):
    return lax.all_to_all(x, axis, split_axis=0, concat_axis=0, tiled=True)


def hop(x, by, chips):
    pairs = []
    for chip in range(chips):
        for core in range(EXP_DEV):
            there = (chip + by) % chips
            pairs.append((chip * EXP_DEV + core, there * EXP_DEV + core))
    return lax.ppermute(x, "exp", pairs)


def spread(x, chips, ready=()):
    half = x.shape[0] // 2
    before, behind = hop(x, 1, chips), hop(x, -1, chips)
    before, behind = (after(side, *ready) if ready else side for side in (before, behind))
    far = (hop(before[:half], 1, chips), hop(behind[half:], -1, chips))
    return (x, before, behind), far


def after(x, *done):
    return lax.optimization_barrier((x, *done))[0]


def body(x_att, w_qk, w_val, w_out, perms, tokens_b, expert_ids, w_gate, w_up, w_down):
    peers, parts = lax.axis_size("seq"), lax.axis_size("exp")
    chips = parts // EXP_DEV
    me = lax.axis_index("seq").astype(I32).reshape(1)
    my_exp = lax.axis_index("exp").astype(I32)
    core = my_exp % EXP_DEV
    where = jnp.stack([my_exp // EXP_DEV, core])
    length, width = x_att.shape
    rounds = perms.shape[0]
    per_peer = length // peers
    tokb = tokens_b.shape[0]
    capacity = tokb // peers
    part = width // chips
    lines = [[chip * EXP_DEV + side for chip in range(chips)] for side in range(EXP_DEV)]
    siblings = [(i, i ^ 1) for i in range(parts)]

    dispatch, token_slot = pack_tokens(
        where, expert_ids.reshape(1, tokb), tokens_b, peers, capacity, part
    )
    received = exchange(dispatch.reshape(peers, capacity, part), "seq")
    outgoing, slot_token = pack_rows(me, perms, x_att, w_qk, w_val)
    def columns_of(by, *ready):
        start = (where[0] + by) % chips * part
        return hop(lax.dynamic_slice_in_dim(after(w_out, *ready), start, part, 1), by, chips)

    near = [columns_of(by, dispatch) for by in (1, chips - 1)]
    received = after(received, outgoing, *near)
    outgoing = after(outgoing, received)
    own = (w_gate, w_up, w_down)
    sibling = [lax.ppermute(after(weight, received), "exp", siblings) for weight in own]
    shards, far_shards = spread(received, chips)
    arrived = exchange(outgoing.reshape(peers, rounds * per_peer, outgoing.shape[1]), "seq")
    expert_part = run_experts(where, shards, far_shards, own, sibling)
    arrived = after(arrived, expert_part)
    rows, last, row_slot = sort_rows(me, perms, arrived, length)
    expert_rows = lax.psum_scatter(
        expert_part,
        "exp",
        scatter_dimension=0,
        tiled=False,
        axis_index_groups=lines,
    )
    last = lax.ppermute(last, "seq", [(i, (i + 1) % peers) for i in range(peers)])
    later = attend_later(me, perms, rows) if length > TILE else rows
    last = after(last, later)
    packed = attend_first(me, perms, rows, last, row_slot, later, peers)
    got = exchange(packed, "seq")
    far = columns_of(2, packed)
    expert_rows = after(expert_rows, packed)
    given = lax.dynamic_index_in_dim(expert_rows, 1 - core, 0, keepdims=False)
    taken = lax.ppermute(given, "exp", siblings)
    expert_rows = place_rows(where, expert_rows, taken)
    mixed_heads = combine(after(got, expert_rows, far), slot_token, w_qk.shape[1])
    expert_back = exchange(after(expert_rows, mixed_heads), "seq")
    heads, far_heads = spread(mixed_heads, chips)
    attn_kept, attn_given = project(where, (*heads, *far_heads), w_out, (*near, far))
    attn_taken = lax.ppermute(attn_given, "exp", siblings)
    expert_back = after(expert_back, attn_taken)
    return finish(
        expert_back.reshape(peers * EXP_DEV * capacity, width // parts),
        token_slot,
        attn_kept,
        attn_taken,
    )


def solution(mesh):
    in_specs = (
        P("seq", None),
        P(None, "exp"),
        P(None, "exp"),
        P("exp", None),
        P(),
        P("seq", None),
        P("seq", None),
        P("seq", None, "exp"),
        P("seq", None, "exp"),
        P("seq", "exp", None),
    )
    out_specs = (P("seq", "exp"), P("seq", "exp"))
    return jax.shard_map(body, mesh=mesh, in_specs=in_specs, out_specs=out_specs, check_vma=False)
```

```python
import functools
import math

import jax
import jax.numpy as jnp
from jax import lax
from jax.experimental import pallas as pl
from jax.experimental.pallas import tpu as pltpu
from jax.sharding import PartitionSpec as P

HEAD_DIM = 128
BLOCK_LEN = 64
EXP_DEV = 2
LANES = 128
F32, BF16, I32 = jnp.float32, jnp.bfloat16, jnp.int32
LONG = 1 << 35
BIG = pltpu.CompilerParams(vmem_limit_bytes=48 * 1024 * 1024)


def dot(a, b):
    return jnp.dot(a, b, preferred_element_type=F32)


def dot_t(a, b):
    return lax.dot_general(a, b, (((1,), (1,)), ((), ())), preferred_element_type=F32)


def to_col(row):
    return jnp.broadcast_to(row, (LANES, row.shape[1])).T[:, :1]


def to_row(col):
    return jnp.broadcast_to(col, (col.shape[0], LANES)).T[:1, :]


def iota(shape, dim):
    return lax.broadcasted_iota(I32, shape, dim)


def flag(mask, kind=BF16):
    return jnp.where(mask, 1.0, 0.0).astype(kind)


def cost(flops, size):
    return pl.CostEstimate(flops=flops, bytes_accessed=size, transcendentals=0)


def upper(count):
    return flag(iota((count, count), 0) <= iota((count, count), 1))


def pack_rows_kernel(me_ref, perms_ref, x_ref, qk_ref, val_ref, out_ref, token_ref, scratch):
    length, span = x_ref.shape[0], qk_ref.shape[1]
    rounds, total = perms_ref.shape
    peers = total // length
    per_peer = length // peers
    for peer in range(peers):
        scratch[peer * rounds : (peer + 1) * rounds, :] = perms_ref[
            :, peer * length : (peer + 1) * length
        ]
    perms = scratch[...]
    token = perms & (length - 1)
    mine = (perms >> (length.bit_length() - 1)) == me_ref[0]
    rank = dot(flag(mine), upper(length)).astype(I32) - 1
    slot = jnp.where(mine, rank, -1)
    groups = peers * rounds
    chosen = slot[:, None, :] == iota((groups, per_peer, length), 1)
    token_3d = jnp.where(chosen, token.astype(F32)[:, None, :], 0.0)
    column = jnp.sum(token_3d, axis=-1, keepdims=True).reshape(groups * per_peer, 1)
    by_round = column.reshape(peers, rounds, per_peer, 1)
    for turn in range(rounds):
        row = to_row(by_round[:, turn].reshape(peers * per_peer, 1)).astype(I32)
        token_ref[turn] = jnp.broadcast_to(row, token_ref.shape[1:])
    pick = flag(column.astype(I32) == iota((groups * per_peer, length), 1))
    for part, weight in enumerate((qk_ref, val_ref)):
        rows = dot(x_ref[...], weight[...]).astype(BF16)
        out_ref[:, part * span : (part + 1) * span] = dot(pick, rows).astype(BF16)


def pack_rows(me, perms, x_att, w_qk, w_val):
    length, width = x_att.shape
    rounds, total = perms.shape
    span = w_qk.shape[1]
    groups = rounds * (total // length)
    slots = rounds * length

    def whole(shape):
        return pl.BlockSpec(shape, lambda i, me_ref: (0, 0))

    return pl.pallas_call(
        pack_rows_kernel,
        grid_spec=pltpu.PrefetchScalarGridSpec(
            num_scalar_prefetch=1,
            grid=(1,),
            in_specs=[
                whole((rounds, total)),
                whole((length, width)),
                whole((width, span)),
                whole((width, span)),
            ],
            out_specs=[
                whole((slots, 2 * span)),
                pl.BlockSpec((rounds, 8, length), lambda i, me_ref: (0, 0, 0)),
            ],
            scratch_shapes=[pltpu.VMEM((groups, length), I32)],
        ),
        out_shape=[
            jax.ShapeDtypeStruct((slots, 2 * span), BF16),
            jax.ShapeDtypeStruct((rounds, 8, length), I32),
        ],
        cost_estimate=cost(4 * length * width * span + 4 * slots * length * span, 6 << 20),
        compiler_params=BIG,
        name="pack_rows",
    )(me, perms, x_att, w_qk, w_val)


def pack_tokens_kernel(
    peers, where_ref, ids_ref, tokens_ref, out_ref, slot_ref, mine_ref, copied
):
    length = tokens_ref.shape[0]
    slots, part = out_ref.shape
    columns = pl.ds(pl.multiple_of(where_ref[0] * part, part), part)
    copy = pltpu.make_async_copy(tokens_ref.at[:, columns], mine_ref, copied)
    copy.start()
    capacity = slots // peers
    experts = EXP_DEV * peers
    ids = ids_ref[...]
    hot = ids == iota((experts, length), 0)
    counts = dot(flag(hot), upper(length))
    rank = jnp.sum(jnp.where(hot, counts, 0.0), axis=0, keepdims=True).astype(I32) - 1
    core = where_ref[1]
    turn = (ids % EXP_DEV + core) % EXP_DEV
    peer = ids // EXP_DEV
    slot_ref[...] = jnp.broadcast_to(
        (peer * EXP_DEV + turn) * capacity + rank, slot_ref.shape
    )
    slot = jnp.where(turn == 0, peer * capacity + rank, -1)
    pick = flag(iota((slots, length), 0) == slot)
    copy.wait()
    out_ref[...] = dot(pick, mine_ref[...]).astype(BF16)


def pack_tokens(where, ids, tokens, peers, capacity, part):
    length = tokens.shape[0]
    slots = peers * capacity
    return pl.pallas_call(
        functools.partial(pack_tokens_kernel, peers),
        grid_spec=pltpu.PrefetchScalarGridSpec(
            num_scalar_prefetch=1,
            grid=(1,),
            in_specs=[
                pl.BlockSpec((1, length), lambda i, e: (0, 0)),
                pl.BlockSpec(memory_space=pltpu.HBM),
            ],
            out_specs=[
                pl.BlockSpec((slots, part), lambda i, e: (0, 0)),
                pl.BlockSpec((8, length), lambda i, e: (0, 0)),
            ],
            scratch_shapes=[pltpu.VMEM((length, part), BF16), pltpu.SemaphoreType.DMA],
        ),
        out_shape=[
            jax.ShapeDtypeStruct((slots, part), BF16),
            jax.ShapeDtypeStruct((8, length), I32),
        ],
        cost_estimate=cost(2 * slots * length * part, 2 << 20),
        compiler_params=BIG,
        name="pack_tokens",
    )(where, ids, tokens)


def experts_kernel(where_ref, *refs):
    step = pl.program_id(0)
    shards, far_refs, weights = refs[0:3], refs[3:5], refs[5:11]
    out_ref, total_ref = refs[11:]
    peers, capacity, part = shards[0].shape
    rows = peers * capacity
    ups = (weights[0], weights[1], weights[3], weights[4])

    def add(x, start):
        for index, weight in enumerate(ups):
            product = dot(x, weight[0])
            total_ref[index] = product if start else total_ref[index] + product

    for turn, shard in enumerate(shards):

        @pl.when(step == turn)
        def _(shard=shard, start=turn == 0):
            add(shard[...].reshape(rows, part), start)

    @pl.when(step == len(shards))
    def _():
        add(jnp.concatenate([ref[...].reshape(rows // 2, part) for ref in far_refs], axis=0), False)
        hiddens = []
        for side in range(EXP_DEV):
            gate, up_val = total_ref[2 * side], total_ref[2 * side + 1]
            hiddens.append((gate / (1.0 + jnp.exp(-gate)) * up_val).astype(BF16))
        half = part // EXP_DEV
        for index in range(out_ref.shape[0]):
            at = index * part
            piece = dot(hiddens[0], weights[2][0, :, at : at + part])
            piece = (piece + dot(hiddens[1], weights[5][0, :, at : at + part])).astype(BF16)
            for side in range(EXP_DEV):
                columns = piece[:, side * half : (side + 1) * half]
                turn = (side + where_ref[1]) % EXP_DEV
                out_ref[index, turn] = columns.reshape(peers, capacity, half)


def run_experts(where, shards, far, own, sibling):
    peers, capacity, part = shards[0].shape
    width, hidden = own[0].shape[1:]
    chips = width // part
    out = (chips, EXP_DEV, peers, capacity, part // EXP_DEV)
    rows = peers * capacity

    def rows_of(i, e):
        ahead = jnp.where(i == 0, 0, jnp.where(i == 1, chips - 1, jnp.where(i == 2, 1, 2)))
        return (e[0] + ahead) % chips

    up_block, down_block = (1, part, hidden), (1, hidden, width)
    own_up = pl.BlockSpec(up_block, lambda i, e: (e[1], rows_of(i, e), 0))
    own_down = pl.BlockSpec(down_block, lambda i, e: (e[1], 0, 0))
    return pl.pallas_call(
        experts_kernel,
        grid_spec=pltpu.PrefetchScalarGridSpec(
            num_scalar_prefetch=1,
            grid=(len(shards) + 1,),
            in_specs=[pl.BlockSpec(x.shape, lambda i, e: (0, 0, 0)) for x in (*shards, *far)]
            + [own_up, own_up, own_down] * 2,
            out_specs=pl.BlockSpec(out, lambda i, e: (0, 0, 0, 0, 0)),
            scratch_shapes=[pltpu.VMEM((4, rows, hidden), F32)],
        ),
        out_shape=jax.ShapeDtypeStruct(out, BF16),
        cost_estimate=cost(15 * 10**9, 10 << 20),
        compiler_params=BIG,
        name="experts",
    )(where, *shards, *far, *own, *sibling)


def place_rows_kernel(rows_ref, taken_ref, out_ref, copied):
    copies = (
        pltpu.make_async_copy(rows_ref.at[0], out_ref.at[:, 0], copied.at[0]),
        pltpu.make_async_copy(taken_ref, out_ref.at[:, 1], copied.at[1]),
    )
    for copy in copies:
        copy.start()
    for copy in copies:
        copy.wait()


def place_rows(rows, taken):
    peers, capacity, half = taken.shape
    return pl.pallas_call(
        place_rows_kernel,
        in_specs=[pl.BlockSpec(memory_space=pltpu.HBM)] * 2,
        out_specs=pl.BlockSpec(memory_space=pltpu.HBM),
        out_shape=jax.ShapeDtypeStruct((peers, EXP_DEV, capacity, half), BF16),
        scratch_shapes=[pltpu.SemaphoreType.DMA((2,))],
        cost_estimate=cost(1 << 20, 1 << 20),
        compiler_params=BIG,
        name="place_rows",
    )(rows, taken)


def finish_kernel(back_ref, slot_ref, kept_ref, taken_ref, attended_ref, mixed_ref):
    length = mixed_ref.shape[0]
    column = to_col(slot_ref[:1, :].astype(F32)).astype(I32)
    pick = flag(column == iota((length, back_ref.shape[0]), 1))
    mixed_ref[...] = dot(pick, back_ref[...]).astype(BF16)
    attended_ref[...] = (kept_ref[...] + taken_ref[...].astype(F32)).astype(BF16)


def finish(back, slot, kept, taken):
    length, width = slot.shape[1], back.shape[1]
    return pl.pallas_call(
        finish_kernel,
        out_shape=[
            jax.ShapeDtypeStruct(kept.shape, BF16),
            jax.ShapeDtypeStruct((length, width), BF16),
        ],
        cost_estimate=cost(2 * length * back.shape[0] * width, 1 << 20),
        compiler_params=BIG,
        name="finish",
    )(back, slot, kept, taken)


def sort_rows_kernel(peers, me_ref, perms_ref, arrived_ref, rows_ref, last_ref, slot_ref):
    rounds, length = perms_ref.shape
    per_peer = length // peers
    for turn in range(rounds):
        source = perms_ref[turn : turn + 1, :] >> (length.bit_length() - 1)
        hot = source == iota((peers, length), 0)
        counts = dot(flag(hot), upper(length))
        rank = jnp.sum(jnp.where(hot, counts, 0.0), axis=0, keepdims=True) - 1.0
        slot = source * per_peer + rank.astype(I32)
        slot_ref[turn] = jnp.broadcast_to(slot, slot_ref.shape[1:])
        pick = flag(to_col(slot.astype(F32)).astype(I32) == iota((length, length), 1))
        have = arrived_ref[:, turn * per_peer : (turn + 1) * per_peer, :]
        rows = dot(pick, have.reshape(length, have.shape[2])).astype(BF16)
        rows_ref[turn] = rows
        last_ref[turn] = rows[length - BLOCK_LEN :]


def sort_rows(me, perms, arrived, length):
    rounds = perms.shape[0]
    peers, _, width = arrived.shape
    return pl.pallas_call(
        functools.partial(sort_rows_kernel, peers),
        grid_spec=pltpu.PrefetchScalarGridSpec(
            num_scalar_prefetch=1,
            grid=(1,),
            in_specs=[
                pl.BlockSpec((rounds, length), lambda i, s: (0, s[0])),
                pl.BlockSpec(arrived.shape, lambda i, s: (0, 0, 0)),
            ],
            out_specs=[
                pl.BlockSpec((rounds, length, width), lambda i, s: (0, 0, 0)),
                pl.BlockSpec((rounds, BLOCK_LEN, width), lambda i, s: (0, 0, 0)),
                pl.BlockSpec((rounds, 8, length), lambda i, s: (0, 0, 0)),
            ],
        ),
        out_shape=[
            jax.ShapeDtypeStruct((rounds, length, width), BF16),
            jax.ShapeDtypeStruct((rounds, BLOCK_LEN, width), BF16),
            jax.ShapeDtypeStruct((rounds, 8, length), I32),
        ],
        cost_estimate=cost(LONG, 4 << 20),
        compiler_params=BIG,
        name="sort_rows",
    )(me, perms, arrived)


def window_scale(keys):
    wide = keys.astype(F32)
    squares = jnp.sum(wide * wide, axis=-1, keepdims=True)
    return to_row(lax.rsqrt(squares + 1e-06) / math.sqrt(HEAD_DIM))


def windows(row, first, last):
    moved = jnp.concatenate([row[:, BLOCK_LEN:], row[:, :BLOCK_LEN]], axis=1)
    spans = []
    for start in range(first, last, BLOCK_LEN):
        odd = start % LANES
        span = (moved if odd else row)[:, start - odd : start - odd + WINDOW]
        spans.append(jnp.broadcast_to(span, (BLOCK_LEN, WINDOW)))
    return jnp.concatenate(spans, axis=0)


def attend_blocks(queries, keys, values, scale, pos_q, pos_k):
    starts = range(0, queries.shape[0], BLOCK_LEN)
    scores = jnp.concatenate(
        [dot_t(queries[at : at + BLOCK_LEN], keys[at : at + WINDOW]) for at in starts], axis=0
    )
    scores = scores * scale
    scores = jnp.where(pos_k == pos_q, scores - 10000.0, scores)
    scores = jnp.where(pos_k <= pos_q, scores, -1e30)
    peak = jnp.max(scores, axis=-1, keepdims=True)
    exponent = jnp.exp(scores - peak)
    total = jnp.sum(exponent, axis=-1, keepdims=True)
    weights = (exponent / total).astype(BF16)
    outs = [dot(weights[at : at + BLOCK_LEN], values[at : at + WINDOW]) for at in starts]
    return jnp.concatenate(outs, axis=0).astype(BF16), peak + jnp.log(total)


TILE, WINDOW, PIECES, GROUP = BLOCK_LEN, 2 * BLOCK_LEN, 3, 8


def put_logs(totals):
    lane = iota((totals[0].shape[0], LANES), 1) % GROUP
    logs = jnp.zeros(lane.shape, F32)
    for head, total in enumerate(totals):
        rest = total
        for piece in range(PIECES):
            part = rest.astype(BF16).astype(F32)
            logs = jnp.where(lane == head * PIECES + piece, part, logs)
            rest = rest - part
    return logs.astype(BF16)


def attend_later_kernel(me_ref, perms_ref, rows_ref, slot_ref, out_ref):
    rounds, length = perms_ref.shape
    span = rows_ref.shape[2] // 2
    for turn in range(rounds):
        position = perms_ref[turn : turn + 1, :].astype(F32)
        pos_q = to_col(position)[TILE:]
        pos_k = windows(position, 0, length - TILE)
        outs, totals = [], []
        for head in range(span // HEAD_DIM):
            at = head * HEAD_DIM
            keys = rows_ref[turn, :, at : at + HEAD_DIM]
            out, total = attend_blocks(
                keys[TILE:],
                keys,
                rows_ref[turn, :, span + at : span + at + HEAD_DIM],
                windows(window_scale(keys), 0, length - TILE),
                pos_q,
                pos_k,
            )
            outs.append(out)
            totals.append(total)
        whole = jnp.concatenate(outs + [put_logs(totals)], axis=1)
        back = flag(iota((length, length), 0) == slot_ref[turn, :1, :])
        whole = jnp.concatenate([jnp.zeros((TILE, whole.shape[1]), BF16), whole], axis=0)
        out_ref[turn] = dot(back, whole).astype(BF16)


def attend_first_kernel(
    peers,
    me_ref,
    perms_ref,
    earlier_ref,
    rows_ref,
    last_ref,
    slot_ref,
    later_ref,
    out_ref,
):
    rounds, length = slot_ref.shape[0], slot_ref.shape[2]
    per_peer = length // peers
    span = rows_ref.shape[2] // 2
    lane_group = iota((peers, per_peer, LANES), 2) // GROUP
    own_group = lane_group == iota((peers, per_peer, LANES), 1)
    log_row = iota((peers, GROUP, LANES), 1)
    all_logs = jnp.zeros((peers, GROUP, LANES), F32)
    lane = iota((1, LANES), 1)
    for turn in range(rounds):
        position = perms_ref[turn : turn + 1, :].astype(F32)
        earlier = earlier_ref[turn : turn + 1, :].astype(F32)
        swapped = jnp.concatenate([position[:, BLOCK_LEN:], position[:, :BLOCK_LEN]], axis=1)
        earlier = jnp.concatenate([earlier[:, BLOCK_LEN:], earlier[:, :BLOCK_LEN]], axis=1)
        pos_k = jnp.where(lane < BLOCK_LEN, earlier, swapped)
        pos_q = to_col(position)[:TILE]
        totals, outs = [], []
        for head in range(span // HEAD_DIM):
            at = head * HEAD_DIM
            own = rows_ref[turn, :TILE, at : at + HEAD_DIM]
            keys = jnp.concatenate([last_ref[turn, :, at : at + HEAD_DIM], own], axis=0)
            at = span + at
            values = jnp.concatenate(
                [
                    last_ref[turn, :, at : at + HEAD_DIM],
                    rows_ref[turn, :TILE, at : at + HEAD_DIM],
                ],
                axis=0,
            )
            out, total = attend_blocks(own, keys, values, window_scale(keys), pos_q, pos_k)
            outs.append(out)
            totals.append(total)
        top = jnp.concatenate(outs + [put_logs(totals)], axis=1)
        top = jnp.concatenate([top, jnp.zeros((LANES - TILE, top.shape[1]), BF16)], axis=0)
        back = flag(iota((length, LANES), 0) == slot_ref[turn, :1, :LANES])
        moved = dot(back, top) + later_ref[turn].astype(F32)
        for head in range(span // HEAD_DIM):
            at = (head * rounds + turn) * per_peer
            lanes = moved[:, head * HEAD_DIM : (head + 1) * HEAD_DIM]
            out_ref[:, at : at + per_peer, :] = lanes.astype(BF16).reshape(
                peers, per_peer, HEAD_DIM
            )
        logs = moved[:, span:].reshape(peers, per_peer, LANES)
        logs = jnp.sum(jnp.where(own_group, logs, 0.0), axis=1, keepdims=True)
        all_logs = jnp.where(log_row == turn, logs, all_logs)
    out_ref[:, out_ref.shape[1] - GROUP :, :] = all_logs.astype(BF16)


def attend_later(me, perms, rows, slot):
    rounds, length, width = rows.shape
    span = width // 2
    out = (rounds, length, span + LANES)
    return pl.pallas_call(
        attend_later_kernel,
        grid_spec=pltpu.PrefetchScalarGridSpec(
            num_scalar_prefetch=1,
            grid=(1,),
            in_specs=[
                pl.BlockSpec((rounds, length), lambda i, s: (0, s[0])),
                pl.BlockSpec(rows.shape, lambda i, s: (0, 0, 0)),
                pl.BlockSpec(slot.shape, lambda i, s: (0, 0, 0)),
            ],
            out_specs=pl.BlockSpec(out, lambda i, s: (0, 0, 0)),
        ),
        out_shape=jax.ShapeDtypeStruct(out, BF16),
        cost_estimate=cost(LONG, 4 << 20),
        compiler_params=BIG,
        name="attend_later",
    )(me, perms, rows, slot)


def attend_first(me, perms, rows, last, slot, later, peers):
    rounds, length, width = rows.shape
    span = width // 2
    per_peer = length // peers
    lane_blocks = length // LANES

    def fixed(shape):
        return pl.BlockSpec(shape, lambda i, s: (0, 0, 0))

    out = (peers, span // HEAD_DIM * rounds * per_peer + GROUP, HEAD_DIM)
    return pl.pallas_call(
        functools.partial(attend_first_kernel, peers),
        grid_spec=pltpu.PrefetchScalarGridSpec(
            num_scalar_prefetch=1,
            grid=(1,),
            in_specs=[
                pl.BlockSpec((rounds, LANES), lambda i, s: (0, s[0] * lane_blocks)),
                pl.BlockSpec(
                    (rounds, LANES),
                    lambda i, s: (
                        0,
                        jnp.where(s[0] == 0, peers * lane_blocks - 1, s[0] * lane_blocks - 1),
                    ),
                ),
                fixed((rounds, LANES, width)),
                fixed(last.shape),
                fixed(slot.shape),
                fixed(later.shape),
            ],
            out_specs=fixed(out),
        ),
        out_shape=jax.ShapeDtypeStruct(out, BF16),
        cost_estimate=cost(LONG, 4 << 20),
        compiler_params=BIG,
        name="attend_first",
    )(me, perms, perms, rows, last, slot, later)


def combine_kernel(got_ref, token_ref, mixed_ref):
    peers = got_ref.shape[0]
    rounds, _, length = token_ref.shape
    per_peer = length // peers
    heads = mixed_ref.shape[1] // HEAD_DIM
    lane_group = iota((peers, per_peer, LANES), 2) // GROUP
    own_group = lane_group == iota((peers, per_peer, LANES), 1)
    lane = iota((length, LANES), 1) % GROUP // PIECES
    column = iota((length, length), 0)
    log_row = iota((peers, GROUP, LANES), 1)
    all_logs = got_ref[:, got_ref.shape[1] - GROUP :, :].astype(F32)
    outs, lses = [], []
    for turn in range(rounds):
        pick = flag(token_ref[turn, :1, :] == column)
        logs = jnp.sum(jnp.where(log_row == turn, all_logs, 0.0), axis=1, keepdims=True)
        logs = jnp.where(own_group, logs, 0.0).astype(BF16)
        sides = []
        for head in range(heads):
            at = (head * rounds + turn) * per_peer
            sides.append(got_ref[:, at : at + per_peer, :].reshape(length, HEAD_DIM))
        outs.append(dot(pick, jnp.concatenate(sides, axis=1)))
        moved = dot(pick, logs.reshape(length, LANES))
        lses.append(
            [
                jnp.sum(jnp.where(lane == head, moved, 0.0), axis=1, keepdims=True)
                for head in range(heads)
            ]
        )
    for head in range(heads):
        logs = [lse[head] for lse in lses]
        peak = functools.reduce(jnp.maximum, logs)
        whole = peak + jnp.log(functools.reduce(jnp.add, [jnp.exp(lse - peak) for lse in logs]))
        at = head * HEAD_DIM
        mixed = jnp.zeros((length, HEAD_DIM), F32)
        for out, lse in zip(outs, logs):
            mixed = mixed + out[:, at : at + HEAD_DIM] * jnp.exp(lse - whole)
        mixed_ref[:, at : at + HEAD_DIM] = mixed.astype(BF16)


def combine(got, token, span):
    rounds, _, length = token.shape
    return pl.pallas_call(
        combine_kernel,
        out_shape=jax.ShapeDtypeStruct((length, span), BF16),
        cost_estimate=cost(2 * rounds * length * length * (span + LANES), 1 << 20),
        compiler_params=BIG,
        name="combine",
    )(got, token)


def project_kernel(where_ref, own_ref, prev_ref, next_ref, far_a_ref, far_b_ref, *refs):
    weights, (kept_ref, given_ref) = refs[:-2], refs[-2:]
    far = jnp.concatenate([far_a_ref[...], far_b_ref[...]], axis=0)
    total = dot(own_ref[...], weights[0][...]) + dot(prev_ref[...], weights[1][...])
    total = total + dot(next_ref[...], weights[2][...]) + dot(far, weights[3][...])
    half = kept_ref.shape[1]
    for core in range(EXP_DEV):

        @pl.when(where_ref[1] == core)
        def _(core=core):
            kept_ref[...] = total[:, core * half : (core + 1) * half]
            other = 1 - core
            given_ref[...] = total[:, other * half : (other + 1) * half].astype(BF16)


def project(where, heads, w_out, others):
    length, span = heads[0].shape
    columns = others[0].shape[1]
    half = columns // EXP_DEV
    weights = (w_out, *others)
    shapes = [x.shape for x in heads] + [(span, columns)] + [x.shape for x in others]

    def first(i, e):
        return (0, 0)

    specs = [pl.BlockSpec(shape, first) for shape in shapes]
    specs[len(heads)] = pl.BlockSpec((span, columns), lambda i, e: (0, e[0]))
    return pl.pallas_call(
        project_kernel,
        grid_spec=pltpu.PrefetchScalarGridSpec(
            num_scalar_prefetch=1,
            grid=(1,),
            in_specs=specs,
            out_specs=[pl.BlockSpec((length, half), first)] * 2,
        ),
        out_shape=[
            jax.ShapeDtypeStruct((length, half), F32),
            jax.ShapeDtypeStruct((length, half), BF16),
        ],
        cost_estimate=cost(55 * 10**8, 3 << 20),
        compiler_params=BIG,
        name="project",
    )(where, *heads, *weights)


def exchange(x, axis):
    return lax.all_to_all(x, axis, split_axis=0, concat_axis=0, tiled=True)


def hop(x, by, chips):
    pairs = []
    for chip in range(chips):
        for core in range(EXP_DEV):
            there = (chip + by) % chips
            pairs.append((chip * EXP_DEV + core, there * EXP_DEV + core))
    return lax.ppermute(x, "exp", pairs)


def spread(x, chips, ready=()):
    half = x.shape[0] // 2
    before, behind = hop(x, 1, chips), hop(x, -1, chips)
    before, behind = (after(side, *ready) if ready else side for side in (before, behind))
    far = (hop(before[:half], 1, chips), hop(behind[half:], -1, chips))
    return (x, before, behind), far


def after(x, *done):
    return lax.optimization_barrier((x, *done))[0]


def body(x_att, w_qk, w_val, w_out, perms, tokens_b, expert_ids, w_gate, w_up, w_down):
    peers, parts = lax.axis_size("seq"), lax.axis_size("exp")
    chips = parts // EXP_DEV
    me = lax.axis_index("seq").astype(I32).reshape(1)
    my_exp = lax.axis_index("exp").astype(I32)
    core = my_exp % EXP_DEV
    where = jnp.stack([my_exp // EXP_DEV, core])
    length, width = x_att.shape
    rounds = perms.shape[0]
    per_peer = length // peers
    tokb = tokens_b.shape[0]
    capacity = tokb // peers
    part = width // chips
    lines = [[chip * EXP_DEV + side for chip in range(chips)] for side in range(EXP_DEV)]
    siblings = [(i, i ^ 1) for i in range(parts)]

    dispatch, token_slot = pack_tokens(
        where, expert_ids.reshape(1, tokb), tokens_b, peers, capacity, part
    )
    received = exchange(dispatch.reshape(peers, capacity, part), "seq")
    outgoing, slot_token = pack_rows(me, perms, x_att, w_qk, w_val)
    def columns_of(by, *ready):
        start = (where[0] + by) % chips * part
        return hop(lax.dynamic_slice_in_dim(after(w_out, *ready), start, part, 1), by, chips)

    near = [columns_of(by, dispatch) for by in (1, chips - 1)]
    received = after(received, outgoing, *near)
    outgoing = after(outgoing, received)
    own = (w_gate, w_up, w_down)
    sibling = [lax.ppermute(after(weight, received), "exp", siblings) for weight in own]
    shards, far_shards = spread(received, chips)
    arrived = exchange(outgoing.reshape(peers, rounds * per_peer, outgoing.shape[1]), "seq")
    far = columns_of(2, *far_shards)
    expert_part = run_experts(where, shards, far_shards, own, sibling)
    arrived = after(arrived, expert_part, far)
    rows, last, row_slot = sort_rows(me, perms, arrived, length)
    expert_rows = lax.psum_scatter(
        expert_part,
        "exp",
        scatter_dimension=0,
        tiled=False,
        axis_index_groups=lines,
    )
    last = lax.ppermute(last, "seq", [(i, (i + 1) % peers) for i in range(peers)])
    later = attend_later(me, perms, rows, row_slot)
    last = after(last, later)
    packed = attend_first(me, perms, rows, last, row_slot, later, peers)
    got = exchange(packed, "seq")
    expert_rows = after(expert_rows, packed)
    taken = lax.ppermute(expert_rows[1], "exp", siblings)
    expert_rows = place_rows(expert_rows, taken)
    mixed_heads = combine(after(got, expert_rows), slot_token, w_qk.shape[1])
    expert_back = exchange(after(expert_rows, mixed_heads), "seq")
    heads, far_heads = spread(mixed_heads, chips)
    attn_kept, attn_given = project(where, (*heads, *far_heads), w_out, (*near, far))
    attn_taken = lax.ppermute(attn_given, "exp", siblings)
    expert_back = after(expert_back, attn_taken)
    return finish(
        expert_back.reshape(peers * EXP_DEV * capacity, width // parts),
        token_slot,
        attn_kept,
        attn_taken,
    )


def solution(mesh):
    in_specs = (
        P("seq", None),
        P(None, "exp"),
        P(None, "exp"),
        P("exp", None),
        P(),
        P("seq", None),
        P("seq", None),
        P("seq", None, "exp"),
        P("seq", None, "exp"),
        P("seq", "exp", None),
    )
    out_specs = (P("seq", "exp"), P("seq", "exp"))
    return jax.shard_map(body, mesh=mesh, in_specs=in_specs, out_specs=out_specs, check_vma=False)
```

```python
import functools
import math

import jax
import jax.numpy as jnp
from jax import lax
from jax.experimental import pallas as pl
from jax.experimental.pallas import tpu as pltpu
from jax.sharding import PartitionSpec as P

HEAD_DIM = 128
BLOCK_LEN = 64
EXP_DEV = 2
LANES = 128
F32, BF16, I32 = jnp.float32, jnp.bfloat16, jnp.int32
LONG = 1 << 35
BIG = pltpu.CompilerParams(vmem_limit_bytes=48 * 1024 * 1024)


def dot(a, b):
    return jnp.dot(a, b, preferred_element_type=F32)


def dot_t(a, b):
    return lax.dot_general(a, b, (((1,), (1,)), ((), ())), preferred_element_type=F32)


def to_col(row):
    return jnp.broadcast_to(row, (LANES, row.shape[1])).T[:, :1]


def to_row(col):
    return jnp.broadcast_to(col, (col.shape[0], LANES)).T[:1, :]


def iota(shape, dim):
    return lax.broadcasted_iota(I32, shape, dim)


def flag(mask, kind=BF16):
    return jnp.where(mask, 1.0, 0.0).astype(kind)


def cost(flops, size):
    return pl.CostEstimate(flops=flops, bytes_accessed=size, transcendentals=0)


def upper(count):
    return flag(iota((count, count), 0) <= iota((count, count), 1))


def pack_rows_kernel(
    me_ref,
    perms_ref,
    x_ref,
    qk_ref,
    val_ref,
    out_ref,
    token_ref,
    order_ref,
    earlier_ref,
    scratch,
):
    length, span = x_ref.shape[0], qk_ref.shape[1]
    rounds, total = perms_ref.shape
    peers = total // length
    per_peer = length // peers
    start = me_ref[0] * length
    order_ref[...] = perms_ref[:, pl.ds(pl.multiple_of(start, length), length)]
    start = jnp.where(start == 0, total, start) - LANES
    earlier_ref[...] = perms_ref[:, pl.ds(pl.multiple_of(start, LANES), LANES)]
    for peer in range(peers):
        scratch[peer * rounds : (peer + 1) * rounds, :] = perms_ref[
            :, peer * length : (peer + 1) * length
        ]
    perms = scratch[...]
    token = perms & (length - 1)
    mine = (perms >> (length.bit_length() - 1)) == me_ref[0]
    rank = dot(flag(mine), upper(length)).astype(I32) - 1
    slot = jnp.where(mine, rank, -1)
    groups = peers * rounds
    chosen = slot[:, None, :] == iota((groups, per_peer, length), 1)
    token_3d = jnp.where(chosen, token.astype(F32)[:, None, :], 0.0)
    column = jnp.sum(token_3d, axis=-1, keepdims=True).reshape(groups * per_peer, 1)
    by_round = column.reshape(peers, rounds, per_peer, 1)
    for turn in range(rounds):
        row = to_row(by_round[:, turn].reshape(peers * per_peer, 1)).astype(I32)
        token_ref[turn] = jnp.broadcast_to(row, token_ref.shape[1:])
    pick = flag(column.astype(I32) == iota((groups * per_peer, length), 1))
    for part, weight in enumerate((qk_ref, val_ref)):
        rows = dot(x_ref[...], weight[...]).astype(BF16)
        out_ref[:, part * span : (part + 1) * span] = dot(pick, rows).astype(BF16)


def pack_rows(me, perms, x_att, w_qk, w_val):
    length, width = x_att.shape
    rounds, total = perms.shape
    span = w_qk.shape[1]
    groups = rounds * (total // length)
    slots = rounds * length

    def whole(shape):
        return pl.BlockSpec(shape, lambda i, me_ref: (0, 0))

    return pl.pallas_call(
        pack_rows_kernel,
        grid_spec=pltpu.PrefetchScalarGridSpec(
            num_scalar_prefetch=1,
            grid=(1,),
            in_specs=[
                whole((rounds, total)),
                whole((length, width)),
                whole((width, span)),
                whole((width, span)),
            ],
            out_specs=[
                whole((slots, 2 * span)),
                pl.BlockSpec((rounds, 8, length), lambda i, me_ref: (0, 0, 0)),
                whole((rounds, length)),
                whole((rounds, LANES)),
            ],
            scratch_shapes=[pltpu.VMEM((groups, length), I32)],
        ),
        out_shape=[
            jax.ShapeDtypeStruct((slots, 2 * span), BF16),
            jax.ShapeDtypeStruct((rounds, 8, length), I32),
            jax.ShapeDtypeStruct((rounds, length), I32),
            jax.ShapeDtypeStruct((rounds, LANES), I32),
        ],
        cost_estimate=cost(4 * length * width * span + 4 * slots * length * span, 6 << 20),
        compiler_params=BIG,
        name="pack_rows",
    )(me, perms, x_att, w_qk, w_val)


def pack_tokens_kernel(peers, where_ref, ids_ref, tokens_ref, out_ref, slot_ref):
    length = tokens_ref.shape[0]
    slots = out_ref.shape[0]
    capacity = slots // peers
    experts = EXP_DEV * peers
    ids = ids_ref[...]
    hot = ids == iota((experts, length), 0)
    counts = dot(flag(hot), upper(length))
    rank = jnp.sum(jnp.where(hot, counts, 0.0), axis=0, keepdims=True).astype(I32) - 1
    core = where_ref[1]
    turn = (ids % EXP_DEV + core) % EXP_DEV
    peer = ids // EXP_DEV
    slot_ref[...] = jnp.broadcast_to(
        (peer * EXP_DEV + turn) * capacity + rank, slot_ref.shape
    )
    slot = jnp.where(turn == 0, peer * capacity + rank, -1)
    pick = flag(iota((slots, length), 0) == slot)
    out_ref[...] = dot(pick, tokens_ref[...]).astype(BF16)


def pack_tokens(where, ids, tokens, peers, capacity):
    length, part = tokens.shape
    slots = peers * capacity
    return pl.pallas_call(
        functools.partial(pack_tokens_kernel, peers),
        grid_spec=pltpu.PrefetchScalarGridSpec(
            num_scalar_prefetch=1,
            grid=(1,),
            in_specs=[
                pl.BlockSpec((1, length), lambda i, e: (0, 0)),
                pl.BlockSpec((length, part), lambda i, e: (0, 0)),
            ],
            out_specs=[
                pl.BlockSpec((slots, part), lambda i, e: (0, 0)),
                pl.BlockSpec((8, length), lambda i, e: (0, 0)),
            ],
        ),
        out_shape=[
            jax.ShapeDtypeStruct((slots, part), BF16),
            jax.ShapeDtypeStruct((8, length), I32),
        ],
        cost_estimate=cost(2 * slots * length * part, 2 << 20),
        compiler_params=BIG,
        name="pack_tokens",
    )(where, ids, tokens)


def experts_kernel(where_ref, *refs):
    step = pl.program_id(0)
    shards, far_refs, weights = refs[0:3], refs[3:5], refs[5:11]
    out_ref, total_ref = refs[11:]
    peers, capacity, part = shards[0].shape
    rows = peers * capacity
    ups = (weights[0], weights[1], weights[3], weights[4])

    def add(x, start):
        for index, weight in enumerate(ups):
            product = dot(x, weight[0])
            total_ref[index] = product if start else total_ref[index] + product

    for turn, shard in enumerate(shards):

        @pl.when(step == turn)
        def _(shard=shard, start=turn == 0):
            add(shard[...].reshape(rows, part), start)

    @pl.when(step == len(shards))
    def _():
        add(jnp.concatenate([ref[...].reshape(rows // 2, part) for ref in far_refs], axis=0), False)
        hiddens = []
        for side in range(EXP_DEV):
            gate, up_val = total_ref[2 * side], total_ref[2 * side + 1]
            hiddens.append((gate / (1.0 + jnp.exp(-gate)) * up_val).astype(BF16))
        half = part // EXP_DEV
        for index in range(out_ref.shape[0]):
            at = index * part
            piece = dot(hiddens[0], weights[2][0, :, at : at + part])
            piece = (piece + dot(hiddens[1], weights[5][0, :, at : at + part])).astype(BF16)
            for side in range(EXP_DEV):
                columns = piece[:, side * half : (side + 1) * half]
                turn = (side + where_ref[1]) % EXP_DEV
                out_ref[index, turn] = columns.reshape(peers, capacity, half)


def run_experts(where, shards, far, own, sibling):
    peers, capacity, part = shards[0].shape
    width, hidden = own[0].shape[1:]
    chips = width // part
    out = (chips, EXP_DEV, peers, capacity, part // EXP_DEV)
    rows = peers * capacity

    def rows_of(i, e):
        ahead = jnp.where(i == 0, 0, jnp.where(i == 1, chips - 1, jnp.where(i == 2, 1, 2)))
        return (e[0] + ahead) % chips

    up_block, down_block = (1, part, hidden), (1, hidden, width)
    own_up = pl.BlockSpec(up_block, lambda i, e: (e[1], rows_of(i, e), 0))
    own_down = pl.BlockSpec(down_block, lambda i, e: (e[1], 0, 0))
    return pl.pallas_call(
        experts_kernel,
        grid_spec=pltpu.PrefetchScalarGridSpec(
            num_scalar_prefetch=1,
            grid=(len(shards) + 1,),
            in_specs=[pl.BlockSpec(memory_space=pltpu.VMEM)] * 5
            + [own_up, own_up, own_down] * 2,
            out_specs=pl.BlockSpec(out, lambda i, e: (0, 0, 0, 0, 0)),
            scratch_shapes=[pltpu.VMEM((4, rows, hidden), F32)],
        ),
        out_shape=jax.ShapeDtypeStruct(out, BF16),
        cost_estimate=cost(15 * 10**9, 10 << 20),
        compiler_params=BIG,
        name="experts",
    )(where, *shards, *far, *own, *sibling)


def place_rows_kernel(rows_ref, taken_ref, out_ref, copied):
    copies = (
        pltpu.make_async_copy(rows_ref.at[0], out_ref.at[:, 0], copied.at[0]),
        pltpu.make_async_copy(taken_ref.at[1], out_ref.at[:, 1], copied.at[1]),
    )
    for copy in copies:
        copy.start()
    for copy in copies:
        copy.wait()


def place_rows(rows, taken):
    _, peers, capacity, half = taken.shape
    return pl.pallas_call(
        place_rows_kernel,
        in_specs=[pl.BlockSpec(memory_space=pltpu.HBM)] * 2,
        out_specs=pl.BlockSpec(memory_space=pltpu.HBM),
        out_shape=jax.ShapeDtypeStruct((peers, EXP_DEV, capacity, half), BF16),
        scratch_shapes=[pltpu.SemaphoreType.DMA((2,))],
        cost_estimate=cost(1 << 20, 1 << 20),
        compiler_params=BIG,
        name="place_rows",
    )(rows, taken)


def finish_kernel(back_ref, pick_ref, kept_ref, taken_ref, attended_ref, mixed_ref):
    mixed_ref[...] = dot(pick_ref[...], back_ref[...]).astype(BF16)
    attended_ref[...] = (kept_ref[...] + taken_ref[...].astype(F32)).astype(BF16)


def finish(back, pick, kept, taken):
    length, width = pick.shape[0], back.shape[1]
    return pl.pallas_call(
        finish_kernel,
        out_shape=[
            jax.ShapeDtypeStruct(kept.shape, BF16),
            jax.ShapeDtypeStruct((length, width), BF16),
        ],
        cost_estimate=cost(2 * length * back.shape[0] * width, 1 << 20),
        compiler_params=BIG,
        name="finish",
    )(back, pick, kept, taken)


def sort_rows_kernel(peers, perms_ref, arrived_ref, rows_ref, last_ref, slot_ref):
    rounds, length = perms_ref.shape
    per_peer = length // peers
    for turn in range(rounds):
        source = perms_ref[turn : turn + 1, :] >> (length.bit_length() - 1)
        hot = source == iota((peers, length), 0)
        counts = dot(flag(hot), upper(length))
        rank = jnp.sum(jnp.where(hot, counts, 0.0), axis=0, keepdims=True) - 1.0
        slot = source * per_peer + rank.astype(I32)
        slot_ref[turn] = jnp.broadcast_to(slot, slot_ref.shape[1:])
        pick = flag(to_col(slot.astype(F32)).astype(I32) == iota((length, length), 1))
        have = arrived_ref[:, turn * per_peer : (turn + 1) * per_peer, :]
        rows = dot(pick, have.reshape(length, have.shape[2])).astype(BF16)
        rows_ref[turn] = rows
        last_ref[turn] = rows[length - BLOCK_LEN :]


def sort_rows(order, arrived):
    rounds, length = order.shape
    peers, _, width = arrived.shape
    return pl.pallas_call(
        functools.partial(sort_rows_kernel, peers),
        out_shape=[
            jax.ShapeDtypeStruct((rounds, length, width), BF16),
            jax.ShapeDtypeStruct((rounds, BLOCK_LEN, width), BF16),
            jax.ShapeDtypeStruct((rounds, 8, length), I32),
        ],
        cost_estimate=cost(LONG, 4 << 20),
        compiler_params=BIG,
        name="sort_rows",
    )(order, arrived)


def window_scale(keys):
    wide = keys.astype(F32)
    squares = jnp.sum(wide * wide, axis=-1, keepdims=True)
    return to_row(lax.rsqrt(squares + 1e-06) / math.sqrt(HEAD_DIM))


def windows(row, first, last):
    moved = jnp.concatenate([row[:, BLOCK_LEN:], row[:, :BLOCK_LEN]], axis=1)
    spans = []
    for start in range(first, last, BLOCK_LEN):
        odd = start % LANES
        span = (moved if odd else row)[:, start - odd : start - odd + WINDOW]
        spans.append(jnp.broadcast_to(span, (BLOCK_LEN, WINDOW)))
    return jnp.concatenate(spans, axis=0)


def attend_blocks(queries, keys, values, scale, pos_q, pos_k):
    starts = range(0, queries.shape[0], BLOCK_LEN)
    scores = jnp.concatenate(
        [dot_t(queries[at : at + BLOCK_LEN], keys[at : at + WINDOW]) for at in starts], axis=0
    )
    scores = scores * scale
    scores = jnp.where(pos_k == pos_q, scores - 10000.0, scores)
    scores = jnp.where(pos_k <= pos_q, scores, -1e30)
    peak = jnp.max(scores, axis=-1, keepdims=True)
    exponent = jnp.exp(scores - peak)
    total = jnp.sum(exponent, axis=-1, keepdims=True)
    weights = (exponent / total).astype(BF16)
    outs = [dot(weights[at : at + BLOCK_LEN], values[at : at + WINDOW]) for at in starts]
    return jnp.concatenate(outs, axis=0).astype(BF16), peak + jnp.log(total)


TILE, WINDOW, PIECES, GROUP = BLOCK_LEN, 2 * BLOCK_LEN, 3, 8


def put_logs(totals):
    lane = iota((totals[0].shape[0], LANES), 1) % GROUP
    logs = jnp.zeros(lane.shape, F32)
    for head, total in enumerate(totals):
        rest = total
        for piece in range(PIECES):
            part = rest.astype(BF16).astype(F32)
            logs = jnp.where(lane == head * PIECES + piece, part, logs)
            rest = rest - part
    return logs.astype(BF16)


def attend_later_kernel(perms_ref, rows_ref, slot_ref, out_ref):
    rounds, length = perms_ref.shape
    span = rows_ref.shape[2] // 2
    for turn in range(rounds):
        position = perms_ref[turn : turn + 1, :].astype(F32)
        pos_q = to_col(position)[TILE:]
        pos_k = windows(position, 0, length - TILE)
        outs, totals = [], []
        for head in range(span // HEAD_DIM):
            at = head * HEAD_DIM
            keys = rows_ref[turn, :, at : at + HEAD_DIM]
            out, total = attend_blocks(
                keys[TILE:],
                keys,
                rows_ref[turn, :, span + at : span + at + HEAD_DIM],
                windows(window_scale(keys), 0, length - TILE),
                pos_q,
                pos_k,
            )
            outs.append(out)
            totals.append(total)
        whole = jnp.concatenate(outs + [put_logs(totals)], axis=1)
        back = flag(iota((length, length), 0) == slot_ref[turn, :1, :])
        whole = jnp.concatenate([jnp.zeros((TILE, whole.shape[1]), BF16), whole], axis=0)
        out_ref[turn] = dot(back, whole).astype(BF16)


def attend_first_kernel(
    peers,
    perms_ref,
    earlier_ref,
    rows_ref,
    last_ref,
    slot_ref,
    later_ref,
    out_ref,
):
    rounds, length = slot_ref.shape[0], slot_ref.shape[2]
    per_peer = length // peers
    span = rows_ref.shape[2] // 2
    lane_group = iota((peers, per_peer, LANES), 2) // GROUP
    own_group = lane_group == iota((peers, per_peer, LANES), 1)
    log_row = iota((peers, GROUP, LANES), 1)
    all_logs = jnp.zeros((peers, GROUP, LANES), F32)
    lane = iota((1, LANES), 1)
    for turn in range(rounds):
        position = perms_ref[turn : turn + 1, :LANES].astype(F32)
        earlier = earlier_ref[turn : turn + 1, :].astype(F32)
        swapped = jnp.concatenate([position[:, BLOCK_LEN:], position[:, :BLOCK_LEN]], axis=1)
        earlier = jnp.concatenate([earlier[:, BLOCK_LEN:], earlier[:, :BLOCK_LEN]], axis=1)
        pos_k = jnp.where(lane < BLOCK_LEN, earlier, swapped)
        pos_q = to_col(position)[:TILE]
        totals, outs = [], []
        for head in range(span // HEAD_DIM):
            at = head * HEAD_DIM
            own = rows_ref[turn, :TILE, at : at + HEAD_DIM]
            keys = jnp.concatenate([last_ref[turn, :, at : at + HEAD_DIM], own], axis=0)
            at = span + at
            values = jnp.concatenate(
                [
                    last_ref[turn, :, at : at + HEAD_DIM],
                    rows_ref[turn, :TILE, at : at + HEAD_DIM],
                ],
                axis=0,
            )
            out, total = attend_blocks(own, keys, values, window_scale(keys), pos_q, pos_k)
            outs.append(out)
            totals.append(total)
        top = jnp.concatenate(outs + [put_logs(totals)], axis=1)
        top = jnp.concatenate([top, jnp.zeros((LANES - TILE, top.shape[1]), BF16)], axis=0)
        back = flag(iota((length, LANES), 0) == slot_ref[turn, :1, :LANES])
        moved = dot(back, top) + later_ref[turn].astype(F32)
        for head in range(span // HEAD_DIM):
            at = (head * rounds + turn) * per_peer
            lanes = moved[:, head * HEAD_DIM : (head + 1) * HEAD_DIM]
            out_ref[:, at : at + per_peer, :] = lanes.astype(BF16).reshape(
                peers, per_peer, HEAD_DIM
            )
        logs = moved[:, span:].reshape(peers, per_peer, LANES)
        logs = jnp.sum(jnp.where(own_group, logs, 0.0), axis=1, keepdims=True)
        all_logs = jnp.where(log_row == turn, logs, all_logs)
    out_ref[:, out_ref.shape[1] - GROUP :, :] = all_logs.astype(BF16)


def attend_later(order, rows, slot):
    rounds, length, width = rows.shape
    return pl.pallas_call(
        attend_later_kernel,
        out_shape=jax.ShapeDtypeStruct((rounds, length, width // 2 + LANES), BF16),
        cost_estimate=cost(LONG, 4 << 20),
        compiler_params=BIG,
        name="attend_later",
    )(order, rows, slot)


def attend_first(order, earlier, rows, last, slot, later, peers):
    rounds, length, width = rows.shape
    out = (peers, width // 2 // HEAD_DIM * rounds * (length // peers) + GROUP, HEAD_DIM)

    def fixed(x):
        return pl.BlockSpec(x.shape, lambda i: (0,) * x.ndim)

    return pl.pallas_call(
        functools.partial(attend_first_kernel, peers),
        grid=(1,),
        in_specs=[
            fixed(order),
            fixed(earlier),
            pl.BlockSpec((rounds, LANES, width), lambda i: (0, 0, 0)),
            fixed(last),
            fixed(slot),
            fixed(later),
        ],
        out_specs=pl.BlockSpec(out, lambda i: (0, 0, 0)),
        out_shape=jax.ShapeDtypeStruct(out, BF16),
        cost_estimate=cost(LONG, 4 << 20),
        compiler_params=BIG,
        name="attend_first",
    )(order, earlier, rows, last, slot, later)


def combine_kernel(got_ref, token_ref, mixed_ref):
    peers = got_ref.shape[0]
    rounds, _, length = token_ref.shape
    per_peer = length // peers
    heads = mixed_ref.shape[1] // HEAD_DIM
    lane_group = iota((peers, per_peer, LANES), 2) // GROUP
    own_group = lane_group == iota((peers, per_peer, LANES), 1)
    lane = iota((length, LANES), 1) % GROUP // PIECES
    column = iota((length, length), 0)
    log_row = iota((peers, GROUP, LANES), 1)
    all_logs = got_ref[:, got_ref.shape[1] - GROUP :, :].astype(F32)
    outs, lses = [], []
    for turn in range(rounds):
        pick = flag(token_ref[turn, :1, :] == column)
        logs = jnp.sum(jnp.where(log_row == turn, all_logs, 0.0), axis=1, keepdims=True)
        logs = jnp.where(own_group, logs, 0.0).astype(BF16)
        sides = []
        for head in range(heads):
            at = (head * rounds + turn) * per_peer
            sides.append(got_ref[:, at : at + per_peer, :].reshape(length, HEAD_DIM))
        outs.append(dot(pick, jnp.concatenate(sides, axis=1)))
        moved = dot(pick, logs.reshape(length, LANES))
        lses.append(
            [
                jnp.sum(jnp.where(lane == head, moved, 0.0), axis=1, keepdims=True)
                for head in range(heads)
            ]
        )
    for head in range(heads):
        logs = [lse[head] for lse in lses]
        peak = functools.reduce(jnp.maximum, logs)
        whole = peak + jnp.log(functools.reduce(jnp.add, [jnp.exp(lse - peak) for lse in logs]))
        at = head * HEAD_DIM
        mixed = jnp.zeros((length, HEAD_DIM), F32)
        for out, lse in zip(outs, logs):
            mixed = mixed + out[:, at : at + HEAD_DIM] * jnp.exp(lse - whole)
        mixed_ref[:, at : at + HEAD_DIM] = mixed.astype(BF16)


def combine(got, token, span):
    rounds, _, length = token.shape
    return pl.pallas_call(
        combine_kernel,
        out_shape=jax.ShapeDtypeStruct((length, span), BF16),
        cost_estimate=cost(2 * rounds * length * length * (span + LANES), 1 << 20),
        compiler_params=BIG,
        name="combine",
    )(got, token)


def project_kernel(where_ref, own_ref, prev_ref, next_ref, far_a_ref, far_b_ref, *refs):
    slot_ref, weights, (kept_ref, given_ref, pick_ref) = refs[0], refs[1:-3], refs[-3:]
    column = to_col(slot_ref[:1, :].astype(F32)).astype(I32)
    pick_ref[...] = flag(column == iota(pick_ref.shape, 1))
    far = jnp.concatenate([far_a_ref[...], far_b_ref[...]], axis=0)
    total = dot(own_ref[...], weights[0][...]) + dot(prev_ref[...], weights[1][...])
    total = total + dot(next_ref[...], weights[2][...]) + dot(far, weights[3][...])
    half = kept_ref.shape[1]
    for core in range(EXP_DEV):

        @pl.when(where_ref[1] == core)
        def _(core=core):
            kept_ref[...] = total[:, core * half : (core + 1) * half]
            other = 1 - core
            given_ref[...] = total[:, other * half : (other + 1) * half].astype(BF16)


def project(where, heads, w_out, others, slot, slots):
    length, span = heads[0].shape
    columns = others[0].shape[1]
    half = columns // EXP_DEV
    weights = (w_out, *others)
    shapes = [x.shape for x in (*heads, slot)] + [(span, columns)] + [x.shape for x in others]

    def first(i, e):
        return (0, 0)

    specs = [pl.BlockSpec(shape, first) for shape in shapes]
    specs[len(heads) + 1] = pl.BlockSpec((span, columns), lambda i, e: (0, e[0]))
    return pl.pallas_call(
        project_kernel,
        grid_spec=pltpu.PrefetchScalarGridSpec(
            num_scalar_prefetch=1,
            grid=(1,),
            in_specs=specs,
            out_specs=[pl.BlockSpec((length, half), first)] * 2
            + [pl.BlockSpec((slot.shape[1], slots), first)],
        ),
        out_shape=[
            jax.ShapeDtypeStruct((length, half), F32),
            jax.ShapeDtypeStruct((length, half), BF16),
            jax.ShapeDtypeStruct((slot.shape[1], slots), BF16),
        ],
        cost_estimate=cost(55 * 10**8, 3 << 20),
        compiler_params=BIG,
        name="project",
    )(where, *heads, slot, *weights)


def exchange(x, axis):
    return lax.all_to_all(x, axis, split_axis=0, concat_axis=0, tiled=True)


def hop(x, by, chips):
    pairs = []
    for chip in range(chips):
        for core in range(EXP_DEV):
            there = (chip + by) % chips
            pairs.append((chip * EXP_DEV + core, there * EXP_DEV + core))
    return lax.ppermute(x, "exp", pairs)


def spread(x, chips, ready=()):
    half = x.shape[0] // 2
    before, behind = hop(x, 1, chips), hop(x, -1, chips)
    before, behind = (after(side, *ready) if ready else side for side in (before, behind))
    far = (hop(before[:half], 1, chips), hop(behind[half:], -1, chips))
    return (x, before, behind), far


def after(x, *done):
    return lax.optimization_barrier((x, *done))[0]


def body(x_att, w_qk, w_val, w_out, perms, tokens_b, expert_ids, w_gate, w_up, w_down):
    peers, parts = lax.axis_size("seq"), lax.axis_size("exp")
    chips = parts // EXP_DEV
    me = lax.axis_index("seq").astype(I32).reshape(1)
    my_exp = lax.axis_index("exp").astype(I32)
    core = my_exp % EXP_DEV
    where = jnp.stack([my_exp // EXP_DEV, core])
    length, width = x_att.shape
    rounds = perms.shape[0]
    per_peer = length // peers
    tokb = tokens_b.shape[0]
    capacity = tokb // peers
    part = width // chips
    lines = [[chip * EXP_DEV + side for chip in range(chips)] for side in range(EXP_DEV)]
    siblings = [(i, i ^ 1) for i in range(parts)]

    token_part = lax.dynamic_slice_in_dim(tokens_b, where[0] * part, part, 1)
    dispatch, token_slot = pack_tokens(
        where, expert_ids.reshape(1, tokb), token_part, peers, capacity
    )
    received = exchange(dispatch.reshape(peers, capacity, part), "seq")
    outgoing, slot_token, order, earlier = pack_rows(me, perms, x_att, w_qk, w_val)
    def columns_of(by, *ready):
        start = (where[0] + by) % chips * part
        return hop(lax.dynamic_slice_in_dim(after(w_out, *ready), start, part, 1), by, chips)

    near = [columns_of(by, dispatch) for by in (1, chips - 1)]
    received = after(received, outgoing, *near)
    outgoing = after(outgoing, received)
    own = (w_gate, w_up, w_down)
    sibling = [lax.ppermute(after(weight, received), "exp", siblings) for weight in own]
    shards, far_shards = spread(received, chips)
    arrived = exchange(outgoing.reshape(peers, rounds * per_peer, outgoing.shape[1]), "seq")
    expert_part = run_experts(where, shards, far_shards, own, sibling)
    arrived = after(arrived, expert_part)
    rows, last, row_slot = sort_rows(order, arrived)
    expert_rows = lax.psum_scatter(
        expert_part,
        "exp",
        scatter_dimension=0,
        tiled=False,
        axis_index_groups=lines,
    )
    last = lax.ppermute(last, "seq", [(i, (i + 1) % peers) for i in range(peers)])
    later = attend_later(order, rows, row_slot)
    last = after(last, later)
    packed = attend_first(order, earlier, rows, last, row_slot, later, peers)
    got = exchange(packed, "seq")
    far = columns_of(2, packed)
    expert_rows = after(expert_rows, packed, far)
    taken = lax.ppermute(expert_rows, "exp", siblings)
    expert_rows = place_rows(expert_rows, taken)
    mixed_heads = combine(after(got, expert_rows), slot_token, w_qk.shape[1])
    expert_back = exchange(after(expert_rows, mixed_heads), "seq")
    heads, far_heads = spread(mixed_heads, chips)
    slots = peers * EXP_DEV * capacity
    attn_kept, attn_given, token_pick = project(
        where, (*heads, *far_heads), w_out, (*near, far), token_slot, slots
    )
    attn_taken = lax.ppermute(attn_given, "exp", siblings)
    expert_back = after(expert_back, attn_taken)
    return finish(
        expert_back.reshape(slots, width // parts),
        token_pick,
        attn_kept,
        attn_taken,
    )


def solution(mesh):
    in_specs = (
        P("seq", None),
        P(None, "exp"),
        P(None, "exp"),
        P("exp", None),
        P(),
        P("seq", None),
        P("seq", None),
        P("seq", None, "exp"),
        P("seq", None, "exp"),
        P("seq", "exp", None),
    )
    out_specs = (P("seq", "exp"), P("seq", "exp"))
    return jax.shard_map(body, mesh=mesh, in_specs=in_specs, out_specs=out_specs, check_vma=False)
```

```python
import functools
import math

import jax
import jax.numpy as jnp
from jax import lax
from jax.experimental import pallas as pl
from jax.experimental.pallas import tpu as pltpu
from jax.sharding import PartitionSpec as P

HEAD_DIM = 128
BLOCK_LEN = 64
EXP_DEV = 2
LANES = 128
F32, BF16, I32 = jnp.float32, jnp.bfloat16, jnp.int32
LONG = 1 << 35
BIG = pltpu.CompilerParams(vmem_limit_bytes=48 * 1024 * 1024)


def dot(a, b):
    return jnp.dot(a, b, preferred_element_type=F32)


def dot_t(a, b):
    return lax.dot_general(a, b, (((1,), (1,)), ((), ())), preferred_element_type=F32)


def to_col(row):
    return jnp.broadcast_to(row, (LANES, row.shape[1])).T[:, :1]


def to_row(col):
    return jnp.broadcast_to(col, (col.shape[0], LANES)).T[:1, :]


def iota(shape, dim):
    return lax.broadcasted_iota(I32, shape, dim)


def flag(mask, kind=BF16):
    return jnp.where(mask, 1.0, 0.0).astype(kind)


def cost(flops, size):
    return pl.CostEstimate(flops=flops, bytes_accessed=size, transcendentals=0)


def upper(count):
    return flag(iota((count, count), 0) <= iota((count, count), 1))


def pack_rows_kernel(
    me_ref,
    perms_ref,
    x_ref,
    qk_ref,
    val_ref,
    out_ref,
    token_ref,
    order_ref,
    earlier_ref,
    scratch,
):
    length, span = x_ref.shape[0], qk_ref.shape[1]
    rounds, total = perms_ref.shape
    peers = total // length
    per_peer = length // peers
    start = me_ref[0] * length
    order_ref[...] = perms_ref[:, pl.ds(pl.multiple_of(start, length), length)]
    start = jnp.where(start == 0, total, start) - LANES
    earlier_ref[...] = perms_ref[:, pl.ds(pl.multiple_of(start, LANES), LANES)]
    for peer in range(peers):
        scratch[peer * rounds : (peer + 1) * rounds, :] = perms_ref[
            :, peer * length : (peer + 1) * length
        ]
    perms = scratch[...]
    token = perms & (length - 1)
    mine = (perms >> (length.bit_length() - 1)) == me_ref[0]
    rank = dot(flag(mine), upper(length)).astype(I32) - 1
    slot = jnp.where(mine, rank, -1)
    groups = peers * rounds
    chosen = slot[:, None, :] == iota((groups, per_peer, length), 1)
    token_3d = jnp.where(chosen, token.astype(F32)[:, None, :], 0.0)
    column = jnp.sum(token_3d, axis=-1, keepdims=True).reshape(groups * per_peer, 1)
    by_round = column.reshape(peers, rounds, per_peer, 1)
    for turn in range(rounds):
        row = to_row(by_round[:, turn].reshape(peers * per_peer, 1)).astype(I32)
        token_ref[turn] = jnp.broadcast_to(row, token_ref.shape[1:])
    pick = flag(column.astype(I32) == iota((groups * per_peer, length), 1))
    for part, weight in enumerate((qk_ref, val_ref)):
        rows = dot(x_ref[...], weight[...]).astype(BF16)
        out_ref[:, part * span : (part + 1) * span] = dot(pick, rows).astype(BF16)


def pack_rows(me, perms, x_att, w_qk, w_val):
    length, width = x_att.shape
    rounds, total = perms.shape
    span = w_qk.shape[1]
    groups = rounds * (total // length)
    slots = rounds * length

    def whole(shape):
        return pl.BlockSpec(shape, lambda i, me_ref: (0, 0))

    return pl.pallas_call(
        pack_rows_kernel,
        grid_spec=pltpu.PrefetchScalarGridSpec(
            num_scalar_prefetch=1,
            grid=(1,),
            in_specs=[
                whole((rounds, total)),
                whole((length, width)),
                whole((width, span)),
                whole((width, span)),
            ],
            out_specs=[
                whole((slots, 2 * span)),
                pl.BlockSpec((rounds, 8, length), lambda i, me_ref: (0, 0, 0)),
                whole((rounds, length)),
                whole((rounds, LANES)),
            ],
            scratch_shapes=[pltpu.VMEM((groups, length), I32)],
        ),
        out_shape=[
            jax.ShapeDtypeStruct((slots, 2 * span), BF16),
            jax.ShapeDtypeStruct((rounds, 8, length), I32),
            jax.ShapeDtypeStruct((rounds, length), I32),
            jax.ShapeDtypeStruct((rounds, LANES), I32),
        ],
        cost_estimate=cost(4 * length * width * span + 4 * slots * length * span, 6 << 20),
        compiler_params=BIG,
        name="pack_rows",
    )(me, perms, x_att, w_qk, w_val)


def pack_tokens_kernel(peers, where_ref, ids_ref, tokens_ref, out_ref, slot_ref):
    length = tokens_ref.shape[0]
    slots = out_ref.shape[0]
    capacity = slots // peers
    experts = EXP_DEV * peers
    ids = ids_ref[...]
    hot = ids == iota((experts, length), 0)
    counts = dot(flag(hot), upper(length))
    rank = jnp.sum(jnp.where(hot, counts, 0.0), axis=0, keepdims=True).astype(I32) - 1
    core = where_ref[1]
    turn = (ids % EXP_DEV + core) % EXP_DEV
    peer = ids // EXP_DEV
    slot_ref[...] = jnp.broadcast_to(
        (peer * EXP_DEV + turn) * capacity + rank, slot_ref.shape
    )
    slot = jnp.where(turn == 0, peer * capacity + rank, -1)
    pick = flag(iota((slots, length), 0) == slot)
    out_ref[...] = dot(pick, tokens_ref[...]).astype(BF16)


def pack_tokens(where, ids, tokens, peers, capacity):
    length, part = tokens.shape
    slots = peers * capacity
    return pl.pallas_call(
        functools.partial(pack_tokens_kernel, peers),
        grid_spec=pltpu.PrefetchScalarGridSpec(
            num_scalar_prefetch=1,
            grid=(1,),
            in_specs=[
                pl.BlockSpec((1, length), lambda i, e: (0, 0)),
                pl.BlockSpec((length, part), lambda i, e: (0, 0)),
            ],
            out_specs=[
                pl.BlockSpec((slots, part), lambda i, e: (0, 0)),
                pl.BlockSpec((8, length), lambda i, e: (0, 0)),
            ],
        ),
        out_shape=[
            jax.ShapeDtypeStruct((slots, part), BF16),
            jax.ShapeDtypeStruct((8, length), I32),
        ],
        cost_estimate=cost(2 * slots * length * part, 2 << 20),
        compiler_params=BIG,
        name="pack_tokens",
    )(where, ids, tokens)


def experts_kernel(where_ref, *refs):
    step = pl.program_id(0)
    shards, far_refs, weights = refs[0:3], refs[3:5], refs[5:11]
    out_ref, total_ref = refs[11:]
    peers, capacity, part = shards[0].shape
    rows = peers * capacity
    ups = (weights[0], weights[1], weights[3], weights[4])

    def add(x, start):
        for index, weight in enumerate(ups):
            product = dot(x, weight[0])
            total_ref[index] = product if start else total_ref[index] + product

    for turn, shard in enumerate(shards):

        @pl.when(step == turn)
        def _(shard=shard, start=turn == 0):
            add(shard[...].reshape(rows, part), start)

    @pl.when(step == len(shards))
    def _():
        add(jnp.concatenate([ref[...].reshape(rows // 2, part) for ref in far_refs], axis=0), False)
        hiddens = []
        for side in range(EXP_DEV):
            gate, up_val = total_ref[2 * side], total_ref[2 * side + 1]
            hiddens.append((gate / (1.0 + jnp.exp(-gate)) * up_val).astype(BF16))
        half = part // EXP_DEV
        for index in range(out_ref.shape[0]):
            at = index * part
            piece = dot(hiddens[0], weights[2][0, :, at : at + part])
            piece = (piece + dot(hiddens[1], weights[5][0, :, at : at + part])).astype(BF16)
            for side in range(EXP_DEV):
                columns = piece[:, side * half : (side + 1) * half]
                turn = (side + where_ref[1]) % EXP_DEV
                out_ref[index, turn] = columns.reshape(peers, capacity, half)


def run_experts(where, shards, far, own, sibling):
    peers, capacity, part = shards[0].shape
    width, hidden = own[0].shape[1:]
    chips = width // part
    out = (chips, EXP_DEV, peers, capacity, part // EXP_DEV)
    rows = peers * capacity

    def rows_of(i, e):
        ahead = jnp.where(i == 0, 0, jnp.where(i == 1, chips - 1, jnp.where(i == 2, 1, 2)))
        return (e[0] + ahead) % chips

    up_block, down_block = (1, part, hidden), (1, hidden, width)
    own_up = pl.BlockSpec(up_block, lambda i, e: (e[1], rows_of(i, e), 0))
    own_down = pl.BlockSpec(down_block, lambda i, e: (e[1], 0, 0))
    return pl.pallas_call(
        experts_kernel,
        grid_spec=pltpu.PrefetchScalarGridSpec(
            num_scalar_prefetch=1,
            grid=(len(shards) + 1,),
            in_specs=[pl.BlockSpec(x.shape, lambda i, e: (0, 0, 0)) for x in (*shards, *far)]
            + [own_up, own_up, own_down] * 2,
            out_specs=pl.BlockSpec(out, lambda i, e: (0, 0, 0, 0, 0)),
            scratch_shapes=[pltpu.VMEM((4, rows, hidden), F32)],
        ),
        out_shape=jax.ShapeDtypeStruct(out, BF16),
        cost_estimate=cost(15 * 10**9, 10 << 20),
        compiler_params=BIG,
        name="experts",
    )(where, *shards, *far, *own, *sibling)


def place_rows_kernel(rows_ref, taken_ref, out_ref, copied):
    copies = (
        pltpu.make_async_copy(rows_ref.at[0], out_ref.at[:, 0], copied.at[0]),
        pltpu.make_async_copy(taken_ref.at[1], out_ref.at[:, 1], copied.at[1]),
    )
    for copy in copies:
        copy.start()
    for copy in copies:
        copy.wait()


def place_rows(rows, taken):
    _, peers, capacity, half = taken.shape
    return pl.pallas_call(
        place_rows_kernel,
        in_specs=[pl.BlockSpec(memory_space=pltpu.HBM)] * 2,
        out_specs=pl.BlockSpec(memory_space=pltpu.HBM),
        out_shape=jax.ShapeDtypeStruct((peers, EXP_DEV, capacity, half), BF16),
        scratch_shapes=[pltpu.SemaphoreType.DMA((2,))],
        cost_estimate=cost(1 << 20, 1 << 20),
        compiler_params=BIG,
        name="place_rows",
    )(rows, taken)


def finish_kernel(back_ref, slot_ref, kept_ref, taken_ref, attended_ref, mixed_ref):
    length = mixed_ref.shape[0]
    column = to_col(slot_ref[:1, :].astype(F32)).astype(I32)
    pick = flag(column == iota((length, back_ref.shape[0]), 1))
    mixed_ref[...] = dot(pick, back_ref[...]).astype(BF16)
    attended_ref[...] = (kept_ref[...] + taken_ref[...].astype(F32)).astype(BF16)


def finish(back, slot, kept, taken):
    length, width = slot.shape[1], back.shape[1]
    return pl.pallas_call(
        finish_kernel,
        out_shape=[
            jax.ShapeDtypeStruct(kept.shape, BF16),
            jax.ShapeDtypeStruct((length, width), BF16),
        ],
        cost_estimate=cost(2 * length * back.shape[0] * width, 1 << 20),
        compiler_params=BIG,
        name="finish",
    )(back, slot, kept, taken)


def sort_rows_kernel(peers, perms_ref, arrived_ref, rows_ref, last_ref, slot_ref):
    rounds, length = perms_ref.shape
    per_peer = length // peers
    for turn in range(rounds):
        source = perms_ref[turn : turn + 1, :] >> (length.bit_length() - 1)
        hot = source == iota((peers, length), 0)
        counts = dot(flag(hot), upper(length))
        rank = jnp.sum(jnp.where(hot, counts, 0.0), axis=0, keepdims=True) - 1.0
        slot = source * per_peer + rank.astype(I32)
        slot_ref[turn] = jnp.broadcast_to(slot, slot_ref.shape[1:])
        pick = flag(to_col(slot.astype(F32)).astype(I32) == iota((length, length), 1))
        have = arrived_ref[:, turn * per_peer : (turn + 1) * per_peer, :]
        rows = dot(pick, have.reshape(length, have.shape[2])).astype(BF16)
        rows_ref[turn] = rows
        last_ref[turn] = rows[length - BLOCK_LEN :]


def sort_rows(order, arrived):
    rounds, length = order.shape
    peers, _, width = arrived.shape
    return pl.pallas_call(
        functools.partial(sort_rows_kernel, peers),
        out_shape=[
            jax.ShapeDtypeStruct((rounds, length, width), BF16),
            jax.ShapeDtypeStruct((rounds, BLOCK_LEN, width), BF16),
            jax.ShapeDtypeStruct((rounds, 8, length), I32),
        ],
        cost_estimate=cost(LONG, 4 << 20),
        compiler_params=BIG,
        name="sort_rows",
    )(order, arrived)


def window_scale(keys):
    wide = keys.astype(F32)
    squares = jnp.sum(wide * wide, axis=-1, keepdims=True)
    return to_row(lax.rsqrt(squares + 1e-06) / math.sqrt(HEAD_DIM))


def windows(row, first, last):
    moved = jnp.concatenate([row[:, BLOCK_LEN:], row[:, :BLOCK_LEN]], axis=1)
    spans = []
    for start in range(first, last, BLOCK_LEN):
        odd = start % LANES
        span = (moved if odd else row)[:, start - odd : start - odd + WINDOW]
        spans.append(jnp.broadcast_to(span, (BLOCK_LEN, WINDOW)))
    return jnp.concatenate(spans, axis=0)


def attend_blocks(queries, keys, values, scale, pos_q, pos_k):
    starts = range(0, queries.shape[0], BLOCK_LEN)
    scores = jnp.concatenate(
        [dot_t(queries[at : at + BLOCK_LEN], keys[at : at + WINDOW]) for at in starts], axis=0
    )
    scores = scores * scale
    scores = jnp.where(pos_k == pos_q, scores - 10000.0, scores)
    scores = jnp.where(pos_k <= pos_q, scores, -1e30)
    peak = jnp.max(scores, axis=-1, keepdims=True)
    exponent = jnp.exp(scores - peak)
    total = jnp.sum(exponent, axis=-1, keepdims=True)
    weights = (exponent / total).astype(BF16)
    outs = [dot(weights[at : at + BLOCK_LEN], values[at : at + WINDOW]) for at in starts]
    return jnp.concatenate(outs, axis=0).astype(BF16), peak + jnp.log(total)


TILE, WINDOW, PIECES, GROUP = BLOCK_LEN, 2 * BLOCK_LEN, 3, 8


def put_logs(totals):
    lane = iota((totals[0].shape[0], LANES), 1) % GROUP
    logs = jnp.zeros(lane.shape, F32)
    for head, total in enumerate(totals):
        rest = total
        for piece in range(PIECES):
            part = rest.astype(BF16).astype(F32)
            logs = jnp.where(lane == head * PIECES + piece, part, logs)
            rest = rest - part
    return logs.astype(BF16)


def attend_later_kernel(perms_ref, rows_ref, slot_ref, out_ref):
    rounds, length = perms_ref.shape
    span = rows_ref.shape[2] // 2
    for turn in range(rounds):
        position = perms_ref[turn : turn + 1, :].astype(F32)
        pos_q = to_col(position)[TILE:]
        pos_k = windows(position, 0, length - TILE)
        outs, totals = [], []
        for head in range(span // HEAD_DIM):
            at = head * HEAD_DIM
            keys = rows_ref[turn, :, at : at + HEAD_DIM]
            out, total = attend_blocks(
                keys[TILE:],
                keys,
                rows_ref[turn, :, span + at : span + at + HEAD_DIM],
                windows(window_scale(keys), 0, length - TILE),
                pos_q,
                pos_k,
            )
            outs.append(out)
            totals.append(total)
        whole = jnp.concatenate(outs + [put_logs(totals)], axis=1)
        back = flag(iota((length, length), 0) == slot_ref[turn, :1, :])
        whole = jnp.concatenate([jnp.zeros((TILE, whole.shape[1]), BF16), whole], axis=0)
        out_ref[turn] = dot(back, whole).astype(BF16)


def attend_first_kernel(
    peers,
    perms_ref,
    earlier_ref,
    rows_ref,
    last_ref,
    slot_ref,
    later_ref,
    out_ref,
):
    rounds, length = slot_ref.shape[0], slot_ref.shape[2]
    per_peer = length // peers
    span = rows_ref.shape[2] // 2
    lane_group = iota((peers, per_peer, LANES), 2) // GROUP
    own_group = lane_group == iota((peers, per_peer, LANES), 1)
    log_row = iota((peers, GROUP, LANES), 1)
    all_logs = jnp.zeros((peers, GROUP, LANES), F32)
    lane = iota((1, LANES), 1)
    for turn in range(rounds):
        position = perms_ref[turn : turn + 1, :LANES].astype(F32)
        earlier = earlier_ref[turn : turn + 1, :].astype(F32)
        swapped = jnp.concatenate([position[:, BLOCK_LEN:], position[:, :BLOCK_LEN]], axis=1)
        earlier = jnp.concatenate([earlier[:, BLOCK_LEN:], earlier[:, :BLOCK_LEN]], axis=1)
        pos_k = jnp.where(lane < BLOCK_LEN, earlier, swapped)
        pos_q = to_col(position)[:TILE]
        totals, outs = [], []
        for head in range(span // HEAD_DIM):
            at = head * HEAD_DIM
            own = rows_ref[turn, :TILE, at : at + HEAD_DIM]
            keys = jnp.concatenate([last_ref[turn, :, at : at + HEAD_DIM], own], axis=0)
            at = span + at
            values = jnp.concatenate(
                [
                    last_ref[turn, :, at : at + HEAD_DIM],
                    rows_ref[turn, :TILE, at : at + HEAD_DIM],
                ],
                axis=0,
            )
            out, total = attend_blocks(own, keys, values, window_scale(keys), pos_q, pos_k)
            outs.append(out)
            totals.append(total)
        top = jnp.concatenate(outs + [put_logs(totals)], axis=1)
        top = jnp.concatenate([top, jnp.zeros((LANES - TILE, top.shape[1]), BF16)], axis=0)
        back = flag(iota((length, LANES), 0) == slot_ref[turn, :1, :LANES])
        moved = dot(back, top) + later_ref[turn].astype(F32)
        for head in range(span // HEAD_DIM):
            at = (head * rounds + turn) * per_peer
            lanes = moved[:, head * HEAD_DIM : (head + 1) * HEAD_DIM]
            out_ref[:, at : at + per_peer, :] = lanes.astype(BF16).reshape(
                peers, per_peer, HEAD_DIM
            )
        logs = moved[:, span:].reshape(peers, per_peer, LANES)
        logs = jnp.sum(jnp.where(own_group, logs, 0.0), axis=1, keepdims=True)
        all_logs = jnp.where(log_row == turn, logs, all_logs)
    out_ref[:, out_ref.shape[1] - GROUP :, :] = all_logs.astype(BF16)


def attend_later(order, rows, slot):
    rounds, length, width = rows.shape
    return pl.pallas_call(
        attend_later_kernel,
        out_shape=jax.ShapeDtypeStruct((rounds, length, width // 2 + LANES), BF16),
        cost_estimate=cost(LONG, 4 << 20),
        compiler_params=BIG,
        name="attend_later",
    )(order, rows, slot)


def attend_first(order, earlier, rows, last, slot, later, peers):
    rounds, length, width = rows.shape
    out = (peers, width // 2 // HEAD_DIM * rounds * (length // peers) + GROUP, HEAD_DIM)

    def fixed(x):
        return pl.BlockSpec(x.shape, lambda i: (0,) * x.ndim)

    return pl.pallas_call(
        functools.partial(attend_first_kernel, peers),
        grid=(1,),
        in_specs=[
            fixed(order),
            fixed(earlier),
            pl.BlockSpec((rounds, LANES, width), lambda i: (0, 0, 0)),
            fixed(last),
            fixed(slot),
            fixed(later),
        ],
        out_specs=pl.BlockSpec(out, lambda i: (0, 0, 0)),
        out_shape=jax.ShapeDtypeStruct(out, BF16),
        cost_estimate=cost(LONG, 4 << 20),
        compiler_params=BIG,
        name="attend_first",
    )(order, earlier, rows, last, slot, later)


def combine_kernel(got_ref, token_ref, mixed_ref):
    peers = got_ref.shape[0]
    rounds, _, length = token_ref.shape
    per_peer = length // peers
    heads = mixed_ref.shape[1] // HEAD_DIM
    lane_group = iota((peers, per_peer, LANES), 2) // GROUP
    own_group = lane_group == iota((peers, per_peer, LANES), 1)
    lane = iota((length, LANES), 1) % GROUP // PIECES
    column = iota((length, length), 0)
    log_row = iota((peers, GROUP, LANES), 1)
    all_logs = got_ref[:, got_ref.shape[1] - GROUP :, :].astype(F32)
    outs, lses = [], []
    for turn in range(rounds):
        pick = flag(token_ref[turn, :1, :] == column)
        logs = jnp.sum(jnp.where(log_row == turn, all_logs, 0.0), axis=1, keepdims=True)
        logs = jnp.where(own_group, logs, 0.0).astype(BF16)
        sides = []
        for head in range(heads):
            at = (head * rounds + turn) * per_peer
            sides.append(got_ref[:, at : at + per_peer, :].reshape(length, HEAD_DIM))
        outs.append(dot(pick, jnp.concatenate(sides, axis=1)))
        moved = dot(pick, logs.reshape(length, LANES))
        lses.append(
            [
                jnp.sum(jnp.where(lane == head, moved, 0.0), axis=1, keepdims=True)
                for head in range(heads)
            ]
        )
    for head in range(heads):
        logs = [lse[head] for lse in lses]
        peak = functools.reduce(jnp.maximum, logs)
        whole = peak + jnp.log(functools.reduce(jnp.add, [jnp.exp(lse - peak) for lse in logs]))
        at = head * HEAD_DIM
        mixed = jnp.zeros((length, HEAD_DIM), F32)
        for out, lse in zip(outs, logs):
            mixed = mixed + out[:, at : at + HEAD_DIM] * jnp.exp(lse - whole)
        mixed_ref[:, at : at + HEAD_DIM] = mixed.astype(BF16)


def combine(got, token, span):
    rounds, _, length = token.shape
    return pl.pallas_call(
        combine_kernel,
        out_shape=jax.ShapeDtypeStruct((length, span), BF16),
        cost_estimate=cost(2 * rounds * length * length * (span + LANES), 1 << 20),
        compiler_params=BIG,
        name="combine",
    )(got, token)


def project_kernel(where_ref, own_ref, prev_ref, next_ref, far_a_ref, far_b_ref, *refs):
    weights, (kept_ref, given_ref) = refs[:-2], refs[-2:]
    far = jnp.concatenate([far_a_ref[...], far_b_ref[...]], axis=0)
    total = dot(own_ref[...], weights[0][...]) + dot(prev_ref[...], weights[1][...])
    total = total + dot(next_ref[...], weights[2][...]) + dot(far, weights[3][...])
    half = kept_ref.shape[1]
    for core in range(EXP_DEV):

        @pl.when(where_ref[1] == core)
        def _(core=core):
            kept_ref[...] = total[:, core * half : (core + 1) * half]
            other = 1 - core
            given_ref[...] = total[:, other * half : (other + 1) * half].astype(BF16)


def project(where, heads, w_out, others):
    length, span = heads[0].shape
    columns = others[0].shape[1]
    half = columns // EXP_DEV
    weights = (w_out, *others)
    shapes = [x.shape for x in heads] + [(span, columns)] + [x.shape for x in others]

    def first(i, e):
        return (0, 0)

    specs = [pl.BlockSpec(shape, first) for shape in shapes]
    specs[len(heads)] = pl.BlockSpec((span, columns), lambda i, e: (0, e[0]))
    return pl.pallas_call(
        project_kernel,
        grid_spec=pltpu.PrefetchScalarGridSpec(
            num_scalar_prefetch=1,
            grid=(1,),
            in_specs=specs,
            out_specs=[pl.BlockSpec((length, half), first)] * 2,
        ),
        out_shape=[
            jax.ShapeDtypeStruct((length, half), F32),
            jax.ShapeDtypeStruct((length, half), BF16),
        ],
        cost_estimate=cost(55 * 10**8, 3 << 20),
        compiler_params=BIG,
        name="project",
    )(where, *heads, *weights)


def exchange(x, axis):
    return lax.all_to_all(x, axis, split_axis=0, concat_axis=0, tiled=True)


def hop(x, by, chips):
    pairs = []
    for chip in range(chips):
        for core in range(EXP_DEV):
            there = (chip + by) % chips
            pairs.append((chip * EXP_DEV + core, there * EXP_DEV + core))
    return lax.ppermute(x, "exp", pairs)


def spread(x, chips, ready=()):
    half = x.shape[0] // 2
    before, behind = hop(x, 1, chips), hop(x, -1, chips)
    before, behind = (after(side, *ready) if ready else side for side in (before, behind))
    far = (hop(before[:half], 1, chips), hop(behind[half:], -1, chips))
    return (x, before, behind), far


def after(x, *done):
    return lax.optimization_barrier((x, *done))[0]


def body(x_att, w_qk, w_val, w_out, perms, tokens_b, expert_ids, w_gate, w_up, w_down):
    peers, parts = lax.axis_size("seq"), lax.axis_size("exp")
    chips = parts // EXP_DEV
    me = lax.axis_index("seq").astype(I32).reshape(1)
    my_exp = lax.axis_index("exp").astype(I32)
    core = my_exp % EXP_DEV
    where = jnp.stack([my_exp // EXP_DEV, core])
    length, width = x_att.shape
    rounds = perms.shape[0]
    per_peer = length // peers
    tokb = tokens_b.shape[0]
    capacity = tokb // peers
    part = width // chips
    lines = [[chip * EXP_DEV + side for chip in range(chips)] for side in range(EXP_DEV)]
    siblings = [(i, i ^ 1) for i in range(parts)]

    token_part = lax.dynamic_slice_in_dim(tokens_b, where[0] * part, part, 1)
    dispatch, token_slot = pack_tokens(
        where, expert_ids.reshape(1, tokb), token_part, peers, capacity
    )
    received = exchange(dispatch.reshape(peers, capacity, part), "seq")
    outgoing, slot_token, order, earlier = pack_rows(me, perms, x_att, w_qk, w_val)
    def columns_of(by, *ready):
        start = (where[0] + by) % chips * part
        return hop(lax.dynamic_slice_in_dim(after(w_out, *ready), start, part, 1), by, chips)

    near = [columns_of(by, dispatch) for by in (1, chips - 1)]
    received = after(received, outgoing, *near)
    outgoing = after(outgoing, received)
    own = (w_gate, w_up, w_down)
    sibling = [lax.ppermute(after(weight, received), "exp", siblings) for weight in own]
    shards, far_shards = spread(received, chips)
    arrived = exchange(outgoing.reshape(peers, rounds * per_peer, outgoing.shape[1]), "seq")
    far = columns_of(2, *far_shards)
    expert_part = run_experts(where, shards, far_shards, own, sibling)
    arrived = after(arrived, expert_part, far)
    rows, last, row_slot = sort_rows(order, arrived)
    expert_rows = lax.psum_scatter(
        expert_part,
        "exp",
        scatter_dimension=0,
        tiled=False,
        axis_index_groups=lines,
    )
    last = lax.ppermute(last, "seq", [(i, (i + 1) % peers) for i in range(peers)])
    later = attend_later(order, rows, row_slot)
    last = after(last, later)
    packed = attend_first(order, earlier, rows, last, row_slot, later, peers)
    got = exchange(packed, "seq")
    expert_rows = after(expert_rows, packed)
    taken = lax.ppermute(expert_rows, "exp", siblings)
    expert_rows = place_rows(expert_rows, taken)
    mixed_heads = combine(after(got, expert_rows), slot_token, w_qk.shape[1])
    expert_back = exchange(after(expert_rows, mixed_heads), "seq")
    heads, far_heads = spread(mixed_heads, chips)
    attn_kept, attn_given = project(where, (*heads, *far_heads), w_out, (*near, far))
    attn_taken = lax.ppermute(attn_given, "exp", siblings)
    expert_back = after(expert_back, attn_taken)
    return finish(
        expert_back.reshape(peers * EXP_DEV * capacity, width // parts),
        token_slot,
        attn_kept,
        attn_taken,
    )


def solution(mesh):
    in_specs = (
        P("seq", None),
        P(None, "exp"),
        P(None, "exp"),
        P("exp", None),
        P(),
        P("seq", None),
        P("seq", None),
        P("seq", None, "exp"),
        P("seq", None, "exp"),
        P("seq", "exp", None),
    )
    out_specs = (P("seq", "exp"), P("seq", "exp"))
    return jax.shard_map(body, mesh=mesh, in_specs=in_specs, out_specs=out_specs, check_vma=False)
```

```python
import functools
import math

import jax
import jax.numpy as jnp
from jax import lax
from jax.experimental import pallas as pl
from jax.experimental.pallas import tpu as pltpu
from jax.sharding import PartitionSpec as P

HEAD_DIM = 128
BLOCK_LEN = 64
EXP_DEV = 2
LANES = 128
F32, BF16, I32 = jnp.float32, jnp.bfloat16, jnp.int32
LONG = 1 << 35
BIG = pltpu.CompilerParams(vmem_limit_bytes=24 * 1024 * 1024)


def dot(a, b):
    return jnp.dot(a, b, preferred_element_type=F32)


def dot_t(a, b):
    return lax.dot_general(a, b, (((1,), (1,)), ((), ())), preferred_element_type=F32)


def to_col(row):
    return jnp.broadcast_to(row, (LANES, row.shape[1])).T[:, :1]


def to_row(col):
    return jnp.broadcast_to(col, (col.shape[0], LANES)).T[:1, :]


def iota(shape, dim):
    return lax.broadcasted_iota(I32, shape, dim)


def flag(mask, kind=BF16):
    return jnp.where(mask, 1.0, 0.0).astype(kind)


def cost(flops, size):
    return pl.CostEstimate(flops=flops, bytes_accessed=size, transcendentals=0)


def upper(count):
    return flag(iota((count, count), 0) <= iota((count, count), 1))


def pack_rows_kernel(
    me_ref,
    perms_ref,
    x_ref,
    qk_ref,
    val_ref,
    out_ref,
    token_ref,
    order_ref,
    earlier_ref,
    scratch,
):
    length, span = x_ref.shape[0], qk_ref.shape[1]
    rounds, total = perms_ref.shape
    peers = total // length
    per_peer = length // peers
    start = me_ref[0] * length
    order_ref[...] = perms_ref[:, pl.ds(pl.multiple_of(start, length), length)]
    start = jnp.where(start == 0, total, start) - LANES
    earlier_ref[...] = perms_ref[:, pl.ds(pl.multiple_of(start, LANES), LANES)]
    for peer in range(peers):
        scratch[peer * rounds : (peer + 1) * rounds, :] = perms_ref[
            :, peer * length : (peer + 1) * length
        ]
    perms = scratch[...]
    token = perms & (length - 1)
    mine = (perms >> (length.bit_length() - 1)) == me_ref[0]
    rank = dot(flag(mine), upper(length)).astype(I32) - 1
    slot = jnp.where(mine, rank, -1)
    groups = peers * rounds
    chosen = slot[:, None, :] == iota((groups, per_peer, length), 1)
    token_3d = jnp.where(chosen, token.astype(F32)[:, None, :], 0.0)
    column = jnp.sum(token_3d, axis=-1, keepdims=True).reshape(groups * per_peer, 1)
    by_round = column.reshape(peers, rounds, per_peer, 1)
    for turn in range(rounds):
        row = to_row(by_round[:, turn].reshape(peers * per_peer, 1)).astype(I32)
        token_ref[turn] = jnp.broadcast_to(row, token_ref.shape[1:])
    pick = flag(column.astype(I32) == iota((groups * per_peer, length), 1))
    for part, weight in enumerate((qk_ref, val_ref)):
        rows = dot(x_ref[...], weight[...]).astype(BF16)
        out_ref[:, part * span : (part + 1) * span] = dot(pick, rows).astype(BF16)


def pack_rows(me, perms, x_att, w_qk, w_val):
    length, width = x_att.shape
    rounds, total = perms.shape
    span = w_qk.shape[1]
    groups = rounds * (total // length)
    slots = rounds * length

    def whole(shape):
        return pl.BlockSpec(shape, lambda i, me_ref: (0, 0))

    return pl.pallas_call(
        pack_rows_kernel,
        grid_spec=pltpu.PrefetchScalarGridSpec(
            num_scalar_prefetch=1,
            grid=(1,),
            in_specs=[
                whole((rounds, total)),
                whole((length, width)),
                whole((width, span)),
                whole((width, span)),
            ],
            out_specs=[
                whole((slots, 2 * span)),
                pl.BlockSpec((rounds, 8, length), lambda i, me_ref: (0, 0, 0)),
                whole((rounds, length)),
                whole((rounds, LANES)),
            ],
            scratch_shapes=[pltpu.VMEM((groups, length), I32)],
        ),
        out_shape=[
            jax.ShapeDtypeStruct((slots, 2 * span), BF16),
            jax.ShapeDtypeStruct((rounds, 8, length), I32),
            jax.ShapeDtypeStruct((rounds, length), I32),
            jax.ShapeDtypeStruct((rounds, LANES), I32),
        ],
        cost_estimate=cost(4 * length * width * span + 4 * slots * length * span, 6 << 20),
        compiler_params=BIG,
        name="pack_rows",
    )(me, perms, x_att, w_qk, w_val)


def pack_tokens_kernel(peers, where_ref, ids_ref, tokens_ref, out_ref, slot_ref):
    length = tokens_ref.shape[0]
    slots = out_ref.shape[0]
    capacity = slots // peers
    experts = EXP_DEV * peers
    ids = ids_ref[...]
    hot = ids == iota((experts, length), 0)
    counts = dot(flag(hot), upper(length))
    rank = jnp.sum(jnp.where(hot, counts, 0.0), axis=0, keepdims=True).astype(I32) - 1
    core = where_ref[1]
    turn = (ids % EXP_DEV + core) % EXP_DEV
    peer = ids // EXP_DEV
    slot_ref[...] = jnp.broadcast_to(
        (peer * EXP_DEV + turn) * capacity + rank, slot_ref.shape
    )
    slot = jnp.where(turn == 0, peer * capacity + rank, -1)
    pick = flag(iota((slots, length), 0) == slot)
    out_ref[...] = dot(pick, tokens_ref[...]).astype(BF16)


def pack_tokens(where, ids, tokens, peers, capacity):
    length, part = tokens.shape
    slots = peers * capacity
    return pl.pallas_call(
        functools.partial(pack_tokens_kernel, peers),
        grid_spec=pltpu.PrefetchScalarGridSpec(
            num_scalar_prefetch=1,
            grid=(1,),
            in_specs=[
                pl.BlockSpec((1, length), lambda i, e: (0, 0)),
                pl.BlockSpec((length, part), lambda i, e: (0, 0)),
            ],
            out_specs=[
                pl.BlockSpec((slots, part), lambda i, e: (0, 0)),
                pl.BlockSpec((8, length), lambda i, e: (0, 0)),
            ],
        ),
        out_shape=[
            jax.ShapeDtypeStruct((slots, part), BF16),
            jax.ShapeDtypeStruct((8, length), I32),
        ],
        cost_estimate=cost(2 * slots * length * part, 2 << 20),
        compiler_params=BIG,
        name="pack_tokens",
    )(where, ids, tokens)


def experts_kernel(where_ref, *refs):
    step = pl.program_id(0)
    shards, far_refs, weights = refs[0:3], refs[3:5], refs[5:11]
    out_ref, total_ref = refs[11:]
    peers, capacity, part = shards[0].shape
    rows = peers * capacity
    ups = (weights[0], weights[1], weights[3], weights[4])

    def add(x, start):
        for index, weight in enumerate(ups):
            product = dot(x, weight[0])
            total_ref[index] = product if start else total_ref[index] + product

    for turn, shard in enumerate(shards):

        @pl.when(step == turn)
        def _(shard=shard, start=turn == 0):
            add(shard[...].reshape(rows, part), start)

    @pl.when(step == len(shards))
    def _():
        add(jnp.concatenate([ref[...].reshape(rows // 2, part) for ref in far_refs], axis=0), False)
        hiddens = []
        for side in range(EXP_DEV):
            gate, up_val = total_ref[2 * side], total_ref[2 * side + 1]
            hiddens.append((gate / (1.0 + jnp.exp(-gate)) * up_val).astype(BF16))
        half = part // EXP_DEV
        for index in range(out_ref.shape[0]):
            at = index * part
            piece = dot(hiddens[0], weights[2][0, :, at : at + part])
            piece = (piece + dot(hiddens[1], weights[5][0, :, at : at + part])).astype(BF16)
            for side in range(EXP_DEV):
                columns = piece[:, side * half : (side + 1) * half]
                turn = (side + where_ref[1]) % EXP_DEV
                out_ref[index, turn] = columns.reshape(peers, capacity, half)


def run_experts(where, shards, far, own, sibling):
    peers, capacity, part = shards[0].shape
    width, hidden = own[0].shape[1:]
    chips = width // part
    out = (chips, EXP_DEV, peers, capacity, part // EXP_DEV)
    rows = peers * capacity

    def rows_of(i, e):
        ahead = jnp.where(i == 0, 0, jnp.where(i == 1, chips - 1, jnp.where(i == 2, 1, 2)))
        return (e[0] + ahead) % chips

    up_block, down_block = (1, part, hidden), (1, hidden, width)
    own_up = pl.BlockSpec(up_block, lambda i, e: (e[1], rows_of(i, e), 0))
    own_down = pl.BlockSpec(down_block, lambda i, e: (e[1], 0, 0))
    return pl.pallas_call(
        experts_kernel,
        grid_spec=pltpu.PrefetchScalarGridSpec(
            num_scalar_prefetch=1,
            grid=(len(shards) + 1,),
            in_specs=[pl.BlockSpec(x.shape, lambda i, e: (0, 0, 0)) for x in (*shards, *far)]
            + [own_up, own_up, own_down] * 2,
            out_specs=pl.BlockSpec(out, lambda i, e: (0, 0, 0, 0, 0)),
            scratch_shapes=[pltpu.VMEM((4, rows, hidden), F32)],
        ),
        out_shape=jax.ShapeDtypeStruct(out, BF16),
        cost_estimate=cost(15 * 10**9, 10 << 20),
        compiler_params=BIG,
        name="experts",
    )(where, *shards, *far, *own, *sibling)


def place_rows_kernel(rows_ref, taken_ref, out_ref, copied):
    copies = (
        pltpu.make_async_copy(rows_ref.at[0], out_ref.at[:, 0], copied.at[0]),
        pltpu.make_async_copy(taken_ref.at[1], out_ref.at[:, 1], copied.at[1]),
    )
    for copy in copies:
        copy.start()
    for copy in copies:
        copy.wait()


def place_rows(rows, taken):
    _, peers, capacity, half = taken.shape
    return pl.pallas_call(
        place_rows_kernel,
        in_specs=[pl.BlockSpec(memory_space=pltpu.HBM)] * 2,
        out_specs=pl.BlockSpec(memory_space=pltpu.HBM),
        out_shape=jax.ShapeDtypeStruct((peers, EXP_DEV, capacity, half), BF16),
        scratch_shapes=[pltpu.SemaphoreType.DMA((2,))],
        cost_estimate=cost(1 << 20, 1 << 20),
        compiler_params=BIG,
        name="place_rows",
    )(rows, taken)


def finish_kernel(back_ref, slot_ref, kept_ref, taken_ref, attended_ref, mixed_ref):
    length = mixed_ref.shape[0]
    column = to_col(slot_ref[:1, :].astype(F32)).astype(I32)
    pick = flag(column == iota((length, back_ref.shape[0]), 1))
    mixed_ref[...] = dot(pick, back_ref[...]).astype(BF16)
    attended_ref[...] = (kept_ref[...] + taken_ref[...].astype(F32)).astype(BF16)


def finish(back, slot, kept, taken):
    length, width = slot.shape[1], back.shape[1]
    return pl.pallas_call(
        finish_kernel,
        out_shape=[
            jax.ShapeDtypeStruct(kept.shape, BF16),
            jax.ShapeDtypeStruct((length, width), BF16),
        ],
        cost_estimate=cost(2 * length * back.shape[0] * width, 1 << 20),
        compiler_params=BIG,
        name="finish",
    )(back, slot, kept, taken)


def sort_rows_kernel(peers, perms_ref, arrived_ref, rows_ref, last_ref, slot_ref):
    rounds, length = perms_ref.shape
    per_peer = length // peers
    for turn in range(rounds):
        source = perms_ref[turn : turn + 1, :] >> (length.bit_length() - 1)
        hot = source == iota((peers, length), 0)
        counts = dot(flag(hot), upper(length))
        rank = jnp.sum(jnp.where(hot, counts, 0.0), axis=0, keepdims=True) - 1.0
        slot = source * per_peer + rank.astype(I32)
        slot_ref[turn] = jnp.broadcast_to(slot, slot_ref.shape[1:])
        pick = flag(to_col(slot.astype(F32)).astype(I32) == iota((length, length), 1))
        have = arrived_ref[:, turn * per_peer : (turn + 1) * per_peer, :]
        rows = dot(pick, have.reshape(length, have.shape[2])).astype(BF16)
        rows_ref[turn] = rows
        last_ref[turn] = rows[length - BLOCK_LEN :]


def sort_rows(order, arrived):
    rounds, length = order.shape
    peers, _, width = arrived.shape
    return pl.pallas_call(
        functools.partial(sort_rows_kernel, peers),
        out_shape=[
            jax.ShapeDtypeStruct((rounds, length, width), BF16),
            jax.ShapeDtypeStruct((rounds, BLOCK_LEN, width), BF16),
            jax.ShapeDtypeStruct((rounds, 8, length), I32),
        ],
        cost_estimate=cost(LONG, 4 << 20),
        compiler_params=BIG,
        name="sort_rows",
    )(order, arrived)


def window_scale(keys):
    wide = keys.astype(F32)
    squares = jnp.sum(wide * wide, axis=-1, keepdims=True)
    return to_row(lax.rsqrt(squares + 1e-06) / math.sqrt(HEAD_DIM))


def windows(row, first, last):
    moved = jnp.concatenate([row[:, BLOCK_LEN:], row[:, :BLOCK_LEN]], axis=1)
    spans = []
    for start in range(first, last, BLOCK_LEN):
        odd = start % LANES
        span = (moved if odd else row)[:, start - odd : start - odd + WINDOW]
        spans.append(jnp.broadcast_to(span, (BLOCK_LEN, WINDOW)))
    return jnp.concatenate(spans, axis=0)


def attend_blocks(queries, keys, values, scale, pos_q, pos_k):
    starts = range(0, queries.shape[0], BLOCK_LEN)
    scores = jnp.concatenate(
        [dot_t(queries[at : at + BLOCK_LEN], keys[at : at + WINDOW]) for at in starts], axis=0
    )
    scores = scores * scale
    scores = jnp.where(pos_k == pos_q, scores - 10000.0, scores)
    scores = jnp.where(pos_k <= pos_q, scores, -1e30)
    peak = jnp.max(scores, axis=-1, keepdims=True)
    exponent = jnp.exp(scores - peak)
    total = jnp.sum(exponent, axis=-1, keepdims=True)
    weights = (exponent / total).astype(BF16)
    outs = [dot(weights[at : at + BLOCK_LEN], values[at : at + WINDOW]) for at in starts]
    return jnp.concatenate(outs, axis=0).astype(BF16), peak + jnp.log(total)


TILE, WINDOW, PIECES, GROUP = BLOCK_LEN, 2 * BLOCK_LEN, 3, 8


def put_logs(totals):
    lane = iota((totals[0].shape[0], LANES), 1) % GROUP
    logs = jnp.zeros(lane.shape, F32)
    for head, total in enumerate(totals):
        rest = total
        for piece in range(PIECES):
            part = rest.astype(BF16).astype(F32)
            logs = jnp.where(lane == head * PIECES + piece, part, logs)
            rest = rest - part
    return logs.astype(BF16)


def attend_later_kernel(perms_ref, rows_ref, slot_ref, out_ref):
    rounds, length = perms_ref.shape
    span = rows_ref.shape[2] // 2
    for turn in range(rounds):
        position = perms_ref[turn : turn + 1, :].astype(F32)
        pos_q = to_col(position)[TILE:]
        pos_k = windows(position, 0, length - TILE)
        outs, totals = [], []
        for head in range(span // HEAD_DIM):
            at = head * HEAD_DIM
            keys = rows_ref[turn, :, at : at + HEAD_DIM]
            out, total = attend_blocks(
                keys[TILE:],
                keys,
                rows_ref[turn, :, span + at : span + at + HEAD_DIM],
                windows(window_scale(keys), 0, length - TILE),
                pos_q,
                pos_k,
            )
            outs.append(out)
            totals.append(total)
        whole = jnp.concatenate(outs + [put_logs(totals)], axis=1)
        back = flag(iota((length, length), 0) == slot_ref[turn, :1, :])
        whole = jnp.concatenate([jnp.zeros((TILE, whole.shape[1]), BF16), whole], axis=0)
        out_ref[turn] = dot(back, whole).astype(BF16)


def attend_first_kernel(
    peers,
    perms_ref,
    earlier_ref,
    rows_ref,
    last_ref,
    slot_ref,
    later_ref,
    out_ref,
):
    rounds, length = slot_ref.shape[0], slot_ref.shape[2]
    per_peer = length // peers
    span = rows_ref.shape[2] // 2
    lane_group = iota((peers, per_peer, LANES), 2) // GROUP
    own_group = lane_group == iota((peers, per_peer, LANES), 1)
    log_row = iota((peers, GROUP, LANES), 1)
    all_logs = jnp.zeros((peers, GROUP, LANES), F32)
    lane = iota((1, LANES), 1)
    for turn in range(rounds):
        position = perms_ref[turn : turn + 1, :LANES].astype(F32)
        earlier = earlier_ref[turn : turn + 1, :].astype(F32)
        swapped = jnp.concatenate([position[:, BLOCK_LEN:], position[:, :BLOCK_LEN]], axis=1)
        earlier = jnp.concatenate([earlier[:, BLOCK_LEN:], earlier[:, :BLOCK_LEN]], axis=1)
        pos_k = jnp.where(lane < BLOCK_LEN, earlier, swapped)
        pos_q = to_col(position)[:TILE]
        totals, outs = [], []
        for head in range(span // HEAD_DIM):
            at = head * HEAD_DIM
            own = rows_ref[turn, :TILE, at : at + HEAD_DIM]
            keys = jnp.concatenate([last_ref[turn, :, at : at + HEAD_DIM], own], axis=0)
            at = span + at
            values = jnp.concatenate(
                [
                    last_ref[turn, :, at : at + HEAD_DIM],
                    rows_ref[turn, :TILE, at : at + HEAD_DIM],
                ],
                axis=0,
            )
            out, total = attend_blocks(own, keys, values, window_scale(keys), pos_q, pos_k)
            outs.append(out)
            totals.append(total)
        top = jnp.concatenate(outs + [put_logs(totals)], axis=1)
        top = jnp.concatenate([top, jnp.zeros((LANES - TILE, top.shape[1]), BF16)], axis=0)
        back = flag(iota((length, LANES), 0) == slot_ref[turn, :1, :LANES])
        moved = dot(back, top) + later_ref[turn].astype(F32)
        for head in range(span // HEAD_DIM):
            at = (head * rounds + turn) * per_peer
            lanes = moved[:, head * HEAD_DIM : (head + 1) * HEAD_DIM]
            out_ref[:, at : at + per_peer, :] = lanes.astype(BF16).reshape(
                peers, per_peer, HEAD_DIM
            )
        logs = moved[:, span:].reshape(peers, per_peer, LANES)
        logs = jnp.sum(jnp.where(own_group, logs, 0.0), axis=1, keepdims=True)
        all_logs = jnp.where(log_row == turn, logs, all_logs)
    out_ref[:, out_ref.shape[1] - GROUP :, :] = all_logs.astype(BF16)


def attend_later(order, rows, slot):
    rounds, length, width = rows.shape
    return pl.pallas_call(
        attend_later_kernel,
        out_shape=jax.ShapeDtypeStruct((rounds, length, width // 2 + LANES), BF16),
        cost_estimate=cost(LONG, 4 << 20),
        compiler_params=BIG,
        name="attend_later",
    )(order, rows, slot)


def attend_first(order, earlier, rows, last, slot, later, peers):
    rounds, length, width = rows.shape
    out = (peers, width // 2 // HEAD_DIM * rounds * (length // peers) + GROUP, HEAD_DIM)

    def fixed(x):
        return pl.BlockSpec(x.shape, lambda i: (0,) * x.ndim)

    return pl.pallas_call(
        functools.partial(attend_first_kernel, peers),
        grid=(1,),
        in_specs=[
            fixed(order),
            fixed(earlier),
            pl.BlockSpec((rounds, LANES, width), lambda i: (0, 0, 0)),
            fixed(last),
            fixed(slot),
            fixed(later),
        ],
        out_specs=pl.BlockSpec(out, lambda i: (0, 0, 0)),
        out_shape=jax.ShapeDtypeStruct(out, BF16),
        cost_estimate=cost(LONG, 4 << 20),
        compiler_params=BIG,
        name="attend_first",
    )(order, earlier, rows, last, slot, later)


def combine_kernel(got_ref, token_ref, mixed_ref):
    peers = got_ref.shape[0]
    rounds, _, length = token_ref.shape
    per_peer = length // peers
    heads = mixed_ref.shape[1] // HEAD_DIM
    lane_group = iota((peers, per_peer, LANES), 2) // GROUP
    own_group = lane_group == iota((peers, per_peer, LANES), 1)
    lane = iota((length, LANES), 1) % GROUP // PIECES
    column = iota((length, length), 0)
    log_row = iota((peers, GROUP, LANES), 1)
    all_logs = got_ref[:, got_ref.shape[1] - GROUP :, :].astype(F32)
    outs, lses = [], []
    for turn in range(rounds):
        pick = flag(token_ref[turn, :1, :] == column)
        logs = jnp.sum(jnp.where(log_row == turn, all_logs, 0.0), axis=1, keepdims=True)
        logs = jnp.where(own_group, logs, 0.0).astype(BF16)
        sides = []
        for head in range(heads):
            at = (head * rounds + turn) * per_peer
            sides.append(got_ref[:, at : at + per_peer, :].reshape(length, HEAD_DIM))
        outs.append(dot(pick, jnp.concatenate(sides, axis=1)))
        moved = dot(pick, logs.reshape(length, LANES))
        lses.append(
            [
                jnp.sum(jnp.where(lane == head, moved, 0.0), axis=1, keepdims=True)
                for head in range(heads)
            ]
        )
    for head in range(heads):
        logs = [lse[head] for lse in lses]
        peak = functools.reduce(jnp.maximum, logs)
        whole = peak + jnp.log(functools.reduce(jnp.add, [jnp.exp(lse - peak) for lse in logs]))
        at = head * HEAD_DIM
        mixed = jnp.zeros((length, HEAD_DIM), F32)
        for out, lse in zip(outs, logs):
            mixed = mixed + out[:, at : at + HEAD_DIM] * jnp.exp(lse - whole)
        mixed_ref[:, at : at + HEAD_DIM] = mixed.astype(BF16)


def combine(got, token, span):
    rounds, _, length = token.shape
    return pl.pallas_call(
        combine_kernel,
        out_shape=jax.ShapeDtypeStruct((length, span), BF16),
        cost_estimate=cost(2 * rounds * length * length * (span + LANES), 1 << 20),
        compiler_params=BIG,
        name="combine",
    )(got, token)


def project_kernel(where_ref, own_ref, prev_ref, next_ref, far_a_ref, far_b_ref, *refs):
    weights, (kept_ref, given_ref) = refs[:-2], refs[-2:]
    far = jnp.concatenate([far_a_ref[...], far_b_ref[...]], axis=0)
    total = dot(own_ref[...], weights[0][...]) + dot(prev_ref[...], weights[1][...])
    total = total + dot(next_ref[...], weights[2][...]) + dot(far, weights[3][...])
    half = kept_ref.shape[1]
    for core in range(EXP_DEV):

        @pl.when(where_ref[1] == core)
        def _(core=core):
            kept_ref[...] = total[:, core * half : (core + 1) * half]
            other = 1 - core
            given_ref[...] = total[:, other * half : (other + 1) * half].astype(BF16)


def project(where, heads, w_out, others):
    length, span = heads[0].shape
    columns = others[0].shape[1]
    half = columns // EXP_DEV
    weights = (w_out, *others)
    shapes = [x.shape for x in heads] + [(span, columns)] + [x.shape for x in others]

    def first(i, e):
        return (0, 0)

    specs = [pl.BlockSpec(shape, first) for shape in shapes]
    specs[len(heads)] = pl.BlockSpec((span, columns), lambda i, e: (0, e[0]))
    return pl.pallas_call(
        project_kernel,
        grid_spec=pltpu.PrefetchScalarGridSpec(
            num_scalar_prefetch=1,
            grid=(1,),
            in_specs=specs,
            out_specs=[pl.BlockSpec((length, half), first)] * 2,
        ),
        out_shape=[
            jax.ShapeDtypeStruct((length, half), F32),
            jax.ShapeDtypeStruct((length, half), BF16),
        ],
        cost_estimate=cost(55 * 10**8, 3 << 20),
        compiler_params=BIG,
        name="project",
    )(where, *heads, *weights)


def exchange(x, axis):
    return lax.all_to_all(x, axis, split_axis=0, concat_axis=0, tiled=True)


def hop(x, by, chips):
    pairs = []
    for chip in range(chips):
        for core in range(EXP_DEV):
            there = (chip + by) % chips
            pairs.append((chip * EXP_DEV + core, there * EXP_DEV + core))
    return lax.ppermute(x, "exp", pairs)


def spread(x, chips, ready=()):
    half = x.shape[0] // 2
    before, behind = hop(x, 1, chips), hop(x, -1, chips)
    before, behind = (after(side, *ready) if ready else side for side in (before, behind))
    far = (hop(before[:half], 1, chips), hop(behind[half:], -1, chips))
    return (x, before, behind), far


def after(x, *done):
    return lax.optimization_barrier((x, *done))[0]


def body(x_att, w_qk, w_val, w_out, perms, tokens_b, expert_ids, w_gate, w_up, w_down):
    peers, parts = lax.axis_size("seq"), lax.axis_size("exp")
    chips = parts // EXP_DEV
    me = lax.axis_index("seq").astype(I32).reshape(1)
    my_exp = lax.axis_index("exp").astype(I32)
    core = my_exp % EXP_DEV
    where = jnp.stack([my_exp // EXP_DEV, core])
    length, width = x_att.shape
    rounds = perms.shape[0]
    per_peer = length // peers
    tokb = tokens_b.shape[0]
    capacity = tokb // peers
    part = width // chips
    lines = [[chip * EXP_DEV + side for chip in range(chips)] for side in range(EXP_DEV)]
    siblings = [(i, i ^ 1) for i in range(parts)]

    token_part = lax.dynamic_slice_in_dim(tokens_b, where[0] * part, part, 1)
    dispatch, token_slot = pack_tokens(
        where, expert_ids.reshape(1, tokb), token_part, peers, capacity
    )
    received = exchange(dispatch.reshape(peers, capacity, part), "seq")
    outgoing, slot_token, order, earlier = pack_rows(me, perms, x_att, w_qk, w_val)
    def columns_of(by, *ready):
        start = (where[0] + by) % chips * part
        return hop(lax.dynamic_slice_in_dim(after(w_out, *ready), start, part, 1), by, chips)

    near = [columns_of(by, dispatch) for by in (1, chips - 1)]
    received = after(received, outgoing, *near)
    outgoing = after(outgoing, received)
    own = (w_gate, w_up, w_down)
    sibling = [lax.ppermute(after(weight, received), "exp", siblings) for weight in own]
    shards, far_shards = spread(received, chips)
    arrived = exchange(outgoing.reshape(peers, rounds * per_peer, outgoing.shape[1]), "seq")
    far = columns_of(2, *far_shards)
    expert_part = run_experts(where, shards, far_shards, own, sibling)
    arrived = after(arrived, expert_part, far)
    rows, last, row_slot = sort_rows(order, arrived)
    expert_rows = lax.psum_scatter(
        expert_part,
        "exp",
        scatter_dimension=0,
        tiled=False,
        axis_index_groups=lines,
    )
    last = lax.ppermute(last, "seq", [(i, (i + 1) % peers) for i in range(peers)])
    later = attend_later(order, rows, row_slot)
    last = after(last, later)
    packed = attend_first(order, earlier, rows, last, row_slot, later, peers)
    got = exchange(packed, "seq")
    expert_rows = after(expert_rows, packed)
    taken = lax.ppermute(expert_rows, "exp", siblings)
    expert_rows = place_rows(expert_rows, taken)
    mixed_heads = combine(after(got, expert_rows), slot_token, w_qk.shape[1])
    expert_back = exchange(after(expert_rows, mixed_heads), "seq")
    heads, far_heads = spread(mixed_heads, chips)
    attn_kept, attn_given = project(where, (*heads, *far_heads), w_out, (*near, far))
    attn_taken = lax.ppermute(attn_given, "exp", siblings)
    expert_back = after(expert_back, attn_taken)
    return finish(
        expert_back.reshape(peers * EXP_DEV * capacity, width // parts),
        token_slot,
        attn_kept,
        attn_taken,
    )


def solution(mesh):
    in_specs = (
        P("seq", None),
        P(None, "exp"),
        P(None, "exp"),
        P("exp", None),
        P(),
        P("seq", None),
        P("seq", None),
        P("seq", None, "exp"),
        P("seq", None, "exp"),
        P("seq", "exp", None),
    )
    out_specs = (P("seq", "exp"), P("seq", "exp"))
    return jax.shard_map(body, mesh=mesh, in_specs=in_specs, out_specs=out_specs, check_vma=False)
```

```python
import functools
import math

import jax
import jax.numpy as jnp
from jax import lax
from jax.experimental import pallas as pl
from jax.experimental.pallas import tpu as pltpu
from jax.sharding import PartitionSpec as P

HEAD_DIM = 128
BLOCK_LEN = 64
EXP_DEV = 2
LANES = 128
F32, BF16, I32 = jnp.float32, jnp.bfloat16, jnp.int32
LONG = 1 << 35
BIG = pltpu.CompilerParams(vmem_limit_bytes=48 * 1024 * 1024)
ALL = pltpu.CompilerParams(vmem_limit_bytes=60 * 1024 * 1024)


def dot(a, b):
    return jnp.dot(a, b, preferred_element_type=F32)


def dot_t(a, b):
    return lax.dot_general(a, b, (((1,), (1,)), ((), ())), preferred_element_type=F32)


def to_col(row):
    return jnp.broadcast_to(row, (LANES, row.shape[1])).T[:, :1]


def to_row(col):
    return jnp.broadcast_to(col, (col.shape[0], LANES)).T[:1, :]


def iota(shape, dim):
    return lax.broadcasted_iota(I32, shape, dim)


def flag(mask, kind=BF16):
    return jnp.where(mask, 1.0, 0.0).astype(kind)


def cost(flops, size):
    return pl.CostEstimate(flops=flops, bytes_accessed=size, transcendentals=0)


def upper(count):
    return flag(iota((count, count), 0) <= iota((count, count), 1))


def pack_rows_kernel(me_ref, perms_ref, x_ref, qk_ref, val_ref, out_ref, token_ref, scratch):
    length, span = x_ref.shape[0], qk_ref.shape[1]
    rounds, total = perms_ref.shape
    peers = total // length
    per_peer = length // peers
    for peer in range(peers):
        scratch[peer * rounds : (peer + 1) * rounds, :] = perms_ref[
            :, peer * length : (peer + 1) * length
        ]
    perms = scratch[...]
    token = perms & (length - 1)
    mine = (perms >> (length.bit_length() - 1)) == me_ref[0]
    rank = dot(flag(mine), upper(length)).astype(I32) - 1
    slot = jnp.where(mine, rank, -1)
    groups = peers * rounds
    chosen = slot[:, None, :] == iota((groups, per_peer, length), 1)
    token_3d = jnp.where(chosen, token.astype(F32)[:, None, :], 0.0)
    column = jnp.sum(token_3d, axis=-1, keepdims=True).reshape(groups * per_peer, 1)
    by_round = column.reshape(peers, rounds, per_peer, 1)
    for turn in range(rounds):
        row = to_row(by_round[:, turn].reshape(peers * per_peer, 1)).astype(I32)
        token_ref[turn] = jnp.broadcast_to(row, token_ref.shape[1:])
    pick = flag(column.astype(I32) == iota((groups * per_peer, length), 1))
    for part, weight in enumerate((qk_ref, val_ref)):
        rows = dot(x_ref[...], weight[...]).astype(BF16)
        out_ref[:, part * span : (part + 1) * span] = dot(pick, rows).astype(BF16)


def pack_rows(me, perms, x_att, w_qk, w_val):
    length, width = x_att.shape
    rounds, total = perms.shape
    span = w_qk.shape[1]
    groups = rounds * (total // length)
    slots = rounds * length

    def whole(shape):
        return pl.BlockSpec(shape, lambda i, me_ref: (0, 0))

    return pl.pallas_call(
        pack_rows_kernel,
        grid_spec=pltpu.PrefetchScalarGridSpec(
            num_scalar_prefetch=1,
            grid=(1,),
            in_specs=[
                whole((rounds, total)),
                whole((length, width)),
                whole((width, span)),
                whole((width, span)),
            ],
            out_specs=[
                whole((slots, 2 * span)),
                pl.BlockSpec((rounds, 8, length), lambda i, me_ref: (0, 0, 0)),
            ],
            scratch_shapes=[pltpu.VMEM((groups, length), I32)],
        ),
        out_shape=[
            jax.ShapeDtypeStruct((slots, 2 * span), BF16),
            jax.ShapeDtypeStruct((rounds, 8, length), I32),
        ],
        cost_estimate=cost(4 * length * width * span + 4 * slots * length * span, 6 << 20),
        compiler_params=BIG,
        name="pack_rows",
    )(me, perms, x_att, w_qk, w_val)


def pack_tokens_kernel(
    peers, where_ref, ids_ref, tokens_ref, out_ref, slot_ref, mine_ref, copied
):
    length = tokens_ref.shape[0]
    slots, part = out_ref.shape
    columns = pl.ds(pl.multiple_of(where_ref[0] * part, part), part)
    copy = pltpu.make_async_copy(tokens_ref.at[:, columns], mine_ref, copied)
    copy.start()
    capacity = slots // peers
    experts = EXP_DEV * peers
    ids = ids_ref[...]
    hot = ids == iota((experts, length), 0)
    counts = dot(flag(hot), upper(length))
    rank = jnp.sum(jnp.where(hot, counts, 0.0), axis=0, keepdims=True).astype(I32) - 1
    core = where_ref[1]
    turn = (ids % EXP_DEV + core) % EXP_DEV
    peer = ids // EXP_DEV
    slot_ref[...] = jnp.broadcast_to(
        (peer * EXP_DEV + turn) * capacity + rank, slot_ref.shape
    )
    slot = jnp.where(turn == 0, peer * capacity + rank, -1)
    pick = flag(iota((slots, length), 0) == slot)
    copy.wait()
    out_ref[...] = dot(pick, mine_ref[...]).astype(BF16)


def pack_tokens(where, ids, tokens, peers, capacity, part):
    length = tokens.shape[0]
    slots = peers * capacity
    return pl.pallas_call(
        functools.partial(pack_tokens_kernel, peers),
        grid_spec=pltpu.PrefetchScalarGridSpec(
            num_scalar_prefetch=1,
            grid=(1,),
            in_specs=[
                pl.BlockSpec((1, length), lambda i, e: (0, 0)),
                pl.BlockSpec(memory_space=pltpu.HBM),
            ],
            out_specs=[
                pl.BlockSpec((slots, part), lambda i, e: (0, 0)),
                pl.BlockSpec((8, length), lambda i, e: (0, 0)),
            ],
            scratch_shapes=[pltpu.VMEM((length, part), BF16), pltpu.SemaphoreType.DMA],
        ),
        out_shape=[
            jax.ShapeDtypeStruct((slots, part), BF16),
            jax.ShapeDtypeStruct((8, length), I32),
        ],
        cost_estimate=cost(2 * slots * length * part, 2 << 20),
        compiler_params=ALL,
        name="pack_tokens",
    )(where, ids, tokens)


def experts_kernel(where_ref, *refs):
    step = pl.program_id(0)
    shards, far_refs, weights = refs[0:3], refs[3:5], refs[5:11]
    out_ref, total_ref = refs[11:]
    peers, capacity, part = shards[0].shape
    rows = peers * capacity
    ups = (weights[0], weights[1], weights[3], weights[4])

    def add(x, start):
        for index, weight in enumerate(ups):
            product = dot(x, weight[0])
            total_ref[index] = product if start else total_ref[index] + product

    for turn, shard in enumerate(shards):

        @pl.when(step == turn)
        def _(shard=shard, start=turn == 0):
            add(shard[...].reshape(rows, part), start)

    @pl.when(step == len(shards))
    def _():
        add(jnp.concatenate([ref[...].reshape(rows // 2, part) for ref in far_refs], axis=0), False)
        hiddens = []
        for side in range(EXP_DEV):
            gate, up_val = total_ref[2 * side], total_ref[2 * side + 1]
            hiddens.append((gate / (1.0 + jnp.exp(-gate)) * up_val).astype(BF16))
        half = part // EXP_DEV
        for index in range(out_ref.shape[0]):
            at = index * part
            piece = dot(hiddens[0], weights[2][0, :, at : at + part])
            piece = (piece + dot(hiddens[1], weights[5][0, :, at : at + part])).astype(BF16)
            for side in range(EXP_DEV):
                columns = piece[:, side * half : (side + 1) * half]
                turn = (side + where_ref[1]) % EXP_DEV
                out_ref[index, turn] = columns.reshape(peers, capacity, half)


def run_experts(where, shards, far, own, sibling):
    peers, capacity, part = shards[0].shape
    width, hidden = own[0].shape[1:]
    chips = width // part
    out = (chips, EXP_DEV, peers, capacity, part // EXP_DEV)
    rows = peers * capacity

    def rows_of(i, e):
        ahead = jnp.where(i == 0, 0, jnp.where(i == 1, chips - 1, jnp.where(i == 2, 1, 2)))
        return (e[0] + ahead) % chips

    up_block, down_block = (1, part, hidden), (1, hidden, width)
    own_up = pl.BlockSpec(up_block, lambda i, e: (e[1], rows_of(i, e), 0))
    own_down = pl.BlockSpec(down_block, lambda i, e: (e[1], 0, 0))
    return pl.pallas_call(
        experts_kernel,
        grid_spec=pltpu.PrefetchScalarGridSpec(
            num_scalar_prefetch=1,
            grid=(len(shards) + 1,),
            in_specs=[pl.BlockSpec(x.shape, lambda i, e: (0, 0, 0)) for x in (*shards, *far)]
            + [own_up, own_up, own_down] * 2,
            out_specs=pl.BlockSpec(out, lambda i, e: (0, 0, 0, 0, 0)),
            scratch_shapes=[pltpu.VMEM((4, rows, hidden), F32)],
        ),
        out_shape=jax.ShapeDtypeStruct(out, BF16),
        cost_estimate=cost(15 * 10**9, 10 << 20),
        compiler_params=BIG,
        name="experts",
    )(where, *shards, *far, *own, *sibling)


def place_rows_kernel(rows_ref, taken_ref, out_ref, copied):
    copies = (
        pltpu.make_async_copy(rows_ref.at[0], out_ref.at[:, 0], copied.at[0]),
        pltpu.make_async_copy(taken_ref, out_ref.at[:, 1], copied.at[1]),
    )
    for copy in copies:
        copy.start()
    for copy in copies:
        copy.wait()


def place_rows(rows, taken):
    peers, capacity, half = taken.shape
    return pl.pallas_call(
        place_rows_kernel,
        in_specs=[pl.BlockSpec(memory_space=pltpu.HBM)] * 2,
        out_specs=pl.BlockSpec(memory_space=pltpu.HBM),
        out_shape=jax.ShapeDtypeStruct((peers, EXP_DEV, capacity, half), BF16),
        scratch_shapes=[pltpu.SemaphoreType.DMA((2,))],
        cost_estimate=cost(1 << 20, 1 << 20),
        compiler_params=BIG,
        name="place_rows",
    )(rows, taken)


def finish_kernel(back_ref, slot_ref, kept_ref, taken_ref, attended_ref, mixed_ref):
    length = mixed_ref.shape[0]
    column = to_col(slot_ref[:1, :].astype(F32)).astype(I32)
    pick = flag(column == iota((length, back_ref.shape[0]), 1))
    mixed_ref[...] = dot(pick, back_ref[...]).astype(BF16)
    attended_ref[...] = (kept_ref[...] + taken_ref[...].astype(F32)).astype(BF16)


def finish(back, slot, kept, taken):
    length, width = slot.shape[1], back.shape[1]
    return pl.pallas_call(
        finish_kernel,
        out_shape=[
            jax.ShapeDtypeStruct(kept.shape, BF16),
            jax.ShapeDtypeStruct((length, width), BF16),
        ],
        cost_estimate=cost(2 * length * back.shape[0] * width, 1 << 20),
        compiler_params=BIG,
        name="finish",
    )(back, slot, kept, taken)


def sort_rows_kernel(peers, me_ref, perms_ref, arrived_ref, rows_ref, last_ref, slot_ref):
    rounds, length = perms_ref.shape
    per_peer = length // peers
    for turn in range(rounds):
        source = perms_ref[turn : turn + 1, :] >> (length.bit_length() - 1)
        hot = source == iota((peers, length), 0)
        counts = dot(flag(hot), upper(length))
        rank = jnp.sum(jnp.where(hot, counts, 0.0), axis=0, keepdims=True) - 1.0
        slot = source * per_peer + rank.astype(I32)
        slot_ref[turn] = jnp.broadcast_to(slot, slot_ref.shape[1:])
        pick = flag(to_col(slot.astype(F32)).astype(I32) == iota((length, length), 1))
        have = arrived_ref[:, turn * per_peer : (turn + 1) * per_peer, :]
        rows = dot(pick, have.reshape(length, have.shape[2])).astype(BF16)
        rows_ref[turn] = rows
        last_ref[turn] = rows[length - BLOCK_LEN :]


def sort_rows(me, perms, arrived, length):
    rounds = perms.shape[0]
    peers, _, width = arrived.shape
    return pl.pallas_call(
        functools.partial(sort_rows_kernel, peers),
        grid_spec=pltpu.PrefetchScalarGridSpec(
            num_scalar_prefetch=1,
            grid=(1,),
            in_specs=[
                pl.BlockSpec((rounds, length), lambda i, s: (0, s[0])),
                pl.BlockSpec(arrived.shape, lambda i, s: (0, 0, 0)),
            ],
            out_specs=[
                pl.BlockSpec((rounds, length, width), lambda i, s: (0, 0, 0)),
                pl.BlockSpec((rounds, BLOCK_LEN, width), lambda i, s: (0, 0, 0)),
                pl.BlockSpec((rounds, 8, length), lambda i, s: (0, 0, 0)),
            ],
        ),
        out_shape=[
            jax.ShapeDtypeStruct((rounds, length, width), BF16),
            jax.ShapeDtypeStruct((rounds, BLOCK_LEN, width), BF16),
            jax.ShapeDtypeStruct((rounds, 8, length), I32),
        ],
        cost_estimate=cost(LONG, 4 << 20),
        compiler_params=BIG,
        name="sort_rows",
    )(me, perms, arrived)


def window_scale(keys):
    wide = keys.astype(F32)
    squares = jnp.sum(wide * wide, axis=-1, keepdims=True)
    return to_row(lax.rsqrt(squares + 1e-06) / math.sqrt(HEAD_DIM))


def windows(row, first, last):
    moved = jnp.concatenate([row[:, BLOCK_LEN:], row[:, :BLOCK_LEN]], axis=1)
    spans = []
    for start in range(first, last, BLOCK_LEN):
        odd = start % LANES
        span = (moved if odd else row)[:, start - odd : start - odd + WINDOW]
        spans.append(jnp.broadcast_to(span, (BLOCK_LEN, WINDOW)))
    return jnp.concatenate(spans, axis=0)


def attend_blocks(queries, keys, values, scale, pos_q, pos_k):
    starts = range(0, queries.shape[0], BLOCK_LEN)
    scores = jnp.concatenate(
        [dot_t(queries[at : at + BLOCK_LEN], keys[at : at + WINDOW]) for at in starts], axis=0
    )
    scores = scores * scale
    scores = jnp.where(pos_k == pos_q, scores - 10000.0, scores)
    scores = jnp.where(pos_k <= pos_q, scores, -1e30)
    peak = jnp.max(scores, axis=-1, keepdims=True)
    exponent = jnp.exp(scores - peak)
    total = jnp.sum(exponent, axis=-1, keepdims=True)
    weights = (exponent / total).astype(BF16)
    outs = [dot(weights[at : at + BLOCK_LEN], values[at : at + WINDOW]) for at in starts]
    return jnp.concatenate(outs, axis=0).astype(BF16), peak + jnp.log(total)


TILE, WINDOW, PIECES, GROUP = BLOCK_LEN, 2 * BLOCK_LEN, 3, 8


def put_logs(totals):
    lane = iota((totals[0].shape[0], LANES), 1) % GROUP
    logs = jnp.zeros(lane.shape, F32)
    for head, total in enumerate(totals):
        rest = total
        for piece in range(PIECES):
            part = rest.astype(BF16).astype(F32)
            logs = jnp.where(lane == head * PIECES + piece, part, logs)
            rest = rest - part
    return logs.astype(BF16)


def attend_later_kernel(me_ref, perms_ref, rows_ref, slot_ref, out_ref):
    rounds, length = perms_ref.shape
    span = rows_ref.shape[2] // 2
    for turn in range(rounds):
        position = perms_ref[turn : turn + 1, :].astype(F32)
        pos_q = to_col(position)[TILE:]
        pos_k = windows(position, 0, length - TILE)
        outs, totals = [], []
        for head in range(span // HEAD_DIM):
            at = head * HEAD_DIM
            keys = rows_ref[turn, :, at : at + HEAD_DIM]
            out, total = attend_blocks(
                keys[TILE:],
                keys,
                rows_ref[turn, :, span + at : span + at + HEAD_DIM],
                windows(window_scale(keys), 0, length - TILE),
                pos_q,
                pos_k,
            )
            outs.append(out)
            totals.append(total)
        whole = jnp.concatenate(outs + [put_logs(totals)], axis=1)
        back = flag(iota((length, length), 0) == slot_ref[turn, :1, :])
        whole = jnp.concatenate([jnp.zeros((TILE, whole.shape[1]), BF16), whole], axis=0)
        out_ref[turn] = dot(back, whole).astype(BF16)


def attend_first_kernel(
    peers,
    me_ref,
    perms_ref,
    earlier_ref,
    rows_ref,
    last_ref,
    slot_ref,
    later_ref,
    out_ref,
):
    rounds, length = slot_ref.shape[0], slot_ref.shape[2]
    per_peer = length // peers
    span = rows_ref.shape[2] // 2
    lane_group = iota((peers, per_peer, LANES), 2) // GROUP
    own_group = lane_group == iota((peers, per_peer, LANES), 1)
    log_row = iota((peers, GROUP, LANES), 1)
    all_logs = jnp.zeros((peers, GROUP, LANES), F32)
    lane = iota((1, LANES), 1)
    for turn in range(rounds):
        position = perms_ref[turn : turn + 1, :].astype(F32)
        earlier = earlier_ref[turn : turn + 1, :].astype(F32)
        swapped = jnp.concatenate([position[:, BLOCK_LEN:], position[:, :BLOCK_LEN]], axis=1)
        earlier = jnp.concatenate([earlier[:, BLOCK_LEN:], earlier[:, :BLOCK_LEN]], axis=1)
        pos_k = jnp.where(lane < BLOCK_LEN, earlier, swapped)
        pos_q = to_col(position)[:TILE]
        totals, outs = [], []
        for head in range(span // HEAD_DIM):
            at = head * HEAD_DIM
            own = rows_ref[turn, :TILE, at : at + HEAD_DIM]
            keys = jnp.concatenate([last_ref[turn, :, at : at + HEAD_DIM], own], axis=0)
            at = span + at
            values = jnp.concatenate(
                [
                    last_ref[turn, :, at : at + HEAD_DIM],
                    rows_ref[turn, :TILE, at : at + HEAD_DIM],
                ],
                axis=0,
            )
            out, total = attend_blocks(own, keys, values, window_scale(keys), pos_q, pos_k)
            outs.append(out)
            totals.append(total)
        top = jnp.concatenate(outs + [put_logs(totals)], axis=1)
        top = jnp.concatenate([top, jnp.zeros((LANES - TILE, top.shape[1]), BF16)], axis=0)
        back = flag(iota((length, LANES), 0) == slot_ref[turn, :1, :LANES])
        moved = dot(back, top) + later_ref[turn].astype(F32)
        for head in range(span // HEAD_DIM):
            at = (head * rounds + turn) * per_peer
            lanes = moved[:, head * HEAD_DIM : (head + 1) * HEAD_DIM]
            out_ref[:, at : at + per_peer, :] = lanes.astype(BF16).reshape(
                peers, per_peer, HEAD_DIM
            )
        logs = moved[:, span:].reshape(peers, per_peer, LANES)
        logs = jnp.sum(jnp.where(own_group, logs, 0.0), axis=1, keepdims=True)
        all_logs = jnp.where(log_row == turn, logs, all_logs)
    out_ref[:, out_ref.shape[1] - GROUP :, :] = all_logs.astype(BF16)


def attend_later(me, perms, rows, slot):
    rounds, length, width = rows.shape
    span = width // 2
    out = (rounds, length, span + LANES)
    return pl.pallas_call(
        attend_later_kernel,
        grid_spec=pltpu.PrefetchScalarGridSpec(
            num_scalar_prefetch=1,
            grid=(1,),
            in_specs=[
                pl.BlockSpec((rounds, length), lambda i, s: (0, s[0])),
                pl.BlockSpec(rows.shape, lambda i, s: (0, 0, 0)),
                pl.BlockSpec(slot.shape, lambda i, s: (0, 0, 0)),
            ],
            out_specs=pl.BlockSpec(out, lambda i, s: (0, 0, 0)),
        ),
        out_shape=jax.ShapeDtypeStruct(out, BF16),
        cost_estimate=cost(LONG, 4 << 20),
        compiler_params=BIG,
        name="attend_later",
    )(me, perms, rows, slot)


def attend_first(me, perms, rows, last, slot, later, peers):
    rounds, length, width = rows.shape
    span = width // 2
    per_peer = length // peers
    lane_blocks = length // LANES

    def fixed(shape):
        return pl.BlockSpec(shape, lambda i, s: (0, 0, 0))

    out = (peers, span // HEAD_DIM * rounds * per_peer + GROUP, HEAD_DIM)
    return pl.pallas_call(
        functools.partial(attend_first_kernel, peers),
        grid_spec=pltpu.PrefetchScalarGridSpec(
            num_scalar_prefetch=1,
            grid=(1,),
            in_specs=[
                pl.BlockSpec((rounds, LANES), lambda i, s: (0, s[0] * lane_blocks)),
                pl.BlockSpec(
                    (rounds, LANES),
                    lambda i, s: (
                        0,
                        jnp.where(s[0] == 0, peers * lane_blocks - 1, s[0] * lane_blocks - 1),
                    ),
                ),
                fixed((rounds, LANES, width)),
                fixed(last.shape),
                fixed(slot.shape),
                fixed(later.shape),
            ],
            out_specs=fixed(out),
        ),
        out_shape=jax.ShapeDtypeStruct(out, BF16),
        cost_estimate=cost(LONG, 4 << 20),
        compiler_params=BIG,
        name="attend_first",
    )(me, perms, perms, rows, last, slot, later)


def combine_kernel(got_ref, token_ref, mixed_ref):
    peers = got_ref.shape[0]
    rounds, _, length = token_ref.shape
    per_peer = length // peers
    heads = mixed_ref.shape[1] // HEAD_DIM
    lane_group = iota((peers, per_peer, LANES), 2) // GROUP
    own_group = lane_group == iota((peers, per_peer, LANES), 1)
    lane = iota((length, LANES), 1) % GROUP // PIECES
    column = iota((length, length), 0)
    log_row = iota((peers, GROUP, LANES), 1)
    all_logs = got_ref[:, got_ref.shape[1] - GROUP :, :].astype(F32)
    outs, lses = [], []
    for turn in range(rounds):
        pick = flag(token_ref[turn, :1, :] == column)
        logs = jnp.sum(jnp.where(log_row == turn, all_logs, 0.0), axis=1, keepdims=True)
        logs = jnp.where(own_group, logs, 0.0).astype(BF16)
        sides = []
        for head in range(heads):
            at = (head * rounds + turn) * per_peer
            sides.append(got_ref[:, at : at + per_peer, :].reshape(length, HEAD_DIM))
        outs.append(dot(pick, jnp.concatenate(sides, axis=1)))
        moved = dot(pick, logs.reshape(length, LANES))
        lses.append(
            [
                jnp.sum(jnp.where(lane == head, moved, 0.0), axis=1, keepdims=True)
                for head in range(heads)
            ]
        )
    for head in range(heads):
        logs = [lse[head] for lse in lses]
        peak = functools.reduce(jnp.maximum, logs)
        whole = peak + jnp.log(functools.reduce(jnp.add, [jnp.exp(lse - peak) for lse in logs]))
        at = head * HEAD_DIM
        mixed = jnp.zeros((length, HEAD_DIM), F32)
        for out, lse in zip(outs, logs):
            mixed = mixed + out[:, at : at + HEAD_DIM] * jnp.exp(lse - whole)
        mixed_ref[:, at : at + HEAD_DIM] = mixed.astype(BF16)


def combine(got, token, span):
    rounds, _, length = token.shape
    return pl.pallas_call(
        combine_kernel,
        out_shape=jax.ShapeDtypeStruct((length, span), BF16),
        cost_estimate=cost(2 * rounds * length * length * (span + LANES), 1 << 20),
        compiler_params=BIG,
        name="combine",
    )(got, token)


def project_kernel(where_ref, own_ref, prev_ref, next_ref, far_a_ref, far_b_ref, *refs):
    weights, (kept_ref, given_ref) = refs[:-2], refs[-2:]
    far = jnp.concatenate([far_a_ref[...], far_b_ref[...]], axis=0)
    total = dot(own_ref[...], weights[0][...]) + dot(prev_ref[...], weights[1][...])
    total = total + dot(next_ref[...], weights[2][...]) + dot(far, weights[3][...])
    half = kept_ref.shape[1]
    for core in range(EXP_DEV):

        @pl.when(where_ref[1] == core)
        def _(core=core):
            kept_ref[...] = total[:, core * half : (core + 1) * half]
            other = 1 - core
            given_ref[...] = total[:, other * half : (other + 1) * half].astype(BF16)


def project(where, heads, w_out, others):
    length, span = heads[0].shape
    columns = others[0].shape[1]
    half = columns // EXP_DEV
    weights = (w_out, *others)
    shapes = [x.shape for x in heads] + [(span, columns)] + [x.shape for x in others]

    def first(i, e):
        return (0, 0)

    specs = [pl.BlockSpec(shape, first) for shape in shapes]
    specs[len(heads)] = pl.BlockSpec((span, columns), lambda i, e: (0, e[0]))
    return pl.pallas_call(
        project_kernel,
        grid_spec=pltpu.PrefetchScalarGridSpec(
            num_scalar_prefetch=1,
            grid=(1,),
            in_specs=specs,
            out_specs=[pl.BlockSpec((length, half), first)] * 2,
        ),
        out_shape=[
            jax.ShapeDtypeStruct((length, half), F32),
            jax.ShapeDtypeStruct((length, half), BF16),
        ],
        cost_estimate=cost(55 * 10**8, 3 << 20),
        compiler_params=BIG,
        name="project",
    )(where, *heads, *weights)


def exchange(x, axis):
    return lax.all_to_all(x, axis, split_axis=0, concat_axis=0, tiled=True)


def hop(x, by, chips):
    pairs = []
    for chip in range(chips):
        for core in range(EXP_DEV):
            there = (chip + by) % chips
            pairs.append((chip * EXP_DEV + core, there * EXP_DEV + core))
    return lax.ppermute(x, "exp", pairs)


def spread(x, chips, ready=()):
    half = x.shape[0] // 2
    before, behind = hop(x, 1, chips), hop(x, -1, chips)
    before, behind = (after(side, *ready) if ready else side for side in (before, behind))
    far = (hop(before[:half], 1, chips), hop(behind[half:], -1, chips))
    return (x, before, behind), far


def after(x, *done):
    return lax.optimization_barrier((x, *done))[0]


def body(x_att, w_qk, w_val, w_out, perms, tokens_b, expert_ids, w_gate, w_up, w_down):
    peers, parts = lax.axis_size("seq"), lax.axis_size("exp")
    chips = parts // EXP_DEV
    me = lax.axis_index("seq").astype(I32).reshape(1)
    my_exp = lax.axis_index("exp").astype(I32)
    core = my_exp % EXP_DEV
    where = jnp.stack([my_exp // EXP_DEV, core])
    length, width = x_att.shape
    rounds = perms.shape[0]
    per_peer = length // peers
    tokb = tokens_b.shape[0]
    capacity = tokb // peers
    part = width // chips
    lines = [[chip * EXP_DEV + side for chip in range(chips)] for side in range(EXP_DEV)]
    siblings = [(i, i ^ 1) for i in range(parts)]

    dispatch, token_slot = pack_tokens(
        where, expert_ids.reshape(1, tokb), tokens_b, peers, capacity, part
    )
    received = exchange(dispatch.reshape(peers, capacity, part), "seq")
    outgoing, slot_token = pack_rows(me, perms, x_att, w_qk, w_val)
    def columns_of(by, *ready):
        start = (where[0] + by) % chips * part
        return hop(lax.dynamic_slice_in_dim(after(w_out, *ready), start, part, 1), by, chips)

    near = [columns_of(by, dispatch) for by in (1, chips - 1)]
    received = after(received, outgoing, *near)
    outgoing = after(outgoing, received)
    own = (w_gate, w_up, w_down)
    sibling = [lax.ppermute(after(weight, received), "exp", siblings) for weight in own]
    shards, far_shards = spread(received, chips)
    arrived = exchange(outgoing.reshape(peers, rounds * per_peer, outgoing.shape[1]), "seq")
    far = columns_of(2, *far_shards)
    expert_part = run_experts(where, shards, far_shards, own, sibling)
    arrived = after(arrived, expert_part, far)
    rows, last, row_slot = sort_rows(me, perms, arrived, length)
    expert_rows = lax.psum_scatter(
        expert_part,
        "exp",
        scatter_dimension=0,
        tiled=False,
        axis_index_groups=lines,
    )
    last = lax.ppermute(last, "seq", [(i, (i + 1) % peers) for i in range(peers)])
    later = attend_later(me, perms, rows, row_slot)
    last = after(last, later)
    packed = attend_first(me, perms, rows, last, row_slot, later, peers)
    got = exchange(packed, "seq")
    expert_rows = after(expert_rows, packed)
    taken = lax.ppermute(expert_rows[1], "exp", siblings)
    expert_rows = place_rows(expert_rows, taken)
    mixed_heads = combine(after(got, expert_rows), slot_token, w_qk.shape[1])
    expert_back = exchange(after(expert_rows, mixed_heads), "seq")
    heads, far_heads = spread(mixed_heads, chips)
    attn_kept, attn_given = project(where, (*heads, *far_heads), w_out, (*near, far))
    attn_taken = lax.ppermute(attn_given, "exp", siblings)
    expert_back = after(expert_back, attn_taken)
    return finish(
        expert_back.reshape(peers * EXP_DEV * capacity, width // parts),
        token_slot,
        attn_kept,
        attn_taken,
    )


def solution(mesh):
    in_specs = (
        P("seq", None),
        P(None, "exp"),
        P(None, "exp"),
        P("exp", None),
        P(),
        P("seq", None),
        P("seq", None),
        P("seq", None, "exp"),
        P("seq", None, "exp"),
        P("seq", "exp", None),
    )
    out_specs = (P("seq", "exp"), P("seq", "exp"))
    return jax.shard_map(body, mesh=mesh, in_specs=in_specs, out_specs=out_specs, check_vma=False)
```

```python
import functools
import math

import jax
import jax.numpy as jnp
from jax import lax
from jax.experimental import pallas as pl
from jax.experimental.pallas import tpu as pltpu
from jax.sharding import PartitionSpec as P

HEAD_DIM = 128
BLOCK_LEN = 64
EXP_DEV = 2
LANES = 128
F32, BF16, I32 = jnp.float32, jnp.bfloat16, jnp.int32
LONG = 1 << 35
BIG = pltpu.CompilerParams(vmem_limit_bytes=48 * 1024 * 1024)


def dot(a, b):
    return jnp.dot(a, b, preferred_element_type=F32)


def dot_t(a, b):
    return lax.dot_general(a, b, (((1,), (1,)), ((), ())), preferred_element_type=F32)


def to_col(row):
    return jnp.broadcast_to(row, (LANES, row.shape[1])).T[:, :1]


def to_row(col):
    return jnp.broadcast_to(col, (col.shape[0], LANES)).T[:1, :]


def iota(shape, dim):
    return lax.broadcasted_iota(I32, shape, dim)


def flag(mask, kind=BF16):
    return jnp.where(mask, 1.0, 0.0).astype(kind)


def cost(flops, size):
    return pl.CostEstimate(flops=flops, bytes_accessed=size, transcendentals=0)


def upper(count):
    return flag(iota((count, count), 0) <= iota((count, count), 1))


def pack_rows_kernel(me_ref, perms_ref, x_ref, qk_ref, val_ref, out_ref, token_ref, scratch):
    length, span = x_ref.shape[0], qk_ref.shape[1]
    rounds, total = perms_ref.shape
    peers = total // length
    per_peer = length // peers
    for peer in range(peers):
        scratch[peer * rounds : (peer + 1) * rounds, :] = perms_ref[
            :, peer * length : (peer + 1) * length
        ]
    perms = scratch[...]
    token = perms & (length - 1)
    mine = (perms >> (length.bit_length() - 1)) == me_ref[0]
    rank = dot(flag(mine), upper(length)).astype(I32) - 1
    slot = jnp.where(mine, rank, -1)
    groups = peers * rounds
    chosen = slot[:, None, :] == iota((groups, per_peer, length), 1)
    token_3d = jnp.where(chosen, token.astype(F32)[:, None, :], 0.0)
    column = jnp.sum(token_3d, axis=-1, keepdims=True).reshape(groups * per_peer, 1)
    by_round = column.reshape(peers, rounds, per_peer, 1)
    for turn in range(rounds):
        row = to_row(by_round[:, turn].reshape(peers * per_peer, 1)).astype(I32)
        token_ref[turn] = jnp.broadcast_to(row, token_ref.shape[1:])
    pick = flag(column.astype(I32) == iota((groups * per_peer, length), 1))
    for part, weight in enumerate((qk_ref, val_ref)):
        rows = dot(x_ref[...], weight[...]).astype(BF16)
        out_ref[:, part * span : (part + 1) * span] = dot(pick, rows).astype(BF16)


def pack_rows(me, perms, x_att, w_qk, w_val):
    length, width = x_att.shape
    rounds, total = perms.shape
    span = w_qk.shape[1]
    groups = rounds * (total // length)
    slots = rounds * length

    def whole(shape):
        return pl.BlockSpec(shape, lambda i, me_ref: (0, 0))

    return pl.pallas_call(
        pack_rows_kernel,
        grid_spec=pltpu.PrefetchScalarGridSpec(
            num_scalar_prefetch=1,
            grid=(1,),
            in_specs=[
                whole((rounds, total)),
                whole((length, width)),
                whole((width, span)),
                whole((width, span)),
            ],
            out_specs=[
                whole((slots, 2 * span)),
                pl.BlockSpec((rounds, 8, length), lambda i, me_ref: (0, 0, 0)),
            ],
            scratch_shapes=[pltpu.VMEM((groups, length), I32)],
        ),
        out_shape=[
            jax.ShapeDtypeStruct((slots, 2 * span), BF16),
            jax.ShapeDtypeStruct((rounds, 8, length), I32),
        ],
        cost_estimate=cost(4 * length * width * span + 4 * slots * length * span, 6 << 20),
        compiler_params=BIG,
        name="pack_rows",
    )(me, perms, x_att, w_qk, w_val)


def pack_tokens_kernel(
    peers, where_ref, ids_ref, tokens_ref, out_ref, slot_ref, mine_ref, copied
):
    length = tokens_ref.shape[0]
    slots, part = out_ref.shape
    columns = pl.ds(pl.multiple_of(where_ref[0] * part, part), part)
    copy = pltpu.make_async_copy(tokens_ref.at[:, columns], mine_ref, copied)
    copy.start()
    capacity = slots // peers
    experts = EXP_DEV * peers
    ids = ids_ref[...]
    hot = ids == iota((experts, length), 0)
    counts = dot(flag(hot), upper(length))
    rank = jnp.sum(jnp.where(hot, counts, 0.0), axis=0, keepdims=True).astype(I32) - 1
    core = where_ref[1]
    turn = (ids % EXP_DEV + core) % EXP_DEV
    peer = ids // EXP_DEV
    slot_ref[...] = jnp.broadcast_to(
        (peer * EXP_DEV + turn) * capacity + rank, slot_ref.shape
    )
    slot = jnp.where(turn == 0, peer * capacity + rank, -1)
    pick = flag(iota((slots, length), 0) == slot)
    copy.wait()
    out_ref[...] = dot(pick, mine_ref[...]).astype(BF16)


def pack_tokens(where, ids, tokens, peers, capacity, part):
    length = tokens.shape[0]
    slots = peers * capacity
    return pl.pallas_call(
        functools.partial(pack_tokens_kernel, peers),
        grid_spec=pltpu.PrefetchScalarGridSpec(
            num_scalar_prefetch=1,
            grid=(1,),
            in_specs=[
                pl.BlockSpec((1, length), lambda i, e: (0, 0)),
                pl.BlockSpec(memory_space=pltpu.HBM),
            ],
            out_specs=[
                pl.BlockSpec((slots, part), lambda i, e: (0, 0)),
                pl.BlockSpec((8, length), lambda i, e: (0, 0)),
            ],
            scratch_shapes=[pltpu.VMEM((length, part), BF16), pltpu.SemaphoreType.DMA],
        ),
        out_shape=[
            jax.ShapeDtypeStruct((slots, part), BF16),
            jax.ShapeDtypeStruct((8, length), I32),
        ],
        cost_estimate=cost(2 * slots * length * part, 2 << 20),
        compiler_params=BIG,
        name="pack_tokens",
    )(where, ids, tokens)


def experts_kernel(where_ref, *refs):
    step = pl.program_id(0)
    shards, far_refs, weights = refs[0:3], refs[3:5], refs[5:11]
    out_ref, total_ref = refs[11:]
    peers, capacity, part = shards[0].shape
    rows = peers * capacity
    ups = (weights[0], weights[1], weights[3], weights[4])

    def add(x, start):
        for index, weight in enumerate(ups):
            product = dot(x, weight[0])
            total_ref[index] = product if start else total_ref[index] + product

    for turn, shard in enumerate(shards):

        @pl.when(step == turn)
        def _(shard=shard, start=turn == 0):
            add(shard[...].reshape(rows, part), start)

    @pl.when(step == len(shards))
    def _():
        add(jnp.concatenate([ref[...].reshape(rows // 2, part) for ref in far_refs], axis=0), False)
        hiddens = []
        for side in range(EXP_DEV):
            gate, up_val = total_ref[2 * side], total_ref[2 * side + 1]
            hiddens.append((gate / (1.0 + jnp.exp(-gate)) * up_val).astype(BF16))
        half = part // EXP_DEV
        for index in range(out_ref.shape[0]):
            at = index * part
            piece = dot(hiddens[0], weights[2][0, :, at : at + part])
            piece = (piece + dot(hiddens[1], weights[5][0, :, at : at + part])).astype(BF16)
            for side in range(EXP_DEV):
                columns = piece[:, side * half : (side + 1) * half]
                turn = (side + where_ref[1]) % EXP_DEV
                out_ref[index, turn] = columns.reshape(peers, capacity, half)


def run_experts(where, shards, far, own, sibling):
    peers, capacity, part = shards[0].shape
    width, hidden = own[0].shape[1:]
    chips = width // part
    out = (chips, EXP_DEV, peers, capacity, part // EXP_DEV)
    rows = peers * capacity

    def rows_of(i, e):
        ahead = jnp.where(i == 0, 0, jnp.where(i == 1, chips - 1, jnp.where(i == 2, 1, 2)))
        return (e[0] + ahead) % chips

    up_block, down_block = (1, part, hidden), (1, hidden, width)
    own_up = pl.BlockSpec(up_block, lambda i, e: (e[1], rows_of(i, e), 0))
    own_down = pl.BlockSpec(down_block, lambda i, e: (e[1], 0, 0))
    return pl.pallas_call(
        experts_kernel,
        grid_spec=pltpu.PrefetchScalarGridSpec(
            num_scalar_prefetch=1,
            grid=(len(shards) + 1,),
            in_specs=[pl.BlockSpec(x.shape, lambda i, e: (0, 0, 0)) for x in (*shards, *far)]
            + [own_up, own_up, own_down] * 2,
            out_specs=pl.BlockSpec(out, lambda i, e: (0, 0, 0, 0, 0)),
            scratch_shapes=[pltpu.VMEM((4, rows, hidden), F32)],
        ),
        out_shape=jax.ShapeDtypeStruct(out, BF16),
        cost_estimate=cost(15 * 10**9, 10 << 20),
        compiler_params=BIG,
        name="experts",
    )(where, *shards, *far, *own, *sibling)


def place_rows_kernel(rows_ref, taken_ref, out_ref, copied):
    copies = (
        pltpu.make_async_copy(rows_ref.at[0], out_ref.at[:, 0], copied.at[0]),
        pltpu.make_async_copy(taken_ref, out_ref.at[:, 1], copied.at[1]),
    )
    for copy in copies:
        copy.start()
    for copy in copies:
        copy.wait()


def place_rows(rows, taken):
    peers, capacity, half = taken.shape
    return pl.pallas_call(
        place_rows_kernel,
        in_specs=[pl.BlockSpec(memory_space=pltpu.HBM)] * 2,
        out_specs=pl.BlockSpec(memory_space=pltpu.HBM),
        out_shape=jax.ShapeDtypeStruct((peers, EXP_DEV, capacity, half), BF16),
        scratch_shapes=[pltpu.SemaphoreType.DMA((2,))],
        cost_estimate=cost(1 << 20, 1 << 20),
        compiler_params=BIG,
        name="place_rows",
    )(rows, taken)


def finish_kernel(back_ref, slot_ref, kept_ref, taken_ref, attended_ref, mixed_ref):
    length = mixed_ref.shape[0]
    column = to_col(slot_ref[:1, :].astype(F32)).astype(I32)
    pick = flag(column == iota((length, back_ref.shape[0]), 1))
    mixed_ref[...] = dot(pick, back_ref[...]).astype(BF16)
    attended_ref[...] = (kept_ref[...] + taken_ref[...].astype(F32)).astype(BF16)


def finish(back, slot, kept, taken):
    length, width = slot.shape[1], back.shape[1]
    return pl.pallas_call(
        finish_kernel,
        out_shape=[
            jax.ShapeDtypeStruct(kept.shape, BF16),
            jax.ShapeDtypeStruct((length, width), BF16),
        ],
        cost_estimate=cost(2 * length * back.shape[0] * width, 1 << 20),
        compiler_params=BIG,
        name="finish",
    )(back, slot, kept, taken)


def sort_rows_kernel(peers, me_ref, perms_ref, arrived_ref, rows_ref, last_ref, slot_ref):
    rounds, length = perms_ref.shape
    per_peer = length // peers
    for turn in range(rounds):
        source = perms_ref[turn : turn + 1, :] >> (length.bit_length() - 1)
        hot = source == iota((peers, length), 0)
        counts = dot(flag(hot), upper(length))
        rank = jnp.sum(jnp.where(hot, counts, 0.0), axis=0, keepdims=True) - 1.0
        slot = source * per_peer + rank.astype(I32)
        slot_ref[turn] = jnp.broadcast_to(slot, slot_ref.shape[1:])
        pick = flag(to_col(slot.astype(F32)).astype(I32) == iota((length, length), 1))
        have = arrived_ref[:, turn * per_peer : (turn + 1) * per_peer, :]
        rows = dot(pick, have.reshape(length, have.shape[2])).astype(BF16)
        rows_ref[turn] = rows
        last_ref[turn] = rows[length - BLOCK_LEN :]


def sort_rows(me, perms, arrived, length):
    rounds = perms.shape[0]
    peers, _, width = arrived.shape
    return pl.pallas_call(
        functools.partial(sort_rows_kernel, peers),
        grid_spec=pltpu.PrefetchScalarGridSpec(
            num_scalar_prefetch=1,
            grid=(1,),
            in_specs=[
                pl.BlockSpec((rounds, length), lambda i, s: (0, s[0])),
                pl.BlockSpec(arrived.shape, lambda i, s: (0, 0, 0)),
            ],
            out_specs=[
                pl.BlockSpec((rounds, length, width), lambda i, s: (0, 0, 0)),
                pl.BlockSpec((rounds, BLOCK_LEN, width), lambda i, s: (0, 0, 0)),
                pl.BlockSpec((rounds, 8, length), lambda i, s: (0, 0, 0)),
            ],
        ),
        out_shape=[
            jax.ShapeDtypeStruct((rounds, length, width), BF16),
            jax.ShapeDtypeStruct((rounds, BLOCK_LEN, width), BF16),
            jax.ShapeDtypeStruct((rounds, 8, length), I32),
        ],
        cost_estimate=cost(LONG, 4 << 20),
        compiler_params=BIG,
        name="sort_rows",
    )(me, perms, arrived)


def window_scale(keys):
    wide = keys.astype(F32)
    squares = jnp.sum(wide * wide, axis=-1, keepdims=True)
    return to_row(lax.rsqrt(squares + 1e-06) / math.sqrt(HEAD_DIM))


def windows(row, first, last):
    moved = jnp.concatenate([row[:, BLOCK_LEN:], row[:, :BLOCK_LEN]], axis=1)
    spans = []
    for start in range(first, last, BLOCK_LEN):
        odd = start % LANES
        span = (moved if odd else row)[:, start - odd : start - odd + WINDOW]
        spans.append(jnp.broadcast_to(span, (BLOCK_LEN, WINDOW)))
    return jnp.concatenate(spans, axis=0)


def attend_blocks(queries, keys, values, scale, pos_q, pos_k):
    starts = range(0, queries.shape[0], BLOCK_LEN)
    scores = jnp.concatenate(
        [dot_t(queries[at : at + BLOCK_LEN], keys[at : at + WINDOW]) for at in starts], axis=0
    )
    scores = scores * scale
    scores = jnp.where(pos_k == pos_q, scores - 10000.0, scores)
    scores = jnp.where(pos_k <= pos_q, scores, -1e30)
    peak = jnp.max(scores, axis=-1, keepdims=True)
    exponent = jnp.exp(scores - peak)
    total = jnp.sum(exponent, axis=-1, keepdims=True)
    weights = (exponent / total).astype(BF16)
    outs = [dot(weights[at : at + BLOCK_LEN], values[at : at + WINDOW]) for at in starts]
    return jnp.concatenate(outs, axis=0).astype(BF16), peak + jnp.log(total)


TILE, WINDOW, PIECES, GROUP = BLOCK_LEN, 2 * BLOCK_LEN, 3, 8


def put_logs(totals):
    lane = iota((totals[0].shape[0], LANES), 1) % GROUP
    logs = jnp.zeros(lane.shape, F32)
    for head, total in enumerate(totals):
        rest = total
        for piece in range(PIECES):
            part = rest.astype(BF16).astype(F32)
            logs = jnp.where(lane == head * PIECES + piece, part, logs)
            rest = rest - part
    return logs.astype(BF16)


def attend_later_kernel(me_ref, perms_ref, rows_ref, slot_ref, out_ref):
    rounds, length = perms_ref.shape
    span = rows_ref.shape[2] // 2
    for turn in range(rounds):
        position = perms_ref[turn : turn + 1, :].astype(F32)
        pos_q = to_col(position)[TILE:]
        pos_k = windows(position, 0, length - TILE)
        outs, totals = [], []
        for head in range(span // HEAD_DIM):
            at = head * HEAD_DIM
            keys = rows_ref[turn, :, at : at + HEAD_DIM]
            out, total = attend_blocks(
                keys[TILE:],
                keys,
                rows_ref[turn, :, span + at : span + at + HEAD_DIM],
                windows(window_scale(keys), 0, length - TILE),
                pos_q,
                pos_k,
            )
            outs.append(out)
            totals.append(total)
        whole = jnp.concatenate(outs + [put_logs(totals)], axis=1)
        back = flag(iota((length, length), 0) == slot_ref[turn, :1, :])
        whole = jnp.concatenate([jnp.zeros((TILE, whole.shape[1]), BF16), whole], axis=0)
        out_ref[turn] = dot(back, whole).astype(BF16)


def attend_first_kernel(
    peers,
    me_ref,
    perms_ref,
    earlier_ref,
    rows_ref,
    last_ref,
    slot_ref,
    later_ref,
    out_ref,
):
    rounds, length = slot_ref.shape[0], slot_ref.shape[2]
    per_peer = length // peers
    span = rows_ref.shape[2] // 2
    lane_group = iota((peers, per_peer, LANES), 2) // GROUP
    own_group = lane_group == iota((peers, per_peer, LANES), 1)
    log_row = iota((peers, GROUP, LANES), 1)
    all_logs = jnp.zeros((peers, GROUP, LANES), F32)
    lane = iota((1, LANES), 1)
    for turn in range(rounds):
        position = perms_ref[turn : turn + 1, :].astype(F32)
        earlier = earlier_ref[turn : turn + 1, :].astype(F32)
        swapped = jnp.concatenate([position[:, BLOCK_LEN:], position[:, :BLOCK_LEN]], axis=1)
        earlier = jnp.concatenate([earlier[:, BLOCK_LEN:], earlier[:, :BLOCK_LEN]], axis=1)
        pos_k = jnp.where(lane < BLOCK_LEN, earlier, swapped)
        pos_q = to_col(position)[:TILE]
        totals, outs = [], []
        for head in range(span // HEAD_DIM):
            at = head * HEAD_DIM
            own = rows_ref[turn, :TILE, at : at + HEAD_DIM]
            keys = jnp.concatenate([last_ref[turn, :, at : at + HEAD_DIM], own], axis=0)
            at = span + at
            values = jnp.concatenate(
                [
                    last_ref[turn, :, at : at + HEAD_DIM],
                    rows_ref[turn, :TILE, at : at + HEAD_DIM],
                ],
                axis=0,
            )
            out, total = attend_blocks(own, keys, values, window_scale(keys), pos_q, pos_k)
            outs.append(out)
            totals.append(total)
        top = jnp.concatenate(outs + [put_logs(totals)], axis=1)
        top = jnp.concatenate([top, jnp.zeros((LANES - TILE, top.shape[1]), BF16)], axis=0)
        back = flag(iota((length, LANES), 0) == slot_ref[turn, :1, :LANES])
        moved = dot(back, top) + later_ref[turn].astype(F32)
        for head in range(span // HEAD_DIM):
            at = (head * rounds + turn) * per_peer
            lanes = moved[:, head * HEAD_DIM : (head + 1) * HEAD_DIM]
            out_ref[:, at : at + per_peer, :] = lanes.astype(BF16).reshape(
                peers, per_peer, HEAD_DIM
            )
        logs = moved[:, span:].reshape(peers, per_peer, LANES)
        logs = jnp.sum(jnp.where(own_group, logs, 0.0), axis=1, keepdims=True)
        all_logs = jnp.where(log_row == turn, logs, all_logs)
    out_ref[:, out_ref.shape[1] - GROUP :, :] = all_logs.astype(BF16)


def attend_later(me, perms, rows, slot):
    rounds, length, width = rows.shape
    span = width // 2
    out = (rounds, length, span + LANES)
    return pl.pallas_call(
        attend_later_kernel,
        grid_spec=pltpu.PrefetchScalarGridSpec(
            num_scalar_prefetch=1,
            grid=(1,),
            in_specs=[
                pl.BlockSpec((rounds, length), lambda i, s: (0, s[0])),
                pl.BlockSpec(rows.shape, lambda i, s: (0, 0, 0)),
                pl.BlockSpec(slot.shape, lambda i, s: (0, 0, 0)),
            ],
            out_specs=pl.BlockSpec(out, lambda i, s: (0, 0, 0)),
        ),
        out_shape=jax.ShapeDtypeStruct(out, BF16),
        cost_estimate=cost(LONG, 4 << 20),
        compiler_params=BIG,
        name="attend_later",
    )(me, perms, rows, slot)


def attend_first(me, perms, rows, last, slot, later, peers):
    rounds, length, width = rows.shape
    span = width // 2
    per_peer = length // peers
    lane_blocks = length // LANES

    def fixed(shape):
        return pl.BlockSpec(shape, lambda i, s: (0, 0, 0))

    out = (peers, span // HEAD_DIM * rounds * per_peer + GROUP, HEAD_DIM)
    return pl.pallas_call(
        functools.partial(attend_first_kernel, peers),
        grid_spec=pltpu.PrefetchScalarGridSpec(
            num_scalar_prefetch=1,
            grid=(1,),
            in_specs=[
                pl.BlockSpec((rounds, LANES), lambda i, s: (0, s[0] * lane_blocks)),
                pl.BlockSpec(
                    (rounds, LANES),
                    lambda i, s: (
                        0,
                        jnp.where(s[0] == 0, peers * lane_blocks - 1, s[0] * lane_blocks - 1),
                    ),
                ),
                fixed((rounds, LANES, width)),
                fixed(last.shape),
                fixed(slot.shape),
                fixed(later.shape),
            ],
            out_specs=fixed(out),
        ),
        out_shape=jax.ShapeDtypeStruct(out, BF16),
        cost_estimate=cost(LONG, 4 << 20),
        compiler_params=BIG,
        name="attend_first",
    )(me, perms, perms, rows, last, slot, later)


def combine_kernel(got_ref, token_ref, mixed_ref):
    peers = got_ref.shape[0]
    rounds, _, length = token_ref.shape
    per_peer = length // peers
    heads = mixed_ref.shape[1] // HEAD_DIM
    lane_group = iota((peers, per_peer, LANES), 2) // GROUP
    own_group = lane_group == iota((peers, per_peer, LANES), 1)
    lane = iota((length, LANES), 1) % GROUP // PIECES
    column = iota((length, length), 0)
    log_row = iota((peers, GROUP, LANES), 1)
    all_logs = got_ref[:, got_ref.shape[1] - GROUP :, :].astype(F32)
    outs, lses = [], []
    for turn in range(rounds):
        pick = flag(token_ref[turn, :1, :] == column)
        logs = jnp.sum(jnp.where(log_row == turn, all_logs, 0.0), axis=1, keepdims=True)
        logs = jnp.where(own_group, logs, 0.0).astype(BF16)
        sides = []
        for head in range(heads):
            at = (head * rounds + turn) * per_peer
            sides.append(got_ref[:, at : at + per_peer, :].reshape(length, HEAD_DIM))
        outs.append(dot(pick, jnp.concatenate(sides, axis=1)))
        moved = dot(pick, logs.reshape(length, LANES))
        lses.append(
            [
                jnp.sum(jnp.where(lane == head, moved, 0.0), axis=1, keepdims=True)
                for head in range(heads)
            ]
        )
    for head in range(heads):
        logs = [lse[head] for lse in lses]
        peak = functools.reduce(jnp.maximum, logs)
        whole = peak + jnp.log(functools.reduce(jnp.add, [jnp.exp(lse - peak) for lse in logs]))
        at = head * HEAD_DIM
        mixed = jnp.zeros((length, HEAD_DIM), F32)
        for out, lse in zip(outs, logs):
            mixed = mixed + out[:, at : at + HEAD_DIM] * jnp.exp(lse - whole)
        mixed_ref[:, at : at + HEAD_DIM] = mixed.astype(BF16)


def combine(got, token, span):
    rounds, _, length = token.shape
    return pl.pallas_call(
        combine_kernel,
        out_shape=jax.ShapeDtypeStruct((length, span), BF16),
        cost_estimate=cost(2 * rounds * length * length * (span + LANES), 1 << 20),
        compiler_params=BIG,
        name="combine",
    )(got, token)


def project_kernel(where_ref, own_ref, prev_ref, next_ref, far_a_ref, far_b_ref, *refs):
    weights, (kept_ref, given_ref) = refs[:-2], refs[-2:]
    far = jnp.concatenate([far_a_ref[...], far_b_ref[...]], axis=0)
    total = dot(own_ref[...], weights[0][...]) + dot(prev_ref[...], weights[1][...])
    total = total + dot(next_ref[...], weights[2][...]) + dot(far, weights[3][...])
    half = kept_ref.shape[1]
    for core in range(EXP_DEV):

        @pl.when(where_ref[1] == core)
        def _(core=core):
            kept_ref[...] = total[:, core * half : (core + 1) * half]
            other = 1 - core
            given_ref[...] = total[:, other * half : (other + 1) * half].astype(BF16)


def project(where, heads, w_out, others):
    length, span = heads[0].shape
    columns = others[0].shape[1]
    half = columns // EXP_DEV
    weights = (w_out, *others)
    shapes = [x.shape for x in heads] + [(span, columns)] + [x.shape for x in others]

    def first(i, e):
        return (0, 0)

    specs = [pl.BlockSpec(shape, first) for shape in shapes]
    specs[len(heads)] = pl.BlockSpec((span, columns), lambda i, e: (0, e[0]))
    return pl.pallas_call(
        project_kernel,
        grid_spec=pltpu.PrefetchScalarGridSpec(
            num_scalar_prefetch=1,
            grid=(1,),
            in_specs=specs,
            out_specs=[pl.BlockSpec((length, half), first)] * 2,
        ),
        out_shape=[
            jax.ShapeDtypeStruct((length, half), F32),
            jax.ShapeDtypeStruct((length, half), BF16),
        ],
        cost_estimate=cost(55 * 10**8, 3 << 20),
        compiler_params=BIG,
        name="project",
    )(where, *heads, *weights)


def exchange(x, axis):
    return lax.all_to_all(x, axis, split_axis=0, concat_axis=0, tiled=True)


def hop(x, by, chips):
    pairs = []
    for chip in range(chips):
        for core in range(EXP_DEV):
            there = (chip + by) % chips
            pairs.append((chip * EXP_DEV + core, there * EXP_DEV + core))
    return lax.ppermute(x, "exp", pairs)


def spread(x, chips, ready=()):
    half = x.shape[0] // 2
    before, behind = hop(x, 1, chips), hop(x, -1, chips)
    before, behind = (after(side, *ready) if ready else side for side in (before, behind))
    far = (hop(before[:half], 1, chips), hop(behind[half:], -1, chips))
    return (x, before, behind), far


def after(x, *done):
    return lax.optimization_barrier((x, *done))[0]


def body(x_att, w_qk, w_val, w_out, perms, tokens_b, expert_ids, w_gate, w_up, w_down):
    peers, parts = lax.axis_size("seq"), lax.axis_size("exp")
    chips = parts // EXP_DEV
    me = lax.axis_index("seq").astype(I32).reshape(1)
    my_exp = lax.axis_index("exp").astype(I32)
    core = my_exp % EXP_DEV
    where = jnp.stack([my_exp // EXP_DEV, core])
    length, width = x_att.shape
    rounds = perms.shape[0]
    per_peer = length // peers
    tokb = tokens_b.shape[0]
    capacity = tokb // peers
    part = width // chips
    lines = [[chip * EXP_DEV + side for chip in range(chips)] for side in range(EXP_DEV)]
    siblings = [(i, i ^ 1) for i in range(parts)]

    dispatch, token_slot = pack_tokens(
        where, expert_ids.reshape(1, tokb), tokens_b, peers, capacity, part
    )
    received = exchange(dispatch.reshape(peers, capacity, part), "seq")
    outgoing, slot_token = pack_rows(me, perms, x_att, w_qk, w_val)
    def columns_of(by, *ready):
        start = (where[0] + by) % chips * part
        return hop(lax.dynamic_slice_in_dim(after(w_out, *ready), start, part, 1), by, chips)

    near = [columns_of(by, dispatch) for by in (1, chips - 1)]
    received = after(received, outgoing, *near)
    outgoing = after(outgoing, received)
    own = (w_gate, w_up, w_down)
    sibling = [lax.ppermute(after(weight, received), "exp", siblings) for weight in own]
    shards, far_shards = spread(received, chips)
    arrived = exchange(outgoing.reshape(peers, rounds * per_peer, outgoing.shape[1]), "seq")
    far = columns_of(2, *far_shards)
    expert_part = run_experts(where, shards, far_shards, own, sibling)
    arrived = after(arrived, expert_part, far)
    rows, last, row_slot = sort_rows(me, perms, arrived, length)
    expert_rows = lax.psum_scatter(
        expert_part,
        "exp",
        scatter_dimension=0,
        tiled=False,
        axis_index_groups=lines,
    )
    last = lax.ppermute(last, "seq", [(i, (i + 1) % peers) for i in range(peers)])
    later = attend_later(me, perms, rows, row_slot)
    last = after(last, later)
    packed = attend_first(me, perms, rows, last, row_slot, later, peers)
    got = exchange(packed, "seq")
    expert_rows = after(expert_rows, packed)
    taken = lax.ppermute(expert_rows[1], "exp", siblings)
    expert_rows = place_rows(expert_rows, taken)
    mixed_heads = combine(got, slot_token, w_qk.shape[1])
    expert_back = exchange(after(expert_rows, mixed_heads), "seq")
    heads, far_heads = spread(mixed_heads, chips)
    attn_kept, attn_given = project(where, (*heads, *far_heads), w_out, (*near, far))
    attn_taken = lax.ppermute(attn_given, "exp", siblings)
    expert_back = after(expert_back, attn_taken)
    return finish(
        expert_back.reshape(peers * EXP_DEV * capacity, width // parts),
        token_slot,
        attn_kept,
        attn_taken,
    )


def solution(mesh):
    in_specs = (
        P("seq", None),
        P(None, "exp"),
        P(None, "exp"),
        P("exp", None),
        P(),
        P("seq", None),
        P("seq", None),
        P("seq", None, "exp"),
        P("seq", None, "exp"),
        P("seq", "exp", None),
    )
    out_specs = (P("seq", "exp"), P("seq", "exp"))
    return jax.shard_map(body, mesh=mesh, in_specs=in_specs, out_specs=out_specs, check_vma=False)
```
